32 devices in a mesh: groups: 2 (over y), pool: 4 (over z), tensor: 2 (over x), sub: 2 (over core).
Axes of the slice: x: 2, y: 2, z: 4, core: 2. Of those that a mesh axis runs over, the one named last changes fastest.
Arguments:
- queries: bfloat16 [8, 160, 8192], P(('groups', 'pool'), None, ('tensor', 'sub')), parts along dimension 0, may hold values from -16 to 16
- new_keys: bfloat16 [8, 160, 1024], P(('groups', 'pool'), None, ('tensor', 'sub')), parts along dimension 0, may hold values from -9.6 to 9.6
- new_values: bfloat16 [8, 160, 1024], P(('groups', 'pool'), None, ('tensor', 'sub')), parts along dimension 0, may hold values from -6 to 6
- store_keys: bfloat16 [256, 256, 1024], P(('groups', 'pool'), None, ('tensor', 'sub')), parts along dimension 0, may hold values from -9.5625 to 9.5625
- store_values: bfloat16 [256, 256, 1024], P(('groups', 'pool'), None, ('tensor', 'sub')), parts along dimension 0, may hold values from -6 to 6
- prefix_blocks: int32 [8], P('groups'), parts along dimension 0, may hold values from 8 to 32, as said below
- hit_store: int32 [8, 32], P('groups'), parts along dimension 0, may hold values from 0 to 3, as said below
- hit_slot: int32 [8, 32], P('groups'), parts along dimension 0, may hold values from 0 to 31, as said below
- decode_owner: int32 [8], P('groups'), parts along dimension 0, may hold values from 0 to 3, as said below
Outputs:
- attended: bfloat16 [8, 160, 8192], P(('groups', 'pool'), None, ('tensor', 'sub')), parts along dimension 0
- pushed_keys: bfloat16 [16, 160, 1024], P(('groups', 'pool'), None, ('tensor', 'sub')), parts along dimension 0
- pushed_values: bfloat16 [16, 160, 1024], P(('groups', 'pool'), None, ('tensor', 'sub')), parts along dimension 0
The draws below stay inside these ranges and needn't reach their ends.
There are 2 independent parts, one for each index of `groups`. The reference program is written for one: setup_inputs(seed, part) draws one part's arguments, and reference() takes and returns one part's arrays. A program takes and returns all parts, laid end to end along the dimension named above; each array names one. Nothing has to cross between parts.
Inputs may be any that keep to these rules, and one draw needn't show every extreme that they name: `prefix_blocks`: some request has exactly 32 cached blocks. `hit_store`: consecutive blocks of a request lie on store devices of consecutive index, wrapping around, so one store device holds at most 8 blocks of a request, and the request with 32 blocks puts exactly 8 on some store device. Entries past a request's count mean nothing. `hit_slot`: the cached blocks held by one store device occupy distinct slots. Entries past a request's count mean nothing. `decode_owner`: no instance decodes more than 2 requests, and some instance decodes exactly 2.
All inputs are finite; a program needn't handle non-finite values.
Results may differ from the reference program's by a relative error of at most 0.004.
Values may be sent and summed in bfloat16 or wider, within the bound.
No kernel may reach another device: no remote copies, remote signals or barrier semaphores. Data moves between devices by JAX's collectives and lax.ppermute only.
A program may use at most 128 MiB of HBM per device.

```python
import math
import jax
import jax.numpy as jnp
from jax import lax

HEADS = 64
KVH = 8
HD = 128
NEW = 160
BLOCK = 256
MAXBLK = 32
MINBLK = 8
CAPP = 2
REQUESTS = 4
SLOTS = 32
STORE = 128
N_POOL = 4


def block_layout(key):
    count_key, pick_key, shift_key, perm_key, spare_key, order_key, unused_key = jax.random.split(key, 7)
    request_ids = jnp.arange(REQUESTS)
    counts = jax.random.randint(count_key, (REQUESTS,), MINBLK, MAXBLK + 1)
    longest = jax.random.randint(pick_key, (), 0, REQUESTS)
    counts = jnp.where(request_ids == longest, MAXBLK, counts).astype(jnp.int32)
    offset = jax.random.randint(shift_key, (), 0, N_POOL)
    request_order = jax.random.permutation(order_key, REQUESTS)
    block_ids = jnp.arange(MAXBLK)
    stores = (offset + request_order[:, None] + block_ids[None, :]) % N_POOL
    live_table = block_ids[None, :] < counts[:, None]
    live_blocks = live_table.reshape(-1)
    flat_store = stores.reshape(-1)
    flat_order = jnp.arange(REQUESTS * MAXBLK)
    earlier = (flat_store[None, :] == flat_store[:, None]) & live_blocks[None, :] & (flat_order[None, :] < flat_order[:, None])
    position = jnp.minimum(jnp.sum(earlier, axis=1), SLOTS - 1)
    shuffles = jax.vmap(lambda store_id: jax.random.permutation(jax.random.fold_in(perm_key, store_id), SLOTS))(jnp.arange(N_POOL))
    placed = shuffles[flat_store, position]
    spare_slots = jax.random.randint(spare_key, (REQUESTS * MAXBLK,), 0, SLOTS)
    slot_table = jnp.where(live_blocks, placed, spare_slots).reshape(REQUESTS, MAXBLK)
    unused_stores = jax.random.randint(unused_key, (REQUESTS, MAXBLK), 0, N_POOL)
    store_table = jnp.where(live_table, stores, unused_stores)
    return (counts, store_table.astype(jnp.int32), slot_table.astype(jnp.int32))


def draw_prefix_blocks(key, part):
    return block_layout(key)[0]


def draw_hit_store(key, part):
    return block_layout(key)[1]


def draw_hit_slot(key, part):
    return block_layout(key)[2]


def draw_decode_owner(key, part):
    key = jax.random.fold_in(key, 11)
    shuffled = jax.random.permutation(key, 2 * N_POOL)
    leading = shuffled[:REQUESTS]
    buddy = jnp.bitwise_xor(shuffled[0], 1)
    present = jnp.any(leading == buddy)
    leading = leading.at[1].set(jnp.where(present, leading[1], buddy))
    return (leading // 2).astype(jnp.int32)


def draw_new_keys(key, part):
    noise_key = jax.random.fold_in(key, 5)
    shape = (REQUESTS, NEW, KVH, HD)
    entries = jnp.clip(jax.random.normal(noise_key, shape, jnp.float32) * 1.6, -9.6, 9.6)
    return entries.reshape(REQUESTS, NEW, KVH * HD).astype(jnp.bfloat16)


def draw_queries(key, part):
    noise_key = jax.random.fold_in(key, 7)
    shape = (REQUESTS, NEW, KVH, HEADS // KVH, HD)
    entries = jnp.clip(jax.random.normal(noise_key, shape, jnp.float32) * 1.6, -9.6, 9.6)
    return entries.reshape(REQUESTS, NEW, HEADS * HD).astype(jnp.bfloat16)


def steps_of(rng, dims, cuts, least, top_value):
    gain = 1.0
    for dim, blocks in cuts:
        draws = jax.random.uniform(jax.random.fold_in(jax.random.fold_in(rng, 6), dim), (blocks,), jnp.float32, least / len(cuts), top_value / len(cuts))
        gain = gain * jnp.repeat(jnp.exp(draws), dims[dim] // blocks).reshape((-1,) + (1,) * (len(dims) - 1 - dim))
    return gain


def normal_values(stream_key, shape, scale, reach, cuts=(), kind=jnp.bfloat16):
    result = scale * jax.random.normal(stream_key, shape, jnp.float32)
    if cuts:
        result = result * steps_of(stream_key, shape, cuts, -0.22, 0.18)
    return jnp.clip(result, -reach, reach).astype(kind)


def setup_inputs(seed: int = 0, part: int = 0) -> dict:
    keys = jax.random.split(jax.random.key(seed), 10)
    own_keys = jax.random.split(jax.random.fold_in(keys[9], part), 10)
    queries = draw_queries(jax.random.fold_in(jax.random.fold_in(keys[9], part), 71), part)
    new_keys = draw_new_keys(jax.random.fold_in(jax.random.fold_in(keys[9], part), 71), part)
    new_values = normal_values(own_keys[2], (REQUESTS, NEW, KVH * HD), 1.0, 6.0, ((0, 4), (2, 4)))
    store_keys = normal_values(own_keys[3], (STORE, BLOCK, KVH * HD), 1.6, 9.5625, ((0, 4), (2, 4)))
    store_values = normal_values(own_keys[4], (STORE, BLOCK, KVH * HD), 1.0, 6.0, ((0, 4), (2, 4)))
    prefix_blocks = draw_prefix_blocks(jax.random.fold_in(jax.random.fold_in(keys[9], part), 71), part)
    hit_store = draw_hit_store(jax.random.fold_in(jax.random.fold_in(keys[9], part), 71), part)
    hit_slot = draw_hit_slot(jax.random.fold_in(jax.random.fold_in(keys[9], part), 71), part)
    decode_owner = draw_decode_owner(jax.random.fold_in(jax.random.fold_in(keys[9], part), 71), part)
    return {"queries": queries, "new_keys": new_keys, "new_values": new_values, "store_keys": store_keys, "store_values": store_values, "prefix_blocks": prefix_blocks, "hit_store": hit_store, "hit_slot": hit_slot, "decode_owner": decode_owner}


def attend_request(query_rows, key_rows, value_rows, allowed):
    group_size = HEADS // KVH
    query_heads = query_rows.reshape(NEW, KVH, group_size, HD).astype(jnp.float32)
    key_heads = key_rows.reshape(-1, KVH, HD).astype(jnp.float32)
    value_heads = value_rows.reshape(-1, KVH, HD).astype(jnp.float32)
    scores = jnp.einsum('ihgd,jhd->hgij', query_heads, key_heads, precision=lax.Precision.HIGHEST) * (1.0 / math.sqrt(HD))
    scores = jnp.where(allowed[None, None], scores, -jnp.inf)
    row_peak = lax.optimization_barrier(jnp.max(scores, axis=3, keepdims=True))
    weights = jnp.exp(scores - row_peak)
    row_total = lax.optimization_barrier(jnp.sum(weights, axis=3))
    rounded = lax.optimization_barrier(weights.astype(jnp.bfloat16)).astype(jnp.float32)
    mixture = jnp.einsum('hgij,jhd->hgid', rounded, value_heads, precision=lax.Precision.HIGHEST) / row_total[..., None]
    return mixture.transpose(2, 0, 1, 3).reshape(NEW, HEADS * HD).astype(jnp.bfloat16)

def reference(queries, new_keys, new_values, store_keys, store_values, prefix_blocks, hit_store, hit_slot, decode_owner):

    def one_request(request):
        store_rows = (hit_store[request] * SLOTS + hit_slot[request]).astype(jnp.int32)
        prefix_keys = store_keys[store_rows].reshape(MAXBLK * BLOCK, KVH * HD)
        prefix_values = store_values[store_rows].reshape(MAXBLK * BLOCK, KVH * HD)
        key_rows = jnp.concatenate([prefix_keys, new_keys[request]], axis=0)
        value_rows = jnp.concatenate([prefix_values, new_values[request]], axis=0)
        live_keys = jnp.repeat(jnp.arange(MAXBLK) < prefix_blocks[request], BLOCK)
        causal = jnp.arange(NEW)[None, :] <= jnp.arange(NEW)[:, None]
        allowed = jnp.concatenate([jnp.broadcast_to(live_keys[None, :], (NEW, MAXBLK * BLOCK)), causal], axis=1)
        return attend_request(queries[request], key_rows, value_rows, allowed)
    attended = lax.map(one_request, jnp.arange(REQUESTS, dtype=jnp.int32))
    request_ids = jnp.arange(REQUESTS)
    owner_rank = lax.optimization_barrier(jnp.sum((decode_owner[None, :] == decode_owner[:, None]) & (request_ids[None, :] < request_ids[:, None]), axis=1))
    targets = jnp.arange(N_POOL)[:, None, None]
    places = jnp.arange(CAPP)[None, :, None]
    chosen = ((decode_owner[None, None, :] == targets) & (owner_rank[None, None, :] == places)).astype(jnp.float32)
    chosen = chosen.reshape(N_POOL * CAPP, REQUESTS)
    pushed_keys = jnp.einsum('sr,rtd->std', chosen, new_keys.astype(jnp.float32), precision=lax.Precision.HIGHEST).astype(jnp.bfloat16)
    pushed_values = jnp.einsum('sr,rtd->std', chosen, new_values.astype(jnp.float32), precision=lax.Precision.HIGHEST).astype(jnp.bfloat16)
    return (attended, pushed_keys, pushed_values)
```

```python
import functools
import math

import jax
import jax.numpy as jnp
from jax import lax
from jax.experimental import pallas as pl
from jax.experimental.pallas import tpu as pltpu
from jax.sharding import PartitionSpec as P

HEADS = 64
KVH = 8
HD = 128
MAXBLK = 32
CAPP = 2
GROUP = HEADS // KVH
EMPTY = -1e30
SCALE = 1.0 / math.sqrt(HD)
EXP2_SCALE = SCALE * math.log2(math.e)
VMEM_LIMIT = 48 * 1024 * 1024


def first_block(meta, request, pool_size):
    me, prefix_ref, store_ref = meta[0], meta[1], meta[2]
    first = lax.rem(me - store_ref[request, 0] + pool_size, pool_size)
    count = lax.max(lax.div(prefix_ref[request] - first + pool_size - 1, pool_size), 0)
    return first, count


def block_copies(meta, request, entry, slot_ref, stores, buffers, sems, parity, pool_size):
    first, _ = first_block(meta, request, pool_size)
    slot = slot_ref[request, first + entry * pool_size]
    return [
        pltpu.make_async_copy(
            stores[i].at[slot], buffers[i].at[parity, entry], sems.at[i, parity, entry]
        )
        for i in range(2)
    ]


def attend(
    query_ref, key_ref, value_ref, count, ready, new_refs, query_rows, scores, peaks, totals, acc, put
):
    new_rows = query_ref.shape[0]
    kv_local = key_ref.shape[2] // HD
    rows = GROUP * new_rows
    for kv in range(kv_local):
        lanes = slice(kv * HD, (kv + 1) * HD)
        for g in range(GROUP):
            head = kv * GROUP + g
            query_rows[g * new_rows : (g + 1) * new_rows, :] = query_ref[
                :, head * HD : (head + 1) * HD
            ]
        peaks[...] = jnp.full(peaks.shape, EMPTY, jnp.float32)
        if new_refs is not None:
            new_key_ref, new_value_ref, new_scores = new_refs
            fresh = lax.dot_general(
                query_rows[...],
                new_key_ref[:, lanes],
                (((1,), (1,)), ((), ())),
                preferred_element_type=jnp.float32,
            )
            row = lax.broadcasted_iota(jnp.int32, (new_rows, new_key_ref.shape[0]), 0)
            column = lax.broadcasted_iota(jnp.int32, (new_rows, new_key_ref.shape[0]), 1)
            for g in range(GROUP):
                part = slice(g * new_rows, (g + 1) * new_rows)
                masked = jnp.where(column <= row, fresh[part], EMPTY)
                new_scores[part, :] = masked
                peaks[part, :] = jnp.maximum(masked[:, :HD], masked[:, HD:])

        def score_block(entry, carry):
            if kv == 0:
                ready(entry)
            block = lax.dot_general(
                query_rows[...],
                key_ref[entry, :, lanes],
                (((1,), (1,)), ((), ())),
                preferred_element_type=jnp.float32,
            )
            scores[entry] = block
            best = peaks[...]
            for piece in range(block.shape[1] // HD):
                best = jnp.maximum(best, block[:, piece * HD : (piece + 1) * HD])
            peaks[...] = best
            return carry

        lax.fori_loop(0, count, score_block, 0)
        peak = jnp.max(peaks[...], axis=1, keepdims=True)
        peaks[...] = jnp.broadcast_to(peak, peaks.shape)

        def weigh(block, values):
            weights = jnp.exp2((block - peaks[:, 0:1]) * EXP2_SCALE)
            total = weights[:, :HD]
            for piece in range(1, weights.shape[1] // HD):
                total = total + weights[:, piece * HD : (piece + 1) * HD]
            mixed = lax.dot_general(
                weights.astype(jnp.bfloat16),
                values,
                (((1,), (0,)), ((), ())),
                preferred_element_type=jnp.float32,
            )
            return total, mixed

        if new_refs is not None:
            total, mixed = weigh(new_scores[...], new_value_ref[:, lanes])
            totals[...] = total
            acc[...] = mixed
        else:
            totals[...] = jnp.zeros(totals.shape, jnp.float32)
            acc[...] = jnp.zeros(acc.shape, jnp.float32)

        def weigh_block(entry, carry):
            total, mixed = weigh(scores[entry], value_ref[entry, :, lanes])
            totals[...] += total
            acc[...] += mixed
            return carry

        lax.fori_loop(0, count, weigh_block, 0)
        total = jnp.sum(totals[...], axis=1, keepdims=True)
        safe = jnp.where(total > 0, total, 1.0)
        out = acc[...] / safe
        log_total = jnp.where(total > 0, peak * SCALE + jnp.log(safe), EMPTY)
        for g in range(GROUP):
            part = slice(g * new_rows, (g + 1) * new_rows)
            put(kv * GROUP + g, out[part], log_total[part])


def add_lane(tile, heads, head, column):
    lane = lax.broadcasted_iota(jnp.int32, tile.shape, 1)
    hit = (lax.rem(lane, heads) == head) & (lane < 3 * heads)
    return jnp.where(hit, column, tile)


def split_lanes(tile, heads):
    lane = lax.broadcasted_iota(jnp.int32, tile.shape, 1)
    high = tile.astype(jnp.bfloat16).astype(jnp.float32)
    middle = (tile - high).astype(jnp.bfloat16).astype(jnp.float32)
    low = tile - high - middle
    return jnp.where(lane < heads, high, jnp.where(lane < 2 * heads, middle, low)).astype(
        jnp.bfloat16
    )


def own_kernel(
    pool_size,
    me_ref,
    prefix_ref,
    store_ref,
    slot_ref,
    query_ref,
    new_key_ref,
    new_value_ref,
    store_keys,
    store_values,
    out_ref,
    log_ref,
    key_buf,
    value_buf,
    query_rows,
    scores,
    new_scores,
    peaks,
    totals,
    acc,
    sems,
):
    me = me_ref[0]
    meta = (me, prefix_ref, store_ref)
    _, count = first_block(meta, me, pool_size)

    def copies(entry):
        return block_copies(
            meta, me, entry, slot_ref, (store_keys, store_values), (key_buf, value_buf), sems, 0, pool_size
        )

    def start(entry, carry):
        for copy in copies(entry):
            copy.start()
        return carry

    lax.fori_loop(0, count, start, 0)

    def ready(entry):
        for copy in copies(entry):
            copy.wait()

    heads = query_ref.shape[1] // HD
    log_ref[...] = jnp.zeros(log_ref.shape, jnp.float32)

    def put(head, out, log_total):
        out_ref[:, head * HD : (head + 1) * HD] = out
        log_ref[...] = add_lane(log_ref[...], heads, head, log_total)

    attend(
        query_ref,
        key_buf.at[0],
        value_buf.at[0],
        count,
        ready,
        (new_key_ref, new_value_ref, new_scores),
        query_rows,
        scores,
        peaks,
        totals,
        acc,
        put,
    )


def other_kernel(
    pool_size,
    me_ref,
    prefix_ref,
    store_ref,
    slot_ref,
    query_ref,
    store_keys,
    store_values,
    out_ref,
    key_buf,
    value_buf,
    query_rows,
    scores,
    peaks,
    totals,
    acc,
    log_tile,
    sems,
):
    step = pl.program_id(0)
    steps = pl.num_programs(0)
    me = me_ref[0]
    meta = (me, prefix_ref, store_ref)

    def request_of(index):
        return lax.rem(me + 1 + index, pool_size)

    def copies(index, entry):
        return block_copies(
            meta,
            request_of(index),
            entry,
            slot_ref,
            (store_keys, store_values),
            (key_buf, value_buf),
            sems,
            lax.rem(index, 2),
            pool_size,
        )

    def start_all(index):
        def start(entry, carry):
            for copy in copies(index, entry):
                copy.start()
            return carry

        lax.fori_loop(0, first_block(meta, request_of(index), pool_size)[1], start, 0)

    @pl.when(step == 0)
    def _():
        start_all(step)

    @pl.when(step + 1 < steps)
    def _():
        start_all(step + 1)

    def ready(entry):
        for copy in copies(step, entry):
            copy.wait()

    width = query_ref.shape[2]
    heads = width // HD
    log_tile[...] = jnp.zeros(log_tile.shape, jnp.float32)

    def put(head, out, log_total):
        out_ref[0, :, head * HD : (head + 1) * HD] = out.astype(jnp.bfloat16)
        log_tile[...] = add_lane(log_tile[...], heads, head, log_total)

    parity = lax.rem(step, 2)
    attend(
        query_ref.at[0],
        key_buf.at[parity],
        value_buf.at[parity],
        first_block(meta, request_of(step), pool_size)[1],
        ready,
        None,
        query_rows,
        scores,
        peaks,
        totals,
        acc,
        put,
    )
    out_ref[0, :, width:] = split_lanes(log_tile[...], heads)


def combine_kernel(sources, me_ref, own_ref, log_ref, got_ref, out_ref):
    width = own_ref.shape[1]
    heads = width // HD
    me = me_ref[0]
    for head in range(heads):
        lanes = slice(head * HD, (head + 1) * HD)
        logs = [log_ref[:, head : head + 1]]
        for i in range(1, sources):
            tile = got_ref[lax.rem(me + i, sources), :, width:].astype(jnp.float32)
            logs.append(
                tile[:, head : head + 1]
                + tile[:, heads + head : heads + head + 1]
                + tile[:, 2 * heads + head : 2 * heads + head + 1]
            )
        peak = functools.reduce(jnp.maximum, logs)
        shares = [jnp.exp(x - peak) for x in logs]
        scale = 1.0 / functools.reduce(jnp.add, shares)
        mixed = own_ref[:, lanes] * (shares[0] * scale)
        for i in range(1, sources):
            part = got_ref[lax.rem(me + i, sources), :, lanes].astype(jnp.float32)
            mixed = mixed + part * (shares[i] * scale)
        out_ref[:, lanes] = mixed.astype(jnp.bfloat16)


def shards(
    queries,
    new_keys,
    new_values,
    store_keys,
    store_values,
    prefix_blocks,
    hit_store,
    hit_slot,
    decode_owner,
):
    pool_size = lax.axis_size("pool")
    my_index = lax.axis_index("pool")
    capacity = (MAXBLK + pool_size - 1) // pool_size
    new_rows = queries.shape[1]
    width = queries.shape[2]
    kv_width = new_keys.shape[2]
    block_len = store_keys.shape[1]
    rows = GROUP * new_rows
    request_count = prefix_blocks.shape[0]
    padded_rows = -(-new_rows // (2 * HD)) * 2 * HD
    scalars = (my_index.reshape(1).astype(jnp.int32), prefix_blocks, hit_store, hit_slot)
    flops_block = 4 * rows * block_len * kv_width
    any_spec = pl.BlockSpec(memory_space=pl.ANY)
    vmem_spec = pl.BlockSpec(memory_space=pltpu.VMEM)
    params = pltpu.CompilerParams(vmem_limit_bytes=VMEM_LIMIT)

    gathered = lax.all_gather(queries[0], "pool", axis=0, tiled=False)
    fresh = jnp.concatenate([new_keys[0], new_values[0]], axis=1)
    gathered_fresh = lax.all_gather(fresh, "pool", axis=0, tiled=False)

    padding = ((0, padded_rows - new_rows), (0, 0))
    work = [
        pltpu.VMEM((rows, HD), jnp.bfloat16),
        pltpu.VMEM((capacity, rows, block_len), jnp.float32),
    ]
    state = [pltpu.VMEM((rows, HD), jnp.float32) for _ in range(3)]
    own_out, own_log = pl.pallas_call(
        functools.partial(own_kernel, pool_size),
        grid_spec=pltpu.PrefetchScalarGridSpec(
            num_scalar_prefetch=4,
            grid=(),
            in_specs=[vmem_spec] * 3 + [any_spec] * 2,
            out_specs=[vmem_spec] * 2,
            scratch_shapes=[
                pltpu.VMEM((1, capacity, block_len, kv_width), jnp.bfloat16),
                pltpu.VMEM((1, capacity, block_len, kv_width), jnp.bfloat16),
                *work,
                pltpu.VMEM((rows, padded_rows), jnp.float32),
                *state,
                pltpu.SemaphoreType.DMA((2, 1, capacity)),
            ],
        ),
        out_shape=[
            jax.ShapeDtypeStruct((new_rows, width), jnp.float32),
            jax.ShapeDtypeStruct((new_rows, HD), jnp.float32),
        ],
        compiler_params=params,
        cost_estimate=pl.CostEstimate(
            flops=4 * flops_block, bytes_accessed=8 * 1024 * 1024, transcendentals=0
        ),
        name="own_part",
    )(
        *scalars,
        queries[0],
        jnp.pad(new_keys[0], padding),
        jnp.pad(new_values[0], padding),
        store_keys,
        store_values,
    )

    packed = pl.pallas_call(
        functools.partial(other_kernel, pool_size),
        grid_spec=pltpu.PrefetchScalarGridSpec(
            num_scalar_prefetch=4,
            grid=(request_count - 1,),
            in_specs=[
                pl.BlockSpec(
                    (1, new_rows, width),
                    lambda i, me, *_: (lax.rem(me[0] + 1 + i, pool_size), 0, 0),
                ),
                any_spec,
                any_spec,
            ],
            out_specs=pl.BlockSpec(
                (1, new_rows, width + HD),
                lambda i, me, *_: (lax.rem(me[0] + 1 + i, pool_size), 0, 0),
            ),
            scratch_shapes=[
                pltpu.VMEM((2, capacity, block_len, kv_width), jnp.bfloat16),
                pltpu.VMEM((2, capacity, block_len, kv_width), jnp.bfloat16),
                *work,
                *state,
                pltpu.VMEM((new_rows, HD), jnp.float32),
                pltpu.SemaphoreType.DMA((2, 2, capacity)),
            ],
        ),
        out_shape=jax.ShapeDtypeStruct((request_count, new_rows, width + HD), jnp.bfloat16),
        compiler_params=params,
        cost_estimate=pl.CostEstimate(
            flops=4 * flops_block, bytes_accessed=16 * 1024 * 1024, transcendentals=0
        ),
        name="other_parts",
    )(*scalars, gathered, store_keys, store_values)

    returned = lax.all_to_all(packed, "pool", split_axis=0, concat_axis=0, tiled=True)

    attended = pl.pallas_call(
        functools.partial(combine_kernel, pool_size),
        in_specs=[pl.BlockSpec(memory_space=pltpu.SMEM)] + [vmem_spec] * 3,
        out_specs=vmem_spec,
        out_shape=jax.ShapeDtypeStruct((new_rows, width), jnp.bfloat16),
        compiler_params=params,
        name="combine",
    )(scalars[0], own_out, own_log, returned)

    request_ids = jnp.arange(request_count)
    mine = decode_owner == my_index
    rank = jnp.cumsum(mine) - 1
    picks = mine[None, :] & (rank[None, :] == jnp.arange(CAPP)[:, None])
    source = jnp.sum(jnp.where(picks, request_ids[None, :], 0), axis=1)
    present = jnp.any(picks, axis=1)
    pushed = jnp.where(present[:, None, None], gathered_fresh[source], 0)
    return (attended[None], pushed[:, :, :kv_width], pushed[:, :, kv_width:])


def solution(mesh):
    in_specs = (
        P(("groups", "pool"), None, ("tensor", "sub")),
        P(("groups", "pool"), None, ("tensor", "sub")),
        P(("groups", "pool"), None, ("tensor", "sub")),
        P(("groups", "pool"), None, ("tensor", "sub")),
        P(("groups", "pool"), None, ("tensor", "sub")),
        P("groups"),
        P("groups", None),
        P("groups", None),
        P("groups"),
    )
    out_specs = (
        P(("groups", "pool"), None, ("tensor", "sub")),
        P(("groups", "pool"), None, ("tensor", "sub")),
        P(("groups", "pool"), None, ("tensor", "sub")),
    )
    return jax.shard_map(shards, mesh=mesh, in_specs=in_specs, out_specs=out_specs, check_vma=False)
```

```python
import functools
import math

import jax
import jax.numpy as jnp
from jax import lax
from jax.experimental import pallas as pl
from jax.experimental.pallas import tpu as pltpu
from jax.sharding import PartitionSpec as P

HEADS = 64
KVH = 8
HD = 128
MAXBLK = 32
CAPP = 2
GROUP = HEADS // KVH
EMPTY = -1e30
LINE = 8
SCALE = 1.0 / math.sqrt(HD)
EXP2_SCALE = SCALE * math.log2(math.e)
VMEM_LIMIT = 48 * 1024 * 1024


def place(meta_ref, request, pool_size):
    prefix = meta_ref[1 + request]
    first = lax.rem(meta_ref[0] - meta_ref[1 + pool_size + request] + pool_size, pool_size)
    count = lax.max(lax.div(prefix - first + pool_size - 1, pool_size), 0)
    return count, 1 + 2 * pool_size + request * MAXBLK + first


def block_copies(meta_ref, base, entry, stores, buffers, sems, pool_size):
    slot = meta_ref[base + entry * pool_size]
    return [
        pltpu.make_async_copy(stores[i].at[slot], buffers[i].at[entry], sems.at[i, entry])
        for i in range(2)
    ]


def attend(
    query_ref, key_ref, value_ref, count, ready, new_refs, query_rows, scores, peaks, totals, acc, put
):
    new_rows = query_ref.shape[0]
    kv_local = key_ref.shape[2] // HD
    rows = GROUP * new_rows
    for kv in range(kv_local):
        lanes = slice(kv * HD, (kv + 1) * HD)
        for g in range(GROUP):
            head = kv * GROUP + g
            query_rows[g * new_rows : (g + 1) * new_rows, :] = query_ref[
                :, head * HD : (head + 1) * HD
            ]
        peaks[...] = jnp.full(peaks.shape, EMPTY, jnp.float32)
        if new_refs is not None:
            new_key_ref, new_value_ref, new_scores = new_refs
            fresh = lax.dot_general(
                query_rows[...],
                new_key_ref[:, lanes],
                (((1,), (1,)), ((), ())),
                preferred_element_type=jnp.float32,
            )
            row = lax.broadcasted_iota(jnp.int32, (new_rows, new_key_ref.shape[0]), 0)
            column = lax.broadcasted_iota(jnp.int32, (new_rows, new_key_ref.shape[0]), 1)
            for g in range(GROUP):
                part = slice(g * new_rows, (g + 1) * new_rows)
                masked = jnp.where(column <= row, fresh[part], EMPTY)
                new_scores[part, :] = masked
                peaks[part, :] = jnp.maximum(masked[:, :HD], masked[:, HD:])

        def score_block(entry, carry):
            if kv == 0:
                ready(entry)
            block = lax.dot_general(
                query_rows[...],
                key_ref[entry, :, lanes],
                (((1,), (1,)), ((), ())),
                preferred_element_type=jnp.float32,
            )
            scores[entry] = block
            best = peaks[...]
            for piece in range(block.shape[1] // HD):
                best = jnp.maximum(best, block[:, piece * HD : (piece + 1) * HD])
            peaks[...] = best
            return carry

        lax.fori_loop(0, count, score_block, 0)
        peak = jnp.max(peaks[...], axis=1, keepdims=True)
        peaks[...] = jnp.broadcast_to(peak, peaks.shape)

        def weigh(block, values):
            weights = jnp.exp2((block - peaks[:, 0:1]) * EXP2_SCALE)
            total = weights[:, :HD]
            for piece in range(1, weights.shape[1] // HD):
                total = total + weights[:, piece * HD : (piece + 1) * HD]
            mixed = lax.dot_general(
                weights.astype(jnp.bfloat16),
                values,
                (((1,), (0,)), ((), ())),
                preferred_element_type=jnp.float32,
            )
            return total, mixed

        if new_refs is not None:
            total, mixed = weigh(new_scores[...], new_value_ref[:, lanes])
            totals[...] = total
            acc[...] = mixed
        else:
            totals[...] = jnp.zeros(totals.shape, jnp.float32)
            acc[...] = jnp.zeros(acc.shape, jnp.float32)

        def weigh_block(entry, carry):
            total, mixed = weigh(scores[entry], value_ref[entry, :, lanes])
            totals[...] += total
            acc[...] += mixed
            return carry

        lax.fori_loop(0, count, weigh_block, 0)
        total = jnp.sum(totals[...], axis=1, keepdims=True)
        safe = jnp.where(total > 0, total, 1.0)
        out = acc[...] / safe
        log_total = jnp.where(total > 0, peak * SCALE + jnp.log(safe), EMPTY)
        for g in range(GROUP):
            part = slice(g * new_rows, (g + 1) * new_rows)
            put(kv * GROUP + g, out[part], log_total[part])


def add_lane(tile, heads, head, column):
    lane = lax.broadcasted_iota(jnp.int32, tile.shape, 1)
    hit = (lax.rem(lane, heads) == head) & (lane < 3 * heads)
    return jnp.where(hit, column, tile)


def split_lanes(tile, heads):
    lane = lax.broadcasted_iota(jnp.int32, tile.shape, 1)
    high = tile.astype(jnp.bfloat16).astype(jnp.float32)
    middle = (tile - high).astype(jnp.bfloat16).astype(jnp.float32)
    low = tile - high - middle
    return jnp.where(lane < heads, high, jnp.where(lane < 2 * heads, middle, low)).astype(
        jnp.bfloat16
    )


def fetch(pool_size, meta_ref, request, stores, buffers, sems):
    count, base = place(meta_ref, request, pool_size)

    def copies(entry):
        return block_copies(meta_ref, base, entry, stores, buffers, sems, pool_size)

    def start(entry, carry):
        for copy in copies(entry):
            copy.start()
        return carry

    lax.fori_loop(0, count, start, 0)

    def ready(entry):
        for copy in copies(entry):
            copy.wait()

    return count, ready


def own_kernel(
    pool_size,
    meta_ref,
    query_ref,
    new_key_ref,
    new_value_ref,
    store_keys,
    store_values,
    out_ref,
    log_ref,
    key_buf,
    value_buf,
    new_key_buf,
    new_value_buf,
    query_rows,
    scores,
    new_scores,
    peaks,
    totals,
    acc,
    sems,
):
    count, ready = fetch(
        pool_size, meta_ref, meta_ref[0], (store_keys, store_values), (key_buf, value_buf), sems
    )
    new_rows, width = query_ref.shape
    heads = width // HD
    for buffer, source in ((new_key_buf, new_key_ref), (new_value_buf, new_value_ref)):
        buffer[:new_rows, :] = source[...]
        buffer[new_rows:, :] = jnp.zeros(
            (buffer.shape[0] - new_rows, buffer.shape[1]), jnp.bfloat16
        )
    log_ref[...] = jnp.zeros(log_ref.shape, jnp.float32)

    def put(head, out, log_total):
        out_ref[:, head * HD : (head + 1) * HD] = out
        log_ref[...] = add_lane(log_ref[...], heads, head, log_total)

    attend(
        query_ref,
        key_buf,
        value_buf,
        count,
        ready,
        (new_key_buf, new_value_buf, new_scores),
        query_rows,
        scores,
        peaks,
        totals,
        acc,
        put,
    )


def other_kernel(
    pool_size,
    offset,
    meta_ref,
    query_ref,
    store_keys,
    store_values,
    out_ref,
    key_buf,
    value_buf,
    query_rows,
    scores,
    peaks,
    totals,
    acc,
    log_tile,
    sems,
):
    if offset is None:
        request = meta_ref[1 + 2 * pool_size + pool_size * MAXBLK]
    else:
        request = meta_ref[0] + offset

    @pl.when((request >= 0) & (request < pool_size))
    def _():
        count, ready = fetch(
            pool_size, meta_ref, request, (store_keys, store_values), (key_buf, value_buf), sems
        )
        width = query_ref.shape[1]
        heads = width // HD
        log_tile[...] = jnp.zeros(log_tile.shape, jnp.float32)

        def put(head, out, log_total):
            out_ref[:, head * HD : (head + 1) * HD] = out.astype(jnp.bfloat16)
            log_tile[...] = add_lane(log_tile[...], heads, head, log_total)

        attend(
            query_ref,
            key_buf,
            value_buf,
            count,
            ready,
            None,
            query_rows,
            scores,
            peaks,
            totals,
            acc,
            put,
        )
        out_ref[:, width:] = split_lanes(log_tile[...], heads)


def combine_kernel(sources, pool_size, meta_ref, own_ref, log_ref, *refs):
    out_ref = refs[-1]
    width = own_ref.shape[1]
    heads = width // HD
    logs = [log_ref[...]]
    valid = []
    for (relative, source), part in zip(sources, refs[:-1]):
        if relative:
            there = (meta_ref[0] + source >= 0) & (meta_ref[0] + source < pool_size)
        else:
            there = meta_ref[0] != source
        valid.append(there)
        tile = part[:, width:].astype(jnp.float32)
        whole = (
            tile + pltpu.roll(tile, HD - heads, 1) + pltpu.roll(tile, HD - 2 * heads, 1)
        )
        logs.append(jnp.where(there, whole, EMPTY))
    peak = functools.reduce(jnp.maximum, logs)
    shares = [jnp.exp(x - peak) for x in logs]
    scale = 1.0 / functools.reduce(jnp.add, shares)
    shares = [x * scale for x in shares]
    for head in range(heads):
        lanes = slice(head * HD, (head + 1) * HD)
        mixed = own_ref[:, lanes] * shares[0][:, head : head + 1]
        for share, there, part in zip(shares[1:], valid, refs[:-1]):
            mixed = mixed + jnp.where(
                there, part[:, lanes].astype(jnp.float32) * share[:, head : head + 1], 0.0
            )
        out_ref[:, lanes] = mixed.astype(jnp.bfloat16)


def shards(
    queries,
    new_keys,
    new_values,
    store_keys,
    store_values,
    prefix_blocks,
    hit_store,
    hit_slot,
    decode_owner,
):
    pool_size = lax.axis_size("pool")
    my_index = lax.axis_index("pool").astype(jnp.int32)
    capacity = (MAXBLK + pool_size - 1) // pool_size
    new_rows = queries.shape[1]
    width = queries.shape[2]
    kv_width = new_keys.shape[2]
    block_len = store_keys.shape[1]
    rows = GROUP * new_rows
    padded_rows = -(-new_rows // (2 * HD)) * 2 * HD
    meta = jnp.concatenate(
        [my_index.reshape(1), prefix_blocks, hit_store[:, 0], hit_slot.reshape(-1)]
    )
    flops = 4 * rows * block_len * kv_width * capacity
    smem_spec = pl.BlockSpec(memory_space=pltpu.SMEM)
    any_spec = pl.BlockSpec(memory_space=pl.ANY)
    vmem_spec = pl.BlockSpec(memory_space=pltpu.VMEM)
    params = pltpu.CompilerParams(vmem_limit_bytes=VMEM_LIMIT)
    cost = pl.CostEstimate(
        flops=8 * flops, bytes_accessed=4 * capacity * block_len * kv_width, transcendentals=0
    )
    buffers = [pltpu.VMEM((capacity, block_len, kv_width), jnp.bfloat16)] * 2
    work = [
        pltpu.VMEM((rows, HD), jnp.bfloat16),
        pltpu.VMEM((capacity, rows, block_len), jnp.float32),
    ]
    state = [pltpu.VMEM((rows, HD), jnp.float32)] * 3
    sems = pltpu.SemaphoreType.DMA((2, capacity))

    def own_part(query):
        return pl.pallas_call(
            functools.partial(own_kernel, pool_size),
            in_specs=[smem_spec] + [vmem_spec] * 3 + [any_spec] * 2,
            out_specs=[vmem_spec] * 2,
            scratch_shapes=[
                *buffers,
                *[pltpu.VMEM((padded_rows, kv_width), jnp.bfloat16)] * 2,
                *work,
                pltpu.VMEM((rows, padded_rows), jnp.float32),
                *state,
                sems,
            ],
            out_shape=[
                jax.ShapeDtypeStruct((new_rows, width), jnp.float32),
                jax.ShapeDtypeStruct((new_rows, HD), jnp.float32),
            ],
            compiler_params=params,
            cost_estimate=cost,
            name="own_part",
        )(meta, query, new_keys[0], new_values[0], store_keys, store_values)

    def other_part(offset, query, meta=meta):
        return pl.pallas_call(
            functools.partial(other_kernel, pool_size, offset),
            in_specs=[smem_spec, vmem_spec] + [any_spec] * 2,
            out_specs=vmem_spec,
            scratch_shapes=[
                *buffers,
                *work,
                *state,
                pltpu.VMEM((new_rows, HD), jnp.float32),
                sems,
            ],
            out_shape=jax.ShapeDtypeStruct((new_rows, width + HD), jnp.bfloat16),
            compiler_params=params,
            cost_estimate=cost,
            name="other_part",
        )(meta, query, store_keys, store_values)

    def shift(array, distance, first=0):
        pairs = [
            (i, i + distance)
            for i in range(pool_size)
            if 0 <= i + distance < pool_size and 0 <= i - first < pool_size
        ]
        return lax.ppermute(array, "pool", pairs)

    query = queries[0]
    fresh = jnp.concatenate([new_keys[0], new_values[0]], axis=1)
    own_out, own_log = own_part(query)
    if pool_size <= LINE:
        sources = []
        parts = []
        right, left = query, query
        for step in range(1, pool_size):
            right = shift(right, 1, step - 1)
            left = shift(left, -1, 1 - step)
            right, left = lax.optimization_barrier((right, left))
            for offset, held in ((-step, right), (step, left)):
                packed = other_part(offset, held)
                sources.append((True, -offset))
                parts.append(shift(packed, offset, -offset))
        fresh, right = lax.optimization_barrier((fresh, right))
        moved = [(my_index, fresh)]
        right, left = fresh, fresh
        for step in range(1, pool_size):
            right = shift(right, 1, step - 1)
            left = shift(left, -1, 1 - step)
            moved.append((my_index - step, right))
            moved.append((my_index + step, left))
    else:
        gathered = lax.all_gather(query, "pool", axis=0, tiled=False)
        packed = lax.map(
            lambda pair: other_part(None, pair[0], jnp.concatenate([meta, pair[1].reshape(1)])),
            (gathered, jnp.arange(pool_size, dtype=jnp.int32)),
        )
        parts = lax.all_to_all(packed, "pool", split_axis=0, concat_axis=0, tiled=True)
        sources = [(False, source) for source in range(pool_size)]
        moved = [
            (jnp.int32(source), array)
            for source, array in enumerate(lax.all_gather(fresh, "pool", axis=0, tiled=False))
        ]

    attended = pl.pallas_call(
        functools.partial(combine_kernel, tuple(sources), pool_size),
        in_specs=[smem_spec] + [vmem_spec] * (2 + len(sources)),
        out_specs=vmem_spec,
        out_shape=jax.ShapeDtypeStruct((new_rows, width), jnp.bfloat16),
        compiler_params=params,
        name="combine",
    )(meta, own_out, own_log, *parts)

    mine = decode_owner == my_index
    rank = jnp.cumsum(mine) - 1
    places = jnp.where(mine, rank, CAPP)
    padded_places = jnp.concatenate(
        [jnp.full((pool_size,), CAPP), places, jnp.full((pool_size,), CAPP)]
    )
    pushed = []
    for place_id in range(CAPP):
        total = jnp.zeros(fresh.shape, fresh.dtype)
        for source, array in moved:
            total = jnp.where(padded_places[source + pool_size] == place_id, array, total)
        pushed.append(total)
    pushed = jnp.stack(pushed)
    return (attended[None], pushed[:, :, :kv_width], pushed[:, :, kv_width:])


def solution(mesh):
    in_specs = (
        P(("groups", "pool"), None, ("tensor", "sub")),
        P(("groups", "pool"), None, ("tensor", "sub")),
        P(("groups", "pool"), None, ("tensor", "sub")),
        P(("groups", "pool"), None, ("tensor", "sub")),
        P(("groups", "pool"), None, ("tensor", "sub")),
        P("groups"),
        P("groups", None),
        P("groups", None),
        P("groups"),
    )
    out_specs = (
        P(("groups", "pool"), None, ("tensor", "sub")),
        P(("groups", "pool"), None, ("tensor", "sub")),
        P(("groups", "pool"), None, ("tensor", "sub")),
    )
    return jax.shard_map(shards, mesh=mesh, in_specs=in_specs, out_specs=out_specs, check_vma=False)
```

```python
import functools
import math

import jax
import jax.numpy as jnp
from jax import lax
from jax.experimental import pallas as pl
from jax.experimental.pallas import tpu as pltpu
from jax.sharding import PartitionSpec as P

HEADS = 64
KVH = 8
HD = 128
MAXBLK = 32
CAPP = 2
GROUP = HEADS // KVH
EMPTY = -1e30
LINE = 8
CHUNK_HEADS = 2
SCALE = 1.0 / math.sqrt(HD)
EXP2_SCALE = SCALE * math.log2(math.e)
VMEM_LIMIT = 48 * 1024 * 1024


def place(meta_ref, request, pool_size):
    prefix = meta_ref[1 + request]
    first = lax.rem(meta_ref[0] - meta_ref[1 + pool_size + request] + pool_size, pool_size)
    count = lax.max(lax.div(prefix - first + pool_size - 1, pool_size), 0)
    return count, 1 + 2 * pool_size + request * MAXBLK + first


def block_copies(meta_ref, base, entry, stores, buffers, sems, pool_size):
    slot = meta_ref[base + entry * pool_size]
    return [
        pltpu.make_async_copy(stores[i].at[slot], buffers[i].at[entry], sems.at[i, entry])
        for i in range(2)
    ]


def attend(
    load,
    key_ref,
    value_ref,
    count,
    ready,
    new_refs,
    new_rows,
    query_rows,
    scores,
    peaks,
    totals,
    acc,
    put,
):
    kv_local = key_ref.shape[2] // HD
    rows = GROUP * new_rows
    chunks = [slice(i, i + CHUNK_HEADS * new_rows) for i in range(0, rows, CHUNK_HEADS * new_rows)]

    def dot_keys(part, keys):
        return lax.dot_general(
            query_rows[part, :], keys, (((1,), (1,)), ((), ())), preferred_element_type=jnp.float32
        )

    def peak_of(block):
        pieces = [block[:, i : i + HD] for i in range(0, block.shape[1], HD)]
        return functools.reduce(jnp.maximum, pieces)

    def weigh(part, block, values):
        peak = peaks[part, :]
        pieces = [
            jnp.exp2(block[:, i : i + HD] * EXP2_SCALE - peak) for i in range(0, block.shape[1], HD)
        ]
        mixed = lax.dot_general(
            jnp.concatenate(pieces, axis=1).astype(jnp.bfloat16),
            values,
            (((1,), (0,)), ((), ())),
            preferred_element_type=jnp.float32,
        )
        return functools.reduce(jnp.add, pieces), mixed

    for kv in range(kv_local):
        lanes = slice(kv * HD, (kv + 1) * HD)
        load(kv)
        if new_refs is None:
            peaks[...] = jnp.full(peaks.shape, EMPTY, jnp.float32)
        else:
            new_key_ref, new_value_ref, new_scores = new_refs
            shape = (new_rows, new_key_ref.shape[0])
            seen = lax.broadcasted_iota(jnp.int32, shape, 1) <= lax.broadcasted_iota(
                jnp.int32, shape, 0
            )
            for g in range(GROUP):
                part = slice(g * new_rows, (g + 1) * new_rows)
                block = jnp.where(seen, dot_keys(part, new_key_ref[:, lanes]), EMPTY)
                new_scores[part, :] = block
                peaks[part, :] = peak_of(block)

        def score_block(entry, carry):
            if kv == 0:
                ready(entry)
            keys = key_ref[entry, :, lanes]
            for part in chunks:
                block = dot_keys(part, keys)
                scores[entry, part, :] = block
                peaks[part, :] = jnp.maximum(peaks[part, :], peak_of(block))
            return carry

        lax.fori_loop(0, count, score_block, 0)
        for part in chunks:
            peak = jnp.max(peaks[part, :], axis=1, keepdims=True) * EXP2_SCALE
            peaks[part, :] = jnp.broadcast_to(peak, (part.stop - part.start, HD))
            if new_refs is None:
                totals[part, :] = jnp.zeros((part.stop - part.start, HD), jnp.float32)
                acc[part, :] = jnp.zeros((part.stop - part.start, HD), jnp.float32)
            else:
                total, mixed = weigh(part, new_scores[part, :], new_value_ref[:, lanes])
                totals[part, :] = total
                acc[part, :] = mixed

        def weigh_block(entry, carry):
            values = value_ref[entry, :, lanes]
            for part in chunks:
                total, mixed = weigh(part, scores[entry, part, :], values)
                totals[part, :] += total
                acc[part, :] += mixed
            return carry

        lax.fori_loop(0, count, weigh_block, 0)
        for g in range(GROUP):
            part = slice(g * new_rows, (g + 1) * new_rows)
            total = jnp.sum(totals[part, :], axis=1, keepdims=True)
            safe = jnp.where(total > 0, total, 1.0)
            log_total = jnp.where(
                total > 0, peaks[part, 0:1] * math.log(2.0) + jnp.log(safe), EMPTY
            )
            put(kv * GROUP + g, acc[part, :] * (1.0 / safe), log_total)


def load_heads(query_ref, query_rows, kv):
    new_rows = query_ref.shape[0]
    for g in range(GROUP):
        head = kv * GROUP + g
        query_rows[g * new_rows : (g + 1) * new_rows, :] = query_ref[
            :, head * HD : (head + 1) * HD
        ]


def add_lane(tile, heads, head, column):
    lane = lax.broadcasted_iota(jnp.int32, tile.shape, 1)
    hit = (lax.rem(lane, heads) == head) & (lane < 3 * heads)
    return jnp.where(hit, column, tile)


def split_lanes(tile, heads):
    lane = lax.broadcasted_iota(jnp.int32, tile.shape, 1)
    high = tile.astype(jnp.bfloat16).astype(jnp.float32)
    middle = (tile - high).astype(jnp.bfloat16).astype(jnp.float32)
    low = tile - high - middle
    return jnp.where(lane < heads, high, jnp.where(lane < 2 * heads, middle, low)).astype(
        jnp.bfloat16
    )


def fetch(pool_size, meta_ref, request, stores, buffers, sems):
    count, base = place(meta_ref, request, pool_size)

    def copies(entry):
        return block_copies(meta_ref, base, entry, stores, buffers, sems, pool_size)

    def start(entry, carry):
        for copy in copies(entry):
            copy.start()
        return carry

    lax.fori_loop(0, count, start, 0)

    def ready(entry):
        for copy in copies(entry):
            copy.wait()

    return count, ready


def own_kernel(
    pool_size,
    meta_ref,
    query_ref,
    new_key_ref,
    new_value_ref,
    store_keys,
    store_values,
    out_ref,
    log_ref,
    key_buf,
    value_buf,
    new_key_buf,
    new_value_buf,
    query_rows,
    scores,
    new_scores,
    peaks,
    totals,
    acc,
    sems,
):
    count, ready = fetch(
        pool_size, meta_ref, meta_ref[0], (store_keys, store_values), (key_buf, value_buf), sems
    )
    new_rows, width = query_ref.shape
    heads = width // HD
    for buffer, source in ((new_key_buf, new_key_ref), (new_value_buf, new_value_ref)):
        buffer[:new_rows, :] = source[...]
        buffer[new_rows:, :] = jnp.zeros(
            (buffer.shape[0] - new_rows, buffer.shape[1]), jnp.bfloat16
        )
    log_ref[...] = jnp.zeros(log_ref.shape, jnp.float32)

    def put(head, out, log_total):
        out_ref[:, head * HD : (head + 1) * HD] = out
        log_ref[...] = add_lane(log_ref[...], heads, head, log_total)

    attend(
        functools.partial(load_heads, query_ref, query_rows),
        key_buf,
        value_buf,
        count,
        ready,
        (new_key_buf, new_value_buf, new_scores),
        new_rows,
        query_rows,
        scores,
        peaks,
        totals,
        acc,
        put,
    )


def other_kernel(pool_size, offsets, meta_ref, *refs):
    query_refs = refs[: len(offsets)]
    (
        store_keys,
        store_values,
        out_ref,
        key_buf,
        value_buf,
        query_rows,
        scores,
        peaks,
        totals,
        acc,
        log_tile,
        sems,
    ) = refs[len(offsets) :]
    if offsets[0] is None:
        wanted = [meta_ref[1 + 2 * pool_size + pool_size * MAXBLK]]
    else:
        wanted = [meta_ref[0] + offset for offset in offsets]
    there = [(x >= 0) & (x < pool_size) for x in wanted]
    request = wanted[0]
    for other, hit in zip(wanted[1:], there[1:]):
        request = jnp.where(hit, other, request)

    @pl.when(functools.reduce(jnp.logical_or, there))
    def _():
        count, ready = fetch(
            pool_size, meta_ref, request, (store_keys, store_values), (key_buf, value_buf), sems
        )
        new_rows, width = query_refs[0].shape
        heads = width // HD
        log_tile[...] = jnp.zeros(log_tile.shape, jnp.float32)

        def load(kv):
            for query_ref, hit in zip(query_refs, there):
                pl.when(hit)(functools.partial(load_heads, query_ref, query_rows, kv))

        def put(head, out, log_total):
            out_ref[:, head * HD : (head + 1) * HD] = out.astype(jnp.bfloat16)
            log_tile[...] = add_lane(log_tile[...], heads, head, log_total)

        attend(
            load,
            key_buf,
            value_buf,
            count,
            ready,
            None,
            new_rows,
            query_rows,
            scores,
            peaks,
            totals,
            acc,
            put,
        )
        out_ref[:, width:] = split_lanes(log_tile[...], heads)


def combine_kernel(sources, pool_size, meta_ref, own_ref, log_ref, *refs):
    out_ref = refs[-1]
    width = own_ref.shape[1]
    heads = width // HD
    logs = [log_ref[...]]
    valid = []
    for (offsets, source), part in zip(sources, refs[:-1]):
        if offsets:
            wanted = [meta_ref[0] + offset for offset in offsets]
            there = functools.reduce(
                jnp.logical_or, [(x >= 0) & (x < pool_size) for x in wanted]
            )
        else:
            there = meta_ref[0] != source
        valid.append(there)
        tile = part[:, width:].astype(jnp.float32)
        whole = (
            tile + pltpu.roll(tile, HD - heads, 1) + pltpu.roll(tile, HD - 2 * heads, 1)
        )
        logs.append(jnp.where(there, whole, EMPTY))
    peak = functools.reduce(jnp.maximum, logs)
    shares = [jnp.exp(x - peak) for x in logs]
    scale = 1.0 / functools.reduce(jnp.add, shares)
    shares = [x * scale for x in shares]
    for head in range(heads):
        lanes = slice(head * HD, (head + 1) * HD)
        mixed = own_ref[:, lanes] * shares[0][:, head : head + 1]
        for share, there, part in zip(shares[1:], valid, refs[:-1]):
            mixed = mixed + jnp.where(
                there, part[:, lanes].astype(jnp.float32) * share[:, head : head + 1], 0.0
            )
        out_ref[:, lanes] = mixed.astype(jnp.bfloat16)


def shards(
    queries,
    new_keys,
    new_values,
    store_keys,
    store_values,
    prefix_blocks,
    hit_store,
    hit_slot,
    decode_owner,
):
    pool_size = lax.axis_size("pool")
    my_index = lax.axis_index("pool").astype(jnp.int32)
    capacity = (MAXBLK + pool_size - 1) // pool_size
    new_rows = queries.shape[1]
    width = queries.shape[2]
    kv_width = new_keys.shape[2]
    block_len = store_keys.shape[1]
    rows = GROUP * new_rows
    padded_rows = -(-new_rows // (2 * HD)) * 2 * HD
    meta = jnp.concatenate(
        [my_index.reshape(1), prefix_blocks, hit_store[:, 0], hit_slot.reshape(-1)]
    )
    smem_spec = pl.BlockSpec(memory_space=pltpu.SMEM)
    hbm_spec = pl.BlockSpec(memory_space=pltpu.HBM)
    vmem_spec = pl.BlockSpec(memory_space=pltpu.VMEM)
    params = pltpu.CompilerParams(vmem_limit_bytes=VMEM_LIMIT)
    cost = pl.CostEstimate(flops=rows, bytes_accessed=rows, transcendentals=0)
    buffers = [pltpu.VMEM((capacity, block_len, kv_width), jnp.bfloat16)] * 2
    work = [
        pltpu.VMEM((rows, HD), jnp.bfloat16),
        pltpu.VMEM((capacity, rows, block_len), jnp.float32),
    ]
    state = [pltpu.VMEM((rows, HD), jnp.float32)] * 3
    sems = pltpu.SemaphoreType.DMA((2, capacity))

    def own_part(query):
        return pl.pallas_call(
            functools.partial(own_kernel, pool_size),
            in_specs=[smem_spec] + [vmem_spec] * 3 + [hbm_spec] * 2,
            out_specs=[vmem_spec] * 2,
            scratch_shapes=[
                *buffers,
                *[pltpu.VMEM((padded_rows, kv_width), jnp.bfloat16)] * 2,
                *work,
                pltpu.VMEM((rows, padded_rows), jnp.float32),
                *state,
                sems,
            ],
            out_shape=[
                jax.ShapeDtypeStruct((new_rows, width), jnp.float32),
                jax.ShapeDtypeStruct((new_rows, HD), jnp.float32),
            ],
            compiler_params=params,
            cost_estimate=cost,
            name="own_part",
        )(meta, query, new_keys[0], new_values[0], store_keys, store_values)

    def other_part(offsets, held, meta=meta):
        return pl.pallas_call(
            functools.partial(other_kernel, pool_size, offsets),
            in_specs=[smem_spec] + [vmem_spec] * len(held) + [hbm_spec] * 2,
            out_specs=vmem_spec,
            scratch_shapes=[
                *buffers,
                *work,
                *state,
                pltpu.VMEM((new_rows, HD), jnp.float32),
                sems,
            ],
            out_shape=jax.ShapeDtypeStruct((new_rows, width + HD), jnp.bfloat16),
            compiler_params=params,
            cost_estimate=cost,
            name="other_part",
        )(meta, *held, store_keys, store_values)

    def inside(index):
        return 0 <= index < pool_size

    def forward(array, distance, first):
        pairs = [
            (i, i + distance)
            for i in range(pool_size)
            if inside(i + distance) and inside(i - first)
        ]
        return lax.ppermute(array, "pool", pairs)

    query = queries[0]
    fresh = jnp.concatenate([new_keys[0], new_values[0]], axis=1)
    own_out, own_log = own_part(query)
    if pool_size <= LINE:
        sources = []
        parts = []
        right, left = query, query
        done = (own_out, own_log)
        for step in range(1, pool_size):
            right = forward(right, 1, step - 1)
            left = forward(left, -1, 1 - step)
            right, left, *done = lax.optimization_barrier((right, left, *done))
            if step == 1:
                own_out, own_log = done
            done = []
            if 2 * step < pool_size:
                groups = [((-step,), (right,)), ((step,), (left,))]
            else:
                groups = [((-step, step), (right, left))]
            for offsets, held in groups:
                packed = other_part(offsets, held)
                done.append(packed)
                pairs = [(i, i + x) for x in offsets for i in range(pool_size) if inside(i + x)]
                parts.append(lax.ppermute(packed, "pool", pairs))
                sources.append((tuple(-x for x in offsets), None))
        fresh, right = lax.optimization_barrier((fresh, right))
        aimed = jnp.where(
            (jnp.arange(pool_size) == decode_owner[my_index])[:, None, None], fresh[None], 0
        )
        moved = lax.all_to_all(aimed, "pool", split_axis=0, concat_axis=0, tiled=True)
    else:
        gathered = lax.all_gather(query, "pool", axis=0, tiled=False)
        packed = lax.map(
            lambda pair: other_part(
                (None,), (pair[0],), jnp.concatenate([meta, pair[1].reshape(1)])
            ),
            (gathered, jnp.arange(pool_size, dtype=jnp.int32)),
        )
        parts = lax.all_to_all(packed, "pool", split_axis=0, concat_axis=0, tiled=True)
        sources = [(None, source) for source in range(pool_size)]
        moved = lax.all_gather(fresh, "pool", axis=0, tiled=False)

    attended = pl.pallas_call(
        functools.partial(combine_kernel, tuple(sources), pool_size),
        in_specs=[smem_spec] + [vmem_spec] * (2 + len(sources)),
        out_specs=vmem_spec,
        out_shape=jax.ShapeDtypeStruct((new_rows, width), jnp.bfloat16),
        compiler_params=params,
        name="combine",
    )(meta, own_out, own_log, *parts)

    mine = decode_owner == my_index
    rank = jnp.cumsum(mine) - 1
    pushed = []
    for place_id in range(CAPP):
        total = jnp.zeros(fresh.shape, fresh.dtype)
        for source in range(pool_size):
            total = jnp.where(mine[source] & (rank[source] == place_id), moved[source], total)
        pushed.append(total)
    pushed = jnp.stack(pushed)
    return (attended[None], pushed[:, :, :kv_width], pushed[:, :, kv_width:])


def solution(mesh):
    in_specs = (
        P(("groups", "pool"), None, ("tensor", "sub")),
        P(("groups", "pool"), None, ("tensor", "sub")),
        P(("groups", "pool"), None, ("tensor", "sub")),
        P(("groups", "pool"), None, ("tensor", "sub")),
        P(("groups", "pool"), None, ("tensor", "sub")),
        P("groups"),
        P("groups", None),
        P("groups", None),
        P("groups"),
    )
    out_specs = (
        P(("groups", "pool"), None, ("tensor", "sub")),
        P(("groups", "pool"), None, ("tensor", "sub")),
        P(("groups", "pool"), None, ("tensor", "sub")),
    )
    return jax.shard_map(shards, mesh=mesh, in_specs=in_specs, out_specs=out_specs, check_vma=False)
```

```python
import functools
import math

import jax
import jax.numpy as jnp
from jax import lax
from jax.experimental import pallas as pl
from jax.experimental.pallas import tpu as pltpu
from jax.sharding import PartitionSpec as P

HEADS = 64
KVH = 8
HD = 128
MAXBLK = 32
CAPP = 2
GROUP = HEADS // KVH
EMPTY = -1e30
LINE = 8
TILE = 256
SCALE = 1.0 / math.sqrt(HD)
EXP2_SCALE = SCALE * math.log2(math.e)
VMEM_LIMIT = 48 * 1024 * 1024


def place(meta_ref, request, pool_size):
    prefix = meta_ref[1 + request]
    first = lax.rem(meta_ref[0] - meta_ref[1 + pool_size + request] + pool_size, pool_size)
    count = lax.max(lax.div(prefix - first + pool_size - 1, pool_size), 0)
    return count, 1 + 2 * pool_size + request * MAXBLK + first


def block_copies(meta_ref, base, entry, stores, buffers, sems, pool_size):
    slot = meta_ref[base + entry * pool_size]
    return [
        pltpu.make_async_copy(stores[i].at[slot], buffers[i].at[entry], sems.at[i, entry])
        for i in range(2)
    ]


def attend(key_ref, value_ref, count, ready, new_refs, new_rows, columns, scores, weights, peaks, totals, acc, put):
    kv_local, _, rows = columns.shape

    def visit(kv, keys, values, seen):
        block = lax.dot_general(
            keys, columns[kv], (((1,), (0,)), ((), ())), preferred_element_type=jnp.float32
        )
        if seen is not None:
            block = jnp.where(seen, block, EMPTY)
        scores[kv] = block
        turned = values.T
        for i in range(0, rows, TILE):
            part = slice(i, i + TILE)
            before = peaks[kv, :, part]
            block = scores[kv, :, part]
            peak = jnp.maximum(before, jnp.max(block, axis=0, keepdims=True))
            factor = jnp.exp2((before - peak) * EXP2_SCALE)
            weight = jnp.exp2(block * EXP2_SCALE - peak[0:1] * EXP2_SCALE)
            weights[kv, :, part] = weight.astype(jnp.bfloat16)
            added = jnp.sum(weight.reshape(-1, 8, TILE), axis=0)
            totals[kv, :, part] = totals[kv, :, part] * factor + added
            peaks[kv, :, part] = peak
            acc[kv, :, part] = acc[kv, :, part] * factor[0:1]
        acc[kv] += lax.dot_general(
            turned, weights[kv], (((1,), (0,)), ((), ())), preferred_element_type=jnp.float32
        )

    peaks[...] = jnp.full(peaks.shape, EMPTY, jnp.float32)
    totals[...] = jnp.zeros(totals.shape, jnp.float32)
    acc[...] = jnp.zeros(acc.shape, jnp.float32)
    if new_refs is not None:
        new_key_ref, new_value_ref = new_refs
        shape = (new_key_ref.shape[0], rows)
        seen = lax.broadcasted_iota(jnp.int32, shape, 0) <= lax.rem(
            lax.broadcasted_iota(jnp.int32, (1, rows), 1), new_rows
        )
        for kv in range(kv_local):
            lanes = slice(kv * HD, (kv + 1) * HD)
            visit(kv, new_key_ref[:, lanes], new_value_ref[:, lanes], seen)

    def visit_block(entry, carry):
        ready(entry)
        for kv in range(kv_local):
            lanes = slice(kv * HD, (kv + 1) * HD)
            visit(kv, key_ref[entry, :, lanes], value_ref[entry, :, lanes], None)
        return carry

    lax.fori_loop(0, count, visit_block, 0)
    for kv in range(kv_local):
        total = jnp.sum(totals[kv], axis=0, keepdims=True)
        safe = jnp.where(total > 0, total, 1.0)
        log_total = jnp.where(total > 0, peaks[kv, 0:1] * SCALE + jnp.log(safe), EMPTY)
        log_column = jnp.broadcast_to(log_total, (8, rows)).T
        out = (acc[kv] * (1.0 / safe)).T
        for g in range(GROUP):
            part = slice(g * new_rows, (g + 1) * new_rows)
            put(kv * GROUP + g, out[part], log_column[part, 0:1])


def load_heads(query_ref, query_rows, columns):
    new_rows = query_ref.shape[0]
    for kv in range(columns.shape[0]):
        for g in range(GROUP):
            head = kv * GROUP + g
            query_rows[g * new_rows : (g + 1) * new_rows, :] = query_ref[
                :, head * HD : (head + 1) * HD
            ]
        columns[kv] = query_rows[...].T


def add_lane(tile, heads, head, column):
    lane = lax.broadcasted_iota(jnp.int32, tile.shape, 1)
    hit = (lax.rem(lane, heads) == head) & (lane < 3 * heads)
    return jnp.where(hit, column, tile)


def split_lanes(tile, heads):
    lane = lax.broadcasted_iota(jnp.int32, tile.shape, 1)
    high = tile.astype(jnp.bfloat16).astype(jnp.float32)
    middle = (tile - high).astype(jnp.bfloat16).astype(jnp.float32)
    low = tile - high - middle
    return jnp.where(lane < heads, high, jnp.where(lane < 2 * heads, middle, low)).astype(
        jnp.bfloat16
    )


def fetch(pool_size, meta_ref, request, stores, buffers, sems):
    count, base = place(meta_ref, request, pool_size)

    def copies(entry):
        return block_copies(meta_ref, base, entry, stores, buffers, sems, pool_size)

    def start(entry, carry):
        for copy in copies(entry):
            copy.start()
        return carry

    lax.fori_loop(0, count, start, 0)

    def ready(entry):
        for copy in copies(entry):
            copy.wait()

    return count, ready


def own_kernel(
    pool_size,
    meta_ref,
    query_ref,
    new_key_ref,
    new_value_ref,
    store_keys,
    store_values,
    out_ref,
    log_ref,
    key_buf,
    value_buf,
    new_key_buf,
    new_value_buf,
    query_rows,
    columns,
    scores,
    weights,
    peaks,
    totals,
    acc,
    sems,
):
    count, ready = fetch(
        pool_size, meta_ref, meta_ref[0], (store_keys, store_values), (key_buf, value_buf), sems
    )
    new_rows, width = query_ref.shape
    heads = width // HD
    for buffer, source in ((new_key_buf, new_key_ref), (new_value_buf, new_value_ref)):
        buffer[:new_rows, :] = source[...]
        buffer[new_rows:, :] = jnp.zeros(
            (buffer.shape[0] - new_rows, buffer.shape[1]), jnp.bfloat16
        )
    log_ref[...] = jnp.zeros(log_ref.shape, jnp.float32)

    def put(head, out, log_total):
        out_ref[:, head * HD : (head + 1) * HD] = out
        log_ref[...] = add_lane(log_ref[...], heads, head, log_total)

    load_heads(query_ref, query_rows, columns)
    attend(
        key_buf,
        value_buf,
        count,
        ready,
        (new_key_buf, new_value_buf),
        new_rows,
        columns,
        scores,
        weights,
        peaks,
        totals,
        acc,
        put,
    )


def other_kernel(pool_size, offsets, meta_ref, *refs):
    query_refs = refs[: len(offsets)]
    (
        store_keys,
        store_values,
        out_ref,
        key_buf,
        value_buf,
        query_rows,
        columns,
        scores,
        weights,
        peaks,
        totals,
        acc,
        log_tile,
        sems,
    ) = refs[len(offsets) :]
    if offsets[0] is None:
        wanted = [meta_ref[1 + 2 * pool_size + pool_size * MAXBLK]]
    else:
        wanted = [meta_ref[0] + offset for offset in offsets]
    there = [(x >= 0) & (x < pool_size) for x in wanted]
    request = wanted[0]
    for other, hit in zip(wanted[1:], there[1:]):
        request = jnp.where(hit, other, request)

    @pl.when(functools.reduce(jnp.logical_or, there))
    def _():
        count, ready = fetch(
            pool_size, meta_ref, request, (store_keys, store_values), (key_buf, value_buf), sems
        )
        new_rows, width = query_refs[0].shape
        heads = width // HD
        log_tile[...] = jnp.zeros(log_tile.shape, jnp.float32)

        for query_ref, hit in zip(query_refs, there):
            pl.when(hit)(functools.partial(load_heads, query_ref, query_rows, columns))

        def put(head, out, log_total):
            out_ref[:, head * HD : (head + 1) * HD] = out.astype(jnp.bfloat16)
            log_tile[...] = add_lane(log_tile[...], heads, head, log_total)

        attend(
            key_buf,
            value_buf,
            count,
            ready,
            None,
            new_rows,
            columns,
            scores,
            weights,
            peaks,
            totals,
            acc,
            put,
        )
        out_ref[:, width:] = split_lanes(log_tile[...], heads)


def combine_kernel(sources, pool_size, meta_ref, own_ref, log_ref, *refs):
    out_ref = refs[-1]
    width = own_ref.shape[1]
    heads = width // HD
    logs = [log_ref[...]]
    valid = []
    for (offsets, source), part in zip(sources, refs[:-1]):
        if offsets:
            wanted = [meta_ref[0] + offset for offset in offsets]
            there = functools.reduce(
                jnp.logical_or, [(x >= 0) & (x < pool_size) for x in wanted]
            )
        else:
            there = meta_ref[0] != source
        valid.append(there)
        tile = part[:, width:].astype(jnp.float32)
        whole = (
            tile + pltpu.roll(tile, HD - heads, 1) + pltpu.roll(tile, HD - 2 * heads, 1)
        )
        logs.append(jnp.where(there, whole, EMPTY))
    peak = functools.reduce(jnp.maximum, logs)
    shares = [jnp.exp(x - peak) for x in logs]
    scale = 1.0 / functools.reduce(jnp.add, shares)
    shares = [x * scale for x in shares]
    for head in range(heads):
        lanes = slice(head * HD, (head + 1) * HD)
        mixed = own_ref[:, lanes] * shares[0][:, head : head + 1]
        for share, there, part in zip(shares[1:], valid, refs[:-1]):
            mixed = mixed + jnp.where(
                there, part[:, lanes].astype(jnp.float32) * share[:, head : head + 1], 0.0
            )
        out_ref[:, lanes] = mixed.astype(jnp.bfloat16)


def shards(
    queries,
    new_keys,
    new_values,
    store_keys,
    store_values,
    prefix_blocks,
    hit_store,
    hit_slot,
    decode_owner,
):
    pool_size = lax.axis_size("pool")
    my_index = lax.axis_index("pool").astype(jnp.int32)
    capacity = (MAXBLK + pool_size - 1) // pool_size
    new_rows = queries.shape[1]
    width = queries.shape[2]
    kv_width = new_keys.shape[2]
    block_len = store_keys.shape[1]
    rows = GROUP * new_rows
    meta = jnp.concatenate(
        [my_index.reshape(1), prefix_blocks, hit_store[:, 0], hit_slot.reshape(-1)]
    )
    smem_spec = pl.BlockSpec(memory_space=pltpu.SMEM)
    hbm_spec = pl.BlockSpec(memory_space=pltpu.HBM)
    vmem_spec = pl.BlockSpec(memory_space=pltpu.VMEM)
    params = pltpu.CompilerParams(vmem_limit_bytes=VMEM_LIMIT)
    cost = pl.CostEstimate(
        flops=8 * rows * block_len * kv_width * capacity, bytes_accessed=rows, transcendentals=0
    )
    buffers = [pltpu.VMEM((capacity, block_len, kv_width), jnp.bfloat16)] * 2
    kv_local = kv_width // HD
    work = [
        pltpu.VMEM((rows, HD), jnp.bfloat16),
        pltpu.VMEM((kv_local, HD, rows), jnp.bfloat16),
        pltpu.VMEM((kv_local, block_len, rows), jnp.float32),
        pltpu.VMEM((kv_local, block_len, rows), jnp.bfloat16),
        pltpu.VMEM((kv_local, 8, rows), jnp.float32),
        pltpu.VMEM((kv_local, 8, rows), jnp.float32),
        pltpu.VMEM((kv_local, HD, rows), jnp.float32),
    ]
    sems = pltpu.SemaphoreType.DMA((2, capacity))

    def own_part(query):
        return pl.pallas_call(
            functools.partial(own_kernel, pool_size),
            in_specs=[smem_spec] + [vmem_spec] * 3 + [hbm_spec] * 2,
            out_specs=[vmem_spec] * 2,
            scratch_shapes=[
                *buffers,
                *[pltpu.VMEM((block_len, kv_width), jnp.bfloat16)] * 2,
                *work,
                sems,
            ],
            out_shape=[
                jax.ShapeDtypeStruct((new_rows, width), jnp.float32),
                jax.ShapeDtypeStruct((new_rows, HD), jnp.float32),
            ],
            compiler_params=params,
            cost_estimate=cost,
            name="own_part",
        )(meta, query, new_keys[0], new_values[0], store_keys, store_values)

    def other_part(offsets, held, meta=meta):
        return pl.pallas_call(
            functools.partial(other_kernel, pool_size, offsets),
            in_specs=[smem_spec] + [vmem_spec] * len(held) + [hbm_spec] * 2,
            out_specs=vmem_spec,
            scratch_shapes=[
                *buffers,
                *work,
                pltpu.VMEM((new_rows, HD), jnp.float32),
                sems,
            ],
            out_shape=jax.ShapeDtypeStruct((new_rows, width + HD), jnp.bfloat16),
            compiler_params=params,
            cost_estimate=cost,
            name="other_part",
        )(meta, *held, store_keys, store_values)

    def inside(index):
        return 0 <= index < pool_size

    def forward(array, distance, first):
        pairs = [
            (i, i + distance)
            for i in range(pool_size)
            if inside(i + distance) and inside(i - first)
        ]
        return lax.ppermute(array, "pool", pairs)

    query = queries[0]
    fresh = jnp.concatenate([new_keys[0], new_values[0]], axis=1)
    own_out, own_log = own_part(query)
    if pool_size <= LINE:
        sources = []
        parts = []
        right, left = query, query
        done = [own_out, own_log]
        for step in range(1, pool_size):
            right = forward(right, 1, step - 1)
            left = forward(left, -1, 1 - step)
            settled = len(parts) - 1 if step > 2 else 0
            right, left, parts[:settled], done = lax.optimization_barrier(
                (right, left, parts[:settled], done)
            )
            if step == 1:
                own_out, own_log = done
            done = []
            if 2 * step < pool_size:
                groups = [((-step,), (right,)), ((step,), (left,))]
            else:
                groups = [((-step, step), (right, left))]
            for offsets, held in groups:
                packed = other_part(offsets, held)
                done.append(packed)
                pairs = [(i, i + x) for x in offsets for i in range(pool_size) if inside(i + x)]
                parts.append(lax.ppermute(packed, "pool", pairs))
                sources.append((tuple(-x for x in offsets), None))
        fresh, right = lax.optimization_barrier((fresh, right))
        aimed = jnp.where(
            (jnp.arange(pool_size) == decode_owner[my_index])[:, None, None], fresh[None], 0
        )
        moved = lax.all_to_all(aimed, "pool", split_axis=0, concat_axis=0, tiled=True)
    else:
        gathered = lax.all_gather(query, "pool", axis=0, tiled=False)
        packed = lax.map(
            lambda pair: other_part(
                (None,), (pair[0],), jnp.concatenate([meta, pair[1].reshape(1)])
            ),
            (gathered, jnp.arange(pool_size, dtype=jnp.int32)),
        )
        parts = lax.all_to_all(packed, "pool", split_axis=0, concat_axis=0, tiled=True)
        sources = [(None, source) for source in range(pool_size)]
        moved = lax.all_gather(fresh, "pool", axis=0, tiled=False)

    attended = pl.pallas_call(
        functools.partial(combine_kernel, tuple(sources), pool_size),
        in_specs=[smem_spec] + [vmem_spec] * (2 + len(sources)),
        out_specs=vmem_spec,
        out_shape=jax.ShapeDtypeStruct((new_rows, width), jnp.bfloat16),
        compiler_params=params,
        name="combine",
    )(meta, own_out, own_log, *parts)

    mine = decode_owner == my_index
    rank = jnp.cumsum(mine) - 1
    pushed = []
    for place_id in range(CAPP):
        total = jnp.zeros(fresh.shape, fresh.dtype)
        for source in range(pool_size):
            total = jnp.where(mine[source] & (rank[source] == place_id), moved[source], total)
        pushed.append(total)
    pushed = jnp.stack(pushed)
    return (attended[None], pushed[:, :, :kv_width], pushed[:, :, kv_width:])


def solution(mesh):
    in_specs = (
        P(("groups", "pool"), None, ("tensor", "sub")),
        P(("groups", "pool"), None, ("tensor", "sub")),
        P(("groups", "pool"), None, ("tensor", "sub")),
        P(("groups", "pool"), None, ("tensor", "sub")),
        P(("groups", "pool"), None, ("tensor", "sub")),
        P("groups"),
        P("groups", None),
        P("groups", None),
        P("groups"),
    )
    out_specs = (
        P(("groups", "pool"), None, ("tensor", "sub")),
        P(("groups", "pool"), None, ("tensor", "sub")),
        P(("groups", "pool"), None, ("tensor", "sub")),
    )
    return jax.shard_map(shards, mesh=mesh, in_specs=in_specs, out_specs=out_specs, check_vma=False)
```

```python
import functools
import math

import jax
import jax.numpy as jnp
from jax import lax
from jax.experimental import pallas as pl
from jax.experimental.pallas import tpu as pltpu
from jax.sharding import PartitionSpec as P

HEADS = 64
KVH = 8
HD = 128
MAXBLK = 32
CAPP = 2
GROUP = HEADS // KVH
EMPTY = -1e30
LINE = 8
TILE = 256
ONES = 16
SCALE = 1.0 / math.sqrt(HD)
EXP2_SCALE = SCALE * math.log2(math.e)
VMEM_LIMIT = 61 * 1024 * 1024


def fetch(pool_size, tables, request, stores, buffers, sems):
    prefix_ref, store_ref, slot_ref = tables
    me = lax.axis_index("pool")
    first = lax.rem(me - store_ref[request, 0] + pool_size, pool_size)
    count = lax.max(lax.div(prefix_ref[request] - first + pool_size - 1, pool_size), 0)

    def copies(entry):
        slot = slot_ref[request, first + entry * pool_size]
        return [
            pltpu.make_async_copy(stores[i].at[slot], buffers[i].at[entry], sems.at[i, entry])
            for i in range(2)
        ]

    def start(entry, carry):
        for copy in copies(entry):
            copy.start()
        return carry

    lax.fori_loop(0, count, start, 0)

    def ready(entry):
        for copy in copies(entry):
            copy.wait()

    return count, ready


def attend(key_ref, value_ref, count, ready, fresh, new_rows, columns, scores, weights, peaks, factors, turned, acc, put):
    kv_local, _, rows = columns.shape

    def visit(kv, keys, values, seen):
        block = lax.dot_general(
            keys, columns[kv], (((1,), (0,)), ((), ())), preferred_element_type=jnp.float32
        )
        if seen is not None:
            block = jnp.where(seen, block, EMPTY)
        scores[kv] = block
        turned[kv, :HD, :] = values.T
        for i in range(0, rows, TILE):
            part = slice(i, i + TILE)
            before = peaks[kv, :, part]
            block = scores[kv, :, part]
            peak = jnp.maximum(before, jnp.max(block, axis=0, keepdims=True))
            factors[kv, :, part] = jnp.exp2((before - peak) * EXP2_SCALE)
            peaks[kv, :, part] = peak
            weight = jnp.exp2(block * EXP2_SCALE - peak[0:1] * EXP2_SCALE)
            weights[kv, :, part] = weight.astype(jnp.bfloat16)
        added = lax.dot_general(
            turned[kv], weights[kv], (((1,), (0,)), ((), ())), preferred_element_type=jnp.float32
        )
        acc[kv] = acc[kv] * factors[kv, 0:1, :] + added

    peaks[...] = jnp.full(peaks.shape, EMPTY, jnp.float32)
    acc[...] = jnp.zeros(acc.shape, jnp.float32)
    turned[:, HD:, :] = jnp.ones((kv_local, ONES, turned.shape[2]), jnp.bfloat16)
    if fresh is not None:
        new_key_ref, new_value_ref = fresh
        shape = (new_key_ref.shape[0], rows)
        seen = lax.broadcasted_iota(jnp.int32, shape, 0) <= lax.rem(
            lax.broadcasted_iota(jnp.int32, (1, rows), 1), new_rows
        )
        for kv in range(kv_local):
            lanes = slice(kv * HD, (kv + 1) * HD)
            visit(kv, new_key_ref[:, lanes], new_value_ref[:, lanes], seen)

    def visit_block(entry, carry):
        ready(entry)
        for kv in range(kv_local):
            lanes = slice(kv * HD, (kv + 1) * HD)
            visit(kv, key_ref[entry, :, lanes], value_ref[entry, :, lanes], None)
        return carry

    lax.fori_loop(0, count, visit_block, 0)
    for kv in range(kv_local):
        total = acc[kv, HD : HD + 1, :]
        safe = jnp.where(total > 0, total, 1.0)
        log_total = jnp.where(total > 0, peaks[kv, 0:1] * SCALE + jnp.log(safe), EMPTY)
        log_column = jnp.broadcast_to(log_total, (8, rows)).T
        out = (acc[kv, :HD, :] * (1.0 / safe)).T
        for g in range(GROUP):
            part = slice(g * new_rows, (g + 1) * new_rows)
            put(kv * GROUP + g, out[part], log_column[part, 0:1])


def load_heads(query_ref, query_rows, columns):
    new_rows = query_ref.shape[0]
    for kv in range(columns.shape[0]):
        for g in range(GROUP):
            head = kv * GROUP + g
            query_rows[g * new_rows : (g + 1) * new_rows, :] = query_ref[
                :, head * HD : (head + 1) * HD
            ]
        columns[kv] = query_rows[...].T


def add_lane(tile, heads, head, column):
    lane = lax.broadcasted_iota(jnp.int32, tile.shape, 1)
    hit = (lax.rem(lane, heads) == head) & (lane < 3 * heads)
    return jnp.where(hit, column, tile)


def split_lanes(tile, heads):
    lane = lax.broadcasted_iota(jnp.int32, tile.shape, 1)
    high = tile.astype(jnp.bfloat16).astype(jnp.float32)
    middle = (tile - high).astype(jnp.bfloat16).astype(jnp.float32)
    low = tile - high - middle
    return jnp.where(lane < heads, high, jnp.where(lane < 2 * heads, middle, low)).astype(
        jnp.bfloat16
    )


def own_kernel(
    pool_size,
    prefix_ref,
    store_ref,
    slot_ref,
    payload_ref,
    store_keys,
    store_values,
    out_ref,
    log_ref,
    key_buf,
    value_buf,
    new_key_buf,
    new_value_buf,
    query_rows,
    columns,
    *state,
):
    *work, sems = state
    count, ready = fetch(
        pool_size,
        (prefix_ref, store_ref, slot_ref),
        lax.axis_index("pool"),
        (store_keys, store_values),
        (key_buf, value_buf),
        sems,
    )
    new_rows, width = out_ref.shape
    kv_width = new_key_buf.shape[1]
    heads = width // HD
    for i, buffer in enumerate((new_key_buf, new_value_buf)):
        buffer[:new_rows, :] = payload_ref[:, width + i * kv_width : width + (i + 1) * kv_width]
        buffer[new_rows:, :] = jnp.zeros((buffer.shape[0] - new_rows, kv_width), jnp.bfloat16)
    log_ref[...] = jnp.zeros(log_ref.shape, jnp.float32)

    def put(head, out, log_total):
        out_ref[:, head * HD : (head + 1) * HD] = out
        log_ref[...] = add_lane(log_ref[...], heads, head, log_total)

    load_heads(payload_ref, query_rows, columns)
    attend(
        key_buf,
        value_buf,
        count,
        ready,
        (new_key_buf, new_value_buf),
        new_rows,
        columns,
        *work,
        put,
    )


def other_kernel(pool_size, offsets, *refs):
    if offsets[0] is None:
        wanted = [refs[0][0]]
        refs = refs[1:]
    else:
        wanted = [lax.axis_index("pool") + offset for offset in offsets]
    tables, refs = refs[:3], refs[3:]
    payload_refs = refs[: len(offsets)]
    store_keys, store_values, out_ref, key_buf, value_buf, query_rows, columns, *state = refs[
        len(offsets) :
    ]
    *work, log_tile, sems = state
    there = [(x >= 0) & (x < pool_size) for x in wanted]
    request = wanted[0]
    for other, hit in zip(wanted[1:], there[1:]):
        request = jnp.where(hit, other, request)

    @pl.when(functools.reduce(jnp.logical_or, there))
    def _():
        count, ready = fetch(
            pool_size, tables, request, (store_keys, store_values), (key_buf, value_buf), sems
        )
        new_rows = out_ref.shape[0]
        width = out_ref.shape[1] - HD
        heads = width // HD
        log_tile[...] = jnp.zeros(log_tile.shape, jnp.float32)
        for payload_ref, hit in zip(payload_refs, there):
            pl.when(hit)(functools.partial(load_heads, payload_ref, query_rows, columns))

        def put(head, out, log_total):
            out_ref[:, head * HD : (head + 1) * HD] = out.astype(jnp.bfloat16)
            log_tile[...] = add_lane(log_tile[...], heads, head, log_total)

        attend(key_buf, value_buf, count, ready, None, new_rows, columns, *work, put)
        out_ref[:, width:] = split_lanes(log_tile[...], heads)


def combine_kernel(sources, pool_size, own_ref, log_ref, *refs):
    out_ref = refs[-1]
    width = own_ref.shape[1]
    heads = width // HD
    logs = [log_ref[...]]
    me = lax.axis_index("pool")
    for (offsets, source), part in zip(sources, refs[:-1]):
        if offsets:
            wanted = [me + offset for offset in offsets]
            there = functools.reduce(
                jnp.logical_or, [(x >= 0) & (x < pool_size) for x in wanted]
            )
        else:
            there = me != source
        tile = part[:, width:].astype(jnp.float32)
        whole = (
            tile + pltpu.roll(tile, HD - heads, 1) + pltpu.roll(tile, HD - 2 * heads, 1)
        )
        logs.append(jnp.where(there, whole, EMPTY))
    peak = functools.reduce(jnp.maximum, logs)
    shares = [jnp.exp(x - peak) for x in logs]
    scale = 1.0 / functools.reduce(jnp.add, shares)
    shares = [x * scale for x in shares]
    for head in range(heads):
        lanes = slice(head * HD, (head + 1) * HD)
        mixed = own_ref[:, lanes] * shares[0][:, head : head + 1]
        for share, part in zip(shares[1:], refs[:-1]):
            mixed = mixed + part[:, lanes].astype(jnp.float32) * share[:, head : head + 1]
        out_ref[:, lanes] = mixed.astype(jnp.bfloat16)


def shards(
    queries,
    new_keys,
    new_values,
    store_keys,
    store_values,
    prefix_blocks,
    hit_store,
    hit_slot,
    decode_owner,
):
    pool_size = lax.axis_size("pool")
    my_index = lax.axis_index("pool").astype(jnp.int32)
    capacity = (MAXBLK + pool_size - 1) // pool_size
    new_rows = queries.shape[1]
    width = queries.shape[2]
    kv_width = new_keys.shape[2]
    block_len = store_keys.shape[1]
    rows = GROUP * new_rows
    tables = (prefix_blocks, hit_store, hit_slot)
    smem_spec = pl.BlockSpec(memory_space=pltpu.SMEM)
    hbm_spec = pl.BlockSpec(memory_space=pltpu.HBM)
    vmem_spec = pl.BlockSpec(memory_space=pltpu.VMEM)
    params = pltpu.CompilerParams(vmem_limit_bytes=VMEM_LIMIT)
    cost = pl.CostEstimate(
        flops=8 * rows * block_len * kv_width * capacity, bytes_accessed=rows, transcendentals=0
    )
    buffers = [pltpu.VMEM((capacity, block_len, kv_width), jnp.bfloat16)] * 2
    kv_local = kv_width // HD
    work = [
        pltpu.VMEM((rows, HD), jnp.bfloat16),
        pltpu.VMEM((kv_local, HD, rows), jnp.bfloat16),
        pltpu.VMEM((kv_local, block_len, rows), jnp.float32),
        pltpu.VMEM((kv_local, block_len, rows), jnp.bfloat16),
        pltpu.VMEM((kv_local, 8, rows), jnp.float32),
        pltpu.VMEM((kv_local, 8, rows), jnp.float32),
        pltpu.VMEM((kv_local, HD + ONES, block_len), jnp.bfloat16),
        pltpu.VMEM((kv_local, HD + ONES, rows), jnp.float32),
    ]
    sems = pltpu.SemaphoreType.DMA((2, capacity))

    def own_part(payload):
        return pl.pallas_call(
            functools.partial(own_kernel, pool_size),
            in_specs=[smem_spec] * 3 + [vmem_spec] + [hbm_spec] * 2,
            out_specs=[vmem_spec] * 2,
            scratch_shapes=[
                *buffers,
                *[pltpu.VMEM((block_len, kv_width), jnp.bfloat16)] * 2,
                *work,
                sems,
            ],
            out_shape=[
                jax.ShapeDtypeStruct((new_rows, width), jnp.float32),
                jax.ShapeDtypeStruct((new_rows, HD), jnp.float32),
            ],
            compiler_params=params,
            cost_estimate=cost,
            name="own_part",
        )(*tables, payload, store_keys, store_values)

    def other_part(offsets, held, *request):
        return pl.pallas_call(
            functools.partial(other_kernel, pool_size, offsets),
            in_specs=[smem_spec] * (3 + len(request)) + [vmem_spec] * len(held) + [hbm_spec] * 2,
            out_specs=vmem_spec,
            scratch_shapes=[
                *buffers,
                *work,
                pltpu.VMEM((new_rows, HD), jnp.float32),
                sems,
            ],
            out_shape=jax.ShapeDtypeStruct((new_rows, width + HD), jnp.bfloat16),
            compiler_params=params,
            cost_estimate=cost,
            name="other_part",
        )(*request, *tables, *held, store_keys, store_values)

    def inside(index):
        return 0 <= index < pool_size

    def forward(array, distance, first):
        pairs = [
            (i, i + distance)
            for i in range(pool_size)
            if inside(i + distance) and inside(i - first)
        ]
        return lax.ppermute(array, "pool", pairs)

    payload = jnp.concatenate([queries[0], new_keys[0], new_values[0]], axis=1)
    own_out, own_log = own_part(payload)
    mine = decode_owner == my_index
    if pool_size <= LINE:
        sources = []
        parts = []
        right, left = payload, payload
        moved = [(mine[my_index], my_index, payload)]
        done = [own_out, own_log]
        for step in range(1, pool_size):
            right = forward(right, 1, step - 1)
            left = forward(left, -1, 1 - step)
            settled = len(parts) - 1 if step > 2 else 0
            right, left, parts[:settled], done = lax.optimization_barrier(
                (right, left, parts[:settled], done)
            )
            if step == 1:
                own_out, own_log = done
            done = []
            for source, array in ((my_index - step, right), (my_index + step, left)):
                there = (source >= 0) & (source < pool_size)
                source = jnp.clip(source, 0, pool_size - 1)
                moved.append((there & mine[source], source, array))
            if 2 * step < pool_size:
                groups = [((-step,), (right,)), ((step,), (left,))]
            else:
                groups = [((-step, step), (right, left))]
            for offsets, held in groups:
                packed = other_part(offsets, held)
                done.append(packed)
                pairs = [(i, i + x) for x in offsets for i in range(pool_size) if inside(i + x)]
                parts.append(lax.ppermute(packed, "pool", pairs))
                sources.append((tuple(-x for x in offsets), None))
    else:
        gathered = lax.all_gather(payload, "pool", axis=0, tiled=False)
        packed = lax.map(
            lambda pair: other_part((None,), (pair[0],), pair[1].reshape(1)),
            (gathered, jnp.arange(pool_size, dtype=jnp.int32)),
        )
        parts = lax.all_to_all(packed, "pool", split_axis=0, concat_axis=0, tiled=True)
        sources = [(None, source) for source in range(pool_size)]
        moved = [(mine[source], source, gathered[source]) for source in range(pool_size)]

    attended = pl.pallas_call(
        functools.partial(combine_kernel, tuple(sources), pool_size),
        in_specs=[vmem_spec] * (2 + len(sources)),
        out_specs=vmem_spec,
        out_shape=jax.ShapeDtypeStruct((new_rows, width), jnp.bfloat16),
        compiler_params=params,
        name="combine",
    )(own_out, own_log, *parts)

    rank = jnp.cumsum(mine) - 1
    pushed = []
    for place in range(CAPP):
        total = jnp.zeros((new_rows, 2 * kv_width), jnp.bfloat16)
        for hit, source, array in moved:
            total = jnp.where(hit & (rank[source] == place), array[:, width:], total)
        pushed.append(total)
    pushed = jnp.stack(pushed)
    return (attended[None], pushed[:, :, :kv_width], pushed[:, :, kv_width:])


def solution(mesh):
    in_specs = (
        P(("groups", "pool"), None, ("tensor", "sub")),
        P(("groups", "pool"), None, ("tensor", "sub")),
        P(("groups", "pool"), None, ("tensor", "sub")),
        P(("groups", "pool"), None, ("tensor", "sub")),
        P(("groups", "pool"), None, ("tensor", "sub")),
        P("groups"),
        P("groups", None),
        P("groups", None),
        P("groups"),
    )
    out_specs = (
        P(("groups", "pool"), None, ("tensor", "sub")),
        P(("groups", "pool"), None, ("tensor", "sub")),
        P(("groups", "pool"), None, ("tensor", "sub")),
    )
    return jax.shard_map(shards, mesh=mesh, in_specs=in_specs, out_specs=out_specs, check_vma=False)
```

```python
import functools
import math

import jax
import jax.numpy as jnp
from jax import lax
from jax.experimental import pallas as pl
from jax.experimental.pallas import tpu as pltpu
from jax.sharding import PartitionSpec as P

HEADS = 64
KVH = 8
HD = 128
MAXBLK = 32
CAPP = 2
GROUP = HEADS // KVH
EMPTY = -1e30
LINE = 8
TILE = 256
ONES = 16
SCALE = 1.0 / math.sqrt(HD)
EXP2_SCALE = SCALE * math.log2(math.e)
VMEM_LIMIT = 60 * 1024 * 1024 + 256 * 1024


def fetch(pool_size, tables, request, stores, buffers, sems):
    prefix_ref, store_ref, slot_ref = tables
    me = lax.axis_index("pool")
    first = lax.rem(me - store_ref[request, 0] + pool_size, pool_size)
    count = lax.max(lax.div(prefix_ref[request] - first + pool_size - 1, pool_size), 0)

    def copies(entry):
        slot = slot_ref[request, first + entry * pool_size]
        return [
            pltpu.make_async_copy(stores[i].at[slot], buffers[i].at[entry], sems.at[i, entry])
            for i in range(2)
        ]

    def start(entry, carry):
        for copy in copies(entry):
            copy.start()
        return carry

    lax.fori_loop(0, count, start, 0)

    def ready(entry):
        for copy in copies(entry):
            copy.wait()

    return count, ready


def attend(
    key_ref, value_ref, count, ready, fresh, new_rows, columns, turned, peaks, acc, log_type, put
):
    kv_local, _, rows = columns.shape

    def visit(keys, values, seen):
        for kv in range(kv_local):
            turned[kv, :HD, :] = values[kv].T
        tiles = [(kv, i) for kv in range(kv_local) for i in range(0, rows, TILE)]
        blocks = {}
        weights = {}
        for step in range(len(tiles) + 2):
            if step < len(tiles):
                kv, i = tiles[step]
                block = lax.dot_general(
                    keys[kv],
                    columns[kv, :, i : i + TILE],
                    (((1,), (0,)), ((), ())),
                    preferred_element_type=jnp.float32,
                )
                if seen is not None:
                    block = jnp.where(seen(i), block, EMPTY)
                blocks[step] = block
            if step >= 2:
                kv, i = tiles[step - 2]
                part = slice(i, i + TILE)
                weight, factor = weights.pop(step - 2)
                added = lax.dot_general(
                    turned[kv], weight, (((1,), (0,)), ((), ())), preferred_element_type=jnp.float32
                )
                acc[kv, :, part] = acc[kv, :, part] * factor + added
            if 1 <= step <= len(tiles):
                kv, i = tiles[step - 1]
                part = slice(i, i + TILE)
                block = blocks.pop(step - 1)
                before = peaks[kv, :, part]
                peak = jnp.maximum(before, jnp.max(block, axis=0, keepdims=True))
                peaks[kv, :, part] = peak
                factor = jnp.exp2((before - peak) * EXP2_SCALE)[0:1]
                weight = jnp.exp2(block * EXP2_SCALE - peak[0:1] * EXP2_SCALE)
                weights[step - 1] = (weight.astype(jnp.bfloat16), factor)

    def lanes_of(ref):
        return [ref[:, kv * HD : (kv + 1) * HD] for kv in range(kv_local)]

    peaks[...] = jnp.full(peaks.shape, EMPTY, jnp.float32)
    acc[...] = jnp.zeros(acc.shape, jnp.float32)
    turned[:, HD:, :] = jnp.ones((kv_local, ONES, turned.shape[2]), jnp.bfloat16)
    if fresh is not None:
        new_key_ref, new_value_ref = fresh

        def seen(i):
            shape = (new_key_ref.shape[0], TILE)
            row = lax.rem(lax.broadcasted_iota(jnp.int32, (1, TILE), 1) + i, new_rows)
            return lax.broadcasted_iota(jnp.int32, shape, 0) <= row

        visit(lanes_of(new_key_ref), lanes_of(new_value_ref), seen)

    def visit_block(entry, carry):
        ready(entry)
        visit(lanes_of(key_ref.at[entry]), lanes_of(value_ref.at[entry]), None)
        return carry

    lax.fori_loop(0, count, visit_block, 0)
    heads = kv_local * GROUP
    logs = []
    for kv in range(kv_local):
        total = acc[kv, HD : HD + 1, :]
        safe = jnp.where(total > 0, total, 1.0)
        logs.append(jnp.where(total > 0, peaks[kv, 0:1] * SCALE + jnp.log(safe), EMPTY))
        out = (acc[kv, :HD, :] * (1.0 / safe)).astype(log_type).T
        for g in range(GROUP):
            put(kv * GROUP + g, out[g * new_rows : (g + 1) * new_rows])
    logs += [logs[-1]] * (8 - len(logs))
    log_columns = jnp.concatenate(logs, axis=0).T
    lane = lax.broadcasted_iota(jnp.int32, (new_rows, HD), 1)
    place = jnp.where(lane < 3 * heads, lax.rem(lane, heads), -1)
    tile = jnp.zeros((new_rows, HD), jnp.float32)
    for kv in range(kv_local):
        for g in range(GROUP):
            column = log_columns[g * new_rows : (g + 1) * new_rows, kv : kv + 1]
            tile = jnp.where(place == kv * GROUP + g, column, tile)
    return tile


def load_heads(query_ref, query_rows, columns):
    new_rows = query_ref.shape[0]
    for kv in range(columns.shape[0]):
        for g in range(GROUP):
            head = kv * GROUP + g
            query_rows[g * new_rows : (g + 1) * new_rows, :] = query_ref[
                :, head * HD : (head + 1) * HD
            ]
        columns[kv] = query_rows[...].T


def split_lanes(tile, heads):
    lane = lax.broadcasted_iota(jnp.int32, tile.shape, 1)
    high = tile.astype(jnp.bfloat16).astype(jnp.float32)
    middle = (tile - high).astype(jnp.bfloat16).astype(jnp.float32)
    low = tile - high - middle
    return jnp.where(lane < heads, high, jnp.where(lane < 2 * heads, middle, low)).astype(
        jnp.bfloat16
    )


def own_kernel(
    pool_size,
    prefix_ref,
    store_ref,
    slot_ref,
    payload_ref,
    store_keys,
    store_values,
    out_ref,
    log_ref,
    key_buf,
    value_buf,
    new_key_buf,
    new_value_buf,
    query_rows,
    columns,
    *state,
):
    *work, sems = state
    count, ready = fetch(
        pool_size,
        (prefix_ref, store_ref, slot_ref),
        lax.axis_index("pool"),
        (store_keys, store_values),
        (key_buf, value_buf),
        sems,
    )
    new_rows, width = out_ref.shape
    kv_width = new_key_buf.shape[1]
    for i, buffer in enumerate((new_key_buf, new_value_buf)):
        buffer[:new_rows, :] = payload_ref[:, width + i * kv_width : width + (i + 1) * kv_width]
        buffer[new_rows:, :] = jnp.zeros((buffer.shape[0] - new_rows, kv_width), jnp.bfloat16)

    def put(head, out):
        out_ref[:, head * HD : (head + 1) * HD] = out

    load_heads(payload_ref, query_rows, columns)
    log_ref[...] = attend(
        key_buf,
        value_buf,
        count,
        ready,
        (new_key_buf, new_value_buf),
        new_rows,
        columns,
        *work,
        jnp.float32,
        put,
    )


def other_kernel(pool_size, offsets, *refs):
    if offsets[0] is None:
        wanted = [refs[0][0]]
        refs = refs[1:]
    else:
        wanted = [lax.axis_index("pool") + offset for offset in offsets]
    tables, refs = refs[:3], refs[3:]
    payload_refs = refs[: len(offsets)]
    store_keys, store_values, out_ref, key_buf, value_buf, query_rows, columns, *state = refs[
        len(offsets) :
    ]
    *work, sems = state
    there = [(x >= 0) & (x < pool_size) for x in wanted]
    request = wanted[0]
    for other, hit in zip(wanted[1:], there[1:]):
        request = jnp.where(hit, other, request)

    @pl.when(functools.reduce(jnp.logical_or, there))
    def _():
        count, ready = fetch(
            pool_size, tables, request, (store_keys, store_values), (key_buf, value_buf), sems
        )
        new_rows = out_ref.shape[0]
        width = out_ref.shape[1] - HD
        for payload_ref, hit in zip(payload_refs, there):
            pl.when(hit)(functools.partial(load_heads, payload_ref, query_rows, columns))

        def put(head, out):
            out_ref[:, head * HD : (head + 1) * HD] = out

        tile = attend(
            key_buf, value_buf, count, ready, None, new_rows, columns, *work, jnp.bfloat16, put
        )
        out_ref[:, width:] = split_lanes(tile, width // HD)


def push_kernel(pool_size, entries, owner_ref, *refs):
    payload_refs = refs[: len(entries)]
    key_out, value_out, zeros, sems = refs[len(entries) :]
    outs = (key_out, value_out)
    new_rows, kv_width = zeros.shape
    me = lax.axis_index("pool")
    zeros[...] = jnp.zeros(zeros.shape, jnp.bfloat16)

    def copy(source, i, place):
        return pltpu.make_async_copy(source, outs[i].at[place], sems.at[i, place])

    for (relative, request), payload_ref in zip(entries, payload_refs):
        source = me + request if relative else jnp.int32(request)
        there = (source >= 0) & (source < pool_size)
        source = jnp.clip(source, 0, pool_size - 1)
        rank = jnp.int32(0)
        for other in range(pool_size):
            rank += ((owner_ref[other] == me) & (other < source)).astype(jnp.int32)
        hit = there & (owner_ref[source] == me)
        width = payload_ref.shape[1] - 2 * kv_width
        for place in range(CAPP):

            @pl.when(hit & (rank == place))
            def _():
                for i in range(2):
                    start = width + i * kv_width
                    copy(payload_ref.at[:, start : start + kv_width], i, place).start()

    total = jnp.int32(0)
    for other in range(pool_size):
        total += (owner_ref[other] == me).astype(jnp.int32)
    for place in range(CAPP):

        @pl.when(total <= place)
        def _():
            for i in range(2):
                copy(zeros, i, place).start()

    for place in range(CAPP):
        for i in range(2):
            copy(zeros, i, place).wait()


def combine_kernel(sources, pool_size, out_ref_count, own_ref, log_ref, *refs):
    parts = refs[: len(sources)]
    out_ref = refs[len(sources)]
    width = own_ref.shape[1]
    heads = width // HD
    logs = [log_ref[...]]
    me = lax.axis_index("pool")
    for (offsets, source), part in zip(sources, parts):
        if offsets:
            wanted = [me + offset for offset in offsets]
            there = functools.reduce(
                jnp.logical_or, [(x >= 0) & (x < pool_size) for x in wanted]
            )
        else:
            there = me != source
        tile = part[:, width:].astype(jnp.float32)
        whole = (
            tile + pltpu.roll(tile, HD - heads, 1) + pltpu.roll(tile, HD - 2 * heads, 1)
        )
        logs.append(jnp.where(there, whole, EMPTY))
    peak = functools.reduce(jnp.maximum, logs)
    shares = [jnp.exp(x - peak) for x in logs]
    total = functools.reduce(jnp.add, shares)
    shares = [x * (1.0 / total) for x in shares]
    for head in range(heads):
        lanes = slice(head * HD, (head + 1) * HD)
        mixed = own_ref[:, lanes] * shares[0][:, head : head + 1]
        for share, part in zip(shares[1:], parts):
            mixed = mixed + part[:, lanes].astype(jnp.float32) * share[:, head : head + 1]
        out_ref[:, lanes] = mixed.astype(out_ref.dtype)
    if out_ref_count == 2:
        refs[len(sources) + 1][...] = peak + jnp.log(total)


def shards(
    queries,
    new_keys,
    new_values,
    store_keys,
    store_values,
    prefix_blocks,
    hit_store,
    hit_slot,
    decode_owner,
):
    pool_size = lax.axis_size("pool")
    capacity = (MAXBLK + pool_size - 1) // pool_size
    new_rows = queries.shape[1]
    width = queries.shape[2]
    kv_width = new_keys.shape[2]
    block_len = store_keys.shape[1]
    rows = GROUP * new_rows
    tables = (prefix_blocks, hit_store, hit_slot)
    smem_spec = pl.BlockSpec(memory_space=pltpu.SMEM)
    hbm_spec = pl.BlockSpec(memory_space=pltpu.HBM)
    vmem_spec = pl.BlockSpec(memory_space=pltpu.VMEM)
    params = pltpu.CompilerParams(vmem_limit_bytes=VMEM_LIMIT)

    def cost(share):
        return pl.CostEstimate(
            flops=share * rows * block_len * kv_width * capacity,
            bytes_accessed=rows,
            transcendentals=0,
        )

    buffers = [pltpu.VMEM((capacity, block_len, kv_width), jnp.bfloat16)] * 2
    kv_local = kv_width // HD
    work = [
        pltpu.VMEM((rows, HD), jnp.bfloat16),
        pltpu.VMEM((kv_local, HD, rows), jnp.bfloat16),
        pltpu.VMEM((kv_local, HD + ONES, block_len), jnp.bfloat16),
        pltpu.VMEM((kv_local, 8, rows), jnp.float32),
        pltpu.VMEM((kv_local, HD + ONES, rows), jnp.float32),
    ]
    sems = pltpu.SemaphoreType.DMA((2, capacity))

    def own_part(payload):
        return pl.pallas_call(
            functools.partial(own_kernel, pool_size),
            in_specs=[smem_spec] * 3 + [vmem_spec] + [hbm_spec] * 2,
            out_specs=[vmem_spec] * 2,
            scratch_shapes=[
                *buffers,
                *[pltpu.VMEM((block_len, kv_width), jnp.bfloat16)] * 2,
                *work,
                sems,
            ],
            out_shape=[
                jax.ShapeDtypeStruct((new_rows, width), jnp.float32),
                jax.ShapeDtypeStruct((new_rows, HD), jnp.float32),
            ],
            compiler_params=params,
            cost_estimate=cost(8),
            name="own_part",
        )(*tables, payload, store_keys, store_values)

    def other_part(offsets, held, *request):
        return pl.pallas_call(
            functools.partial(other_kernel, pool_size, offsets),
            in_specs=[smem_spec] * (3 + len(request)) + [vmem_spec] * len(held) + [hbm_spec] * 2,
            out_specs=vmem_spec,
            scratch_shapes=[
                *buffers,
                *work,
                sems,
            ],
            out_shape=jax.ShapeDtypeStruct((new_rows, width + HD), jnp.bfloat16),
            compiler_params=params,
            cost_estimate=cost(0 if len(held) == 1 else 8),
            name="other_part",
        )(*request, *tables, *held, store_keys, store_values)

    def combine(own, log, sources, parts, last=True):
        out_shape = [jax.ShapeDtypeStruct((new_rows, width), jnp.bfloat16 if last else jnp.float32)]
        if not last:
            out_shape.append(jax.ShapeDtypeStruct((new_rows, HD), jnp.float32))
        out = pl.pallas_call(
            functools.partial(combine_kernel, tuple(sources), pool_size, len(out_shape)),
            in_specs=[vmem_spec] * (2 + len(sources)),
            out_specs=[vmem_spec] * len(out_shape),
            out_shape=out_shape,
            compiler_params=params,
            name="combine",
        )(own, log, *parts)
        return out[0] if last else out

    def inside(index):
        return 0 <= index < pool_size

    def forward(array, distance, first):
        pairs = [
            (i, i + distance)
            for i in range(pool_size)
            if inside(i + distance) and inside(i - first)
        ]
        return lax.ppermute(array, "pool", pairs)

    payload = jnp.concatenate([queries[0], new_keys[0], new_values[0]], axis=1)
    own_out, own_log = own_part(payload)
    if pool_size <= LINE:
        sources = []
        parts = []
        right, left = payload, payload
        moved = [((True, 0), payload)]
        done = [own_out, own_log]
        for step in range(1, pool_size):
            right = forward(right, 1, step - 1)
            left = forward(left, -1, 1 - step)
            right, left, done = lax.optimization_barrier((right, left, done))
            if step == 1:
                own_out, own_log = done
            done = []
            moved += [((True, -step), right), ((True, step), left)]
            held_right, held_left = right, left
            if step == 2:
                held_right, held_left, parts = lax.optimization_barrier((right, left, parts))
            if 2 * step < pool_size:
                groups = [((-step,), (held_right,)), ((step,), (held_left,))]
            else:
                groups = [((-step, step), (held_right, held_left))]
            for offsets, held in groups:
                packed = other_part(offsets, held)
                done.append(packed)
                pairs = [(i, i + x) for x in offsets for i in range(pool_size) if inside(i + x)]
                parts.append(lax.ppermute(packed, "pool", pairs))
                sources.append((tuple(-x for x in offsets), None))
        if len(parts) > 2:
            own_out, own_log, done = lax.optimization_barrier((own_out, own_log, done))
            own_out, own_log = combine(own_out, own_log, sources[:-2], parts[:-2], last=False)
            sources, parts = sources[-2:], parts[-2:]
    else:
        gathered = lax.all_gather(payload, "pool", axis=0, tiled=False)
        packed = lax.map(
            lambda pair: other_part((None,), (pair[0],), pair[1].reshape(1)),
            (gathered, jnp.arange(pool_size, dtype=jnp.int32)),
        )
        parts = lax.all_to_all(packed, "pool", split_axis=0, concat_axis=0, tiled=True)
        sources = [(None, source) for source in range(pool_size)]
        moved = [((False, source), gathered[source]) for source in range(pool_size)]

    attended = combine(own_out, own_log, sources, parts)
    pushed_keys, pushed_values = pl.pallas_call(
        functools.partial(push_kernel, pool_size, tuple(entry for entry, _ in moved)),
        in_specs=[smem_spec] + [hbm_spec] * len(moved),
        out_specs=[hbm_spec] * 2,
        scratch_shapes=[
            pltpu.VMEM((new_rows, kv_width), jnp.bfloat16),
            pltpu.SemaphoreType.DMA((2, CAPP)),
        ],
        out_shape=[jax.ShapeDtypeStruct((CAPP, new_rows, kv_width), jnp.bfloat16)] * 2,
        compiler_params=params,
        name="push",
    )(decode_owner, *[array for _, array in moved])
    return (attended[None], pushed_keys, pushed_values)


def solution(mesh):
    in_specs = (
        P(("groups", "pool"), None, ("tensor", "sub")),
        P(("groups", "pool"), None, ("tensor", "sub")),
        P(("groups", "pool"), None, ("tensor", "sub")),
        P(("groups", "pool"), None, ("tensor", "sub")),
        P(("groups", "pool"), None, ("tensor", "sub")),
        P("groups"),
        P("groups", None),
        P("groups", None),
        P("groups"),
    )
    out_specs = (
        P(("groups", "pool"), None, ("tensor", "sub")),
        P(("groups", "pool"), None, ("tensor", "sub")),
        P(("groups", "pool"), None, ("tensor", "sub")),
    )
    return jax.shard_map(shards, mesh=mesh, in_specs=in_specs, out_specs=out_specs, check_vma=False)
```

```python
import functools
import math

import jax
import jax.numpy as jnp
from jax import lax
from jax.experimental import pallas as pl
from jax.experimental.pallas import tpu as pltpu
from jax.sharding import PartitionSpec as P

HEADS = 64
KVH = 8
HD = 128
MAXBLK = 32
CAPP = 2
GROUP = HEADS // KVH
EMPTY = -1e30
TILE = 256
ONES = 16
SCALE = 1.0 / math.sqrt(HD)
EXP2_SCALE = SCALE * math.log2(math.e)
VMEM_LIMIT = 63 * 1024 * 1024


def fetch(pool_size, tables, request, stores, buffers, sems):
    prefix_ref, store_ref, slot_ref = tables
    me = lax.axis_index("pool")
    first = lax.rem(me - store_ref[request, 0] + pool_size, pool_size)
    count = lax.max(lax.div(prefix_ref[request] - first + pool_size - 1, pool_size), 0)

    def copies(entry):
        slot = slot_ref[request, first + entry * pool_size]
        return [
            pltpu.make_async_copy(stores[i].at[slot], buffers[i].at[entry], sems.at[i, entry])
            for i in range(2)
        ]

    def start(entry, carry):
        for copy in copies(entry):
            copy.start()
        return carry

    lax.fori_loop(0, count, start, 0)

    def ready(entry):
        for copy in copies(entry):
            copy.wait()

    return count, ready


def attend(
    key_ref,
    value_ref,
    count,
    ready,
    fresh,
    new_rows,
    columns,
    scores,
    weights,
    peaks,
    factors,
    turned,
    acc,
    log_type,
    put,
):
    kv_local, _, rows = columns.shape

    def visit(keys, values, seen):
        def score(kv):
            turned[kv, :HD, :] = values[kv].T
            block = lax.dot_general(
                keys[kv], columns[kv], (((1,), (0,)), ((), ())), preferred_element_type=jnp.float32
            )
            if seen is not None:
                block = jnp.where(seen, block, EMPTY)
            scores[kv] = block

        def weigh(kv):
            for i in range(0, rows, TILE):
                part = slice(i, i + TILE)
                before = peaks[kv, :, part]
                block = scores[kv, :, part]
                peak = jnp.maximum(before, jnp.max(block, axis=0, keepdims=True))
                factors[kv, :, part] = jnp.exp2((before - peak) * EXP2_SCALE)
                peaks[kv, :, part] = peak
                weight = jnp.exp2(block * EXP2_SCALE - peak[0:1] * EXP2_SCALE)
                weights[kv, :, part] = weight.astype(jnp.bfloat16)

        def mix(kv):
            added = lax.dot_general(
                turned[kv], weights[kv], (((1,), (0,)), ((), ())), preferred_element_type=jnp.float32
            )
            acc[kv] = acc[kv] * factors[kv, 0:1, :] + added

        for step in range(kv_local + 2):
            for offset, stage in ((0, score), (2, mix), (1, weigh)):
                if 0 <= step - offset < kv_local:
                    stage(step - offset)

    def lanes_of(ref):
        return [ref[:, kv * HD : (kv + 1) * HD] for kv in range(kv_local)]

    peaks[...] = jnp.full(peaks.shape, EMPTY, jnp.float32)
    acc[...] = jnp.zeros(acc.shape, jnp.float32)
    turned[:, HD:, :] = jnp.ones((kv_local, ONES, turned.shape[2]), jnp.bfloat16)
    if fresh is not None:
        new_key_ref, new_value_ref = fresh

        row = lax.rem(lax.broadcasted_iota(jnp.int32, (1, rows), 1), new_rows)
        seen = lax.broadcasted_iota(jnp.int32, (new_key_ref.shape[0], rows), 0) <= row
        visit(lanes_of(new_key_ref), lanes_of(new_value_ref), seen)

    def visit_block(entry, carry):
        ready(entry)
        visit(lanes_of(key_ref.at[entry]), lanes_of(value_ref.at[entry]), None)
        return carry

    lax.fori_loop(0, count, visit_block, 0)
    heads = kv_local * GROUP
    logs = []
    for kv in range(kv_local):
        total = acc[kv, HD : HD + 1, :]
        safe = jnp.where(total > 0, total, 1.0)
        logs.append(jnp.where(total > 0, peaks[kv, 0:1] * SCALE + jnp.log(safe), EMPTY))
        out = (acc[kv, :HD, :] * (1.0 / safe)).astype(log_type).T
        for g in range(GROUP):
            put(kv * GROUP + g, out[g * new_rows : (g + 1) * new_rows])
    logs += [logs[-1]] * (8 - len(logs))
    log_columns = jnp.concatenate(logs, axis=0).T
    lane = lax.broadcasted_iota(jnp.int32, (new_rows, HD), 1)
    place = jnp.where(lane < 3 * heads, lax.rem(lane, heads), -1)
    tile = jnp.zeros((new_rows, HD), jnp.float32)
    for kv in range(kv_local):
        for g in range(GROUP):
            column = log_columns[g * new_rows : (g + 1) * new_rows, kv : kv + 1]
            tile = jnp.where(place == kv * GROUP + g, column, tile)
    return tile


def load_heads(query_ref, query_rows, columns):
    new_rows = query_ref.shape[0]
    for kv in range(columns.shape[0]):
        for g in range(GROUP):
            head = kv * GROUP + g
            query_rows[g * new_rows : (g + 1) * new_rows, :] = query_ref[
                :, head * HD : (head + 1) * HD
            ]
        columns[kv] = query_rows[...].T


def split_lanes(tile, heads):
    lane = lax.broadcasted_iota(jnp.int32, tile.shape, 1)
    high = tile.astype(jnp.bfloat16).astype(jnp.float32)
    middle = (tile - high).astype(jnp.bfloat16).astype(jnp.float32)
    low = tile - high - middle
    return jnp.where(lane < heads, high, jnp.where(lane < 2 * heads, middle, low)).astype(
        jnp.bfloat16
    )


def own_kernel(
    pool_size,
    prefix_ref,
    store_ref,
    slot_ref,
    payload_ref,
    store_keys,
    store_values,
    out_ref,
    log_ref,
    key_buf,
    value_buf,
    new_key_buf,
    new_value_buf,
    query_rows,
    columns,
    *state,
):
    *work, sems = state
    count, ready = fetch(
        pool_size,
        (prefix_ref, store_ref, slot_ref),
        lax.axis_index("pool"),
        (store_keys, store_values),
        (key_buf, value_buf),
        sems,
    )
    new_rows, width = out_ref.shape
    kv_width = new_key_buf.shape[1]
    for i, buffer in enumerate((new_key_buf, new_value_buf)):
        buffer[:new_rows, :] = payload_ref[:, width + i * kv_width : width + (i + 1) * kv_width]
        buffer[new_rows:, :] = jnp.zeros((buffer.shape[0] - new_rows, kv_width), jnp.bfloat16)

    def put(head, out):
        out_ref[:, head * HD : (head + 1) * HD] = out

    load_heads(payload_ref, query_rows, columns)
    log_ref[...] = attend(
        key_buf,
        value_buf,
        count,
        ready,
        (new_key_buf, new_value_buf),
        new_rows,
        columns,
        *work,
        jnp.float32,
        put,
    )


def other_kernel(pool_size, partners, *refs):
    if partners is None:
        request = refs[0][0]
        choice = [None]
        refs = refs[1:]
    else:
        me = lax.axis_index("pool")
        inner = is_inner(me)
        request = me ^ jnp.where(inner, partners[0], partners[1])
        choice = [inner, jnp.logical_not(inner)]
    tables, refs = refs[:3], refs[3:]
    payload_refs = refs[: len(choice)]
    store_keys, store_values, out_ref, key_buf, value_buf, query_rows, columns, *state = refs[
        len(choice) :
    ]
    *work, query_buf, query_sem, sems = state
    new_rows = out_ref.shape[0]
    width = out_ref.shape[1] - HD

    def query_copy(payload_ref):
        return pltpu.make_async_copy(payload_ref.at[:, :width], query_buf, query_sem)

    for payload_ref, hit in zip(payload_refs, choice):
        if hit is None:
            query_copy(payload_ref).start()
        else:
            pl.when(hit)(functools.partial(query_copy(payload_ref).start))
    count, ready = fetch(
        pool_size, tables, request, (store_keys, store_values), (key_buf, value_buf), sems
    )
    query_copy(payload_refs[0]).wait()
    load_heads(query_buf, query_rows, columns)

    def put(head, out):
        out_ref[:, head * HD : (head + 1) * HD] = out

    tile = attend(
        key_buf, value_buf, count, ready, None, new_rows, columns, *work, jnp.bfloat16, put
    )
    out_ref[:, width:] = split_lanes(tile, width // HD)


def is_inner(place):
    return (place == 1) | (place == 2)


def source_of(me, entry):
    if isinstance(entry, int):
        return jnp.bool_(True), jnp.int32(entry)
    inner = is_inner(me)
    masks = [0 if mask is None else mask for mask in entry]
    there = jnp.where(inner, entry[0] is not None, entry[1] is not None)
    return there, me ^ jnp.where(inner, masks[0], masks[1])


def push_kernel(pool_size, entries, owner_ref, *refs):
    payload_refs = refs[: len(entries)]
    key_out, value_out, zeros, sems = refs[len(entries) :]
    outs = (key_out, value_out)
    new_rows, kv_width = zeros.shape
    me = lax.axis_index("pool")
    zeros[...] = jnp.zeros(zeros.shape, jnp.bfloat16)

    def copy(source, i, place):
        return pltpu.make_async_copy(source, outs[i].at[place], sems.at[i, place])

    for entry, payload_ref in zip(entries, payload_refs):
        there, source = source_of(me, entry)
        rank = jnp.int32(0)
        for other in range(pool_size):
            rank += ((owner_ref[other] == me) & (other < source)).astype(jnp.int32)
        hit = there & (owner_ref[source] == me)
        width = payload_ref.shape[1] - 2 * kv_width
        for place in range(CAPP):

            @pl.when(hit & (rank == place))
            def _():
                for i in range(2):
                    start = width + i * kv_width
                    copy(payload_ref.at[:, start : start + kv_width], i, place).start()

    total = jnp.int32(0)
    for other in range(pool_size):
        total += (owner_ref[other] == me).astype(jnp.int32)
    for place in range(CAPP):

        @pl.when(total <= place)
        def _():
            for i in range(2):
                copy(zeros, i, place).start()

    for place in range(CAPP):
        for i in range(2):
            copy(zeros, i, place).wait()


def combine_kernel(sources, pool_size, out_ref_count, own_ref, log_ref, *refs):
    parts = refs[: len(sources)]
    out_ref = refs[len(sources)]
    width = own_ref.shape[1]
    heads = width // HD
    logs = [log_ref[...]]
    me = lax.axis_index("pool")
    for source, part in zip(sources, parts):
        there, request = source_of(me, source)
        there = there & (request != me)
        tile = part[:, width:].astype(jnp.float32)
        whole = (
            tile + pltpu.roll(tile, HD - heads, 1) + pltpu.roll(tile, HD - 2 * heads, 1)
        )
        logs.append(jnp.where(there, whole, EMPTY))
    peak = functools.reduce(jnp.maximum, logs)
    shares = [jnp.exp(x - peak) for x in logs]
    total = functools.reduce(jnp.add, shares)
    shares = [x * (1.0 / total) for x in shares]
    for head in range(heads):
        lanes = slice(head * HD, (head + 1) * HD)
        mixed = own_ref[:, lanes] * shares[0][:, head : head + 1]
        for share, part in zip(shares[1:], parts):
            mixed = mixed + part[:, lanes].astype(jnp.float32) * share[:, head : head + 1]
        out_ref[:, lanes] = mixed.astype(out_ref.dtype)
    if out_ref_count == 2:
        refs[len(sources) + 1][...] = peak + jnp.log(total)


def shards(
    queries,
    new_keys,
    new_values,
    store_keys,
    store_values,
    prefix_blocks,
    hit_store,
    hit_slot,
    decode_owner,
):
    pool_size = lax.axis_size("pool")
    capacity = (MAXBLK + pool_size - 1) // pool_size
    new_rows = queries.shape[1]
    width = queries.shape[2]
    kv_width = new_keys.shape[2]
    block_len = store_keys.shape[1]
    rows = GROUP * new_rows
    tables = (prefix_blocks, hit_store, hit_slot)
    smem_spec = pl.BlockSpec(memory_space=pltpu.SMEM)
    hbm_spec = pl.BlockSpec(memory_space=pltpu.HBM)
    vmem_spec = pl.BlockSpec(memory_space=pltpu.VMEM)
    params = pltpu.CompilerParams(vmem_limit_bytes=VMEM_LIMIT)

    def cost(share):
        return pl.CostEstimate(
            flops=share * rows * block_len * kv_width * capacity,
            bytes_accessed=rows,
            transcendentals=0,
        )

    buffers = [pltpu.VMEM((capacity, block_len, kv_width), jnp.bfloat16)] * 2
    kv_local = kv_width // HD
    work = [
        pltpu.VMEM((rows, HD), jnp.bfloat16),
        pltpu.VMEM((kv_local, HD, rows), jnp.bfloat16),
        pltpu.VMEM((kv_local, block_len, rows), jnp.float32),
        pltpu.VMEM((kv_local, block_len, rows), jnp.bfloat16),
        pltpu.VMEM((kv_local, 8, rows), jnp.float32),
        pltpu.VMEM((kv_local, 8, rows), jnp.float32),
        pltpu.VMEM((kv_local, HD + ONES, block_len), jnp.bfloat16),
        pltpu.VMEM((kv_local, HD + ONES, rows), jnp.float32),
    ]
    sems = pltpu.SemaphoreType.DMA((2, capacity))

    def own_part(payload):
        return pl.pallas_call(
            functools.partial(own_kernel, pool_size),
            in_specs=[smem_spec] * 3 + [vmem_spec] + [hbm_spec] * 2,
            out_specs=[vmem_spec] * 2,
            scratch_shapes=[
                *buffers,
                *[pltpu.VMEM((block_len, kv_width), jnp.bfloat16)] * 2,
                *work,
                sems,
            ],
            out_shape=[
                jax.ShapeDtypeStruct((new_rows, width), jnp.float32),
                jax.ShapeDtypeStruct((new_rows, HD), jnp.float32),
            ],
            compiler_params=params,
            cost_estimate=cost(8),
            name="own_part",
        )(*tables, payload, store_keys, store_values)

    def other_part(partners, held, *request, share=8):
        return pl.pallas_call(
            functools.partial(other_kernel, pool_size, partners),
            in_specs=[smem_spec] * (3 + len(request)) + [hbm_spec] * (len(held) + 2),
            out_specs=vmem_spec,
            scratch_shapes=[
                *buffers,
                *work,
                pltpu.VMEM((new_rows, width), jnp.bfloat16),
                pltpu.SemaphoreType.DMA,
                sems,
            ],
            out_shape=jax.ShapeDtypeStruct((new_rows, width + HD), jnp.bfloat16),
            compiler_params=params,
            cost_estimate=cost(share),
            name="other_part",
        )(*request, *tables, *held, store_keys, store_values)

    def combine(own, log, sources, parts, last=True):
        out_shape = [jax.ShapeDtypeStruct((new_rows, width), jnp.bfloat16 if last else jnp.float32)]
        if not last:
            out_shape.append(jax.ShapeDtypeStruct((new_rows, HD), jnp.float32))
        out = pl.pallas_call(
            functools.partial(combine_kernel, tuple(sources), pool_size, len(out_shape)),
            in_specs=[vmem_spec] * (2 + len(sources)),
            out_specs=[vmem_spec] * len(out_shape),
            out_shape=out_shape,
            compiler_params=params,
            name="combine",
        )(own, log, *parts)
        return out[0] if last else out

    payload = jnp.concatenate([queries[0], new_keys[0], new_values[0]], axis=1)
    own_out, own_log = own_part(payload)
    if pool_size == 4:
        def send(array, *pairs):
            return lax.ppermute(array, "pool", pairs)

        near = send(payload, (0, 1), (1, 0), (2, 3), (3, 2))
        middle = send(payload, (1, 2), (2, 1))
        near, middle, own_out, own_log = lax.optimization_barrier((near, middle, own_out, own_log))
        crossed = send(near, (1, 2), (2, 1))
        outward = send(middle, (1, 0), (2, 3))
        first = other_part((3, 1), (middle, near))
        crossed, outward, first = lax.optimization_barrier((crossed, outward, first))
        across = send(first, (1, 2), (2, 1))
        inward = send(first, (0, 1), (3, 2))
        far = send(crossed, (1, 0), (2, 3))
        second = other_part((2, 2), (crossed, outward))
        far, second = lax.optimization_barrier((far, second))
        apart = send(second, (0, 2), (2, 0), (1, 3), (3, 1))
        third = other_part((1, 3), (near, far), share=8)
        ends = send(third, (0, 3), (3, 0))
        back = send(third, (1, 0), (2, 3))
        own_out, own_log, third = lax.optimization_barrier((own_out, own_log, third))
        own_out, own_log = combine(
            own_out, own_log, [(3, None), (1, None), (2, 2)], [across, inward, apart], last=False
        )
        sources = [(None, 1), (None, 3)]
        parts = [back, ends]
        moved = [
            ((0, 0), payload),
            ((1, 1), near),
            ((3, None), middle),
            ((2, None), crossed),
            ((None, 2), outward),
            ((None, 3), far),
        ]
    else:
        gathered = lax.all_gather(payload, "pool", axis=0, tiled=False)
        packed = lax.map(
            lambda pair: other_part(None, (pair[0],), pair[1].reshape(1)),
            (gathered, jnp.arange(pool_size, dtype=jnp.int32)),
        )
        parts = lax.all_to_all(packed, "pool", split_axis=0, concat_axis=0, tiled=True)
        sources = list(range(pool_size))
        moved = [(source, gathered[source]) for source in range(pool_size)]

    attended = combine(own_out, own_log, sources, parts)
    pushed_keys, pushed_values = pl.pallas_call(
        functools.partial(push_kernel, pool_size, tuple(entry for entry, _ in moved)),
        in_specs=[smem_spec] + [hbm_spec] * len(moved),
        out_specs=[hbm_spec] * 2,
        scratch_shapes=[
            pltpu.VMEM((new_rows, kv_width), jnp.bfloat16),
            pltpu.SemaphoreType.DMA((2, CAPP)),
        ],
        out_shape=[jax.ShapeDtypeStruct((CAPP, new_rows, kv_width), jnp.bfloat16)] * 2,
        compiler_params=params,
        name="push",
    )(decode_owner, *[array for _, array in moved])
    return (attended[None], pushed_keys, pushed_values)


def solution(mesh):
    in_specs = (
        P(("groups", "pool"), None, ("tensor", "sub")),
        P(("groups", "pool"), None, ("tensor", "sub")),
        P(("groups", "pool"), None, ("tensor", "sub")),
        P(("groups", "pool"), None, ("tensor", "sub")),
        P(("groups", "pool"), None, ("tensor", "sub")),
        P("groups"),
        P("groups", None),
        P("groups", None),
        P("groups"),
    )
    out_specs = (
        P(("groups", "pool"), None, ("tensor", "sub")),
        P(("groups", "pool"), None, ("tensor", "sub")),
        P(("groups", "pool"), None, ("tensor", "sub")),
    )
    return jax.shard_map(shards, mesh=mesh, in_specs=in_specs, out_specs=out_specs, check_vma=False)
```

```python
import functools
import math

import jax
import jax.numpy as jnp
from jax import lax
from jax.experimental import pallas as pl
from jax.experimental.pallas import tpu as pltpu
from jax.sharding import PartitionSpec as P

HEADS = 64
KVH = 8
HD = 128
MAXBLK = 32
CAPP = 2
GROUP = HEADS // KVH
EMPTY = -1e30
TILE = 256
ONES = 16
MERGE_STEPS = 5
SCALE = 1.0 / math.sqrt(HD)
EXP2_SCALE = SCALE * math.log2(math.e)
VMEM_LIMIT = 63 * 1024 * 1024


def fetch(pool_size, tables, request, stores, buffers, sems):
    prefix_ref, store_ref, slot_ref = tables
    me = lax.axis_index("pool")
    first = lax.rem(me - store_ref[request, 0] + pool_size, pool_size)
    count = lax.max(lax.div(prefix_ref[request] - first + pool_size - 1, pool_size), 0)

    def copies(entry):
        slot = slot_ref[request, first + entry * pool_size]
        return [
            pltpu.make_async_copy(stores[i].at[slot], buffers[i].at[entry], sems.at[i, entry])
            for i in range(2)
        ]

    def start(entry, carry):
        for copy in copies(entry):
            copy.start()
        return carry

    lax.fori_loop(0, count, start, 0)

    def ready(entry):
        for copy in copies(entry):
            copy.wait()

    return count, ready


def attend(
    key_ref,
    value_ref,
    count,
    ready,
    fresh,
    new_rows,
    columns,
    scores,
    weights,
    peaks,
    factors,
    turned,
    acc,
    log_type,
    put,
):
    kv_local, _, rows = columns.shape

    def visit(keys, values, seen):
        def score(kv):
            turned[kv, :HD, :] = values[kv].T
            block = lax.dot_general(
                keys[kv], columns[kv], (((1,), (0,)), ((), ())), preferred_element_type=jnp.float32
            )
            if seen is not None:
                block = jnp.where(seen, block, EMPTY)
            scores[kv] = block

        def weigh(kv):
            for i in range(0, rows, TILE):
                part = slice(i, i + TILE)
                before = peaks[kv, :, part]
                block = scores[kv, :, part]
                peak = jnp.maximum(before, jnp.max(block, axis=0, keepdims=True))
                factors[kv, :, part] = jnp.exp2((before - peak) * EXP2_SCALE)
                peaks[kv, :, part] = peak
                weight = jnp.exp2(block * EXP2_SCALE - peak[0:1] * EXP2_SCALE)
                weights[kv, :, part] = weight.astype(jnp.bfloat16)

        def mix(kv):
            added = lax.dot_general(
                turned[kv], weights[kv], (((1,), (0,)), ((), ())), preferred_element_type=jnp.float32
            )
            acc[kv] = acc[kv] * factors[kv, 0:1, :] + added

        for step in range(kv_local + 2):
            for offset, stage in ((0, score), (2, mix), (1, weigh)):
                if 0 <= step - offset < kv_local:
                    stage(step - offset)

    def lanes_of(ref):
        return [ref[:, kv * HD : (kv + 1) * HD] for kv in range(kv_local)]

    peaks[...] = jnp.full(peaks.shape, EMPTY, jnp.float32)
    acc[...] = jnp.zeros(acc.shape, jnp.float32)
    turned[:, HD:, :] = jnp.ones((kv_local, ONES, turned.shape[2]), jnp.bfloat16)
    if fresh is not None:
        new_key_ref, new_value_ref = fresh

        row = lax.rem(lax.broadcasted_iota(jnp.int32, (1, rows), 1), new_rows)
        seen = lax.broadcasted_iota(jnp.int32, (new_key_ref.shape[0], rows), 0) <= row
        visit(lanes_of(new_key_ref), lanes_of(new_value_ref), seen)

    def visit_block(entry, carry):
        ready(entry)
        visit(lanes_of(key_ref.at[entry]), lanes_of(value_ref.at[entry]), None)
        return carry

    lax.fori_loop(0, count, visit_block, 0)
    heads = kv_local * GROUP
    logs = []
    for kv in range(kv_local):
        total = acc[kv, HD : HD + 1, :]
        safe = jnp.where(total > 0, total, 1.0)
        logs.append(jnp.where(total > 0, peaks[kv, 0:1] * SCALE + jnp.log(safe), EMPTY))
        out = (acc[kv, :HD, :] * (1.0 / safe)).astype(log_type).T
        for g in range(GROUP):
            put(kv * GROUP + g, out[g * new_rows : (g + 1) * new_rows])
    logs += [logs[-1]] * (8 - len(logs))
    log_columns = jnp.concatenate(logs, axis=0).T
    lane = lax.broadcasted_iota(jnp.int32, (new_rows, HD), 1)
    place = jnp.where(lane < 3 * heads, lax.rem(lane, heads), -1)
    tile = jnp.zeros((new_rows, HD), jnp.float32)
    for kv in range(kv_local):
        for g in range(GROUP):
            column = log_columns[g * new_rows : (g + 1) * new_rows, kv : kv + 1]
            tile = jnp.where(place == kv * GROUP + g, column, tile)
    return tile


def load_heads(query_ref, query_rows, columns):
    new_rows = query_ref.shape[0]
    for kv in range(columns.shape[0]):
        for g in range(GROUP):
            head = kv * GROUP + g
            query_rows[g * new_rows : (g + 1) * new_rows, :] = query_ref[
                :, head * HD : (head + 1) * HD
            ]
        columns[kv] = query_rows[...].T


def split_lanes(tile, heads):
    lane = lax.broadcasted_iota(jnp.int32, tile.shape, 1)
    high = tile.astype(jnp.bfloat16).astype(jnp.float32)
    middle = (tile - high).astype(jnp.bfloat16).astype(jnp.float32)
    low = tile - high - middle
    return jnp.where(lane < heads, high, jnp.where(lane < 2 * heads, middle, low)).astype(
        jnp.bfloat16
    )


def own_kernel(
    pool_size,
    prefix_ref,
    store_ref,
    slot_ref,
    payload_ref,
    store_keys,
    store_values,
    out_ref,
    log_ref,
    key_buf,
    value_buf,
    new_key_buf,
    new_value_buf,
    query_rows,
    columns,
    *state,
):
    *work, sems = state
    count, ready = fetch(
        pool_size,
        (prefix_ref, store_ref, slot_ref),
        lax.axis_index("pool"),
        (store_keys, store_values),
        (key_buf, value_buf),
        sems,
    )
    new_rows, width = out_ref.shape
    kv_width = new_key_buf.shape[1]
    for i, buffer in enumerate((new_key_buf, new_value_buf)):
        buffer[:new_rows, :] = payload_ref[:, width + i * kv_width : width + (i + 1) * kv_width]
        buffer[new_rows:, :] = jnp.zeros((buffer.shape[0] - new_rows, kv_width), jnp.bfloat16)

    def put(head, out):
        out_ref[:, head * HD : (head + 1) * HD] = out

    load_heads(payload_ref, query_rows, columns)
    log_ref[...] = attend(
        key_buf,
        value_buf,
        count,
        ready,
        (new_key_buf, new_value_buf),
        new_rows,
        columns,
        *work,
        jnp.float32,
        put,
    )


def other_kernel(pool_size, partners, *refs):
    if partners is None:
        request = refs[0][0]
        choice = [None]
        refs = refs[1:]
    else:
        me = lax.axis_index("pool")
        inner = is_inner(me)
        request = me ^ jnp.where(inner, partners[0], partners[1])
        choice = [inner, jnp.logical_not(inner)]
    tables, refs = refs[:3], refs[3:]
    payload_refs = refs[: len(choice)]
    store_keys, store_values, out_ref, key_buf, value_buf, query_rows, columns, *state = refs[
        len(choice) :
    ]
    *work, query_buf, query_sem, sems = state
    new_rows = out_ref.shape[0]
    width = out_ref.shape[1] - HD

    def query_copy(payload_ref):
        return pltpu.make_async_copy(payload_ref.at[:, :width], query_buf, query_sem)

    for payload_ref, hit in zip(payload_refs, choice):
        if hit is None:
            query_copy(payload_ref).start()
        else:
            pl.when(hit)(functools.partial(query_copy(payload_ref).start))
    count, ready = fetch(
        pool_size, tables, request, (store_keys, store_values), (key_buf, value_buf), sems
    )
    query_copy(payload_refs[0]).wait()
    load_heads(query_buf, query_rows, columns)

    def put(head, out):
        out_ref[:, head * HD : (head + 1) * HD] = out

    tile = attend(
        key_buf, value_buf, count, ready, None, new_rows, columns, *work, jnp.bfloat16, put
    )
    out_ref[:, width:] = split_lanes(tile, width // HD)


def is_inner(place):
    return (place == 1) | (place == 2)


def source_of(me, entry):
    if isinstance(entry, int):
        return jnp.bool_(True), jnp.int32(entry)
    inner = is_inner(me)
    masks = [0 if mask is None else mask for mask in entry]
    there = jnp.where(inner, entry[0] is not None, entry[1] is not None)
    return there, me ^ jnp.where(inner, masks[0], masks[1])


def push_kernel(pool_size, entries, owner_ref, *refs):
    payload_refs = refs[: len(entries)]
    key_out, value_out, sems = refs[len(entries) :]
    outs = (key_out, value_out)
    kv_width = key_out.shape[2]
    me = lax.axis_index("pool")
    total = jnp.int32(0)
    for other in range(pool_size):
        total += (owner_ref[other] == me).astype(jnp.int32)

    def copy(payload_ref, i, place):
        start = payload_ref.shape[1] - (2 - i) * kv_width
        return pltpu.make_async_copy(
            payload_ref.at[:, start : start + kv_width], outs[i].at[place], sems.at[i, place]
        )

    for entry, payload_ref in zip(entries, payload_refs):
        there, source = source_of(me, entry)
        rank = jnp.int32(0)
        for other in range(pool_size):
            rank += ((owner_ref[other] == me) & (other < source)).astype(jnp.int32)
        hit = there & (owner_ref[source] == me)
        for place in range(CAPP):

            @pl.when(hit & (rank == place))
            def _():
                for i in range(2):
                    copy(payload_ref, i, place).start()

    for place in range(CAPP):

        @pl.when(total <= place)
        def _():
            for out in outs:
                out[place] = jnp.zeros(out.shape[1:], jnp.bfloat16)

        @pl.when(total > place)
        def _():
            for i in range(2):
                copy(payload_refs[0], i, place).wait()


def combine_kernel(sources, pool_size, out_ref_count, own_ref, log_ref, *refs):
    parts = refs[: len(sources)]
    out_ref = refs[len(sources)]
    width = own_ref.shape[1]
    heads = width // HD
    logs = [log_ref[...]]
    me = lax.axis_index("pool")
    for source, part in zip(sources, parts):
        there, request = source_of(me, source)
        there = there & (request != me)
        tile = part[:, width:].astype(jnp.float32)
        whole = (
            tile + pltpu.roll(tile, HD - heads, 1) + pltpu.roll(tile, HD - 2 * heads, 1)
        )
        logs.append(jnp.where(there, whole, EMPTY))
    peak = functools.reduce(jnp.maximum, logs)
    shares = [jnp.exp(x - peak) for x in logs]
    total = functools.reduce(jnp.add, shares)
    shares = [x * (1.0 / total) for x in shares]
    for head in range(heads):
        lanes = slice(head * HD, (head + 1) * HD)
        mixed = own_ref[:, lanes] * shares[0][:, head : head + 1]
        for share, part in zip(shares[1:], parts):
            mixed = mixed + part[:, lanes].astype(jnp.float32) * share[:, head : head + 1]
        out_ref[:, lanes] = mixed.astype(out_ref.dtype)
    if out_ref_count == 2:
        refs[len(sources) + 1][...] = peak + jnp.log(total)


def shards(
    queries,
    new_keys,
    new_values,
    store_keys,
    store_values,
    prefix_blocks,
    hit_store,
    hit_slot,
    decode_owner,
):
    pool_size = lax.axis_size("pool")
    capacity = (MAXBLK + pool_size - 1) // pool_size
    new_rows = queries.shape[1]
    width = queries.shape[2]
    kv_width = new_keys.shape[2]
    block_len = store_keys.shape[1]
    rows = GROUP * new_rows
    tables = (prefix_blocks, hit_store, hit_slot)
    smem_spec = pl.BlockSpec(memory_space=pltpu.SMEM)
    hbm_spec = pl.BlockSpec(memory_space=pltpu.HBM)
    vmem_spec = pl.BlockSpec(memory_space=pltpu.VMEM)
    params = pltpu.CompilerParams(vmem_limit_bytes=VMEM_LIMIT)

    def cost(share):
        return pl.CostEstimate(
            flops=share * rows * block_len * kv_width * capacity,
            bytes_accessed=rows,
            transcendentals=0,
        )

    buffers = [pltpu.VMEM((capacity, block_len, kv_width), jnp.bfloat16)] * 2
    kv_local = kv_width // HD
    work = [
        pltpu.VMEM((rows, HD), jnp.bfloat16),
        pltpu.VMEM((kv_local, HD, rows), jnp.bfloat16),
        pltpu.VMEM((kv_local, block_len, rows), jnp.float32),
        pltpu.VMEM((kv_local, block_len, rows), jnp.bfloat16),
        pltpu.VMEM((kv_local, 8, rows), jnp.float32),
        pltpu.VMEM((kv_local, 8, rows), jnp.float32),
        pltpu.VMEM((kv_local, HD + ONES, block_len), jnp.bfloat16),
        pltpu.VMEM((kv_local, HD + ONES, rows), jnp.float32),
    ]
    sems = pltpu.SemaphoreType.DMA((2, capacity))

    def own_part(payload):
        return pl.pallas_call(
            functools.partial(own_kernel, pool_size),
            in_specs=[smem_spec] * 3 + [vmem_spec] + [hbm_spec] * 2,
            out_specs=[vmem_spec] * 2,
            scratch_shapes=[
                *buffers,
                *[pltpu.VMEM((block_len, kv_width), jnp.bfloat16)] * 2,
                *work,
                sems,
            ],
            out_shape=[
                jax.ShapeDtypeStruct((new_rows, width), jnp.float32),
                jax.ShapeDtypeStruct((new_rows, HD), jnp.float32),
            ],
            compiler_params=params,
            cost_estimate=cost(8),
            name="own_part",
        )(*tables, payload, store_keys, store_values)

    def other_part(partners, held, *request, share=8):
        return pl.pallas_call(
            functools.partial(other_kernel, pool_size, partners),
            in_specs=[smem_spec] * (3 + len(request)) + [hbm_spec] * (len(held) + 2),
            out_specs=vmem_spec,
            scratch_shapes=[
                *buffers,
                *work,
                pltpu.VMEM((new_rows, width), jnp.bfloat16),
                pltpu.SemaphoreType.DMA,
                sems,
            ],
            out_shape=jax.ShapeDtypeStruct((new_rows, width + HD), jnp.bfloat16),
            compiler_params=params,
            cost_estimate=cost(share),
            name="other_part",
        )(*request, *tables, *held, store_keys, store_values)

    def combine(own, log, sources, parts, last=True):
        out_shape = [jax.ShapeDtypeStruct((new_rows, width), jnp.bfloat16 if last else jnp.float32)]
        if not last:
            out_shape.append(jax.ShapeDtypeStruct((new_rows, HD), jnp.float32))
        arrays = [own, log, *parts]

        def by_rows(array):
            return pl.BlockSpec((new_rows // MERGE_STEPS, array.shape[1]), lambda i: (i, 0))

        out = pl.pallas_call(
            functools.partial(combine_kernel, tuple(sources), pool_size, len(out_shape)),
            grid=(MERGE_STEPS,),
            in_specs=[by_rows(array) for array in arrays],
            out_specs=[by_rows(array) for array in out_shape],
            out_shape=out_shape,
            compiler_params=params,
            cost_estimate=cost(0 if last else 32),
            name="combine",
        )(*arrays)
        return out[0] if last else out

    payload = jnp.concatenate([queries[0], new_keys[0], new_values[0]], axis=1)
    own_out, own_log = own_part(payload)
    if pool_size == 4:
        def send(array, *pairs):
            return lax.ppermute(array, "pool", pairs)

        near = send(payload, (0, 1), (1, 0), (2, 3), (3, 2))
        middle = send(payload, (1, 2), (2, 1))
        near, middle, own_out, own_log, payload = lax.optimization_barrier(
            (near, middle, own_out, own_log, payload)
        )
        crossed = send(payload, (0, 2), (3, 1))
        outward = send(middle, (1, 0), (2, 3))
        first = other_part((3, 1), (middle, near))
        crossed, outward, first = lax.optimization_barrier((crossed, outward, first))
        across = send(first, (1, 2), (2, 1))
        inward = send(first, (0, 1), (3, 2))
        far = send(crossed, (1, 0), (2, 3))
        second = other_part((2, 2), (crossed, outward), share=0)
        near, second = lax.optimization_barrier((near, second))
        apart = send(second, (0, 2), (2, 0), (1, 3), (3, 1))
        own_out, own_log = combine(
            own_out, own_log, [(3, None), (1, None)], [across, inward], last=False
        )
        near, own_out, own_log = lax.optimization_barrier((near, own_out, own_log))
        third = other_part((1, 3), (near, far), share=8)
        ends = send(third, (0, 3), (3, 0))
        back = send(third, (1, 0), (2, 3))
        own_out, own_log, third = lax.optimization_barrier((own_out, own_log, third))
        own_out, own_log = combine(own_out, own_log, [(2, 2)], [apart], last=False)
        sources = [(None, 1), (None, 3)]
        parts = [back, ends]
        moved = [
            ((0, 0), payload),
            ((1, 1), near),
            ((3, None), middle),
            ((2, None), crossed),
            ((None, 2), outward),
            ((None, 3), far),
        ]
    else:
        gathered = lax.all_gather(payload, "pool", axis=0, tiled=False)
        packed = lax.map(
            lambda pair: other_part(None, (pair[0],), pair[1].reshape(1)),
            (gathered, jnp.arange(pool_size, dtype=jnp.int32)),
        )
        parts = lax.all_to_all(packed, "pool", split_axis=0, concat_axis=0, tiled=True)
        sources = list(range(pool_size))
        moved = [(source, gathered[source]) for source in range(pool_size)]

    attended = combine(own_out, own_log, sources, parts)
    pushed_keys, pushed_values = pl.pallas_call(
        functools.partial(push_kernel, pool_size, tuple(entry for entry, _ in moved)),
        in_specs=[smem_spec] + [hbm_spec] * len(moved),
        out_specs=[vmem_spec] * 2,
        scratch_shapes=[pltpu.SemaphoreType.DMA((2, CAPP))],
        out_shape=[jax.ShapeDtypeStruct((CAPP, new_rows, kv_width), jnp.bfloat16)] * 2,
        compiler_params=params,
        name="push",
    )(decode_owner, *[array for _, array in moved])
    return (attended[None], pushed_keys, pushed_values)


def solution(mesh):
    in_specs = (
        P(("groups", "pool"), None, ("tensor", "sub")),
        P(("groups", "pool"), None, ("tensor", "sub")),
        P(("groups", "pool"), None, ("tensor", "sub")),
        P(("groups", "pool"), None, ("tensor", "sub")),
        P(("groups", "pool"), None, ("tensor", "sub")),
        P("groups"),
        P("groups", None),
        P("groups", None),
        P("groups"),
    )
    out_specs = (
        P(("groups", "pool"), None, ("tensor", "sub")),
        P(("groups", "pool"), None, ("tensor", "sub")),
        P(("groups", "pool"), None, ("tensor", "sub")),
    )
    return jax.shard_map(shards, mesh=mesh, in_specs=in_specs, out_specs=out_specs, check_vma=False)
```

```python
import functools
import math

import jax
import jax.numpy as jnp
from jax import lax
from jax.experimental import pallas as pl
from jax.experimental.pallas import tpu as pltpu
from jax.sharding import PartitionSpec as P

HEADS = 64
KVH = 8
HD = 128
MAXBLK = 32
CAPP = 2
GROUP = HEADS // KVH
EMPTY = -1e30
TILE = 256
ONES = 16
PIECE = 32
SCALE = 1.0 / math.sqrt(HD)
EXP2_SCALE = SCALE * math.log2(math.e)
VMEM_LIMIT = 63 * 1024 * 1024 + 512 * 1024


def fetch(pool_size, tables, request, stores, buffers, sems):
    prefix_ref, store_ref, slot_ref = tables
    me = lax.axis_index("pool")
    first = lax.rem(me - store_ref[request, 0] + pool_size, pool_size)
    count = lax.max(lax.div(prefix_ref[request] - first + pool_size - 1, pool_size), 0)

    def copies(entry):
        slot = slot_ref[request, first + entry * pool_size]
        return [
            pltpu.make_async_copy(stores[i].at[slot], buffers[i].at[entry], sems.at[i, entry])
            for i in range(2)
        ]

    def start(entry, carry):
        for copy in copies(entry):
            copy.start()
        return carry

    lax.fori_loop(0, count, start, 0)

    def ready(entry):
        for copy in copies(entry):
            copy.wait()

    return count, ready


def attend(
    key_ref,
    value_ref,
    count,
    ready,
    fresh,
    new_rows,
    columns,
    scores,
    weights,
    peaks,
    factors,
    turned,
    acc,
):
    rows = columns.shape[1]
    kv_local = columns.shape[0] // HD

    def visit(keys, values, seen):
        size = keys[0].shape[0]

        def score(kv):
            turned[kv, :HD, :size] = values[kv].T
            block = lax.dot_general(
                keys[kv],
                columns[kv * HD : (kv + 1) * HD, :],
                (((1,), (0,)), ((), ())),
                preferred_element_type=jnp.float32,
            )
            if seen is not None:
                block = jnp.where(seen, block, EMPTY)
            scores[kv, :size, :] = block

        def weigh(kv):
            for i in range(0, rows, TILE):
                part = slice(i, i + TILE)
                before = peaks[kv, :, part]
                block = scores[kv, :size, part]
                peak = jnp.maximum(before, jnp.max(block, axis=0, keepdims=True))
                factors[kv, :, part] = jnp.exp2((before - peak) * EXP2_SCALE)
                peaks[kv, :, part] = peak
                weight = jnp.exp2(block * EXP2_SCALE - peak[0:1] * EXP2_SCALE)
                weights[kv, :size, part] = weight.astype(jnp.bfloat16)

        def mix(kv):
            added = lax.dot_general(
                turned[kv, :, :size],
                weights[kv, :size, :],
                (((1,), (0,)), ((), ())),
                preferred_element_type=jnp.float32,
            )
            acc[kv] = acc[kv] * factors[kv, 0:1, :] + added

        for step in range(kv_local + 2):
            for offset, stage in ((0, score), (2, mix), (1, weigh)):
                if 0 <= step - offset < kv_local:
                    stage(step - offset)

    def lanes_of(array):
        return [array[:, kv * HD : (kv + 1) * HD] for kv in range(kv_local)]

    def blocks_of(ref, first, number):
        return lanes_of(ref[pl.ds(first, number)].reshape(number * ref.shape[1], ref.shape[2]))

    peaks[...] = jnp.full(peaks.shape, EMPTY, jnp.float32)
    acc[...] = jnp.zeros(acc.shape, jnp.float32)
    turned[:, HD:, :] = jnp.ones((kv_local, ONES, turned.shape[2]), jnp.bfloat16)
    if fresh is not None:
        new_key_ref, new_value_ref = fresh
        row = lax.rem(lax.broadcasted_iota(jnp.int32, (1, rows), 1), new_rows)
        seen = lax.broadcasted_iota(jnp.int32, (new_key_ref.shape[0], rows), 0) <= row
        visit(lanes_of(new_key_ref), lanes_of(new_value_ref), seen)

    def visit_blocks(number):
        def body(index, carry):
            for i in range(number):
                ready(index * number + i)
            visit(
                blocks_of(key_ref, index * number, number),
                blocks_of(value_ref, index * number, number),
                None,
            )
            return carry

        return body

    pairs = count // 2 if key_ref.shape[0] > 1 else 0
    if key_ref.shape[0] > 1:
        lax.fori_loop(0, pairs, visit_blocks(2), 0)
    lax.fori_loop(2 * pairs, count, visit_blocks(1), 0)
    outs = []
    logs = []
    for kv in range(kv_local):
        total = acc[kv, HD : HD + 1, :]
        safe = jnp.where(total > 0, total, 1.0)
        logs.append(jnp.where(total > 0, peaks[kv, 0:1] * SCALE + jnp.log(safe), EMPTY))
        outs.append(acc[kv, :HD, :] * (1.0 / safe))
    return outs, logs


def prepare_kernel(query_ref, new_key_ref, new_value_ref, payload_ref, query_rows):
    new_rows = query_ref.shape[0]
    kv_width = new_key_ref.shape[1]
    for kv in range(kv_width // HD):
        for g in range(GROUP):
            head = kv * GROUP + g
            query_rows[g * new_rows : (g + 1) * new_rows, :] = query_ref[
                :, head * HD : (head + 1) * HD
            ]
        payload_ref[kv * HD : (kv + 1) * HD, :] = query_rows[...].T
    for i, new_ref in enumerate((new_key_ref, new_value_ref)):
        for piece in range(new_rows // PIECE):
            row, lane = piece_place(i, piece, new_rows, kv_width)
            payload_ref[row : row + PIECE, lane : lane + kv_width] = new_ref[
                piece * PIECE : (piece + 1) * PIECE, :
            ]


def piece_place(i, piece, new_rows, kv_width):
    index = i * (new_rows // PIECE) + piece
    beside = GROUP * new_rows // kv_width
    return kv_width + index // beside * PIECE, index % beside * kv_width


def payload_rows(new_rows, kv_width):
    return piece_place(1, new_rows // PIECE - 1, new_rows, kv_width)[0] + PIECE


def own_kernel(
    pool_size,
    prefix_ref,
    store_ref,
    slot_ref,
    payload_ref,
    new_key_ref,
    new_value_ref,
    store_keys,
    store_values,
    out_ref,
    log_ref,
    key_buf,
    value_buf,
    new_key_buf,
    new_value_buf,
    *state,
):
    *work, sems = state
    count, ready = fetch(
        pool_size,
        (prefix_ref, store_ref, slot_ref),
        lax.axis_index("pool"),
        (store_keys, store_values),
        (key_buf, value_buf),
        sems,
    )
    new_rows, kv_width = new_key_ref.shape
    for buffer, source in ((new_key_buf, new_key_ref), (new_value_buf, new_value_ref)):
        buffer[:new_rows, :] = source[...]
        buffer[new_rows:, :] = jnp.zeros((buffer.shape[0] - new_rows, kv_width), jnp.bfloat16)
    fresh = (new_key_buf, new_value_buf)
    outs, logs = attend(
        key_buf, value_buf, count, ready, fresh, new_rows, payload_ref.at[:kv_width], *work
    )
    log_ref[...] = jnp.zeros(log_ref.shape, jnp.float32)
    for kv, (out, log) in enumerate(zip(outs, logs)):
        out_ref[kv * HD : (kv + 1) * HD, :] = out
        log_ref[kv : kv + 1, :] = log


def other_kernel(pool_size, new_rows, partners, *refs):
    if partners is None:
        request = refs[0][0]
        choice = [None]
        refs = refs[1:]
    else:
        me = lax.axis_index("pool")
        inner = is_inner(me)
        request = me ^ jnp.where(inner, partners[0], partners[1])
        choice = [inner, jnp.logical_not(inner)]
    tables, refs = refs[:3], refs[3:]
    payload_refs = refs[: len(choice)]
    store_keys, store_values, out_ref, key_buf, value_buf, *state = refs[len(choice) :]
    *work, columns, query_sem, sems = state
    kv_width = columns.shape[0]

    def query_copy(payload_ref):
        return pltpu.make_async_copy(payload_ref.at[:kv_width], columns, query_sem)

    for payload_ref, hit in zip(payload_refs, choice):
        if hit is None:
            query_copy(payload_ref).start()
        else:
            pl.when(hit)(query_copy(payload_ref).start)
    count, ready = fetch(
        pool_size, tables, request, (store_keys, store_values), (key_buf, value_buf), sems
    )
    query_copy(payload_refs[0]).wait()
    outs, logs = attend(key_buf, value_buf, count, ready, None, new_rows, columns, *work)
    tail = []
    for kv, (out, log) in enumerate(zip(outs, logs)):
        out_ref[kv * HD : (kv + 1) * HD, :] = out.astype(jnp.bfloat16)
        high = log.astype(jnp.bfloat16).astype(jnp.float32)
        middle = (log - high).astype(jnp.bfloat16).astype(jnp.float32)
        tail += [high, middle, log - high - middle]
    tail.append(jnp.zeros((ONES - len(tail), columns.shape[1]), jnp.float32))
    out_ref[kv_width:, :] = jnp.concatenate(tail, axis=0).astype(jnp.bfloat16)


def is_inner(place):
    return (place == 1) | (place == 2)


def source_of(me, entry):
    if isinstance(entry, int):
        return jnp.bool_(True), jnp.int32(entry)
    inner = is_inner(me)
    masks = [0 if mask is None else mask for mask in entry]
    there = jnp.where(inner, entry[0] is not None, entry[1] is not None)
    return there, me ^ jnp.where(inner, masks[0], masks[1])


def push_kernel(pool_size, entries, owner_ref, *refs):
    payload_refs = refs[: len(entries)]
    key_out, value_out, sems = refs[len(entries) :]
    outs = (key_out, value_out)
    kv_width = key_out.shape[2]
    me = lax.axis_index("pool")
    total = jnp.int32(0)
    for other in range(pool_size):
        total += (owner_ref[other] == me).astype(jnp.int32)

    new_rows = key_out.shape[1]

    def copies(payload_ref, place):
        for i in range(2):
            for piece in range(new_rows // PIECE):
                row, lane = piece_place(i, piece, new_rows, kv_width)
                yield pltpu.make_async_copy(
                    payload_ref.at[row : row + PIECE, lane : lane + kv_width],
                    outs[i].at[place, piece * PIECE : (piece + 1) * PIECE],
                    sems.at[i, place, piece],
                )

    for entry, payload_ref in zip(entries, payload_refs):
        there, source = source_of(me, entry)
        rank = jnp.int32(0)
        for other in range(pool_size):
            rank += ((owner_ref[other] == me) & (other < source)).astype(jnp.int32)
        hit = there & (owner_ref[source] == me)
        for place in range(CAPP):

            @pl.when(hit & (rank == place))
            def _():
                for copy in copies(payload_ref, place):
                    copy.start()

    for place in range(CAPP):

        @pl.when(total <= place)
        def _():
            for out in outs:
                out[place] = jnp.zeros(out.shape[1:], jnp.bfloat16)

        @pl.when(total > place)
        def _():
            for copy in copies(payload_refs[0], place):
                copy.wait()


def combine_kernel(sources, last, own_ref, log_ref, *refs):
    parts = refs[: len(sources)]
    out_ref = refs[len(sources)]
    kv_width, rows = own_ref.shape
    me = lax.axis_index("pool")
    arrived = []
    tails = []
    for source, part in zip(sources, parts):
        there, request = source_of(me, source)
        arrived.append(there & (request != me))
        tails.append(part[kv_width:, :].astype(jnp.float32))
    if not last:
        refs[len(sources) + 1][...] = log_ref[...]
    for kv in range(kv_width // HD):
        logs = [log_ref[kv : kv + 1, :]]
        for there, tail in zip(arrived, tails):
            log = sum(tail[3 * kv + i : 3 * kv + i + 1] for i in range(3))
            logs.append(jnp.where(there, log, EMPTY))
        peak = functools.reduce(jnp.maximum, logs)
        shares = [jnp.exp(x - peak) for x in logs]
        total = functools.reduce(jnp.add, shares)
        shares = [x * (1.0 / total) for x in shares]
        band = slice(kv * HD, (kv + 1) * HD)
        for i in range(0, rows, TILE):
            part = slice(i, i + TILE)
            mixed = own_ref[band, part] * shares[0][:, part]
            for share, ref in zip(shares[1:], parts):
                mixed = mixed + ref[band, part].astype(jnp.float32) * share[:, part]
            if last:
                refs[len(sources) + 1][part, :] = mixed.astype(jnp.bfloat16).T
            else:
                out_ref[band, part] = mixed
        if last:
            turned = refs[len(sources) + 1]
            new_rows = out_ref.shape[0]
            for g in range(GROUP):
                head = kv * GROUP + g
                out_ref[:, head * HD : (head + 1) * HD] = turned[g * new_rows : (g + 1) * new_rows, :]
        else:
            refs[len(sources) + 1][kv : kv + 1, :] = peak + jnp.log(total)


def shards(
    queries,
    new_keys,
    new_values,
    store_keys,
    store_values,
    prefix_blocks,
    hit_store,
    hit_slot,
    decode_owner,
):
    pool_size = lax.axis_size("pool")
    capacity = (MAXBLK + pool_size - 1) // pool_size
    new_rows = queries.shape[1]
    width = queries.shape[2]
    kv_width = new_keys.shape[2]
    block_len = store_keys.shape[1]
    rows = GROUP * new_rows
    tables = (prefix_blocks, hit_store, hit_slot)
    smem_spec = pl.BlockSpec(memory_space=pltpu.SMEM)
    hbm_spec = pl.BlockSpec(memory_space=pltpu.HBM)
    vmem_spec = pl.BlockSpec(memory_space=pltpu.VMEM)
    params = pltpu.CompilerParams(vmem_limit_bytes=VMEM_LIMIT)

    def cost(share):
        return pl.CostEstimate(
            flops=share * rows * block_len * kv_width * capacity,
            bytes_accessed=rows,
            transcendentals=0,
        )

    buffers = [pltpu.VMEM((capacity, block_len, kv_width), jnp.bfloat16)] * 2
    kv_local = kv_width // HD
    widest = block_len * min(2, capacity)
    work = [
        pltpu.VMEM((kv_local, widest, rows), jnp.float32),
        pltpu.VMEM((kv_local, widest, rows), jnp.bfloat16),
        pltpu.VMEM((kv_local, 8, rows), jnp.float32),
        pltpu.VMEM((kv_local, 8, rows), jnp.float32),
        pltpu.VMEM((kv_local, HD + ONES, widest), jnp.bfloat16),
        pltpu.VMEM((kv_local, HD + ONES, rows), jnp.float32),
    ]
    sems = pltpu.SemaphoreType.DMA((2, capacity))

    def own_part(payload):
        return pl.pallas_call(
            functools.partial(own_kernel, pool_size),
            in_specs=[smem_spec] * 3 + [vmem_spec] * 3 + [hbm_spec] * 2,
            out_specs=[vmem_spec] * 2,
            scratch_shapes=[
                *buffers,
                *[pltpu.VMEM((block_len, kv_width), jnp.bfloat16)] * 2,
                *work,
                sems,
            ],
            out_shape=[
                jax.ShapeDtypeStruct((kv_width, rows), jnp.float32),
                jax.ShapeDtypeStruct((8, rows), jnp.float32),
            ],
            compiler_params=params,
            cost_estimate=cost(8),
            name="own_part",
        )(*tables, payload, new_keys[0], new_values[0], store_keys, store_values)

    def other_part(partners, held, *request, share=8):
        return pl.pallas_call(
            functools.partial(other_kernel, pool_size, new_rows, partners),
            in_specs=[smem_spec] * (3 + len(request)) + [hbm_spec] * (len(held) + 2),
            out_specs=vmem_spec,
            scratch_shapes=[
                *buffers,
                *work,
                pltpu.VMEM((kv_width, rows), jnp.bfloat16),
                pltpu.SemaphoreType.DMA,
                sems,
            ],
            out_shape=jax.ShapeDtypeStruct((kv_width + ONES, rows), jnp.bfloat16),
            compiler_params=params,
            cost_estimate=cost(share),
            name="other_part",
        )(*request, *tables, *held, store_keys, store_values)

    def combine(own, log, sources, parts, last=True):
        if last:
            out_shape = jax.ShapeDtypeStruct((new_rows, width), jnp.bfloat16)
        else:
            out_shape = [
                jax.ShapeDtypeStruct((kv_width, rows), jnp.float32),
                jax.ShapeDtypeStruct((8, rows), jnp.float32),
            ]
        return pl.pallas_call(
            functools.partial(combine_kernel, tuple(sources), last),
            in_specs=[vmem_spec] * (2 + len(parts)),
            out_specs=vmem_spec if last else [vmem_spec] * 2,
            scratch_shapes=[pltpu.VMEM((rows, HD), jnp.bfloat16)] if last else [],
            out_shape=out_shape,
            compiler_params=params,
            cost_estimate=cost(0),
            name="combine",
        )(own, log, *parts)

    payload = pl.pallas_call(
        prepare_kernel,
        in_specs=[vmem_spec] * 3,
        out_specs=vmem_spec,
        scratch_shapes=[pltpu.VMEM((rows, HD), jnp.bfloat16)],
        out_shape=jax.ShapeDtypeStruct((payload_rows(new_rows, kv_width), rows), jnp.bfloat16),
        compiler_params=params,
        name="prepare",
    )(queries[0], new_keys[0], new_values[0])
    own_out, own_log = own_part(payload)
    if pool_size == 4:
        def send(array, *pairs):
            return lax.ppermute(array, "pool", pairs)

        near = send(payload, (0, 1), (1, 0), (2, 3), (3, 2))
        middle = send(payload, (1, 2), (2, 1))
        near, middle, own_out, own_log = lax.optimization_barrier((near, middle, own_out, own_log))
        crossed = send(near, (1, 2), (2, 1))
        outward = send(middle, (1, 0), (2, 3))
        first = other_part((3, 1), (middle, near))
        crossed, outward, first = lax.optimization_barrier((crossed, outward, first))
        across = send(first, (1, 2), (2, 1))
        inward = send(first, (0, 1), (3, 2))
        far = send(crossed, (1, 0), (2, 3))
        second = other_part((2, 2), (crossed, outward), share=0)
        near, second = lax.optimization_barrier((near, second))
        apart = send(second, (0, 2), (2, 0), (1, 3), (3, 1))
        own_out, own_log = combine(
            own_out, own_log, [(3, None), (1, None)], [across, inward], last=False
        )
        near, own_out, own_log = lax.optimization_barrier((near, own_out, own_log))
        third = other_part((1, 3), (near, far), share=8)
        ends = send(third, (0, 3), (3, 0))
        back = send(third, (1, 0), (2, 3))
        own_out, own_log, third = lax.optimization_barrier((own_out, own_log, third))
        own_out, own_log = combine(own_out, own_log, [(2, 2)], [apart], last=False)
        sources = [(None, 1), (None, 3)]
        parts = [back, ends]
        moved = [
            ((0, 0), payload),
            ((1, 1), near),
            ((3, None), middle),
            ((2, None), crossed),
            ((None, 2), outward),
            ((None, 3), far),
        ]
    else:
        gathered = lax.all_gather(payload, "pool", axis=0, tiled=False)
        packed = lax.map(
            lambda pair: other_part(None, (pair[0],), pair[1].reshape(1)),
            (gathered, jnp.arange(pool_size, dtype=jnp.int32)),
        )
        parts = lax.all_to_all(packed, "pool", split_axis=0, concat_axis=0, tiled=True)
        sources = list(range(pool_size))
        moved = [(source, gathered[source]) for source in range(pool_size)]

    attended = combine(own_out, own_log, sources, parts)
    pushed_keys, pushed_values = pl.pallas_call(
        functools.partial(push_kernel, pool_size, tuple(entry for entry, _ in moved)),
        in_specs=[smem_spec] + [hbm_spec] * len(moved),
        out_specs=[vmem_spec] * 2,
        scratch_shapes=[pltpu.SemaphoreType.DMA((2, CAPP, new_rows // PIECE))],
        out_shape=[jax.ShapeDtypeStruct((CAPP, new_rows, kv_width), jnp.bfloat16)] * 2,
        compiler_params=params,
        name="push",
    )(decode_owner, *[array for _, array in moved])
    return (attended[None], pushed_keys, pushed_values)


def solution(mesh):
    in_specs = (
        P(("groups", "pool"), None, ("tensor", "sub")),
        P(("groups", "pool"), None, ("tensor", "sub")),
        P(("groups", "pool"), None, ("tensor", "sub")),
        P(("groups", "pool"), None, ("tensor", "sub")),
        P(("groups", "pool"), None, ("tensor", "sub")),
        P("groups"),
        P("groups", None),
        P("groups", None),
        P("groups"),
    )
    out_specs = (
        P(("groups", "pool"), None, ("tensor", "sub")),
        P(("groups", "pool"), None, ("tensor", "sub")),
        P(("groups", "pool"), None, ("tensor", "sub")),
    )
    return jax.shard_map(shards, mesh=mesh, in_specs=in_specs, out_specs=out_specs, check_vma=False)
```

```python
import functools
import math

import jax
import jax.numpy as jnp
from jax import lax
from jax.experimental import pallas as pl
from jax.experimental.pallas import tpu as pltpu
from jax.sharding import PartitionSpec as P

HEADS = 64
KVH = 8
HD = 128
MAXBLK = 32
CAPP = 2
GROUP = HEADS // KVH
EMPTY = -1e30
TILE = 256
ONES = 16
PIECE = 32
SCALE = 1.0 / math.sqrt(HD)
EXP2_SCALE = SCALE * math.log2(math.e)
VMEM_LIMIT = 63 * 1024 * 1024 + 512 * 1024


def blocks_at(tables, request, place, pool_size):
    prefix_ref, store_ref, slot_ref = tables
    first = lax.rem(place - store_ref[request, 0] + pool_size, pool_size)
    count = lax.max(lax.div(prefix_ref[request] - first + pool_size - 1, pool_size), 0)
    return count, lambda entry: slot_ref[request, first + entry * pool_size]


def fetch(pool_size, tables, request, stores, buffers, sems, moved=None):
    me = lax.axis_index("pool")
    count, slot_of = blocks_at(tables, request, me, pool_size)

    def copies(slot, entry):
        return [
            pltpu.make_async_copy(stores[i].at[slot], buffers[i].at[entry], sems.at[i, entry])
            for i in range(2)
        ]

    def start(entry, carry):
        for copy in copies(slot_of(entry), entry):
            copy.start()
        return carry

    lax.fori_loop(0, count, start, 0)
    total = count
    if moved is not None:
        extra, _ = blocks_at(tables, request, me ^ 1, pool_size)
        capacity = moved.shape[0] // 2

        def start_moved(index, carry):
            for i in range(2):
                pltpu.make_async_copy(
                    moved.at[i * capacity + index],
                    buffers[i].at[count + index],
                    sems.at[i, count + index],
                ).start()
            return carry

        lax.fori_loop(0, extra, start_moved, 0)
        total = count + extra

    def ready(entry):
        for copy in copies(0, entry):
            copy.wait()

    return total, ready


def gather_kernel(pool_size, prefix_ref, store_ref, slot_ref, store_keys, store_values, out_ref, sems):
    me = lax.axis_index("pool")
    capacity = out_ref.shape[0] // 2

    @pl.when(jnp.logical_not(is_inner(me)))
    def _():
        tables = (prefix_ref, store_ref, slot_ref)
        count, slot_of = blocks_at(tables, me ^ 3, me, pool_size)

        def copies(entry):
            return [
                pltpu.make_async_copy(
                    store.at[slot_of(entry)], out_ref.at[i * capacity + entry], sems.at[i, entry]
                )
                for i, store in enumerate((store_keys, store_values))
            ]

        def start(entry, carry):
            for copy in copies(entry):
                copy.start()
            return carry

        def wait(entry, carry):
            for copy in copies(entry):
                copy.wait()
            return carry

        lax.fori_loop(0, count, start, 0)
        lax.fori_loop(0, count, wait, 0)


def attend(
    key_ref,
    value_ref,
    count,
    ready,
    fresh,
    new_rows,
    columns,
    scores,
    weights,
    peaks,
    factors,
    turned,
    acc,
):
    rows = columns.shape[1]
    kv_local = columns.shape[0] // HD

    def visit(keys, values, seen):
        size = keys[0].shape[0]

        def score(kv):
            turned[kv, :HD, :size] = values[kv].T
            block = lax.dot_general(
                keys[kv],
                columns[kv * HD : (kv + 1) * HD, :],
                (((1,), (0,)), ((), ())),
                preferred_element_type=jnp.float32,
            )
            if seen is not None:
                block = jnp.where(seen, block, EMPTY)
            scores[kv, :size, :] = block

        def weigh(kv):
            for i in range(0, rows, TILE):
                part = slice(i, i + TILE)
                before = peaks[kv, :, part]
                block = scores[kv, :size, part]
                peak = jnp.maximum(before, jnp.max(block, axis=0, keepdims=True))
                factors[kv, :, part] = jnp.exp2((before - peak) * EXP2_SCALE)
                peaks[kv, :, part] = peak
                weight = jnp.exp2(block * EXP2_SCALE - peak[0:1] * EXP2_SCALE)
                weights[kv, :size, part] = weight.astype(jnp.bfloat16)

        def mix(kv):
            added = lax.dot_general(
                turned[kv, :, :size],
                weights[kv, :size, :],
                (((1,), (0,)), ((), ())),
                preferred_element_type=jnp.float32,
            )
            acc[kv] = acc[kv] * factors[kv, 0:1, :] + added

        for step in range(kv_local + 2):
            for offset, stage in ((0, score), (2, mix), (1, weigh)):
                if 0 <= step - offset < kv_local:
                    stage(step - offset)

    def lanes_of(array):
        return [array[:, kv * HD : (kv + 1) * HD] for kv in range(kv_local)]

    def blocks_of(ref, first, number):
        return lanes_of(ref[pl.ds(first, number)].reshape(number * ref.shape[1], ref.shape[2]))

    peaks[...] = jnp.full(peaks.shape, EMPTY, jnp.float32)
    acc[...] = jnp.zeros(acc.shape, jnp.float32)
    turned[:, HD:, :] = jnp.ones((kv_local, ONES, turned.shape[2]), jnp.bfloat16)
    if fresh is not None:
        new_key_ref, new_value_ref = fresh
        row = lax.rem(lax.broadcasted_iota(jnp.int32, (1, rows), 1), new_rows)
        seen = lax.broadcasted_iota(jnp.int32, (new_key_ref.shape[0], rows), 0) <= row
        visit(lanes_of(new_key_ref), lanes_of(new_value_ref), seen)

    def visit_blocks(number):
        def body(index, carry):
            for i in range(number):
                ready(index * number + i)
            visit(
                blocks_of(key_ref, index * number, number),
                blocks_of(value_ref, index * number, number),
                None,
            )
            return carry

        return body

    pairs = count // 2 if key_ref.shape[0] > 1 else 0
    if key_ref.shape[0] > 1:
        lax.fori_loop(0, pairs, visit_blocks(2), 0)
    lax.fori_loop(2 * pairs, count, visit_blocks(1), 0)
    outs = []
    logs = []
    for kv in range(kv_local):
        total = acc[kv, HD : HD + 1, :]
        safe = jnp.where(total > 0, total, 1.0)
        logs.append(jnp.where(total > 0, peaks[kv, 0:1] * SCALE + jnp.log(safe), EMPTY))
        outs.append(acc[kv, :HD, :] * (1.0 / safe))
    return outs, logs


def prepare_kernel(query_ref, new_key_ref, new_value_ref, payload_ref, fresh_ref, query_rows):
    new_rows = query_ref.shape[0]
    kv_width = new_key_ref.shape[1]
    for kv in range(kv_width // HD):
        for g in range(GROUP):
            head = kv * GROUP + g
            query_rows[g * new_rows : (g + 1) * new_rows, :] = query_ref[
                :, head * HD : (head + 1) * HD
            ]
        payload_ref[kv * HD : (kv + 1) * HD, :] = query_rows[...].T
    for i, new_ref in enumerate((new_key_ref, new_value_ref)):
        for piece in range(new_rows // PIECE):
            row, lane = piece_place(i, piece, new_rows, kv_width)
            values = new_ref[piece * PIECE : (piece + 1) * PIECE, :]
            payload_ref[row : row + PIECE, lane : lane + kv_width] = values
            fresh_ref[row - kv_width : row - kv_width + PIECE, lane : lane + kv_width] = values


def piece_place(i, piece, new_rows, kv_width):
    index = i * (new_rows // PIECE) + piece
    beside = GROUP * new_rows // kv_width
    return kv_width + index // beside * PIECE, index % beside * kv_width


def payload_rows(new_rows, kv_width):
    return piece_place(1, new_rows // PIECE - 1, new_rows, kv_width)[0] + PIECE


def own_kernel(
    pool_size,
    prefix_ref,
    store_ref,
    slot_ref,
    payload_ref,
    new_key_ref,
    new_value_ref,
    store_keys,
    store_values,
    out_ref,
    log_ref,
    key_buf,
    value_buf,
    new_key_buf,
    new_value_buf,
    *state,
):
    *work, sems = state
    count, ready = fetch(
        pool_size,
        (prefix_ref, store_ref, slot_ref),
        lax.axis_index("pool"),
        (store_keys, store_values),
        (key_buf, value_buf),
        sems,
    )
    new_rows, kv_width = new_key_ref.shape
    for buffer, source in ((new_key_buf, new_key_ref), (new_value_buf, new_value_ref)):
        buffer[:new_rows, :] = source[...]
        buffer[new_rows:, :] = jnp.zeros((buffer.shape[0] - new_rows, kv_width), jnp.bfloat16)
    fresh = (new_key_buf, new_value_buf)
    outs, logs = attend(
        key_buf, value_buf, count, ready, fresh, new_rows, payload_ref.at[:kv_width], *work
    )
    log_ref[...] = jnp.zeros(log_ref.shape, jnp.float32)
    for kv, (out, log) in enumerate(zip(outs, logs)):
        out_ref[kv * HD : (kv + 1) * HD, :] = out
        log_ref[kv : kv + 1, :] = log


def other_kernel(pool_size, new_rows, partners, with_moved, *refs):
    if partners is None:
        request = refs[0][0]
        choice = [None]
        refs = refs[1:]
    else:
        inner = is_inner(lax.axis_index("pool"))
        _, request = source_of(lax.axis_index("pool"), partners)
        choice = [
            hit for hit, mask in zip((inner, jnp.logical_not(inner)), partners) if mask is not None
        ]
    tables, refs = refs[:3], refs[3:]
    payload_refs, refs = refs[: len(choice)], refs[len(choice) :]
    moved = None
    if with_moved:
        moved, refs = refs[0], refs[1:]
    store_keys, store_values, out_ref, key_buf, value_buf, *state = refs
    *work, columns, query_sem, sems = state
    kv_width = columns.shape[0]

    def query_copy(payload_ref):
        return pltpu.make_async_copy(payload_ref.at[:kv_width], columns, query_sem)

    def run():
        for payload_ref, hit in zip(payload_refs, choice):
            if len(choice) == 1:
                query_copy(payload_ref).start()
            else:
                pl.when(hit)(query_copy(payload_ref).start)
        count, ready = fetch(
            pool_size,
            tables,
            request,
            (store_keys, store_values),
            (key_buf, value_buf),
            sems,
            moved,
        )
        query_copy(payload_refs[0]).wait()
        outs, logs = attend(key_buf, value_buf, count, ready, None, new_rows, columns, *work)
        tail = []
        for kv, (out, log) in enumerate(zip(outs, logs)):
            out_ref[kv * HD : (kv + 1) * HD, :] = out.astype(jnp.bfloat16)
            high = log.astype(jnp.bfloat16).astype(jnp.float32)
            middle = (log - high).astype(jnp.bfloat16).astype(jnp.float32)
            tail += [high, middle, log - high - middle]
        tail.append(jnp.zeros((ONES - len(tail), columns.shape[1]), jnp.float32))
        out_ref[kv_width:, :] = jnp.concatenate(tail, axis=0).astype(jnp.bfloat16)

    if len(choice) == 1 and choice[0] is not None:
        pl.when(choice[0])(run)
    else:
        run()


def is_inner(place):
    return (place == 1) | (place == 2)


def source_of(me, entry):
    if isinstance(entry, int):
        return jnp.bool_(True), jnp.int32(entry)
    inner = is_inner(me)
    masks = [0 if mask is None else mask for mask in entry]
    there = jnp.where(inner, entry[0] is not None, entry[1] is not None)
    return there, me ^ jnp.where(inner, masks[0], masks[1])


def push_kernel(pool_size, entries, owner_ref, *refs):
    payload_refs = refs[: len(entries)]
    key_out, value_out, sems = refs[len(entries) :]
    outs = (key_out, value_out)
    kv_width = key_out.shape[2]
    me = lax.axis_index("pool")
    total = jnp.int32(0)
    for other in range(pool_size):
        total += (owner_ref[other] == me).astype(jnp.int32)

    new_rows = key_out.shape[1]

    def copies(payload_ref, place):
        for i in range(2):
            for piece in range(new_rows // PIECE):
                row, lane = piece_place(i, piece, new_rows, kv_width)
                row += payload_ref.shape[0] - payload_rows(new_rows, kv_width)
                yield pltpu.make_async_copy(
                    payload_ref.at[row : row + PIECE, lane : lane + kv_width],
                    outs[i].at[place, piece * PIECE : (piece + 1) * PIECE],
                    sems.at[i, place, piece],
                )

    for entry, payload_ref in zip(entries, payload_refs):
        there, source = source_of(me, entry)
        rank = jnp.int32(0)
        for other in range(pool_size):
            rank += ((owner_ref[other] == me) & (other < source)).astype(jnp.int32)
        hit = there & (owner_ref[source] == me)
        for place in range(CAPP):

            @pl.when(hit & (rank == place))
            def _():
                for copy in copies(payload_ref, place):
                    copy.start()

    for place in range(CAPP):

        @pl.when(total <= place)
        def _():
            for out in outs:
                out[place] = jnp.zeros(out.shape[1:], jnp.bfloat16)

        @pl.when(total > place)
        def _():
            for copy in copies(payload_refs[0], place):
                copy.wait()


def combine_kernel(sources, last, own_ref, log_ref, *refs):
    parts = refs[: len(sources)]
    out_ref = refs[len(sources)]
    kv_width, rows = own_ref.shape
    me = lax.axis_index("pool")
    arrived = []
    tails = []
    for source, part in zip(sources, parts):
        there, request = source_of(me, source)
        arrived.append(there & (request != me))
        tails.append(part[kv_width:, :].astype(jnp.float32))
    if not last:
        refs[len(sources) + 1][...] = log_ref[...]
    for kv in range(kv_width // HD):
        logs = [log_ref[kv : kv + 1, :]]
        for there, tail in zip(arrived, tails):
            log = sum(tail[3 * kv + i : 3 * kv + i + 1] for i in range(3))
            logs.append(jnp.where(there, log, EMPTY))
        peak = functools.reduce(jnp.maximum, logs)
        shares = [jnp.exp(x - peak) for x in logs]
        total = functools.reduce(jnp.add, shares)
        shares = [x * (1.0 / total) for x in shares]
        band = slice(kv * HD, (kv + 1) * HD)
        for i in range(0, rows, TILE):
            part = slice(i, i + TILE)
            mixed = own_ref[band, part] * shares[0][:, part]
            for share, ref in zip(shares[1:], parts):
                mixed = mixed + ref[band, part].astype(jnp.float32) * share[:, part]
            if last:
                refs[len(sources) + 1][part, :] = mixed.astype(jnp.bfloat16).T
            else:
                out_ref[band, part] = mixed
        if last:
            turned = refs[len(sources) + 1]
            new_rows = out_ref.shape[0]
            for g in range(GROUP):
                head = kv * GROUP + g
                out_ref[:, head * HD : (head + 1) * HD] = turned[g * new_rows : (g + 1) * new_rows, :]
        else:
            refs[len(sources) + 1][kv : kv + 1, :] = peak + jnp.log(total)


def shards(
    queries,
    new_keys,
    new_values,
    store_keys,
    store_values,
    prefix_blocks,
    hit_store,
    hit_slot,
    decode_owner,
):
    pool_size = lax.axis_size("pool")
    capacity = (MAXBLK + pool_size - 1) // pool_size
    new_rows = queries.shape[1]
    width = queries.shape[2]
    kv_width = new_keys.shape[2]
    block_len = store_keys.shape[1]
    rows = GROUP * new_rows
    tables = (prefix_blocks, hit_store, hit_slot)
    smem_spec = pl.BlockSpec(memory_space=pltpu.SMEM)
    hbm_spec = pl.BlockSpec(memory_space=pltpu.HBM)
    vmem_spec = pl.BlockSpec(memory_space=pltpu.VMEM)
    params = pltpu.CompilerParams(vmem_limit_bytes=VMEM_LIMIT)

    def cost(share):
        return pl.CostEstimate(
            flops=share * rows * block_len * kv_width * capacity,
            bytes_accessed=rows,
            transcendentals=0,
        )

    buffers = [pltpu.VMEM((capacity, block_len, kv_width), jnp.bfloat16)] * 2
    kv_local = kv_width // HD
    widest = block_len * min(2, capacity)
    work = [
        pltpu.VMEM((kv_local, widest, rows), jnp.float32),
        pltpu.VMEM((kv_local, widest, rows), jnp.bfloat16),
        pltpu.VMEM((kv_local, 8, rows), jnp.float32),
        pltpu.VMEM((kv_local, 8, rows), jnp.float32),
        pltpu.VMEM((kv_local, HD + ONES, widest), jnp.bfloat16),
        pltpu.VMEM((kv_local, HD + ONES, rows), jnp.float32),
    ]
    sems = pltpu.SemaphoreType.DMA((2, capacity))

    def own_part(payload):
        return pl.pallas_call(
            functools.partial(own_kernel, pool_size),
            in_specs=[smem_spec] * 3 + [vmem_spec] * 3 + [hbm_spec] * 2,
            out_specs=[vmem_spec] * 2,
            scratch_shapes=[
                *buffers,
                *[pltpu.VMEM((block_len, kv_width), jnp.bfloat16)] * 2,
                *work,
                sems,
            ],
            out_shape=[
                jax.ShapeDtypeStruct((kv_width, rows), jnp.float32),
                jax.ShapeDtypeStruct((8, rows), jnp.float32),
            ],
            compiler_params=params,
            cost_estimate=cost(8),
            name="own_part",
        )(*tables, payload, new_keys[0], new_values[0], store_keys, store_values)

    def other_part(partners, held, *request, share=8, moved=()):
        room = capacity * (1 + len(moved))
        return pl.pallas_call(
            functools.partial(other_kernel, pool_size, new_rows, partners, bool(moved)),
            in_specs=[smem_spec] * (3 + len(request)) + [hbm_spec] * (len(held) + len(moved) + 2),
            out_specs=vmem_spec,
            scratch_shapes=[
                *[pltpu.VMEM((room, block_len, kv_width), jnp.bfloat16)] * 2,
                *work,
                pltpu.VMEM((kv_width, rows), jnp.bfloat16),
                pltpu.SemaphoreType.DMA,
                pltpu.SemaphoreType.DMA((2, room)),
            ],
            out_shape=jax.ShapeDtypeStruct((kv_width + ONES, rows), jnp.bfloat16),
            compiler_params=params,
            cost_estimate=cost(share),
            name="other_part",
        )(*request, *tables, *held, *moved, store_keys, store_values)

    def combine(own, log, sources, parts, last=True):
        if last:
            out_shape = jax.ShapeDtypeStruct((new_rows, width), jnp.bfloat16)
        else:
            out_shape = [
                jax.ShapeDtypeStruct((kv_width, rows), jnp.float32),
                jax.ShapeDtypeStruct((8, rows), jnp.float32),
            ]
        return pl.pallas_call(
            functools.partial(combine_kernel, tuple(sources), last),
            in_specs=[vmem_spec] * (2 + len(parts)),
            out_specs=vmem_spec if last else [vmem_spec] * 2,
            scratch_shapes=[pltpu.VMEM((rows, HD), jnp.bfloat16)] if last else [],
            out_shape=out_shape,
            compiler_params=params,
            cost_estimate=cost(0),
            name="combine",
        )(own, log, *parts)

    all_rows = payload_rows(new_rows, kv_width)
    payload, fresh = pl.pallas_call(
        prepare_kernel,
        in_specs=[vmem_spec] * 3,
        out_specs=[vmem_spec] * 2,
        scratch_shapes=[pltpu.VMEM((rows, HD), jnp.bfloat16)],
        out_shape=[
            jax.ShapeDtypeStruct((all_rows, rows), jnp.bfloat16),
            jax.ShapeDtypeStruct((all_rows - kv_width, rows), jnp.bfloat16),
        ],
        compiler_params=params,
        name="prepare",
    )(queries[0], new_keys[0], new_values[0])
    own_out, own_log = own_part(payload)
    if pool_size == 4:
        def send(array, *pairs):
            return lax.ppermute(array, "pool", pairs)

        near = send(payload, (0, 1), (1, 0), (2, 3), (3, 2))
        middle = send(payload, (1, 2), (2, 1))
        far = send(fresh, (0, 3), (3, 0))
        blocks = pl.pallas_call(
            functools.partial(gather_kernel, pool_size),
            in_specs=[smem_spec] * 3 + [hbm_spec] * 2,
            out_specs=vmem_spec,
            scratch_shapes=[sems],
            out_shape=jax.ShapeDtypeStruct((2 * capacity, block_len, kv_width), jnp.bfloat16),
            compiler_params=params,
            name="gather_blocks",
        )(*tables, store_keys, store_values)
        near, middle, own_out, own_log, blocks = lax.optimization_barrier(
            (near, middle, own_out, own_log, blocks)
        )
        crossed = send(near, (1, 2), (2, 1))
        outward = send(middle, (1, 0), (2, 3))
        blocks = send(blocks, (0, 1), (3, 2))
        first = other_part((3, 1), (middle, near))
        across = send(first, (1, 2), (2, 1))
        near, outward, first = lax.optimization_barrier((near, outward, first))
        second = other_part((1, 2), (near, outward), share=0)
        back = send(second, (1, 0), (2, 3))
        apart = send(second, (0, 2), (3, 1))
        first, crossed, second = lax.optimization_barrier((first, crossed, second))
        inward = send(first, (0, 1), (3, 2))
        third = other_part((2, None), (crossed,), moved=(blocks,))
        ends = send(third, (1, 3), (2, 0))
        own_out, own_log, third = lax.optimization_barrier((own_out, own_log, third))
        own_out, own_log = combine(
            own_out,
            own_log,
            [(3, None), (1, None), (2, None), (None, 1)],
            [across, inward, apart, back],
            last=False,
        )
        sources = [(None, 2)]
        parts = [ends]
        moved = [
            ((0, 0), payload),
            ((1, 1), near),
            ((3, None), middle),
            ((2, None), crossed),
            ((None, 2), outward),
            ((None, 3), far),
        ]
    else:
        gathered = lax.all_gather(payload, "pool", axis=0, tiled=False)
        packed = lax.map(
            lambda pair: other_part(None, (pair[0],), pair[1].reshape(1)),
            (gathered, jnp.arange(pool_size, dtype=jnp.int32)),
        )
        parts = lax.all_to_all(packed, "pool", split_axis=0, concat_axis=0, tiled=True)
        sources = list(range(pool_size))
        moved = [(source, gathered[source]) for source in range(pool_size)]

    attended = combine(own_out, own_log, sources, parts)
    pushed_keys, pushed_values = pl.pallas_call(
        functools.partial(push_kernel, pool_size, tuple(entry for entry, _ in moved)),
        in_specs=[smem_spec] + [hbm_spec] * len(moved),
        out_specs=[vmem_spec] * 2,
        scratch_shapes=[pltpu.SemaphoreType.DMA((2, CAPP, new_rows // PIECE))],
        out_shape=[jax.ShapeDtypeStruct((CAPP, new_rows, kv_width), jnp.bfloat16)] * 2,
        compiler_params=params,
        name="push",
    )(decode_owner, *[array for _, array in moved])
    return (attended[None], pushed_keys, pushed_values)


def solution(mesh):
    in_specs = (
        P(("groups", "pool"), None, ("tensor", "sub")),
        P(("groups", "pool"), None, ("tensor", "sub")),
        P(("groups", "pool"), None, ("tensor", "sub")),
        P(("groups", "pool"), None, ("tensor", "sub")),
        P(("groups", "pool"), None, ("tensor", "sub")),
        P("groups"),
        P("groups", None),
        P("groups", None),
        P("groups"),
    )
    out_specs = (
        P(("groups", "pool"), None, ("tensor", "sub")),
        P(("groups", "pool"), None, ("tensor", "sub")),
        P(("groups", "pool"), None, ("tensor", "sub")),
    )
    return jax.shard_map(shards, mesh=mesh, in_specs=in_specs, out_specs=out_specs, check_vma=False)
```

```python
import functools
import math

import jax
import jax.numpy as jnp
from jax import lax
from jax.experimental import pallas as pl
from jax.experimental.pallas import tpu as pltpu
from jax.sharding import PartitionSpec as P

HEADS = 64
KVH = 8
HD = 128
MAXBLK = 32
CAPP = 2
GROUP = HEADS // KVH
EMPTY = -1e30
TILE = 256
ONES = 16
PIECE = 32
SCALE = 1.0 / math.sqrt(HD)
EXP2_SCALE = SCALE * math.log2(math.e)
VMEM_LIMIT = 63 * 1024 * 1024 + 512 * 1024


def blocks_at(tables, request, place, pool_size):
    prefix_ref, store_ref, slot_ref = tables
    first = lax.rem(place - store_ref[request, 0] + pool_size, pool_size)
    count = lax.max(lax.div(prefix_ref[request] - first + pool_size - 1, pool_size), 0)
    return count, lambda entry: slot_ref[request, first + entry * pool_size]


def fetch(pool_size, tables, request, stores, buffers, sems, moved=None):
    me = lax.axis_index("pool")
    count, slot_of = blocks_at(tables, request, me if moved is None else me ^ 1, pool_size)

    def copies(entry):
        for i in range(2):
            if moved is None:
                source = stores[i].at[slot_of(entry)]
            else:
                source = moved.at[i * (moved.shape[0] // 2) + entry]
            yield pltpu.make_async_copy(source, buffers[i].at[entry], sems.at[i, entry])

    def start(entry, carry):
        for copy in copies(entry):
            copy.start()
        return carry

    lax.fori_loop(0, count, start, 0)

    def ready(entry):
        for copy in copies(entry):
            copy.wait()

    return count, ready


def gather_kernel(pool_size, prefix_ref, store_ref, slot_ref, store_keys, store_values, out_ref, sems):
    me = lax.axis_index("pool")
    capacity = out_ref.shape[0] // 2

    @pl.when(jnp.logical_not(is_inner(me)))
    def _():
        tables = (prefix_ref, store_ref, slot_ref)
        count, slot_of = blocks_at(tables, me ^ 3, me, pool_size)

        def copies(entry):
            return [
                pltpu.make_async_copy(
                    store.at[slot_of(entry)], out_ref.at[i * capacity + entry], sems.at[i, entry]
                )
                for i, store in enumerate((store_keys, store_values))
            ]

        def start(entry, carry):
            for copy in copies(entry):
                copy.start()
            return carry

        def wait(entry, carry):
            for copy in copies(entry):
                copy.wait()
            return carry

        lax.fori_loop(0, count, start, 0)
        lax.fori_loop(0, count, wait, 0)


def attend(
    key_ref,
    value_ref,
    count,
    ready,
    fresh,
    new_rows,
    columns,
    scores,
    weights,
    peaks,
    factors,
    turned,
    acc,
    initial=None,
    raw=False,
):
    rows = columns.shape[1]
    kv_local = columns.shape[0] // HD

    def visit(keys, values, seen):
        size = keys[0].shape[0]

        def score(kv):
            turned[kv, :HD, :size] = values[kv].T
            block = lax.dot_general(
                keys[kv],
                columns[kv * HD : (kv + 1) * HD, :],
                (((1,), (0,)), ((), ())),
                preferred_element_type=jnp.float32,
            )
            if seen is not None:
                block = jnp.where(seen, block, EMPTY)
            scores[kv, :size, :] = block

        def weigh(kv):
            for i in range(0, rows, TILE):
                part = slice(i, i + TILE)
                before = peaks[kv, :, part]
                block = scores[kv, :size, part]
                peak = jnp.maximum(before, jnp.max(block, axis=0, keepdims=True))
                factors[kv, :, part] = jnp.exp2((before - peak) * EXP2_SCALE)
                peaks[kv, :, part] = peak
                weight = jnp.exp2(block * EXP2_SCALE - peak[0:1] * EXP2_SCALE)
                weights[kv, :size, part] = weight.astype(jnp.bfloat16)

        def mix(kv):
            added = lax.dot_general(
                turned[kv, :, :size],
                weights[kv, :size, :],
                (((1,), (0,)), ((), ())),
                preferred_element_type=jnp.float32,
            )
            acc[kv] = acc[kv] * factors[kv, 0:1, :] + added

        for step in range(kv_local + 2):
            for offset, stage in ((0, score), (2, mix), (1, weigh)):
                if 0 <= step - offset < kv_local:
                    stage(step - offset)

    def lanes_of(array):
        return [array[:, kv * HD : (kv + 1) * HD] for kv in range(kv_local)]

    def blocks_of(ref, first, number):
        return lanes_of(ref[pl.ds(first, number)].reshape(number * ref.shape[1], ref.shape[2]))

    if initial is None:
        peaks[...] = jnp.full(peaks.shape, EMPTY, jnp.float32)
        acc[...] = jnp.zeros(acc.shape, jnp.float32)
    else:
        acc[...] = initial[0][...]
        peaks[...] = initial[1][...]
    turned[:, HD:, :] = jnp.ones((kv_local, ONES, turned.shape[2]), jnp.bfloat16)
    if fresh is not None:
        new_key_ref, new_value_ref = fresh
        row = lax.rem(lax.broadcasted_iota(jnp.int32, (1, rows), 1), new_rows)
        seen = lax.broadcasted_iota(jnp.int32, (new_key_ref.shape[0], rows), 0) <= row
        visit(lanes_of(new_key_ref), lanes_of(new_value_ref), seen)

    def visit_blocks(number):
        def body(index, carry):
            for i in range(number):
                ready(index * number + i)
            visit(
                blocks_of(key_ref, index * number, number),
                blocks_of(value_ref, index * number, number),
                None,
            )
            return carry

        return body

    pairs = count // 2 if key_ref.shape[0] > 1 else 0
    if key_ref.shape[0] > 1:
        lax.fori_loop(0, pairs, visit_blocks(2), 0)
    lax.fori_loop(2 * pairs, count, visit_blocks(1), 0)
    if raw:
        return acc[...], peaks[...]
    outs = []
    logs = []
    for kv in range(kv_local):
        total = acc[kv, HD : HD + 1, :]
        safe = jnp.where(total > 0, total, 1.0)
        logs.append(jnp.where(total > 0, peaks[kv, 0:1] * SCALE + jnp.log(safe), EMPTY))
        outs.append(acc[kv, :HD, :] * (1.0 / safe))
    return outs, logs


def prepare_kernel(query_ref, new_key_ref, new_value_ref, payload_ref, fresh_ref, query_rows):
    new_rows = query_ref.shape[0]
    kv_width = new_key_ref.shape[1]
    for kv in range(kv_width // HD):
        for g in range(GROUP):
            head = kv * GROUP + g
            query_rows[g * new_rows : (g + 1) * new_rows, :] = query_ref[
                :, head * HD : (head + 1) * HD
            ]
        payload_ref[kv * HD : (kv + 1) * HD, :] = query_rows[...].T
    for i, new_ref in enumerate((new_key_ref, new_value_ref)):
        for piece in range(new_rows // PIECE):
            row, lane = piece_place(i, piece, new_rows, kv_width)
            values = new_ref[piece * PIECE : (piece + 1) * PIECE, :]
            payload_ref[row : row + PIECE, lane : lane + kv_width] = values
            fresh_ref[row - kv_width : row - kv_width + PIECE, lane : lane + kv_width] = values


def piece_place(i, piece, new_rows, kv_width):
    index = i * (new_rows // PIECE) + piece
    beside = GROUP * new_rows // kv_width
    return kv_width + index // beside * PIECE, index % beside * kv_width


def payload_rows(new_rows, kv_width):
    return piece_place(1, new_rows // PIECE - 1, new_rows, kv_width)[0] + PIECE


def own_kernel(
    pool_size,
    prefix_ref,
    store_ref,
    slot_ref,
    payload_ref,
    new_key_ref,
    new_value_ref,
    store_keys,
    store_values,
    out_ref,
    log_ref,
    key_buf,
    value_buf,
    new_key_buf,
    new_value_buf,
    *state,
):
    *work, sems = state
    count, ready = fetch(
        pool_size,
        (prefix_ref, store_ref, slot_ref),
        lax.axis_index("pool"),
        (store_keys, store_values),
        (key_buf, value_buf),
        sems,
    )
    new_rows, kv_width = new_key_ref.shape
    for buffer, source in ((new_key_buf, new_key_ref), (new_value_buf, new_value_ref)):
        buffer[:new_rows, :] = source[...]
        buffer[new_rows:, :] = jnp.zeros((buffer.shape[0] - new_rows, kv_width), jnp.bfloat16)
    fresh = (new_key_buf, new_value_buf)
    outs, logs = attend(
        key_buf, value_buf, count, ready, fresh, new_rows, payload_ref.at[:kv_width], *work
    )
    log_ref[...] = jnp.zeros(log_ref.shape, jnp.float32)
    for kv, (out, log) in enumerate(zip(outs, logs)):
        out_ref[kv * HD : (kv + 1) * HD, :] = out
        log_ref[kv : kv + 1, :] = log


def other_kernel(pool_size, new_rows, partners, with_moved, raw, *refs):
    if partners is None:
        request = refs[0][0]
        choice = [None]
        refs = refs[1:]
    else:
        inner = is_inner(lax.axis_index("pool"))
        _, request = source_of(lax.axis_index("pool"), partners)
        choice = [
            hit for hit, mask in zip((inner, jnp.logical_not(inner)), partners) if mask is not None
        ]
    tables, refs = refs[:3], refs[3:]
    payload_refs, refs = refs[: len(choice)], refs[len(choice) :]
    moved = initial = None
    if with_moved:
        moved, *initial = refs[:3]
        refs = refs[3:]
    store_keys, store_values, *refs = refs
    out_refs, (key_buf, value_buf, *state) = refs[: 1 + raw], refs[1 + raw :]
    *work, columns, query_sem, sems = state
    kv_width = columns.shape[0]

    def query_copy(payload_ref):
        return pltpu.make_async_copy(payload_ref.at[:kv_width], columns, query_sem)

    def run():
        for payload_ref, hit in zip(payload_refs, choice):
            if len(choice) == 1:
                query_copy(payload_ref).start()
            else:
                pl.when(hit)(query_copy(payload_ref).start)
        count, ready = fetch(
            pool_size,
            tables,
            request,
            (store_keys, store_values),
            (key_buf, value_buf),
            sems,
            moved,
        )
        query_copy(payload_refs[0]).wait()
        results = attend(
            key_buf, value_buf, count, ready, None, new_rows, columns, *work, initial, raw
        )
        if raw:
            for out_ref, result in zip(out_refs, results):
                out_ref[...] = result
            return
        outs, logs = results
        out_ref = out_refs[0]
        tail = []
        for kv, (out, log) in enumerate(zip(outs, logs)):
            out_ref[kv * HD : (kv + 1) * HD, :] = out.astype(jnp.bfloat16)
            high = log.astype(jnp.bfloat16).astype(jnp.float32)
            middle = (log - high).astype(jnp.bfloat16).astype(jnp.float32)
            tail += [high, middle, log - high - middle]
        tail.append(jnp.zeros((ONES - len(tail), columns.shape[1]), jnp.float32))
        out_ref[kv_width:, :] = jnp.concatenate(tail, axis=0).astype(jnp.bfloat16)

    if len(choice) == 1 and choice[0] is not None:
        pl.when(choice[0])(run)
    else:
        run()


def is_inner(place):
    return (place == 1) | (place == 2)


def source_of(me, entry):
    if isinstance(entry, int):
        return jnp.bool_(True), jnp.int32(entry)
    inner = is_inner(me)
    masks = [0 if mask is None else mask for mask in entry]
    there = jnp.where(inner, entry[0] is not None, entry[1] is not None)
    return there, me ^ jnp.where(inner, masks[0], masks[1])


def push_kernel(pool_size, entries, owner_ref, *refs):
    payload_refs = refs[: len(entries)]
    key_out, value_out, sems = refs[len(entries) :]
    outs = (key_out, value_out)
    kv_width = key_out.shape[2]
    me = lax.axis_index("pool")
    total = jnp.int32(0)
    for other in range(pool_size):
        total += (owner_ref[other] == me).astype(jnp.int32)

    new_rows = key_out.shape[1]

    def copies(payload_ref, place):
        for i in range(2):
            for piece in range(new_rows // PIECE):
                row, lane = piece_place(i, piece, new_rows, kv_width)
                row += payload_ref.shape[0] - payload_rows(new_rows, kv_width)
                yield pltpu.make_async_copy(
                    payload_ref.at[row : row + PIECE, lane : lane + kv_width],
                    outs[i].at[place, piece * PIECE : (piece + 1) * PIECE],
                    sems.at[i, place, piece],
                )

    for entry, payload_ref in zip(entries, payload_refs):
        there, source = source_of(me, entry)
        rank = jnp.int32(0)
        for other in range(pool_size):
            rank += ((owner_ref[other] == me) & (other < source)).astype(jnp.int32)
        hit = there & (owner_ref[source] == me)
        for place in range(CAPP):

            @pl.when(hit & (rank == place))
            def _():
                for copy in copies(payload_ref, place):
                    copy.start()

    for place in range(CAPP):

        @pl.when(total <= place)
        def _():
            for out in outs:
                out[place] = jnp.zeros(out.shape[1:], jnp.bfloat16)

        @pl.when(total > place)
        def _():
            for copy in copies(payload_refs[0], place):
                copy.wait()


def combine_kernel(sources, last, own_ref, log_ref, *refs):
    parts = refs[: len(sources)]
    out_ref = refs[len(sources)]
    kv_width, rows = own_ref.shape
    me = lax.axis_index("pool")
    arrived = []
    tails = []
    for source, part in zip(sources, parts):
        there, request = source_of(me, source)
        arrived.append(there & (request != me))
        tails.append(part[kv_width:, :].astype(jnp.float32))
    if not last:
        refs[len(sources) + 1][...] = log_ref[...]
    for kv in range(kv_width // HD):
        logs = [log_ref[kv : kv + 1, :]]
        for there, tail in zip(arrived, tails):
            log = sum(tail[3 * kv + i : 3 * kv + i + 1] for i in range(3))
            logs.append(jnp.where(there, log, EMPTY))
        peak = functools.reduce(jnp.maximum, logs)
        shares = [jnp.exp(x - peak) for x in logs]
        total = functools.reduce(jnp.add, shares)
        shares = [x * (1.0 / total) for x in shares]
        band = slice(kv * HD, (kv + 1) * HD)
        for i in range(0, rows, TILE):
            part = slice(i, i + TILE)
            mixed = own_ref[band, part] * shares[0][:, part]
            for share, ref in zip(shares[1:], parts):
                mixed = mixed + ref[band, part].astype(jnp.float32) * share[:, part]
            if last:
                refs[len(sources) + 1][part, :] = mixed.astype(jnp.bfloat16).T
            else:
                out_ref[band, part] = mixed
        if last:
            turned = refs[len(sources) + 1]
            new_rows = out_ref.shape[0]
            for g in range(GROUP):
                head = kv * GROUP + g
                out_ref[:, head * HD : (head + 1) * HD] = turned[g * new_rows : (g + 1) * new_rows, :]
        else:
            refs[len(sources) + 1][kv : kv + 1, :] = peak + jnp.log(total)


def shards(
    queries,
    new_keys,
    new_values,
    store_keys,
    store_values,
    prefix_blocks,
    hit_store,
    hit_slot,
    decode_owner,
):
    pool_size = lax.axis_size("pool")
    capacity = (MAXBLK + pool_size - 1) // pool_size
    new_rows = queries.shape[1]
    width = queries.shape[2]
    kv_width = new_keys.shape[2]
    block_len = store_keys.shape[1]
    rows = GROUP * new_rows
    tables = (prefix_blocks, hit_store, hit_slot)
    smem_spec = pl.BlockSpec(memory_space=pltpu.SMEM)
    hbm_spec = pl.BlockSpec(memory_space=pltpu.HBM)
    vmem_spec = pl.BlockSpec(memory_space=pltpu.VMEM)
    params = pltpu.CompilerParams(vmem_limit_bytes=VMEM_LIMIT)

    def cost(share):
        return pl.CostEstimate(
            flops=share * rows * block_len * kv_width * capacity,
            bytes_accessed=rows,
            transcendentals=0,
        )

    buffers = [pltpu.VMEM((capacity, block_len, kv_width), jnp.bfloat16)] * 2
    kv_local = kv_width // HD
    widest = block_len * min(2, capacity)
    work = [
        pltpu.VMEM((kv_local, widest, rows), jnp.float32),
        pltpu.VMEM((kv_local, widest, rows), jnp.bfloat16),
        pltpu.VMEM((kv_local, 8, rows), jnp.float32),
        pltpu.VMEM((kv_local, 8, rows), jnp.float32),
        pltpu.VMEM((kv_local, HD + ONES, widest), jnp.bfloat16),
        pltpu.VMEM((kv_local, HD + ONES, rows), jnp.float32),
    ]
    sems = pltpu.SemaphoreType.DMA((2, capacity))

    def own_part(payload):
        return pl.pallas_call(
            functools.partial(own_kernel, pool_size),
            in_specs=[smem_spec] * 3 + [vmem_spec] * 3 + [hbm_spec] * 2,
            out_specs=[vmem_spec] * 2,
            scratch_shapes=[
                *buffers,
                *[pltpu.VMEM((block_len, kv_width), jnp.bfloat16)] * 2,
                *work,
                sems,
            ],
            out_shape=[
                jax.ShapeDtypeStruct((kv_width, rows), jnp.float32),
                jax.ShapeDtypeStruct((8, rows), jnp.float32),
            ],
            compiler_params=params,
            cost_estimate=cost(8),
            name="own_part",
        )(*tables, payload, new_keys[0], new_values[0], store_keys, store_values)

    def other_part(partners, held, *request, share=8, moved=(), raw=False):
        if raw:
            out_shape = [
                jax.ShapeDtypeStruct((kv_local, HD + ONES, rows), jnp.float32),
                jax.ShapeDtypeStruct((kv_local, 8, rows), jnp.float32),
            ]
        else:
            out_shape = jax.ShapeDtypeStruct((kv_width + ONES, rows), jnp.bfloat16)
        more_specs = [hbm_spec, vmem_spec, vmem_spec] if moved else []
        return pl.pallas_call(
            functools.partial(other_kernel, pool_size, new_rows, partners, bool(moved), raw),
            in_specs=[smem_spec] * (3 + len(request))
            + [hbm_spec] * len(held)
            + more_specs
            + [hbm_spec] * 2,
            out_specs=[vmem_spec] * 2 if raw else vmem_spec,
            scratch_shapes=[
                *buffers,
                *work,
                pltpu.VMEM((kv_width, rows), jnp.bfloat16),
                pltpu.SemaphoreType.DMA,
                sems,
            ],
            out_shape=out_shape,
            compiler_params=params,
            cost_estimate=cost(share),
            name="other_part",
        )(*request, *tables, *held, *moved, store_keys, store_values)

    def combine(own, log, sources, parts, last=True):
        if last:
            out_shape = jax.ShapeDtypeStruct((new_rows, width), jnp.bfloat16)
        else:
            out_shape = [
                jax.ShapeDtypeStruct((kv_width, rows), jnp.float32),
                jax.ShapeDtypeStruct((8, rows), jnp.float32),
            ]
        return pl.pallas_call(
            functools.partial(combine_kernel, tuple(sources), last),
            in_specs=[vmem_spec] * (2 + len(parts)),
            out_specs=vmem_spec if last else [vmem_spec] * 2,
            scratch_shapes=[pltpu.VMEM((rows, HD), jnp.bfloat16)] if last else [],
            out_shape=out_shape,
            compiler_params=params,
            cost_estimate=cost(0),
            name="combine",
        )(own, log, *parts)

    all_rows = payload_rows(new_rows, kv_width)
    payload, fresh = pl.pallas_call(
        prepare_kernel,
        in_specs=[vmem_spec] * 3,
        out_specs=[vmem_spec] * 2,
        scratch_shapes=[pltpu.VMEM((rows, HD), jnp.bfloat16)],
        out_shape=[
            jax.ShapeDtypeStruct((all_rows, rows), jnp.bfloat16),
            jax.ShapeDtypeStruct((all_rows - kv_width, rows), jnp.bfloat16),
        ],
        compiler_params=params,
        name="prepare",
    )(queries[0], new_keys[0], new_values[0])
    own_out, own_log = own_part(payload)
    if pool_size == 4:
        def send(array, *pairs):
            return lax.ppermute(array, "pool", pairs)

        near = send(payload, (0, 1), (1, 0), (2, 3), (3, 2))
        middle = send(payload, (1, 2), (2, 1))
        blocks = pl.pallas_call(
            functools.partial(gather_kernel, pool_size),
            in_specs=[smem_spec] * 3 + [hbm_spec] * 2,
            out_specs=vmem_spec,
            scratch_shapes=[sems],
            out_shape=jax.ShapeDtypeStruct((2 * capacity, block_len, kv_width), jnp.bfloat16),
            compiler_params=params,
            name="gather_blocks",
        )(*tables, store_keys, store_values)
        blocks = send(blocks, (0, 1), (3, 2))
        near, middle, own_out, own_log = lax.optimization_barrier((near, middle, own_out, own_log))
        crossed = send(near, (1, 2), (2, 1))
        outward = send(middle, (1, 0), (2, 3))
        first = other_part((3, 1), (middle, near))
        across = send(first, (1, 2), (2, 1))
        near, outward, first = lax.optimization_barrier((near, outward, first))
        second = other_part((1, 2), (near, outward), share=0)
        back = send(second, (1, 0), (2, 3))
        apart = send(second, (0, 2), (3, 1))
        first, crossed, second, fresh = lax.optimization_barrier((first, crossed, second, fresh))
        state = other_part((2, None), (crossed,), raw=True)
        inward = send(first, (0, 1), (3, 2))
        far = send(fresh, (0, 3), (3, 0))
        crossed, state = lax.optimization_barrier((crossed, state))
        third = other_part((2, None), (crossed,), moved=(blocks, *state))
        ends = send(third, (1, 3), (2, 0))
        own_out, own_log, third = lax.optimization_barrier((own_out, own_log, third))
        own_out, own_log = combine(
            own_out,
            own_log,
            [(3, None), (1, None), (2, None), (None, 1)],
            [across, inward, apart, back],
            last=False,
        )
        sources = [(None, 2)]
        parts = [ends]
        moved = [
            ((0, 0), payload),
            ((1, 1), near),
            ((3, None), middle),
            ((2, None), crossed),
            ((None, 2), outward),
            ((None, 3), far),
        ]
    else:
        gathered = lax.all_gather(payload, "pool", axis=0, tiled=False)
        packed = lax.map(
            lambda pair: other_part(None, (pair[0],), pair[1].reshape(1)),
            (gathered, jnp.arange(pool_size, dtype=jnp.int32)),
        )
        parts = lax.all_to_all(packed, "pool", split_axis=0, concat_axis=0, tiled=True)
        sources = list(range(pool_size))
        moved = [(source, gathered[source]) for source in range(pool_size)]

    attended = combine(own_out, own_log, sources, parts)
    pushed_keys, pushed_values = pl.pallas_call(
        functools.partial(push_kernel, pool_size, tuple(entry for entry, _ in moved)),
        in_specs=[smem_spec] + [hbm_spec] * len(moved),
        out_specs=[vmem_spec] * 2,
        scratch_shapes=[pltpu.SemaphoreType.DMA((2, CAPP, new_rows // PIECE))],
        out_shape=[jax.ShapeDtypeStruct((CAPP, new_rows, kv_width), jnp.bfloat16)] * 2,
        compiler_params=params,
        name="push",
    )(decode_owner, *[array for _, array in moved])
    return (attended[None], pushed_keys, pushed_values)


def solution(mesh):
    in_specs = (
        P(("groups", "pool"), None, ("tensor", "sub")),
        P(("groups", "pool"), None, ("tensor", "sub")),
        P(("groups", "pool"), None, ("tensor", "sub")),
        P(("groups", "pool"), None, ("tensor", "sub")),
        P(("groups", "pool"), None, ("tensor", "sub")),
        P("groups"),
        P("groups", None),
        P("groups", None),
        P("groups"),
    )
    out_specs = (
        P(("groups", "pool"), None, ("tensor", "sub")),
        P(("groups", "pool"), None, ("tensor", "sub")),
        P(("groups", "pool"), None, ("tensor", "sub")),
    )
    return jax.shard_map(shards, mesh=mesh, in_specs=in_specs, out_specs=out_specs, check_vma=False)
```

```python
import functools
import math

import jax
import jax.numpy as jnp
from jax import lax
from jax.experimental import pallas as pl
from jax.experimental.pallas import tpu as pltpu
from jax.sharding import PartitionSpec as P

HEADS = 64
KVH = 8
HD = 128
MAXBLK = 32
CAPP = 2
GROUP = HEADS // KVH
EMPTY = -1e30
TILE = 256
ONES = 16
PIECE = 32
SCALE = 1.0 / math.sqrt(HD)
EXP2_SCALE = SCALE * math.log2(math.e)
VMEM_LIMIT = 63 * 1024 * 1024 + 512 * 1024


def blocks_at(tables, request, place, pool_size):
    prefix_ref, store_ref, slot_ref = tables
    first = lax.rem(place - store_ref[request, 0] + pool_size, pool_size)
    count = lax.max(lax.div(prefix_ref[request] - first + pool_size - 1, pool_size), 0)
    return count, lambda entry: slot_ref[request, first + entry * pool_size]


def fetch(pool_size, tables, request, stores, buffers, sems, moved=None):
    me = lax.axis_index("pool")
    count, slot_of = blocks_at(tables, request, me if moved is None else me ^ 1, pool_size)

    def copies(entry):
        for i in range(2):
            if moved is None:
                source = stores[i].at[slot_of(entry)]
            else:
                source = moved.at[i * (moved.shape[0] // 2) + entry]
            yield pltpu.make_async_copy(source, buffers[i].at[entry], sems.at[i, entry])

    def start(entry, carry):
        for copy in copies(entry):
            copy.start()
        return carry

    lax.fori_loop(0, count, start, 0)

    def ready(entry):
        for copy in copies(entry):
            copy.wait()

    return count, ready


def gather_kernel(pool_size, prefix_ref, store_ref, slot_ref, store_keys, store_values, out_ref, sems):
    me = lax.axis_index("pool")
    capacity = out_ref.shape[0] // 2

    @pl.when(jnp.logical_not(is_inner(me)))
    def _():
        tables = (prefix_ref, store_ref, slot_ref)
        count, slot_of = blocks_at(tables, me ^ 3, me, pool_size)

        def copies(entry):
            return [
                pltpu.make_async_copy(
                    store.at[slot_of(entry)], out_ref.at[i * capacity + entry], sems.at[i, entry]
                )
                for i, store in enumerate((store_keys, store_values))
            ]

        def start(entry, carry):
            for copy in copies(entry):
                copy.start()
            return carry

        def wait(entry, carry):
            for copy in copies(entry):
                copy.wait()
            return carry

        lax.fori_loop(0, count, start, 0)
        lax.fori_loop(0, count, wait, 0)


def attend(
    key_ref,
    value_ref,
    count,
    ready,
    fresh,
    new_rows,
    columns,
    scores,
    weights,
    peaks,
    factors,
    turned,
    acc,
    initial=None,
    raw=False,
):
    rows = columns.shape[1]
    kv_local = columns.shape[0] // HD

    def visit(keys, values, seen):
        size = keys[0].shape[0]

        def score(kv):
            turned[kv, :HD, :size] = values[kv].T
            block = lax.dot_general(
                keys[kv],
                columns[kv * HD : (kv + 1) * HD, :],
                (((1,), (0,)), ((), ())),
                preferred_element_type=jnp.float32,
            )
            if seen is not None:
                block = jnp.where(seen, block, EMPTY)
            scores[kv, :size, :] = block

        def weigh(kv):
            for i in range(0, rows, TILE):
                part = slice(i, i + TILE)
                before = peaks[kv, :, part]
                block = scores[kv, :size, part]
                peak = jnp.maximum(before, jnp.max(block, axis=0, keepdims=True))
                factors[kv, :, part] = jnp.exp2((before - peak) * EXP2_SCALE)
                peaks[kv, :, part] = peak
                weight = jnp.exp2(block * EXP2_SCALE - peak[0:1] * EXP2_SCALE)
                weights[kv, :size, part] = weight.astype(jnp.bfloat16)

        def mix(kv):
            added = lax.dot_general(
                turned[kv, :, :size],
                weights[kv, :size, :],
                (((1,), (0,)), ((), ())),
                preferred_element_type=jnp.float32,
            )
            acc[kv] = acc[kv] * factors[kv, 0:1, :] + added

        for step in range(kv_local + 2):
            for offset, stage in ((0, score), (2, mix), (1, weigh)):
                if 0 <= step - offset < kv_local:
                    stage(step - offset)

    def lanes_of(array):
        return [array[:, kv * HD : (kv + 1) * HD] for kv in range(kv_local)]

    def blocks_of(ref, first, number):
        return lanes_of(ref[pl.ds(first, number)].reshape(number * ref.shape[1], ref.shape[2]))

    if initial is None:
        peaks[...] = jnp.full(peaks.shape, EMPTY, jnp.float32)
        acc[...] = jnp.zeros(acc.shape, jnp.float32)
    else:
        acc[...] = initial[0][...]
        peaks[...] = initial[1][...]
    turned[:, HD:, :] = jnp.ones((kv_local, ONES, turned.shape[2]), jnp.bfloat16)
    if fresh is not None:
        new_key_ref, new_value_ref = fresh
        row = lax.rem(lax.broadcasted_iota(jnp.int32, (1, rows), 1), new_rows)
        seen = lax.broadcasted_iota(jnp.int32, (new_key_ref.shape[0], rows), 0) <= row
        visit(lanes_of(new_key_ref), lanes_of(new_value_ref), seen)

    def visit_blocks(number):
        def body(index, carry):
            for i in range(number):
                ready(index * number + i)
            visit(
                blocks_of(key_ref, index * number, number),
                blocks_of(value_ref, index * number, number),
                None,
            )
            return carry

        return body

    pairs = count // 2 if key_ref.shape[0] > 1 else 0
    if key_ref.shape[0] > 1:
        lax.fori_loop(0, pairs, visit_blocks(2), 0)
    lax.fori_loop(2 * pairs, count, visit_blocks(1), 0)
    if raw:
        return acc[...], peaks[...]
    outs = []
    logs = []
    for kv in range(kv_local):
        total = acc[kv, HD : HD + 1, :]
        safe = jnp.where(total > 0, total, 1.0)
        logs.append(jnp.where(total > 0, peaks[kv, 0:1] * SCALE + jnp.log(safe), EMPTY))
        outs.append(acc[kv, :HD, :] * (1.0 / safe))
    return outs, logs


def prepare_kernel(query_ref, new_key_ref, new_value_ref, payload_ref, fresh_ref, query_rows):
    new_rows = query_ref.shape[0]
    kv_width = new_key_ref.shape[1]
    for kv in range(kv_width // HD):
        for g in range(GROUP):
            head = kv * GROUP + g
            query_rows[g * new_rows : (g + 1) * new_rows, :] = query_ref[
                :, head * HD : (head + 1) * HD
            ]
        payload_ref[kv * HD : (kv + 1) * HD, :] = query_rows[...].T
    for i, new_ref in enumerate((new_key_ref, new_value_ref)):
        for piece in range(new_rows // PIECE):
            row, lane = piece_place(i, piece, new_rows, kv_width)
            values = new_ref[piece * PIECE : (piece + 1) * PIECE, :]
            payload_ref[row : row + PIECE, lane : lane + kv_width] = values
            fresh_ref[row - kv_width : row - kv_width + PIECE, lane : lane + kv_width] = values


def piece_place(i, piece, new_rows, kv_width):
    index = i * (new_rows // PIECE) + piece
    beside = GROUP * new_rows // kv_width
    return kv_width + index // beside * PIECE, index % beside * kv_width


def payload_rows(new_rows, kv_width):
    return piece_place(1, new_rows // PIECE - 1, new_rows, kv_width)[0] + PIECE


def own_kernel(
    pool_size,
    prefix_ref,
    store_ref,
    slot_ref,
    payload_ref,
    new_key_ref,
    new_value_ref,
    store_keys,
    store_values,
    out_ref,
    log_ref,
    key_buf,
    value_buf,
    new_key_buf,
    new_value_buf,
    *state,
):
    *work, sems = state
    count, ready = fetch(
        pool_size,
        (prefix_ref, store_ref, slot_ref),
        lax.axis_index("pool"),
        (store_keys, store_values),
        (key_buf, value_buf),
        sems,
    )
    new_rows, kv_width = new_key_ref.shape
    for buffer, source in ((new_key_buf, new_key_ref), (new_value_buf, new_value_ref)):
        buffer[:new_rows, :] = source[...]
        buffer[new_rows:, :] = jnp.zeros((buffer.shape[0] - new_rows, kv_width), jnp.bfloat16)
    fresh = (new_key_buf, new_value_buf)
    outs, logs = attend(
        key_buf, value_buf, count, ready, fresh, new_rows, payload_ref.at[:kv_width], *work
    )
    log_ref[...] = jnp.zeros(log_ref.shape, jnp.float32)
    for kv, (out, log) in enumerate(zip(outs, logs)):
        out_ref[kv * HD : (kv + 1) * HD, :] = out
        log_ref[kv : kv + 1, :] = log


def other_kernel(pool_size, new_rows, partners, with_moved, raw, *refs):
    if partners is None:
        request = refs[0][0]
        choice = [None]
        refs = refs[1:]
    else:
        inner = is_inner(lax.axis_index("pool"))
        _, request = source_of(lax.axis_index("pool"), partners)
        choice = [
            hit for hit, mask in zip((inner, jnp.logical_not(inner)), partners) if mask is not None
        ]
    tables, refs = refs[:3], refs[3:]
    payload_refs, refs = refs[: len(choice)], refs[len(choice) :]
    moved = initial = None
    if with_moved:
        moved, *initial = refs[:3]
        refs = refs[3:]
    store_keys, store_values, *refs = refs
    out_refs, (key_buf, value_buf, *state) = refs[: 1 + raw], refs[1 + raw :]
    *work, columns, query_sem, sems = state
    kv_width = columns.shape[0]

    def query_copy(payload_ref):
        return pltpu.make_async_copy(payload_ref.at[:kv_width], columns, query_sem)

    def run():
        for payload_ref, hit in zip(payload_refs, choice):
            if len(choice) == 1:
                query_copy(payload_ref).start()
            else:
                pl.when(hit)(query_copy(payload_ref).start)
        count, ready = fetch(
            pool_size,
            tables,
            request,
            (store_keys, store_values),
            (key_buf, value_buf),
            sems,
            moved,
        )
        query_copy(payload_refs[0]).wait()
        results = attend(
            key_buf, value_buf, count, ready, None, new_rows, columns, *work, initial, raw
        )
        if raw:
            for out_ref, result in zip(out_refs, results):
                out_ref[...] = result
            return
        outs, logs = results
        out_ref = out_refs[0]
        tail = []
        for kv, (out, log) in enumerate(zip(outs, logs)):
            out_ref[kv * HD : (kv + 1) * HD, :] = out.astype(jnp.bfloat16)
            high = log.astype(jnp.bfloat16).astype(jnp.float32)
            middle = (log - high).astype(jnp.bfloat16).astype(jnp.float32)
            tail += [high, middle, log - high - middle]
        tail.append(jnp.zeros((ONES - len(tail), columns.shape[1]), jnp.float32))
        out_ref[kv_width:, :] = jnp.concatenate(tail, axis=0).astype(jnp.bfloat16)

    if len(choice) == 1 and choice[0] is not None:
        pl.when(choice[0])(run)
    else:
        run()


def is_inner(place):
    return (place == 1) | (place == 2)


def source_of(me, entry):
    if isinstance(entry, int):
        return jnp.bool_(True), jnp.int32(entry)
    inner = is_inner(me)
    masks = [0 if mask is None else mask for mask in entry]
    there = jnp.where(inner, entry[0] is not None, entry[1] is not None)
    return there, me ^ jnp.where(inner, masks[0], masks[1])


def push_kernel(pool_size, entries, owner_ref, *refs):
    payload_refs = refs[: len(entries)]
    key_out, value_out, sems = refs[len(entries) :]
    outs = (key_out, value_out)
    kv_width = key_out.shape[2]
    me = lax.axis_index("pool")
    total = jnp.int32(0)
    for other in range(pool_size):
        total += (owner_ref[other] == me).astype(jnp.int32)

    new_rows = key_out.shape[1]

    def copies(payload_ref, place):
        for i in range(2):
            for piece in range(new_rows // PIECE):
                row, lane = piece_place(i, piece, new_rows, kv_width)
                row += payload_ref.shape[0] - payload_rows(new_rows, kv_width)
                yield pltpu.make_async_copy(
                    payload_ref.at[row : row + PIECE, lane : lane + kv_width],
                    outs[i].at[place, piece * PIECE : (piece + 1) * PIECE],
                    sems.at[i, place, piece],
                )

    for entry, payload_ref in zip(entries, payload_refs):
        there, source = source_of(me, entry)
        rank = jnp.int32(0)
        for other in range(pool_size):
            rank += ((owner_ref[other] == me) & (other < source)).astype(jnp.int32)
        hit = there & (owner_ref[source] == me)
        for place in range(CAPP):

            @pl.when(hit & (rank == place))
            def _():
                for copy in copies(payload_ref, place):
                    copy.start()

    for place in range(CAPP):

        @pl.when(total <= place)
        def _():
            for out in outs:
                out[place] = jnp.zeros(out.shape[1:], jnp.bfloat16)

        @pl.when(total > place)
        def _():
            for copy in copies(payload_refs[0], place):
                copy.wait()


def combine_kernel(sources, last, own_ref, log_ref, *refs):
    parts = refs[: len(sources)]
    out_ref = refs[len(sources)]
    kv_width, rows = own_ref.shape
    me = lax.axis_index("pool")
    arrived = []
    tails = []
    for source, part in zip(sources, parts):
        there, request = source_of(me, source)
        arrived.append(there & (request != me))
        tails.append(part[kv_width:, :].astype(jnp.float32))
    if not last:
        refs[len(sources) + 1][...] = log_ref[...]
    for kv in range(kv_width // HD):
        logs = [log_ref[kv : kv + 1, :]]
        for there, tail in zip(arrived, tails):
            log = sum(tail[3 * kv + i : 3 * kv + i + 1] for i in range(3))
            logs.append(jnp.where(there, log, EMPTY))
        peak = functools.reduce(jnp.maximum, logs)
        shares = [jnp.exp(x - peak) for x in logs]
        total = functools.reduce(jnp.add, shares)
        shares = [x * (1.0 / total) for x in shares]
        band = slice(kv * HD, (kv + 1) * HD)
        for i in range(0, rows, TILE):
            part = slice(i, i + TILE)
            mixed = own_ref[band, part] * shares[0][:, part]
            for share, ref in zip(shares[1:], parts):
                mixed = mixed + ref[band, part].astype(jnp.float32) * share[:, part]
            if last:
                refs[len(sources) + 1][part, :] = mixed.astype(jnp.bfloat16).T
            else:
                out_ref[band, part] = mixed
        if last:
            turned = refs[len(sources) + 1]
            new_rows = out_ref.shape[0]
            for g in range(GROUP):
                head = kv * GROUP + g
                out_ref[:, head * HD : (head + 1) * HD] = turned[g * new_rows : (g + 1) * new_rows, :]
        else:
            refs[len(sources) + 1][kv : kv + 1, :] = peak + jnp.log(total)


def final_kernel(own_ref, log_ref, *refs):
    part_refs, (out_ref, buffer, turned, sems) = refs[:4], refs[4:]
    inner = is_inner(lax.axis_index("pool"))

    def copies(first):
        return [
            pltpu.make_async_copy(part_refs[first + i], buffer.at[i], sems.at[i]) for i in range(2)
        ]

    for hit, first in ((inner, 0), (jnp.logical_not(inner), 2)):

        @pl.when(hit)
        def _():
            for copy in copies(first):
                copy.start()

    for copy in copies(0):
        copy.wait()
    combine_kernel(
        [(1, 1), (2, 2)], True, own_ref, log_ref, buffer.at[0], buffer.at[1], out_ref, turned
    )


def shards(
    queries,
    new_keys,
    new_values,
    store_keys,
    store_values,
    prefix_blocks,
    hit_store,
    hit_slot,
    decode_owner,
):
    pool_size = lax.axis_size("pool")
    capacity = (MAXBLK + pool_size - 1) // pool_size
    new_rows = queries.shape[1]
    width = queries.shape[2]
    kv_width = new_keys.shape[2]
    block_len = store_keys.shape[1]
    rows = GROUP * new_rows
    tables = (prefix_blocks, hit_store, hit_slot)
    smem_spec = pl.BlockSpec(memory_space=pltpu.SMEM)
    hbm_spec = pl.BlockSpec(memory_space=pltpu.HBM)
    vmem_spec = pl.BlockSpec(memory_space=pltpu.VMEM)
    params = pltpu.CompilerParams(vmem_limit_bytes=VMEM_LIMIT)

    def cost(share):
        return pl.CostEstimate(
            flops=share * rows * block_len * kv_width * capacity,
            bytes_accessed=rows,
            transcendentals=0,
        )

    buffers = [pltpu.VMEM((capacity, block_len, kv_width), jnp.bfloat16)] * 2
    kv_local = kv_width // HD
    widest = block_len * min(2, capacity)
    work = [
        pltpu.VMEM((kv_local, widest, rows), jnp.float32),
        pltpu.VMEM((kv_local, widest, rows), jnp.bfloat16),
        pltpu.VMEM((kv_local, 8, rows), jnp.float32),
        pltpu.VMEM((kv_local, 8, rows), jnp.float32),
        pltpu.VMEM((kv_local, HD + ONES, widest), jnp.bfloat16),
        pltpu.VMEM((kv_local, HD + ONES, rows), jnp.float32),
    ]
    sems = pltpu.SemaphoreType.DMA((2, capacity))

    def own_part(payload):
        return pl.pallas_call(
            functools.partial(own_kernel, pool_size),
            in_specs=[smem_spec] * 3 + [vmem_spec] * 3 + [hbm_spec] * 2,
            out_specs=[vmem_spec] * 2,
            scratch_shapes=[
                *buffers,
                *[pltpu.VMEM((block_len, kv_width), jnp.bfloat16)] * 2,
                *work,
                sems,
            ],
            out_shape=[
                jax.ShapeDtypeStruct((kv_width, rows), jnp.float32),
                jax.ShapeDtypeStruct((8, rows), jnp.float32),
            ],
            compiler_params=params,
            cost_estimate=cost(8),
            name="own_part",
        )(*tables, payload, new_keys[0], new_values[0], store_keys, store_values)

    def other_part(partners, held, *request, share=8, moved=(), raw=False):
        if raw:
            out_shape = [
                jax.ShapeDtypeStruct((kv_local, HD + ONES, rows), jnp.float32),
                jax.ShapeDtypeStruct((kv_local, 8, rows), jnp.float32),
            ]
        else:
            out_shape = jax.ShapeDtypeStruct((kv_width + ONES, rows), jnp.bfloat16)
        more_specs = [hbm_spec, vmem_spec, vmem_spec] if moved else []
        return pl.pallas_call(
            functools.partial(other_kernel, pool_size, new_rows, partners, bool(moved), raw),
            in_specs=[smem_spec] * (3 + len(request))
            + [hbm_spec] * len(held)
            + more_specs
            + [hbm_spec] * 2,
            out_specs=[vmem_spec] * 2 if raw else vmem_spec,
            scratch_shapes=[
                *buffers,
                *work,
                pltpu.VMEM((kv_width, rows), jnp.bfloat16),
                pltpu.SemaphoreType.DMA,
                sems,
            ],
            out_shape=out_shape,
            compiler_params=params,
            cost_estimate=cost(share),
            name="other_part",
        )(*request, *tables, *held, *moved, store_keys, store_values)

    def combine(own, log, sources, parts, last=True):
        if last:
            out_shape = jax.ShapeDtypeStruct((new_rows, width), jnp.bfloat16)
        else:
            out_shape = [
                jax.ShapeDtypeStruct((kv_width, rows), jnp.float32),
                jax.ShapeDtypeStruct((8, rows), jnp.float32),
            ]
        return pl.pallas_call(
            functools.partial(combine_kernel, tuple(sources), last),
            in_specs=[vmem_spec] * (2 + len(parts)),
            out_specs=vmem_spec if last else [vmem_spec] * 2,
            scratch_shapes=[pltpu.VMEM((rows, HD), jnp.bfloat16)] if last else [],
            out_shape=out_shape,
            compiler_params=params,
            cost_estimate=cost(0),
            name="combine",
        )(own, log, *parts)

    all_rows = payload_rows(new_rows, kv_width)
    def final(own, log, parts):
        return pl.pallas_call(
            final_kernel,
            in_specs=[vmem_spec] * 2 + [hbm_spec] * 4,
            out_specs=vmem_spec,
            scratch_shapes=[
                pltpu.VMEM((2, kv_width + ONES, rows), jnp.bfloat16),
                pltpu.VMEM((rows, HD), jnp.bfloat16),
                pltpu.SemaphoreType.DMA((2,)),
            ],
            out_shape=jax.ShapeDtypeStruct((new_rows, width), jnp.bfloat16),
            compiler_params=params,
            name="final",
        )(own, log, *parts)

    payload, fresh = pl.pallas_call(
        prepare_kernel,
        in_specs=[vmem_spec] * 3,
        out_specs=[vmem_spec] * 2,
        scratch_shapes=[pltpu.VMEM((rows, HD), jnp.bfloat16)],
        out_shape=[
            jax.ShapeDtypeStruct((all_rows, rows), jnp.bfloat16),
            jax.ShapeDtypeStruct((all_rows - kv_width, rows), jnp.bfloat16),
        ],
        compiler_params=params,
        name="prepare",
    )(queries[0], new_keys[0], new_values[0])
    own_out, own_log = own_part(payload)
    if pool_size == 4:
        def send(array, *pairs):
            return lax.ppermute(array, "pool", pairs)

        near = send(payload, (0, 1), (1, 0), (2, 3), (3, 2))
        middle = send(payload, (1, 2), (2, 1))
        blocks = pl.pallas_call(
            functools.partial(gather_kernel, pool_size),
            in_specs=[smem_spec] * 3 + [hbm_spec] * 2,
            out_specs=vmem_spec,
            scratch_shapes=[sems],
            out_shape=jax.ShapeDtypeStruct((2 * capacity, block_len, kv_width), jnp.bfloat16),
            compiler_params=params,
            name="gather_blocks",
        )(*tables, store_keys, store_values)
        blocks = send(blocks, (0, 1), (3, 2))
        far = send(fresh, (0, 3), (3, 0))
        near, middle, far, own_out, own_log = lax.optimization_barrier(
            (near, middle, far, own_out, own_log)
        )
        crossed = send(near, (1, 2), (2, 1))
        outward = send(middle, (1, 0), (2, 3))
        first = other_part((3, 1), (middle, near))
        across = send(first, (1, 2), (2, 1))
        near, outward, first = lax.optimization_barrier((near, outward, first))
        second = other_part((1, 2), (near, outward), share=0)
        back = send(second, (1, 0), (2, 3))
        apart = send(second, (0, 2), (3, 1))
        first, crossed, second = lax.optimization_barrier((first, crossed, second))
        state = other_part((2, None), (crossed,), raw=True)
        inward = send(first, (0, 1), (3, 2))
        crossed, state = lax.optimization_barrier((crossed, state))
        third = other_part((2, None), (crossed,), moved=(blocks, *state))
        ends = send(third, (1, 3), (2, 0))
        own_out, own_log, third = lax.optimization_barrier((own_out, own_log, third))
        own_out, own_log = combine(own_out, own_log, [(3, None)], [across], last=False)
        attended = final(own_out, own_log, (inward, apart, back, ends))
        moved = [
            ((0, 0), payload),
            ((1, 1), near),
            ((3, None), middle),
            ((2, None), crossed),
            ((None, 2), outward),
            ((None, 3), far),
        ]
    else:
        gathered = lax.all_gather(payload, "pool", axis=0, tiled=False)
        packed = lax.map(
            lambda pair: other_part(None, (pair[0],), pair[1].reshape(1)),
            (gathered, jnp.arange(pool_size, dtype=jnp.int32)),
        )
        parts = lax.all_to_all(packed, "pool", split_axis=0, concat_axis=0, tiled=True)
        attended = combine(own_out, own_log, list(range(pool_size)), parts)
        moved = [(source, gathered[source]) for source in range(pool_size)]

    pushed_keys, pushed_values = pl.pallas_call(
        functools.partial(push_kernel, pool_size, tuple(entry for entry, _ in moved)),
        in_specs=[smem_spec] + [hbm_spec] * len(moved),
        out_specs=[vmem_spec] * 2,
        scratch_shapes=[pltpu.SemaphoreType.DMA((2, CAPP, new_rows // PIECE))],
        out_shape=[jax.ShapeDtypeStruct((CAPP, new_rows, kv_width), jnp.bfloat16)] * 2,
        compiler_params=params,
        name="push",
    )(decode_owner, *[array for _, array in moved])
    return (attended[None], pushed_keys, pushed_values)


def solution(mesh):
    in_specs = (
        P(("groups", "pool"), None, ("tensor", "sub")),
        P(("groups", "pool"), None, ("tensor", "sub")),
        P(("groups", "pool"), None, ("tensor", "sub")),
        P(("groups", "pool"), None, ("tensor", "sub")),
        P(("groups", "pool"), None, ("tensor", "sub")),
        P("groups"),
        P("groups", None),
        P("groups", None),
        P("groups"),
    )
    out_specs = (
        P(("groups", "pool"), None, ("tensor", "sub")),
        P(("groups", "pool"), None, ("tensor", "sub")),
        P(("groups", "pool"), None, ("tensor", "sub")),
    )
    return jax.shard_map(shards, mesh=mesh, in_specs=in_specs, out_specs=out_specs, check_vma=False)
```

```python
import functools
import math

import jax
import jax.numpy as jnp
from jax import lax
from jax.experimental import pallas as pl
from jax.experimental.pallas import tpu as pltpu
from jax.sharding import PartitionSpec as P

HEADS = 64
KVH = 8
HD = 128
MAXBLK = 32
CAPP = 2
GROUP = HEADS // KVH
EMPTY = -1e30
TILE = 256
ONES = 16
PIECE = 32
SCALE = 1.0 / math.sqrt(HD)
EXP2_SCALE = SCALE * math.log2(math.e)
VMEM_LIMIT = 63 * 1024 * 1024 + 512 * 1024


def blocks_at(tables, request, place, pool_size):
    prefix_ref, store_ref, slot_ref = tables
    first = lax.rem(place - store_ref[request, 0] + pool_size, pool_size)
    count = lax.max(lax.div(prefix_ref[request] - first + pool_size - 1, pool_size), 0)
    return count, lambda entry: slot_ref[request, first + entry * pool_size]


def fetch(pool_size, tables, request, stores, buffers, sems, moved=None):
    me = lax.axis_index("pool")
    count, slot_of = blocks_at(tables, request, me if moved is None else me ^ 1, pool_size)

    def copies(entry):
        for i in range(2):
            if moved is None:
                source = stores[i].at[slot_of(entry)]
            else:
                source = moved.at[i * (moved.shape[0] // 2) + entry]
            yield pltpu.make_async_copy(source, buffers[i].at[entry], sems.at[i, entry])

    def start(entry, carry):
        for copy in copies(entry):
            copy.start()
        return carry

    lax.fori_loop(0, count, start, 0)

    def ready(entry):
        for copy in copies(entry):
            copy.wait()

    return count, ready


def gather_kernel(pool_size, prefix_ref, store_ref, slot_ref, store_keys, store_values, out_ref, sems):
    me = lax.axis_index("pool")
    capacity = out_ref.shape[0] // 2

    @pl.when(jnp.logical_not(is_inner(me)))
    def _():
        tables = (prefix_ref, store_ref, slot_ref)
        count, slot_of = blocks_at(tables, me ^ 3, me, pool_size)

        def copies(entry):
            return [
                pltpu.make_async_copy(
                    store.at[slot_of(entry)], out_ref.at[i * capacity + entry], sems.at[i, entry]
                )
                for i, store in enumerate((store_keys, store_values))
            ]

        def start(entry, carry):
            for copy in copies(entry):
                copy.start()
            return carry

        def wait(entry, carry):
            for copy in copies(entry):
                copy.wait()
            return carry

        lax.fori_loop(0, count, start, 0)
        lax.fori_loop(0, count, wait, 0)


def attend(
    key_ref,
    value_ref,
    count,
    ready,
    fresh,
    new_rows,
    columns,
    scores,
    weights,
    peaks,
    factors,
    turned,
    acc,
    initial=None,
    raw=False,
):
    rows = columns.shape[1]
    kv_local = columns.shape[0] // HD

    def visit(keys, values, seen):
        size = keys[0].shape[0]

        def score(kv):
            turned[kv, :HD, :size] = values[kv].T
            block = lax.dot_general(
                keys[kv],
                columns[kv * HD : (kv + 1) * HD, :],
                (((1,), (0,)), ((), ())),
                preferred_element_type=jnp.float32,
            )
            if seen is not None:
                block = jnp.where(seen, block, EMPTY)
            scores[kv, :size, :] = block

        def weigh(kv):
            for i in range(0, rows, TILE):
                part = slice(i, i + TILE)
                before = peaks[kv, :, part]
                block = scores[kv, :size, part]
                peak = jnp.maximum(before, jnp.max(block, axis=0, keepdims=True))
                factors[kv, :, part] = jnp.exp2((before - peak) * EXP2_SCALE)
                peaks[kv, :, part] = peak
                weight = jnp.exp2(block * EXP2_SCALE - peak[0:1] * EXP2_SCALE)
                weights[kv, :size, part] = weight.astype(jnp.bfloat16)

        def mix(kv):
            added = lax.dot_general(
                turned[kv, :, :size],
                weights[kv, :size, :],
                (((1,), (0,)), ((), ())),
                preferred_element_type=jnp.float32,
            )
            acc[kv] = acc[kv] * factors[kv, 0:1, :] + added

        for step in range(kv_local + 2):
            for offset, stage in ((0, score), (2, mix), (1, weigh)):
                if 0 <= step - offset < kv_local:
                    stage(step - offset)

    def lanes_of(array):
        return [array[:, kv * HD : (kv + 1) * HD] for kv in range(kv_local)]

    def blocks_of(ref, first, number):
        return lanes_of(ref[pl.ds(first, number)].reshape(number * ref.shape[1], ref.shape[2]))

    if initial is None:
        peaks[...] = jnp.full(peaks.shape, EMPTY, jnp.float32)
        acc[...] = jnp.zeros(acc.shape, jnp.float32)
    else:
        acc[...] = initial[0][...]
        peaks[...] = initial[1][...]
    turned[:, HD:, :] = jnp.ones((kv_local, ONES, turned.shape[2]), jnp.bfloat16)
    if fresh is not None:
        new_key_ref, new_value_ref = fresh
        row = lax.rem(lax.broadcasted_iota(jnp.int32, (1, rows), 1), new_rows)
        seen = lax.broadcasted_iota(jnp.int32, (new_key_ref.shape[0], rows), 0) <= row
        visit(lanes_of(new_key_ref), lanes_of(new_value_ref), seen)

    def visit_blocks(number):
        def body(index, carry):
            for i in range(number):
                ready(index * number + i)
            visit(
                blocks_of(key_ref, index * number, number),
                blocks_of(value_ref, index * number, number),
                None,
            )
            return carry

        return body

    pairs = count // 2 if key_ref.shape[0] > 1 else 0
    if key_ref.shape[0] > 1:
        lax.fori_loop(0, pairs, visit_blocks(2), 0)
    lax.fori_loop(2 * pairs, count, visit_blocks(1), 0)
    if raw:
        return acc[...], peaks[...]
    outs = []
    logs = []
    for kv in range(kv_local):
        total = acc[kv, HD : HD + 1, :]
        safe = jnp.where(total > 0, total, 1.0)
        logs.append(jnp.where(total > 0, peaks[kv, 0:1] * SCALE + jnp.log(safe), EMPTY))
        outs.append(acc[kv, :HD, :] * (1.0 / safe))
    return outs, logs


def prepare_kernel(query_ref, new_key_ref, new_value_ref, payload_ref, query_rows):
    new_rows = query_ref.shape[0]
    kv_width = new_key_ref.shape[1]
    for kv in range(kv_width // HD):
        for g in range(GROUP):
            head = kv * GROUP + g
            query_rows[g * new_rows : (g + 1) * new_rows, :] = query_ref[
                :, head * HD : (head + 1) * HD
            ]
        payload_ref[kv * HD : (kv + 1) * HD, :] = query_rows[...].T
    for i, new_ref in enumerate((new_key_ref, new_value_ref)):
        for piece in range(new_rows // PIECE):
            row, lane = piece_place(i, piece, new_rows, kv_width)
            payload_ref[row : row + PIECE, lane : lane + kv_width] = new_ref[
                piece * PIECE : (piece + 1) * PIECE, :
            ]


def piece_place(i, piece, new_rows, kv_width):
    index = i * (new_rows // PIECE) + piece
    beside = GROUP * new_rows // kv_width
    return kv_width + index // beside * PIECE, index % beside * kv_width


def payload_rows(new_rows, kv_width):
    return piece_place(1, new_rows // PIECE - 1, new_rows, kv_width)[0] + PIECE


def own_kernel(
    pool_size,
    prefix_ref,
    store_ref,
    slot_ref,
    payload_ref,
    new_key_ref,
    new_value_ref,
    store_keys,
    store_values,
    out_ref,
    log_ref,
    key_buf,
    value_buf,
    new_key_buf,
    new_value_buf,
    *state,
):
    *work, sems = state
    count, ready = fetch(
        pool_size,
        (prefix_ref, store_ref, slot_ref),
        lax.axis_index("pool"),
        (store_keys, store_values),
        (key_buf, value_buf),
        sems,
    )
    new_rows, kv_width = new_key_ref.shape
    for buffer, source in ((new_key_buf, new_key_ref), (new_value_buf, new_value_ref)):
        buffer[:new_rows, :] = source[...]
        buffer[new_rows:, :] = jnp.zeros((buffer.shape[0] - new_rows, kv_width), jnp.bfloat16)
    fresh = (new_key_buf, new_value_buf)
    outs, logs = attend(
        key_buf, value_buf, count, ready, fresh, new_rows, payload_ref.at[:kv_width], *work
    )
    log_ref[...] = jnp.zeros(log_ref.shape, jnp.float32)
    for kv, (out, log) in enumerate(zip(outs, logs)):
        out_ref[kv * HD : (kv + 1) * HD, :] = out
        log_ref[kv : kv + 1, :] = log


def other_kernel(pool_size, new_rows, partners, with_moved, raw, *refs):
    if partners is None:
        request = refs[0][0]
        choice = [None]
        refs = refs[1:]
    else:
        inner = is_inner(lax.axis_index("pool"))
        _, request = source_of(lax.axis_index("pool"), partners)
        choice = [
            hit for hit, mask in zip((inner, jnp.logical_not(inner)), partners) if mask is not None
        ]
    tables, refs = refs[:3], refs[3:]
    payload_refs, refs = refs[: len(choice)], refs[len(choice) :]
    moved = initial = None
    if with_moved:
        moved, *initial = refs[:3]
        refs = refs[3:]
    store_keys, store_values, *refs = refs
    out_refs, (key_buf, value_buf, *state) = refs[: 1 + raw], refs[1 + raw :]
    *work, columns, query_sem, sems = state
    kv_width = columns.shape[0]

    def query_copy(payload_ref):
        return pltpu.make_async_copy(payload_ref.at[:kv_width], columns, query_sem)

    def run():
        for payload_ref, hit in zip(payload_refs, choice):
            if len(choice) == 1:
                query_copy(payload_ref).start()
            else:
                pl.when(hit)(query_copy(payload_ref).start)
        count, ready = fetch(
            pool_size,
            tables,
            request,
            (store_keys, store_values),
            (key_buf, value_buf),
            sems,
            moved,
        )
        query_copy(payload_refs[0]).wait()
        results = attend(
            key_buf, value_buf, count, ready, None, new_rows, columns, *work, initial, raw
        )
        if raw:
            for out_ref, result in zip(out_refs, results):
                out_ref[...] = result
            return
        outs, logs = results
        out_ref = out_refs[0]
        tail = []
        for kv, (out, log) in enumerate(zip(outs, logs)):
            out_ref[kv * HD : (kv + 1) * HD, :] = out.astype(jnp.bfloat16)
            high = log.astype(jnp.bfloat16).astype(jnp.float32)
            middle = (log - high).astype(jnp.bfloat16).astype(jnp.float32)
            tail += [high, middle, log - high - middle]
        tail.append(jnp.zeros((ONES - len(tail), columns.shape[1]), jnp.float32))
        out_ref[kv_width:, :] = jnp.concatenate(tail, axis=0).astype(jnp.bfloat16)

    if len(choice) == 1 and choice[0] is not None:
        pl.when(choice[0])(run)
    else:
        run()


def is_inner(place):
    return (place == 1) | (place == 2)


def source_of(me, entry):
    if isinstance(entry, int):
        return jnp.bool_(True), jnp.int32(entry)
    inner = is_inner(me)
    masks = [0 if mask is None else mask for mask in entry]
    there = jnp.where(inner, entry[0] is not None, entry[1] is not None)
    return there, me ^ jnp.where(inner, masks[0], masks[1])


def push_kernel(pool_size, entries, owner_ref, *refs):
    payload_refs = refs[: len(entries)]
    key_out, value_out, sems = refs[len(entries) :]
    outs = (key_out, value_out)
    kv_width = key_out.shape[2]
    me = lax.axis_index("pool")
    total = jnp.int32(0)
    for other in range(pool_size):
        total += (owner_ref[other] == me).astype(jnp.int32)

    new_rows = key_out.shape[1]

    def copies(payload_ref, place):
        for i in range(2):
            for piece in range(new_rows // PIECE):
                row, lane = piece_place(i, piece, new_rows, kv_width)
                row += payload_ref.shape[0] - payload_rows(new_rows, kv_width)
                yield pltpu.make_async_copy(
                    payload_ref.at[row : row + PIECE, lane : lane + kv_width],
                    outs[i].at[place, piece * PIECE : (piece + 1) * PIECE],
                    sems.at[i, place, piece],
                )

    for entry, payload_ref in zip(entries, payload_refs):
        there, source = source_of(me, entry)
        rank = jnp.int32(0)
        for other in range(pool_size):
            rank += ((owner_ref[other] == me) & (other < source)).astype(jnp.int32)
        hit = there & (owner_ref[source] == me)
        for place in range(CAPP):

            @pl.when(hit & (rank == place))
            def _():
                for copy in copies(payload_ref, place):
                    copy.start()

    for place in range(CAPP):

        @pl.when(total <= place)
        def _():
            for out in outs:
                out[place] = jnp.zeros(out.shape[1:], jnp.bfloat16)

        @pl.when(total > place)
        def _():
            for copy in copies(payload_refs[0], place):
                copy.wait()


def combine_kernel(sources, last, own_ref, log_ref, *refs):
    parts = refs[: len(sources)]
    out_ref = refs[len(sources)]
    kv_width, rows = own_ref.shape
    me = lax.axis_index("pool")
    arrived = []
    tails = []
    for source, part in zip(sources, parts):
        there, request = source_of(me, source)
        arrived.append(there & (request != me))
        tails.append(part[kv_width:, :].astype(jnp.float32))
    if not last:
        refs[len(sources) + 1][...] = log_ref[...]
    for kv in range(kv_width // HD):
        logs = [log_ref[kv : kv + 1, :]]
        for there, tail in zip(arrived, tails):
            log = sum(tail[3 * kv + i : 3 * kv + i + 1] for i in range(3))
            logs.append(jnp.where(there, log, EMPTY))
        peak = functools.reduce(jnp.maximum, logs)
        shares = [jnp.exp(x - peak) for x in logs]
        total = functools.reduce(jnp.add, shares)
        shares = [x * (1.0 / total) for x in shares]
        band = slice(kv * HD, (kv + 1) * HD)
        for i in range(0, rows, TILE):
            part = slice(i, i + TILE)
            mixed = own_ref[band, part] * shares[0][:, part]
            for share, ref in zip(shares[1:], parts):
                mixed = mixed + ref[band, part].astype(jnp.float32) * share[:, part]
            if last:
                refs[len(sources) + 1][part, :] = mixed.astype(jnp.bfloat16).T
            else:
                out_ref[band, part] = mixed
        if last:
            turned = refs[len(sources) + 1]
            new_rows = out_ref.shape[0]
            for g in range(GROUP):
                head = kv * GROUP + g
                out_ref[:, head * HD : (head + 1) * HD] = turned[g * new_rows : (g + 1) * new_rows, :]
        else:
            refs[len(sources) + 1][kv : kv + 1, :] = peak + jnp.log(total)


def final_kernel(own_ref, log_ref, *refs):
    part_refs, (out_ref, buffer, turned, sems) = refs[:4], refs[4:]
    inner = is_inner(lax.axis_index("pool"))

    def copies(first):
        return [
            pltpu.make_async_copy(part_refs[first + i], buffer.at[i], sems.at[i]) for i in range(2)
        ]

    for hit, first in ((inner, 0), (jnp.logical_not(inner), 2)):

        @pl.when(hit)
        def _():
            for copy in copies(first):
                copy.start()

    for copy in copies(0):
        copy.wait()
    combine_kernel(
        [(1, 1), (2, 2)], True, own_ref, log_ref, buffer.at[0], buffer.at[1], out_ref, turned
    )


def shards(
    queries,
    new_keys,
    new_values,
    store_keys,
    store_values,
    prefix_blocks,
    hit_store,
    hit_slot,
    decode_owner,
):
    pool_size = lax.axis_size("pool")
    capacity = (MAXBLK + pool_size - 1) // pool_size
    new_rows = queries.shape[1]
    width = queries.shape[2]
    kv_width = new_keys.shape[2]
    block_len = store_keys.shape[1]
    rows = GROUP * new_rows
    tables = (prefix_blocks, hit_store, hit_slot)
    smem_spec = pl.BlockSpec(memory_space=pltpu.SMEM)
    hbm_spec = pl.BlockSpec(memory_space=pltpu.HBM)
    vmem_spec = pl.BlockSpec(memory_space=pltpu.VMEM)
    params = pltpu.CompilerParams(vmem_limit_bytes=VMEM_LIMIT)

    def cost(share):
        return pl.CostEstimate(
            flops=share * rows * block_len * kv_width * capacity,
            bytes_accessed=rows,
            transcendentals=0,
        )

    buffers = [pltpu.VMEM((capacity, block_len, kv_width), jnp.bfloat16)] * 2
    kv_local = kv_width // HD
    widest = block_len * min(2, capacity)
    work = [
        pltpu.VMEM((kv_local, widest, rows), jnp.float32),
        pltpu.VMEM((kv_local, widest, rows), jnp.bfloat16),
        pltpu.VMEM((kv_local, 8, rows), jnp.float32),
        pltpu.VMEM((kv_local, 8, rows), jnp.float32),
        pltpu.VMEM((kv_local, HD + ONES, widest), jnp.bfloat16),
        pltpu.VMEM((kv_local, HD + ONES, rows), jnp.float32),
    ]
    sems = pltpu.SemaphoreType.DMA((2, capacity))

    def own_part(payload):
        return pl.pallas_call(
            functools.partial(own_kernel, pool_size),
            in_specs=[smem_spec] * 3 + [vmem_spec] * 3 + [hbm_spec] * 2,
            out_specs=[vmem_spec] * 2,
            scratch_shapes=[
                *buffers,
                *[pltpu.VMEM((block_len, kv_width), jnp.bfloat16)] * 2,
                *work,
                sems,
            ],
            out_shape=[
                jax.ShapeDtypeStruct((kv_width, rows), jnp.float32),
                jax.ShapeDtypeStruct((8, rows), jnp.float32),
            ],
            compiler_params=params,
            cost_estimate=cost(8),
            name="own_part",
        )(*tables, payload, new_keys[0], new_values[0], store_keys, store_values)

    def other_part(partners, held, *request, share=8, moved=(), raw=False):
        if raw:
            out_shape = [
                jax.ShapeDtypeStruct((kv_local, HD + ONES, rows), jnp.float32),
                jax.ShapeDtypeStruct((kv_local, 8, rows), jnp.float32),
            ]
        else:
            out_shape = jax.ShapeDtypeStruct((kv_width + ONES, rows), jnp.bfloat16)
        more_specs = [hbm_spec, vmem_spec, vmem_spec] if moved else []
        return pl.pallas_call(
            functools.partial(other_kernel, pool_size, new_rows, partners, bool(moved), raw),
            in_specs=[smem_spec] * (3 + len(request))
            + [hbm_spec] * len(held)
            + more_specs
            + [hbm_spec] * 2,
            out_specs=[vmem_spec] * 2 if raw else vmem_spec,
            scratch_shapes=[
                *buffers,
                *work,
                pltpu.VMEM((kv_width, rows), jnp.bfloat16),
                pltpu.SemaphoreType.DMA,
                sems,
            ],
            out_shape=out_shape,
            compiler_params=params,
            cost_estimate=cost(share),
            name="other_part",
        )(*request, *tables, *held, *moved, store_keys, store_values)

    def combine(own, log, sources, parts, last=True):
        if last:
            out_shape = jax.ShapeDtypeStruct((new_rows, width), jnp.bfloat16)
        else:
            out_shape = [
                jax.ShapeDtypeStruct((kv_width, rows), jnp.float32),
                jax.ShapeDtypeStruct((8, rows), jnp.float32),
            ]
        return pl.pallas_call(
            functools.partial(combine_kernel, tuple(sources), last),
            in_specs=[vmem_spec] * (2 + len(parts)),
            out_specs=vmem_spec if last else [vmem_spec] * 2,
            scratch_shapes=[pltpu.VMEM((rows, HD), jnp.bfloat16)] if last else [],
            out_shape=out_shape,
            compiler_params=params,
            cost_estimate=cost(0),
            name="combine",
        )(own, log, *parts)

    def final(own, log, parts):
        return pl.pallas_call(
            final_kernel,
            in_specs=[vmem_spec] * 2 + [hbm_spec] * 4,
            out_specs=vmem_spec,
            scratch_shapes=[
                pltpu.VMEM((2, kv_width + ONES, rows), jnp.bfloat16),
                pltpu.VMEM((rows, HD), jnp.bfloat16),
                pltpu.SemaphoreType.DMA((2,)),
            ],
            out_shape=jax.ShapeDtypeStruct((new_rows, width), jnp.bfloat16),
            compiler_params=params,
            name="final",
        )(own, log, *parts)

    payload = pl.pallas_call(
        prepare_kernel,
        in_specs=[vmem_spec] * 3,
        out_specs=vmem_spec,
        scratch_shapes=[pltpu.VMEM((rows, HD), jnp.bfloat16)],
        out_shape=jax.ShapeDtypeStruct((payload_rows(new_rows, kv_width), rows), jnp.bfloat16),
        compiler_params=params,
        name="prepare",
    )(queries[0], new_keys[0], new_values[0])
    own_out, own_log = own_part(payload)
    if pool_size == 4:
        def send(array, *pairs):
            return lax.ppermute(array, "pool", pairs)

        near = send(payload, (0, 1), (1, 0), (2, 3), (3, 2))
        middle = send(payload, (1, 2), (2, 1))
        blocks = pl.pallas_call(
            functools.partial(gather_kernel, pool_size),
            in_specs=[smem_spec] * 3 + [hbm_spec] * 2,
            out_specs=vmem_spec,
            scratch_shapes=[sems],
            out_shape=jax.ShapeDtypeStruct((2 * capacity, block_len, kv_width), jnp.bfloat16),
            compiler_params=params,
            name="gather_blocks",
        )(*tables, store_keys, store_values)
        blocks = send(blocks, (0, 1), (3, 2))
        near, middle, own_out, own_log = lax.optimization_barrier((near, middle, own_out, own_log))
        crossed = send(near, (1, 2), (2, 1))
        outward = send(middle, (1, 0), (2, 3))
        first = other_part((3, 1), (middle, near))
        across = send(first, (1, 2), (2, 1))
        near, outward, first = lax.optimization_barrier((near, outward, first))
        second = other_part((1, 2), (near, outward), share=0)
        back = send(second, (1, 0), (2, 3))
        apart = send(second, (0, 2), (3, 1))
        first, crossed, second = lax.optimization_barrier((first, crossed, second))
        state = other_part((2, None), (crossed,), raw=True)
        inward = send(first, (0, 1), (3, 2))
        crossed, state = lax.optimization_barrier((crossed, state))
        third = other_part((2, None), (crossed,), moved=(blocks, *state))
        ends = send(third, (1, 3), (2, 0))
        own_out, own_log, third, crossed = lax.optimization_barrier(
            (own_out, own_log, third, crossed)
        )
        far = send(crossed[kv_width:], (1, 0), (2, 3))
        own_out, own_log = combine(own_out, own_log, [(3, None)], [across], last=False)
        attended = final(own_out, own_log, (inward, apart, back, ends))
        moved = [
            ((0, 0), payload),
            ((1, 1), near),
            ((3, None), middle),
            ((2, None), crossed),
            ((None, 2), outward),
            ((None, 3), far),
        ]
    else:
        gathered = lax.all_gather(payload, "pool", axis=0, tiled=False)
        packed = lax.map(
            lambda pair: other_part(None, (pair[0],), pair[1].reshape(1)),
            (gathered, jnp.arange(pool_size, dtype=jnp.int32)),
        )
        parts = lax.all_to_all(packed, "pool", split_axis=0, concat_axis=0, tiled=True)
        attended = combine(own_out, own_log, list(range(pool_size)), parts)
        moved = [(source, gathered[source]) for source in range(pool_size)]

    pushed_keys, pushed_values = pl.pallas_call(
        functools.partial(push_kernel, pool_size, tuple(entry for entry, _ in moved)),
        in_specs=[smem_spec] + [hbm_spec] * len(moved),
        out_specs=[vmem_spec] * 2,
        scratch_shapes=[pltpu.SemaphoreType.DMA((2, CAPP, new_rows // PIECE))],
        out_shape=[jax.ShapeDtypeStruct((CAPP, new_rows, kv_width), jnp.bfloat16)] * 2,
        compiler_params=params,
        name="push",
    )(decode_owner, *[array for _, array in moved])
    return (attended[None], pushed_keys, pushed_values)


def solution(mesh):
    in_specs = (
        P(("groups", "pool"), None, ("tensor", "sub")),
        P(("groups", "pool"), None, ("tensor", "sub")),
        P(("groups", "pool"), None, ("tensor", "sub")),
        P(("groups", "pool"), None, ("tensor", "sub")),
        P(("groups", "pool"), None, ("tensor", "sub")),
        P("groups"),
        P("groups", None),
        P("groups", None),
        P("groups"),
    )
    out_specs = (
        P(("groups", "pool"), None, ("tensor", "sub")),
        P(("groups", "pool"), None, ("tensor", "sub")),
        P(("groups", "pool"), None, ("tensor", "sub")),
    )
    return jax.shard_map(shards, mesh=mesh, in_specs=in_specs, out_specs=out_specs, check_vma=False)
```

```python
import functools
import math

import jax
import jax.numpy as jnp
from jax import lax
from jax.experimental import pallas as pl
from jax.experimental.pallas import tpu as pltpu
from jax.sharding import PartitionSpec as P

HEADS = 64
KVH = 8
HD = 128
MAXBLK = 32
CAPP = 2
GROUP = HEADS // KVH
EMPTY = -1e30
TILE = 256
ONES = 16
PIECE = 32
SCALE = 1.0 / math.sqrt(HD)
EXP2_SCALE = SCALE * math.log2(math.e)
VMEM_LIMIT = 63 * 1024 * 1024 + 512 * 1024


def blocks_at(tables, request, place, pool_size):
    prefix_ref, store_ref, slot_ref = tables
    first = lax.rem(place - store_ref[request, 0] + pool_size, pool_size)
    count = lax.max(lax.div(prefix_ref[request] - first + pool_size - 1, pool_size), 0)
    return count, lambda entry: slot_ref[request, first + entry * pool_size]


def fetch(pool_size, tables, request, stores, buffers, sems, moved=None):
    me = lax.axis_index("pool")
    count, slot_of = blocks_at(tables, request, me if moved is None else me ^ 1, pool_size)

    def copies(entry):
        for i in range(2):
            if moved is None:
                source = stores[i].at[slot_of(entry)]
            else:
                source = moved.at[i * (moved.shape[0] // 2) + entry]
            yield pltpu.make_async_copy(source, buffers[i].at[entry], sems.at[i, entry])

    def start(entry, carry):
        for copy in copies(entry):
            copy.start()
        return carry

    lax.fori_loop(0, count, start, 0)

    def ready(entry):
        for copy in copies(entry):
            copy.wait()

    return count, ready


def gather_kernel(pool_size, prefix_ref, store_ref, slot_ref, store_keys, store_values, out_ref, sems):
    me = lax.axis_index("pool")
    capacity = out_ref.shape[0] // 2

    @pl.when(jnp.logical_not(is_inner(me)))
    def _():
        tables = (prefix_ref, store_ref, slot_ref)
        count, slot_of = blocks_at(tables, me ^ 3, me, pool_size)

        def copies(entry):
            return [
                pltpu.make_async_copy(
                    store.at[slot_of(entry)], out_ref.at[i * capacity + entry], sems.at[i, entry]
                )
                for i, store in enumerate((store_keys, store_values))
            ]

        def start(entry, carry):
            for copy in copies(entry):
                copy.start()
            return carry

        def wait(entry, carry):
            for copy in copies(entry):
                copy.wait()
            return carry

        lax.fori_loop(0, count, start, 0)
        lax.fori_loop(0, count, wait, 0)


def attend(
    key_ref,
    value_ref,
    count,
    ready,
    fresh,
    new_rows,
    columns,
    scores,
    weights,
    peaks,
    factors,
    turned,
    acc,
    initial=None,
    raw=False,
):
    rows = columns.shape[1]
    kv_local = columns.shape[0] // HD

    def visit(keys, values, seen):
        size = keys[0].shape[0]

        def score(kv):
            turned[kv, :HD, :size] = values[kv].T
            block = lax.dot_general(
                keys[kv],
                columns[kv * HD : (kv + 1) * HD, :],
                (((1,), (0,)), ((), ())),
                preferred_element_type=jnp.float32,
            )
            if seen is not None:
                block = jnp.where(seen, block, EMPTY)
            scores[kv, :size, :] = block

        def weigh(kv):
            for i in range(0, rows, TILE):
                part = slice(i, i + TILE)
                before = peaks[kv, :, part]
                block = scores[kv, :size, part]
                peak = jnp.maximum(before, jnp.max(block, axis=0, keepdims=True))
                factors[kv, :, part] = jnp.exp2((before - peak) * EXP2_SCALE)
                peaks[kv, :, part] = peak
                weight = jnp.exp2(block * EXP2_SCALE - peak[0:1] * EXP2_SCALE)
                weights[kv, :size, part] = weight.astype(jnp.bfloat16)

        def mix(kv):
            added = lax.dot_general(
                turned[kv, :, :size],
                weights[kv, :size, :],
                (((1,), (0,)), ((), ())),
                preferred_element_type=jnp.float32,
            )
            acc[kv] = acc[kv] * factors[kv, 0:1, :] + added

        for step in range(kv_local + 2):
            for offset, stage in ((0, score), (2, mix), (1, weigh)):
                if 0 <= step - offset < kv_local:
                    stage(step - offset)

    def lanes_of(array):
        return [array[:, kv * HD : (kv + 1) * HD] for kv in range(kv_local)]

    def blocks_of(ref, first, number):
        return lanes_of(ref[pl.ds(first, number)].reshape(number * ref.shape[1], ref.shape[2]))

    if initial is None:
        peaks[...] = jnp.full(peaks.shape, EMPTY, jnp.float32)
        acc[...] = jnp.zeros(acc.shape, jnp.float32)
    else:
        acc[...] = initial[0][...]
        peaks[...] = initial[1][...]
    turned[:, HD:, :] = jnp.ones((kv_local, ONES, turned.shape[2]), jnp.bfloat16)
    if fresh is not None:
        new_key_ref, new_value_ref = fresh
        row = lax.rem(lax.broadcasted_iota(jnp.int32, (1, rows), 1), new_rows)
        seen = lax.broadcasted_iota(jnp.int32, (new_key_ref.shape[0], rows), 0) <= row
        visit(lanes_of(new_key_ref), lanes_of(new_value_ref), seen)

    def visit_blocks(number):
        def body(index, carry):
            for i in range(number):
                ready(index * number + i)
            visit(
                blocks_of(key_ref, index * number, number),
                blocks_of(value_ref, index * number, number),
                None,
            )
            return carry

        return body

    pairs = count // 2 if key_ref.shape[0] > 1 else 0
    if key_ref.shape[0] > 1:
        lax.fori_loop(0, pairs, visit_blocks(2), 0)
    lax.fori_loop(2 * pairs, count, visit_blocks(1), 0)
    if raw:
        return acc[...], peaks[...]
    outs = []
    logs = []
    for kv in range(kv_local):
        total = acc[kv, HD : HD + 1, :]
        safe = jnp.where(total > 0, total, 1.0)
        logs.append(jnp.where(total > 0, peaks[kv, 0:1] * SCALE + jnp.log(safe), EMPTY))
        outs.append(acc[kv, :HD, :] * (1.0 / safe))
    return outs, logs


def prepare_kernel(query_ref, new_key_ref, new_value_ref, payload_ref, query_rows):
    new_rows = query_ref.shape[0]
    kv_width = new_key_ref.shape[1]
    for kv in range(kv_width // HD):
        for g in range(GROUP):
            head = kv * GROUP + g
            query_rows[g * new_rows : (g + 1) * new_rows, :] = query_ref[
                :, head * HD : (head + 1) * HD
            ]
        payload_ref[kv * HD : (kv + 1) * HD, :] = query_rows[...].T
    for i, new_ref in enumerate((new_key_ref, new_value_ref)):
        for piece in range(new_rows // PIECE):
            row, lane = piece_place(i, piece, new_rows, kv_width)
            payload_ref[row : row + PIECE, lane : lane + kv_width] = new_ref[
                piece * PIECE : (piece + 1) * PIECE, :
            ]


def piece_place(i, piece, new_rows, kv_width):
    index = i * (new_rows // PIECE) + piece
    beside = GROUP * new_rows // kv_width
    return kv_width + index // beside * PIECE, index % beside * kv_width


def payload_rows(new_rows, kv_width):
    return piece_place(1, new_rows // PIECE - 1, new_rows, kv_width)[0] + PIECE


def own_kernel(
    pool_size,
    prefix_ref,
    store_ref,
    slot_ref,
    payload_ref,
    new_key_ref,
    new_value_ref,
    store_keys,
    store_values,
    out_ref,
    log_ref,
    key_buf,
    value_buf,
    new_key_buf,
    new_value_buf,
    *state,
):
    *work, sems = state
    count, ready = fetch(
        pool_size,
        (prefix_ref, store_ref, slot_ref),
        lax.axis_index("pool"),
        (store_keys, store_values),
        (key_buf, value_buf),
        sems,
    )
    new_rows, kv_width = new_key_ref.shape
    for buffer, source in ((new_key_buf, new_key_ref), (new_value_buf, new_value_ref)):
        buffer[:new_rows, :] = source[...]
        buffer[new_rows:, :] = jnp.zeros((buffer.shape[0] - new_rows, kv_width), jnp.bfloat16)
    fresh = (new_key_buf, new_value_buf)
    outs, logs = attend(
        key_buf, value_buf, count, ready, fresh, new_rows, payload_ref.at[:kv_width], *work
    )
    log_ref[...] = jnp.zeros(log_ref.shape, jnp.float32)
    for kv, (out, log) in enumerate(zip(outs, logs)):
        out_ref[kv * HD : (kv + 1) * HD, :] = out
        log_ref[kv : kv + 1, :] = log


def other_kernel(pool_size, new_rows, partners, with_moved, raw, *refs):
    if partners is None:
        request = refs[0][0]
        choice = [None]
        refs = refs[1:]
    else:
        inner = is_inner(lax.axis_index("pool"))
        _, request = source_of(lax.axis_index("pool"), partners)
        choice = [
            hit for hit, mask in zip((inner, jnp.logical_not(inner)), partners) if mask is not None
        ]
    tables, refs = refs[:3], refs[3:]
    payload_refs, refs = refs[: len(choice)], refs[len(choice) :]
    moved = initial = None
    if with_moved:
        moved, *initial = refs[:3]
        refs = refs[3:]
    store_keys, store_values, *refs = refs
    out_refs, (key_buf, value_buf, *state) = refs[: 1 + raw], refs[1 + raw :]
    *work, columns, query_sem, sems = state
    kv_width = columns.shape[0]

    def query_copy(payload_ref):
        return pltpu.make_async_copy(payload_ref.at[:kv_width], columns, query_sem)

    def run():
        for payload_ref, hit in zip(payload_refs, choice):
            if len(choice) == 1:
                query_copy(payload_ref).start()
            else:
                pl.when(hit)(query_copy(payload_ref).start)
        count, ready = fetch(
            pool_size,
            tables,
            request,
            (store_keys, store_values),
            (key_buf, value_buf),
            sems,
            moved,
        )
        query_copy(payload_refs[0]).wait()
        results = attend(
            key_buf, value_buf, count, ready, None, new_rows, columns, *work, initial, raw
        )
        if raw:
            for out_ref, result in zip(out_refs, results):
                out_ref[...] = result
            return
        outs, logs = results
        out_ref = out_refs[0]
        tail = []
        for kv, (out, log) in enumerate(zip(outs, logs)):
            out_ref[kv * HD : (kv + 1) * HD, :] = out.astype(jnp.bfloat16)
            high = log.astype(jnp.bfloat16).astype(jnp.float32)
            middle = (log - high).astype(jnp.bfloat16).astype(jnp.float32)
            tail += [high, middle, log - high - middle]
        tail.append(jnp.zeros((ONES - len(tail), columns.shape[1]), jnp.float32))
        out_ref[kv_width:, :] = jnp.concatenate(tail, axis=0).astype(jnp.bfloat16)

    if len(choice) == 1 and choice[0] is not None:
        pl.when(choice[0])(run)
    else:
        run()


def is_inner(place):
    return (place == 1) | (place == 2)


def source_of(me, entry):
    if isinstance(entry, int):
        return jnp.bool_(True), jnp.int32(entry)
    inner = is_inner(me)
    masks = [0 if mask is None else mask for mask in entry]
    there = jnp.where(inner, entry[0] is not None, entry[1] is not None)
    return there, me ^ jnp.where(inner, masks[0], masks[1])


def push_kernel(pool_size, entries, owner_ref, *refs):
    payload_refs = refs[: len(entries)]
    key_out, value_out, sems = refs[len(entries) :]
    outs = (key_out, value_out)
    kv_width = key_out.shape[2]
    me = lax.axis_index("pool")
    total = jnp.int32(0)
    for other in range(pool_size):
        total += (owner_ref[other] == me).astype(jnp.int32)

    new_rows = key_out.shape[1]

    def copies(payload_ref, place):
        for i in range(2):
            for piece in range(new_rows // PIECE):
                row, lane = piece_place(i, piece, new_rows, kv_width)
                row += payload_ref.shape[0] - payload_rows(new_rows, kv_width)
                yield pltpu.make_async_copy(
                    payload_ref.at[row : row + PIECE, lane : lane + kv_width],
                    outs[i].at[place, piece * PIECE : (piece + 1) * PIECE],
                    sems.at[i, place, piece],
                )

    for entry, payload_ref in zip(entries, payload_refs):
        there, source = source_of(me, entry)
        rank = jnp.int32(0)
        for other in range(pool_size):
            rank += ((owner_ref[other] == me) & (other < source)).astype(jnp.int32)
        hit = there & (owner_ref[source] == me)
        for place in range(CAPP):

            @pl.when(hit & (rank == place))
            def _():
                for copy in copies(payload_ref, place):
                    copy.start()

    for place in range(CAPP):

        @pl.when(total <= place)
        def _():
            for out in outs:
                out[place] = jnp.zeros(out.shape[1:], jnp.bfloat16)

        @pl.when(total > place)
        def _():
            for copy in copies(payload_refs[0], place):
                copy.wait()


def combine_kernel(sources, last, own_ref, log_ref, *refs):
    parts = refs[: len(sources)]
    out_ref = refs[len(sources)]
    kv_width, rows = own_ref.shape
    me = lax.axis_index("pool")
    arrived = []
    tails = []
    for source, part in zip(sources, parts):
        there, request = source_of(me, source)
        arrived.append(there & (request != me))
        tails.append(part[kv_width:, :].astype(jnp.float32))
    if not last:
        refs[len(sources) + 1][...] = log_ref[...]
    for kv in range(kv_width // HD):
        logs = [log_ref[kv : kv + 1, :]]
        for there, tail in zip(arrived, tails):
            log = sum(tail[3 * kv + i : 3 * kv + i + 1] for i in range(3))
            logs.append(jnp.where(there, log, EMPTY))
        peak = functools.reduce(jnp.maximum, logs)
        shares = [jnp.exp(x - peak) for x in logs]
        total = functools.reduce(jnp.add, shares)
        shares = [x * (1.0 / total) for x in shares]
        band = slice(kv * HD, (kv + 1) * HD)
        for i in range(0, rows, TILE):
            part = slice(i, i + TILE)
            mixed = own_ref[band, part] * shares[0][:, part]
            for share, ref in zip(shares[1:], parts):
                mixed = mixed + ref[band, part].astype(jnp.float32) * share[:, part]
            if last:
                refs[len(sources) + 1][part, :] = mixed.astype(jnp.bfloat16).T
            else:
                out_ref[band, part] = mixed
        if last:
            turned = refs[len(sources) + 1]
            new_rows = out_ref.shape[0]
            for g in range(GROUP):
                head = kv * GROUP + g
                out_ref[:, head * HD : (head + 1) * HD] = turned[g * new_rows : (g + 1) * new_rows, :]
        else:
            refs[len(sources) + 1][kv : kv + 1, :] = peak + jnp.log(total)


def final_kernel(own_ref, log_ref, *refs):
    part_refs, (out_ref, buffer, turned, sems) = refs[:4], refs[4:]
    inner = is_inner(lax.axis_index("pool"))

    def copies(first):
        return [
            pltpu.make_async_copy(part_refs[first + i], buffer.at[i], sems.at[i]) for i in range(2)
        ]

    for hit, first in ((inner, 0), (jnp.logical_not(inner), 2)):

        @pl.when(hit)
        def _():
            for copy in copies(first):
                copy.start()

    for copy in copies(0):
        copy.wait()
    combine_kernel(
        [(1, 1), (2, 2)], True, own_ref, log_ref, buffer.at[0], buffer.at[1], out_ref, turned
    )


def shards(
    queries,
    new_keys,
    new_values,
    store_keys,
    store_values,
    prefix_blocks,
    hit_store,
    hit_slot,
    decode_owner,
):
    pool_size = lax.axis_size("pool")
    capacity = (MAXBLK + pool_size - 1) // pool_size
    new_rows = queries.shape[1]
    width = queries.shape[2]
    kv_width = new_keys.shape[2]
    block_len = store_keys.shape[1]
    rows = GROUP * new_rows
    tables = (prefix_blocks, hit_store, hit_slot)
    smem_spec = pl.BlockSpec(memory_space=pltpu.SMEM)
    hbm_spec = pl.BlockSpec(memory_space=pltpu.HBM)
    vmem_spec = pl.BlockSpec(memory_space=pltpu.VMEM)
    params = pltpu.CompilerParams(vmem_limit_bytes=VMEM_LIMIT)

    def cost(share):
        return pl.CostEstimate(
            flops=share * rows * block_len * kv_width * capacity,
            bytes_accessed=rows,
            transcendentals=0,
        )

    buffers = [pltpu.VMEM((capacity, block_len, kv_width), jnp.bfloat16)] * 2
    kv_local = kv_width // HD
    widest = block_len * min(2, capacity)
    work = [
        pltpu.VMEM((kv_local, widest, rows), jnp.float32),
        pltpu.VMEM((kv_local, widest, rows), jnp.bfloat16),
        pltpu.VMEM((kv_local, 8, rows), jnp.float32),
        pltpu.VMEM((kv_local, 8, rows), jnp.float32),
        pltpu.VMEM((kv_local, HD + ONES, widest), jnp.bfloat16),
        pltpu.VMEM((kv_local, HD + ONES, rows), jnp.float32),
    ]
    sems = pltpu.SemaphoreType.DMA((2, capacity))

    def own_part(payload):
        return pl.pallas_call(
            functools.partial(own_kernel, pool_size),
            in_specs=[smem_spec] * 3 + [vmem_spec] * 3 + [hbm_spec] * 2,
            out_specs=[vmem_spec] * 2,
            scratch_shapes=[
                *buffers,
                *[pltpu.VMEM((block_len, kv_width), jnp.bfloat16)] * 2,
                *work,
                sems,
            ],
            out_shape=[
                jax.ShapeDtypeStruct((kv_width, rows), jnp.float32),
                jax.ShapeDtypeStruct((8, rows), jnp.float32),
            ],
            compiler_params=params,
            cost_estimate=cost(8),
            name="own_part",
        )(*tables, payload, new_keys[0], new_values[0], store_keys, store_values)

    def other_part(partners, held, *request, share=8, moved=(), raw=False):
        if raw:
            out_shape = [
                jax.ShapeDtypeStruct((kv_local, HD + ONES, rows), jnp.float32),
                jax.ShapeDtypeStruct((kv_local, 8, rows), jnp.float32),
            ]
        else:
            out_shape = jax.ShapeDtypeStruct((kv_width + ONES, rows), jnp.bfloat16)
        more_specs = [hbm_spec, vmem_spec, vmem_spec] if moved else []
        return pl.pallas_call(
            functools.partial(other_kernel, pool_size, new_rows, partners, bool(moved), raw),
            in_specs=[smem_spec] * (3 + len(request))
            + [hbm_spec] * len(held)
            + more_specs
            + [hbm_spec] * 2,
            out_specs=[vmem_spec] * 2 if raw else vmem_spec,
            scratch_shapes=[
                *buffers,
                *work,
                pltpu.VMEM((kv_width, rows), jnp.bfloat16),
                pltpu.SemaphoreType.DMA,
                sems,
            ],
            out_shape=out_shape,
            compiler_params=params,
            cost_estimate=cost(share),
            name="other_part",
        )(*request, *tables, *held, *moved, store_keys, store_values)

    def combine(own, log, sources, parts, last=True):
        if last:
            out_shape = jax.ShapeDtypeStruct((new_rows, width), jnp.bfloat16)
        else:
            out_shape = [
                jax.ShapeDtypeStruct((kv_width, rows), jnp.float32),
                jax.ShapeDtypeStruct((8, rows), jnp.float32),
            ]
        return pl.pallas_call(
            functools.partial(combine_kernel, tuple(sources), last),
            in_specs=[vmem_spec] * (2 + len(parts)),
            out_specs=vmem_spec if last else [vmem_spec] * 2,
            scratch_shapes=[pltpu.VMEM((rows, HD), jnp.bfloat16)] if last else [],
            out_shape=out_shape,
            compiler_params=params,
            cost_estimate=cost(0),
            name="combine",
        )(own, log, *parts)

    def final(own, log, parts):
        return pl.pallas_call(
            final_kernel,
            in_specs=[vmem_spec] * 2 + [hbm_spec] * 4,
            out_specs=vmem_spec,
            scratch_shapes=[
                pltpu.VMEM((2, kv_width + ONES, rows), jnp.bfloat16),
                pltpu.VMEM((rows, HD), jnp.bfloat16),
                pltpu.SemaphoreType.DMA((2,)),
            ],
            out_shape=jax.ShapeDtypeStruct((new_rows, width), jnp.bfloat16),
            compiler_params=params,
            name="final",
        )(own, log, *parts)

    payload = pl.pallas_call(
        prepare_kernel,
        in_specs=[vmem_spec] * 3,
        out_specs=vmem_spec,
        scratch_shapes=[pltpu.VMEM((rows, HD), jnp.bfloat16)],
        out_shape=jax.ShapeDtypeStruct((payload_rows(new_rows, kv_width), rows), jnp.bfloat16),
        compiler_params=params,
        name="prepare",
    )(queries[0], new_keys[0], new_values[0])
    own_out, own_log = own_part(payload)
    if pool_size == 4:
        def send(array, *pairs):
            return lax.ppermute(array, "pool", pairs)

        near = send(payload, (0, 1), (1, 0), (2, 3), (3, 2))
        middle = send(payload, (1, 2), (2, 1))
        blocks = pl.pallas_call(
            functools.partial(gather_kernel, pool_size),
            in_specs=[smem_spec] * 3 + [hbm_spec] * 2,
            out_specs=vmem_spec,
            scratch_shapes=[sems],
            out_shape=jax.ShapeDtypeStruct((2 * capacity, block_len, kv_width), jnp.bfloat16),
            compiler_params=params,
            name="gather_blocks",
        )(*tables, store_keys, store_values)
        blocks = send(blocks, (0, 1), (3, 2))
        near, middle, own_out, own_log = lax.optimization_barrier((near, middle, own_out, own_log))
        crossed = send(near, (1, 2), (2, 1))
        outward = send(middle, (1, 0), (2, 3))
        first = other_part((3, 1), (middle, near))
        across = send(first, (1, 2), (2, 1))
        inward = send(first, (0, 1), (3, 2))
        near, outward, first = lax.optimization_barrier((near, outward, first))
        second = other_part((1, 2), (near, outward), share=0)
        back = send(second, (1, 0), (2, 3))
        crossed, second = lax.optimization_barrier((crossed, second))
        state = other_part((2, None), (crossed,), raw=True)
        crossed, state, second = lax.optimization_barrier((crossed, state, second))
        apart = send(second, (0, 2), (3, 1))
        far = send(crossed[kv_width:], (1, 0), (2, 3))
        third = other_part((2, None), (crossed,), moved=(blocks, *state))
        ends = send(third, (1, 3), (2, 0))
        own_out, own_log, third = lax.optimization_barrier((own_out, own_log, third))
        own_out, own_log = combine(own_out, own_log, [(3, None)], [across], last=False)
        attended = final(own_out, own_log, (inward, apart, back, ends))
        moved = [
            ((0, 0), payload),
            ((1, 1), near),
            ((3, None), middle),
            ((2, None), crossed),
            ((None, 2), outward),
            ((None, 3), far),
        ]
    else:
        gathered = lax.all_gather(payload, "pool", axis=0, tiled=False)
        packed = lax.map(
            lambda pair: other_part(None, (pair[0],), pair[1].reshape(1)),
            (gathered, jnp.arange(pool_size, dtype=jnp.int32)),
        )
        parts = lax.all_to_all(packed, "pool", split_axis=0, concat_axis=0, tiled=True)
        attended = combine(own_out, own_log, list(range(pool_size)), parts)
        moved = [(source, gathered[source]) for source in range(pool_size)]

    pushed_keys, pushed_values = pl.pallas_call(
        functools.partial(push_kernel, pool_size, tuple(entry for entry, _ in moved)),
        in_specs=[smem_spec] + [hbm_spec] * len(moved),
        out_specs=[vmem_spec] * 2,
        scratch_shapes=[pltpu.SemaphoreType.DMA((2, CAPP, new_rows // PIECE))],
        out_shape=[jax.ShapeDtypeStruct((CAPP, new_rows, kv_width), jnp.bfloat16)] * 2,
        compiler_params=params,
        name="push",
    )(decode_owner, *[array for _, array in moved])
    return (attended[None], pushed_keys, pushed_values)


def solution(mesh):
    in_specs = (
        P(("groups", "pool"), None, ("tensor", "sub")),
        P(("groups", "pool"), None, ("tensor", "sub")),
        P(("groups", "pool"), None, ("tensor", "sub")),
        P(("groups", "pool"), None, ("tensor", "sub")),
        P(("groups", "pool"), None, ("tensor", "sub")),
        P("groups"),
        P("groups", None),
        P("groups", None),
        P("groups"),
    )
    out_specs = (
        P(("groups", "pool"), None, ("tensor", "sub")),
        P(("groups", "pool"), None, ("tensor", "sub")),
        P(("groups", "pool"), None, ("tensor", "sub")),
    )
    return jax.shard_map(shards, mesh=mesh, in_specs=in_specs, out_specs=out_specs, check_vma=False)
```

```python
import functools
import math

import jax
import jax.numpy as jnp
from jax import lax
from jax.experimental import pallas as pl
from jax.experimental.pallas import tpu as pltpu
from jax.sharding import PartitionSpec as P

HEADS = 64
KVH = 8
HD = 128
MAXBLK = 32
CAPP = 2
GROUP = HEADS // KVH
EMPTY = -1e30
TILE = 256
ONES = 16
PIECE = 32
SCALE = 1.0 / math.sqrt(HD)
EXP2_SCALE = SCALE * math.log2(math.e)
VMEM_LIMIT = 63 * 1024 * 1024 + 512 * 1024


def blocks_at(tables, request, place, pool_size):
    prefix_ref, store_ref, slot_ref = tables
    first = lax.rem(place - store_ref[request, 0] + pool_size, pool_size)
    count = lax.max(lax.div(prefix_ref[request] - first + pool_size - 1, pool_size), 0)
    return count, lambda entry: slot_ref[request, first + entry * pool_size]


def fetch(pool_size, tables, request, stores, buffers, sems, moved=None):
    me = lax.axis_index("pool")
    count, slot_of = blocks_at(tables, request, me if moved is None else me ^ 1, pool_size)

    def copies(entry):
        for i in range(2):
            if moved is None:
                source = stores[i].at[slot_of(entry)]
            else:
                source = moved.at[i * (moved.shape[0] // 2) + entry]
            yield pltpu.make_async_copy(source, buffers[i].at[entry], sems.at[i, entry])

    def start(entry, carry):
        for copy in copies(entry):
            copy.start()
        return carry

    lax.fori_loop(0, count, start, 0)

    def ready(entry):
        for copy in copies(entry):
            copy.wait()

    return count, ready


def gather_kernel(pool_size, prefix_ref, store_ref, slot_ref, store_keys, store_values, out_ref, sems):
    me = lax.axis_index("pool")
    capacity = out_ref.shape[0] // 2

    @pl.when(jnp.logical_not(is_inner(me)))
    def _():
        tables = (prefix_ref, store_ref, slot_ref)
        count, slot_of = blocks_at(tables, me ^ 3, me, pool_size)

        def copies(entry):
            return [
                pltpu.make_async_copy(
                    store.at[slot_of(entry)], out_ref.at[i * capacity + entry], sems.at[i, entry]
                )
                for i, store in enumerate((store_keys, store_values))
            ]

        def start(entry, carry):
            for copy in copies(entry):
                copy.start()
            return carry

        def wait(entry, carry):
            for copy in copies(entry):
                copy.wait()
            return carry

        lax.fori_loop(0, count, start, 0)
        lax.fori_loop(0, count, wait, 0)


def attend(
    key_ref,
    value_ref,
    count,
    ready,
    fresh,
    new_rows,
    columns,
    scores,
    weights,
    peaks,
    factors,
    turned,
    acc,
    initial=None,
    raw=False,
):
    rows = columns.shape[1]
    kv_local = columns.shape[0] // HD

    def visit(keys, values, seen):
        size = keys[0].shape[0]

        def score(kv):
            turned[kv, :HD, :size] = values[kv].T
            block = lax.dot_general(
                keys[kv],
                columns[kv * HD : (kv + 1) * HD, :],
                (((1,), (0,)), ((), ())),
                preferred_element_type=jnp.float32,
            )
            if seen is not None:
                block = jnp.where(seen, block, EMPTY)
            scores[kv, :size, :] = block

        def weigh(kv):
            for i in range(0, rows, TILE):
                part = slice(i, i + TILE)
                before = peaks[kv, :, part]
                block = scores[kv, :size, part]
                peak = jnp.maximum(before, jnp.max(block, axis=0, keepdims=True))
                factors[kv, :, part] = jnp.exp2((before - peak) * EXP2_SCALE)
                peaks[kv, :, part] = peak
                weight = jnp.exp2(block * EXP2_SCALE - peak[0:1] * EXP2_SCALE)
                weights[kv, :size, part] = weight.astype(jnp.bfloat16)

        def mix(kv):
            added = lax.dot_general(
                turned[kv, :, :size],
                weights[kv, :size, :],
                (((1,), (0,)), ((), ())),
                preferred_element_type=jnp.float32,
            )
            acc[kv] = acc[kv] * factors[kv, 0:1, :] + added

        for step in range(kv_local + 2):
            for offset, stage in ((0, score), (2, mix), (1, weigh)):
                if 0 <= step - offset < kv_local:
                    stage(step - offset)

    def lanes_of(array):
        return [array[:, kv * HD : (kv + 1) * HD] for kv in range(kv_local)]

    def blocks_of(ref, first, number):
        return lanes_of(ref[pl.ds(first, number)].reshape(number * ref.shape[1], ref.shape[2]))

    if initial is None:
        peaks[...] = jnp.full(peaks.shape, EMPTY, jnp.float32)
        acc[...] = jnp.zeros(acc.shape, jnp.float32)
    else:
        for copy in initial(acc, peaks):
            copy.wait()
    turned[:, HD:, :] = jnp.ones((kv_local, ONES, turned.shape[2]), jnp.bfloat16)
    if fresh is not None:
        new_key_ref, new_value_ref = fresh
        row = lax.rem(lax.broadcasted_iota(jnp.int32, (1, rows), 1), new_rows)
        seen = lax.broadcasted_iota(jnp.int32, (new_key_ref.shape[0], rows), 0) <= row
        visit(lanes_of(new_key_ref), lanes_of(new_value_ref), seen)

    def visit_blocks(number):
        def body(index, carry):
            for i in range(number):
                ready(index * number + i)
            visit(
                blocks_of(key_ref, index * number, number),
                blocks_of(value_ref, index * number, number),
                None,
            )
            return carry

        return body

    pairs = count // 2 if key_ref.shape[0] > 1 else 0
    if key_ref.shape[0] > 1:
        lax.fori_loop(0, pairs, visit_blocks(2), 0)
    lax.fori_loop(2 * pairs, count, visit_blocks(1), 0)
    if raw:
        return acc, peaks
    outs = []
    logs = []
    for kv in range(kv_local):
        total = acc[kv, HD : HD + 1, :]
        safe = jnp.where(total > 0, total, 1.0)
        logs.append(jnp.where(total > 0, peaks[kv, 0:1] * SCALE + jnp.log(safe), EMPTY))
        outs.append(acc[kv, :HD, :] * (1.0 / safe))
    return outs, logs


def prepare_kernel(query_ref, new_key_ref, new_value_ref, payload_ref, query_rows):
    new_rows = query_ref.shape[0]
    kv_width = new_key_ref.shape[1]
    for kv in range(kv_width // HD):
        for g in range(GROUP):
            head = kv * GROUP + g
            query_rows[g * new_rows : (g + 1) * new_rows, :] = query_ref[
                :, head * HD : (head + 1) * HD
            ]
        payload_ref[kv * HD : (kv + 1) * HD, :] = query_rows[...].T
    for i, new_ref in enumerate((new_key_ref, new_value_ref)):
        for piece in range(new_rows // PIECE):
            row, lane = piece_place(i, piece, new_rows, kv_width)
            payload_ref[row : row + PIECE, lane : lane + kv_width] = new_ref[
                piece * PIECE : (piece + 1) * PIECE, :
            ]


def piece_place(i, piece, new_rows, kv_width):
    index = i * (new_rows // PIECE) + piece
    beside = GROUP * new_rows // kv_width
    return kv_width + index // beside * PIECE, index % beside * kv_width


def payload_rows(new_rows, kv_width):
    return piece_place(1, new_rows // PIECE - 1, new_rows, kv_width)[0] + PIECE


def own_kernel(
    pool_size,
    prefix_ref,
    store_ref,
    slot_ref,
    payload_ref,
    new_key_ref,
    new_value_ref,
    store_keys,
    store_values,
    out_ref,
    log_ref,
    key_buf,
    value_buf,
    new_key_buf,
    new_value_buf,
    *state,
):
    *work, sems = state
    count, ready = fetch(
        pool_size,
        (prefix_ref, store_ref, slot_ref),
        lax.axis_index("pool"),
        (store_keys, store_values),
        (key_buf, value_buf),
        sems,
    )
    new_rows, kv_width = new_key_ref.shape
    for buffer, source in ((new_key_buf, new_key_ref), (new_value_buf, new_value_ref)):
        buffer[:new_rows, :] = source[...]
        buffer[new_rows:, :] = jnp.zeros((buffer.shape[0] - new_rows, kv_width), jnp.bfloat16)
    fresh = (new_key_buf, new_value_buf)
    outs, logs = attend(
        key_buf, value_buf, count, ready, fresh, new_rows, payload_ref.at[:kv_width], *work
    )
    log_ref[...] = jnp.zeros(log_ref.shape, jnp.float32)
    for kv, (out, log) in enumerate(zip(outs, logs)):
        out_ref[kv * HD : (kv + 1) * HD, :] = out
        log_ref[kv : kv + 1, :] = log


def other_kernel(pool_size, new_rows, partners, with_moved, raw, *refs):
    if partners is None:
        request = refs[0][0]
        choice = [None]
        refs = refs[1:]
    else:
        inner = is_inner(lax.axis_index("pool"))
        _, request = source_of(lax.axis_index("pool"), partners)
        choice = [
            hit for hit, mask in zip((inner, jnp.logical_not(inner)), partners) if mask is not None
        ]
    tables, refs = refs[:3], refs[3:]
    payload_refs, refs = refs[: len(choice)], refs[len(choice) :]
    moved = initial = None
    if with_moved:
        moved, *initial = refs[:3]
        refs = refs[3:]
    store_keys, store_values, *refs = refs
    results_ref, (key_buf, value_buf, *state) = refs[: 1 + raw], refs[1 + raw :]
    *work, columns, query_sem, out_buf, out_sem, sems = state
    kv_width = columns.shape[0]

    def query_copy(payload_ref):
        return pltpu.make_async_copy(payload_ref.at[:kv_width], columns, query_sem)

    def run():
        for payload_ref, hit in zip(payload_refs, choice):
            if len(choice) == 1:
                query_copy(payload_ref).start()
            else:
                pl.when(hit)(query_copy(payload_ref).start)
        count, ready = fetch(
            pool_size,
            tables,
            request,
            (store_keys, store_values),
            (key_buf, value_buf),
            sems,
            moved,
        )
        restore = None
        if initial is not None:

            def restore(*targets):
                return [
                    pltpu.make_async_copy(source, target, out_sem.at[i])
                    for i, (source, target) in enumerate(zip(initial, targets))
                ]

            for copy in restore(work[-1], work[2]):
                copy.start()
        query_copy(payload_refs[0]).wait()
        results = attend(
            key_buf, value_buf, count, ready, None, new_rows, columns, *work, restore, raw
        )
        if raw:
            copies = [
                pltpu.make_async_copy(result, out_ref, out_sem.at[i])
                for i, (out_ref, result) in enumerate(zip(results_ref, results))
            ]
            for copy in copies:
                copy.start()
            for copy in copies:
                copy.wait()
            return
        outs, logs = results
        tail = []
        copies = []

        def send_rows(start, size):
            copies.append(
                pltpu.make_async_copy(
                    out_buf.at[start : start + size],
                    results_ref[0].at[start : start + size],
                    out_sem.at[len(copies)],
                )
            )
            copies[-1].start()

        for kv, (out, log) in enumerate(zip(outs, logs)):
            out_buf[kv * HD : (kv + 1) * HD, :] = out.astype(jnp.bfloat16)
            send_rows(kv * HD, HD)
            high = log.astype(jnp.bfloat16).astype(jnp.float32)
            middle = (log - high).astype(jnp.bfloat16).astype(jnp.float32)
            tail += [high, middle, log - high - middle]
        tail.append(jnp.zeros((ONES - len(tail), columns.shape[1]), jnp.float32))
        out_buf[kv_width:, :] = jnp.concatenate(tail, axis=0).astype(jnp.bfloat16)
        send_rows(kv_width, ONES)
        for copy in copies:
            copy.wait()

    if len(choice) == 1 and choice[0] is not None:
        pl.when(choice[0])(run)
    else:
        run()


def is_inner(place):
    return (place == 1) | (place == 2)


def source_of(me, entry):
    if isinstance(entry, int):
        return jnp.bool_(True), jnp.int32(entry)
    inner = is_inner(me)
    masks = [0 if mask is None else mask for mask in entry]
    there = jnp.where(inner, entry[0] is not None, entry[1] is not None)
    return there, me ^ jnp.where(inner, masks[0], masks[1])


def push_kernel(pool_size, entries, owner_ref, *refs):
    payload_refs = refs[: len(entries)]
    key_out, value_out, sems = refs[len(entries) :]
    outs = (key_out, value_out)
    kv_width = key_out.shape[2]
    me = lax.axis_index("pool")
    total = jnp.int32(0)
    for other in range(pool_size):
        total += (owner_ref[other] == me).astype(jnp.int32)

    new_rows = key_out.shape[1]

    def copies(payload_ref, place):
        for i in range(2):
            for piece in range(new_rows // PIECE):
                row, lane = piece_place(i, piece, new_rows, kv_width)
                row += payload_ref.shape[0] - payload_rows(new_rows, kv_width)
                yield pltpu.make_async_copy(
                    payload_ref.at[row : row + PIECE, lane : lane + kv_width],
                    outs[i].at[place, piece * PIECE : (piece + 1) * PIECE],
                    sems.at[i, place, piece],
                )

    for entry, payload_ref in zip(entries, payload_refs):
        there, source = source_of(me, entry)
        rank = jnp.int32(0)
        for other in range(pool_size):
            rank += ((owner_ref[other] == me) & (other < source)).astype(jnp.int32)
        hit = there & (owner_ref[source] == me)
        for place in range(CAPP):

            @pl.when(hit & (rank == place))
            def _():
                for copy in copies(payload_ref, place):
                    copy.start()

    for place in range(CAPP):

        @pl.when(total <= place)
        def _():
            for out in outs:
                out[place] = jnp.zeros(out.shape[1:], jnp.bfloat16)

        @pl.when(total > place)
        def _():
            for copy in copies(payload_refs[0], place):
                copy.wait()


def combine_kernel(sources, last, own_ref, log_ref, *refs):
    parts = refs[: len(sources)]
    out_ref = refs[len(sources)]
    kv_width, rows = own_ref.shape
    me = lax.axis_index("pool")
    arrived = []
    tails = []
    for source, part in zip(sources, parts):
        there, request = source_of(me, source)
        arrived.append(there & (request != me))
        tails.append(part[kv_width:, :].astype(jnp.float32))
    if not last:
        refs[len(sources) + 1][...] = log_ref[...]
    for kv in range(kv_width // HD):
        logs = [log_ref[kv : kv + 1, :]]
        for there, tail in zip(arrived, tails):
            log = sum(tail[3 * kv + i : 3 * kv + i + 1] for i in range(3))
            logs.append(jnp.where(there, log, EMPTY))
        peak = functools.reduce(jnp.maximum, logs)
        shares = [jnp.exp(x - peak) for x in logs]
        total = functools.reduce(jnp.add, shares)
        shares = [x * (1.0 / total) for x in shares]
        band = slice(kv * HD, (kv + 1) * HD)
        for i in range(0, rows, TILE):
            part = slice(i, i + TILE)
            mixed = own_ref[band, part] * shares[0][:, part]
            for share, ref in zip(shares[1:], parts):
                mixed = mixed + ref[band, part].astype(jnp.float32) * share[:, part]
            if last:
                refs[len(sources) + 1][part, :] = mixed.astype(jnp.bfloat16).T
            else:
                out_ref[band, part] = mixed
        if last:
            turned = refs[len(sources) + 1]
            new_rows = out_ref.shape[0]
            for g in range(GROUP):
                head = kv * GROUP + g
                out_ref[:, head * HD : (head + 1) * HD] = turned[g * new_rows : (g + 1) * new_rows, :]
        else:
            refs[len(sources) + 1][kv : kv + 1, :] = peak + jnp.log(total)


def final_kernel(own_ref, log_ref, *refs):
    part_refs, (out_ref, buffer, turned, sems) = refs[:4], refs[4:]
    inner = is_inner(lax.axis_index("pool"))

    def copies(first):
        return [
            pltpu.make_async_copy(part_refs[first + i], buffer.at[i], sems.at[i]) for i in range(2)
        ]

    for hit, first in ((inner, 0), (jnp.logical_not(inner), 2)):

        @pl.when(hit)
        def _():
            for copy in copies(first):
                copy.start()

    for copy in copies(0):
        copy.wait()
    combine_kernel(
        [(1, 1), (2, 2)], True, own_ref, log_ref, buffer.at[0], buffer.at[1], out_ref, turned
    )


def shards(
    queries,
    new_keys,
    new_values,
    store_keys,
    store_values,
    prefix_blocks,
    hit_store,
    hit_slot,
    decode_owner,
):
    pool_size = lax.axis_size("pool")
    capacity = (MAXBLK + pool_size - 1) // pool_size
    new_rows = queries.shape[1]
    width = queries.shape[2]
    kv_width = new_keys.shape[2]
    block_len = store_keys.shape[1]
    rows = GROUP * new_rows
    tables = (prefix_blocks, hit_store, hit_slot)
    smem_spec = pl.BlockSpec(memory_space=pltpu.SMEM)
    hbm_spec = pl.BlockSpec(memory_space=pltpu.HBM)
    vmem_spec = pl.BlockSpec(memory_space=pltpu.VMEM)
    params = pltpu.CompilerParams(vmem_limit_bytes=VMEM_LIMIT)

    def cost(share):
        return pl.CostEstimate(
            flops=share * rows * block_len * kv_width * capacity,
            bytes_accessed=rows,
            transcendentals=0,
        )

    buffers = [pltpu.VMEM((capacity, block_len, kv_width), jnp.bfloat16)] * 2
    kv_local = kv_width // HD
    widest = block_len * min(2, capacity)
    work = [
        pltpu.VMEM((kv_local, widest, rows), jnp.float32),
        pltpu.VMEM((kv_local, widest, rows), jnp.bfloat16),
        pltpu.VMEM((kv_local, 8, rows), jnp.float32),
        pltpu.VMEM((kv_local, 8, rows), jnp.float32),
        pltpu.VMEM((kv_local, HD + ONES, widest), jnp.bfloat16),
        pltpu.VMEM((kv_local, HD + ONES, rows), jnp.float32),
    ]
    sems = pltpu.SemaphoreType.DMA((2, capacity))

    def own_part(payload):
        return pl.pallas_call(
            functools.partial(own_kernel, pool_size),
            in_specs=[smem_spec] * 3 + [vmem_spec] * 3 + [hbm_spec] * 2,
            out_specs=[vmem_spec] * 2,
            scratch_shapes=[
                *buffers,
                *[pltpu.VMEM((block_len, kv_width), jnp.bfloat16)] * 2,
                *work,
                sems,
            ],
            out_shape=[
                jax.ShapeDtypeStruct((kv_width, rows), jnp.float32),
                jax.ShapeDtypeStruct((8, rows), jnp.float32),
            ],
            compiler_params=params,
            cost_estimate=cost(8),
            name="own_part",
        )(*tables, payload, new_keys[0], new_values[0], store_keys, store_values)

    def other_part(partners, held, *request, share=8, moved=(), raw=False):
        if raw:
            out_shape = [
                jax.ShapeDtypeStruct((kv_local, HD + ONES, rows), jnp.float32),
                jax.ShapeDtypeStruct((kv_local, 8, rows), jnp.float32),
            ]
        else:
            out_shape = jax.ShapeDtypeStruct((kv_width + ONES, rows), jnp.bfloat16)
        more_specs = [hbm_spec] * 3 if moved else []
        return pl.pallas_call(
            functools.partial(other_kernel, pool_size, new_rows, partners, bool(moved), raw),
            in_specs=[smem_spec] * (3 + len(request))
            + [hbm_spec] * len(held)
            + more_specs
            + [hbm_spec] * 2,
            out_specs=[hbm_spec] * 2 if raw else hbm_spec,
            scratch_shapes=[
                *buffers,
                *work,
                pltpu.VMEM((kv_width, rows), jnp.bfloat16),
                pltpu.SemaphoreType.DMA,
                pltpu.VMEM((kv_width + ONES, rows), jnp.bfloat16),
                pltpu.SemaphoreType.DMA((max(2, kv_local + 1),)),
                sems,
            ],
            out_shape=out_shape,
            compiler_params=params,
            cost_estimate=cost(share),
            name="other_part",
        )(*request, *tables, *held, *moved, store_keys, store_values)

    def combine(own, log, sources, parts, last=True):
        if last:
            out_shape = jax.ShapeDtypeStruct((new_rows, width), jnp.bfloat16)
        else:
            out_shape = [
                jax.ShapeDtypeStruct((kv_width, rows), jnp.float32),
                jax.ShapeDtypeStruct((8, rows), jnp.float32),
            ]
        return pl.pallas_call(
            functools.partial(combine_kernel, tuple(sources), last),
            in_specs=[vmem_spec] * (2 + len(parts)),
            out_specs=vmem_spec if last else [vmem_spec] * 2,
            scratch_shapes=[pltpu.VMEM((rows, HD), jnp.bfloat16)] if last else [],
            out_shape=out_shape,
            compiler_params=params,
            cost_estimate=cost(0),
            name="combine",
        )(own, log, *parts)

    def final(own, log, parts):
        return pl.pallas_call(
            final_kernel,
            in_specs=[vmem_spec] * 2 + [hbm_spec] * 4,
            out_specs=vmem_spec,
            scratch_shapes=[
                pltpu.VMEM((2, kv_width + ONES, rows), jnp.bfloat16),
                pltpu.VMEM((rows, HD), jnp.bfloat16),
                pltpu.SemaphoreType.DMA((2,)),
            ],
            out_shape=jax.ShapeDtypeStruct((new_rows, width), jnp.bfloat16),
            compiler_params=params,
            name="final",
        )(own, log, *parts)

    payload = pl.pallas_call(
        prepare_kernel,
        in_specs=[vmem_spec] * 3,
        out_specs=vmem_spec,
        scratch_shapes=[pltpu.VMEM((rows, HD), jnp.bfloat16)],
        out_shape=jax.ShapeDtypeStruct((payload_rows(new_rows, kv_width), rows), jnp.bfloat16),
        compiler_params=params,
        name="prepare",
    )(queries[0], new_keys[0], new_values[0])
    own_out, own_log = own_part(payload)
    if pool_size == 4:
        def send(array, *pairs):
            return lax.ppermute(array, "pool", pairs)

        near = send(payload, (0, 1), (1, 0), (2, 3), (3, 2))
        middle = send(payload, (1, 2), (2, 1))
        blocks = pl.pallas_call(
            functools.partial(gather_kernel, pool_size),
            in_specs=[smem_spec] * 3 + [hbm_spec] * 2,
            out_specs=vmem_spec,
            scratch_shapes=[sems],
            out_shape=jax.ShapeDtypeStruct((2 * capacity, block_len, kv_width), jnp.bfloat16),
            compiler_params=params,
            name="gather_blocks",
        )(*tables, store_keys, store_values)
        blocks = send(blocks, (0, 1), (3, 2))
        near, middle, own_out, own_log = lax.optimization_barrier((near, middle, own_out, own_log))
        crossed = send(near, (1, 2), (2, 1))
        outward = send(middle, (1, 0), (2, 3))
        first = other_part((3, 1), (middle, near))
        across = send(first, (1, 2), (2, 1))
        near, first = lax.optimization_barrier((near, first))
        second = other_part((1, None), (near,))
        outward, second = lax.optimization_barrier((outward, second))
        outer_second = other_part((None, 2), (outward,))
        crossed, second, outer_second = lax.optimization_barrier((crossed, second, outer_second))
        state = other_part((2, None), (crossed,), raw=True)
        crossed, state, first, second, outer_second = lax.optimization_barrier(
            (crossed, state, first, second, outer_second)
        )
        apart = send(outer_second, (0, 2), (3, 1))
        inward = send(first, (0, 1), (3, 2))
        back = send(second, (1, 0), (2, 3))
        far = send(crossed[kv_width:], (1, 0), (2, 3))
        third = other_part((2, None), (crossed,), moved=(blocks, *state))
        ends = send(third, (1, 3), (2, 0))
        own_out, own_log, third = lax.optimization_barrier((own_out, own_log, third))
        own_out, own_log = combine(own_out, own_log, [(3, None)], [across], last=False)
        attended = final(own_out, own_log, (apart, inward, back, ends))
        moved = [
            ((0, 0), payload),
            ((1, 1), near),
            ((3, None), middle),
            ((2, None), crossed),
            ((None, 2), outward),
            ((None, 3), far),
        ]
    else:
        gathered = lax.all_gather(payload, "pool", axis=0, tiled=False)
        packed = lax.map(
            lambda pair: other_part(None, (pair[0],), pair[1].reshape(1)),
            (gathered, jnp.arange(pool_size, dtype=jnp.int32)),
        )
        parts = lax.all_to_all(packed, "pool", split_axis=0, concat_axis=0, tiled=True)
        attended = combine(own_out, own_log, list(range(pool_size)), parts)
        moved = [(source, gathered[source]) for source in range(pool_size)]

    pushed_keys, pushed_values = pl.pallas_call(
        functools.partial(push_kernel, pool_size, tuple(entry for entry, _ in moved)),
        in_specs=[smem_spec] + [hbm_spec] * len(moved),
        out_specs=[vmem_spec] * 2,
        scratch_shapes=[pltpu.SemaphoreType.DMA((2, CAPP, new_rows // PIECE))],
        out_shape=[jax.ShapeDtypeStruct((CAPP, new_rows, kv_width), jnp.bfloat16)] * 2,
        compiler_params=params,
        name="push",
    )(decode_owner, *[array for _, array in moved])
    return (attended[None], pushed_keys, pushed_values)


def solution(mesh):
    in_specs = (
        P(("groups", "pool"), None, ("tensor", "sub")),
        P(("groups", "pool"), None, ("tensor", "sub")),
        P(("groups", "pool"), None, ("tensor", "sub")),
        P(("groups", "pool"), None, ("tensor", "sub")),
        P(("groups", "pool"), None, ("tensor", "sub")),
        P("groups"),
        P("groups", None),
        P("groups", None),
        P("groups"),
    )
    out_specs = (
        P(("groups", "pool"), None, ("tensor", "sub")),
        P(("groups", "pool"), None, ("tensor", "sub")),
        P(("groups", "pool"), None, ("tensor", "sub")),
    )
    return jax.shard_map(shards, mesh=mesh, in_specs=in_specs, out_specs=out_specs, check_vma=False)
```

```python
import functools
import math

import jax
import jax.numpy as jnp
from jax import lax
from jax.experimental import pallas as pl
from jax.experimental.pallas import tpu as pltpu
from jax.sharding import PartitionSpec as P

HEADS = 64
KVH = 8
HD = 128
MAXBLK = 32
CAPP = 2
GROUP = HEADS // KVH
EMPTY = -1e30
TILE = 256
ONES = 16
PIECE = 32
SCALE = 1.0 / math.sqrt(HD)
EXP2_SCALE = SCALE * math.log2(math.e)
VMEM_LIMIT = 63 * 1024 * 1024 + 512 * 1024


def blocks_at(tables, request, place, pool_size):
    prefix_ref, store_ref, slot_ref = tables
    first = lax.rem(place - store_ref[request, 0] + pool_size, pool_size)
    count = lax.max(lax.div(prefix_ref[request] - first + pool_size - 1, pool_size), 0)
    return count, lambda entry: slot_ref[request, first + entry * pool_size]


def fetch(pool_size, tables, request, stores, buffers, sems, moved=None):
    me = lax.axis_index("pool")
    count, slot_of = blocks_at(tables, request, me if moved is None else me ^ 1, pool_size)

    def copies(entry):
        for i in range(2):
            if moved is None:
                source = stores[i].at[slot_of(entry)]
            else:
                source = moved.at[i * (moved.shape[0] // 2) + entry]
            yield pltpu.make_async_copy(source, buffers[i].at[entry], sems.at[i, entry])

    def start(entry, carry):
        for copy in copies(entry):
            copy.start()
        return carry

    lax.fori_loop(0, count, start, 0)

    def ready(entry):
        for copy in copies(entry):
            copy.wait()

    return count, ready


def gather_kernel(pool_size, prefix_ref, store_ref, slot_ref, store_keys, store_values, out_ref, sems):
    me = lax.axis_index("pool")
    capacity = out_ref.shape[0] // 2

    @pl.when(jnp.logical_not(is_inner(me)))
    def _():
        tables = (prefix_ref, store_ref, slot_ref)
        count, slot_of = blocks_at(tables, me ^ 3, me, pool_size)

        def copies(entry):
            return [
                pltpu.make_async_copy(
                    store.at[slot_of(entry)], out_ref.at[i * capacity + entry], sems.at[i, entry]
                )
                for i, store in enumerate((store_keys, store_values))
            ]

        def start(entry, carry):
            for copy in copies(entry):
                copy.start()
            return carry

        def wait(entry, carry):
            for copy in copies(entry):
                copy.wait()
            return carry

        lax.fori_loop(0, count, start, 0)
        lax.fori_loop(0, count, wait, 0)


def attend(
    key_ref,
    value_ref,
    count,
    ready,
    fresh,
    new_rows,
    columns,
    scores,
    weights,
    peaks,
    factors,
    turned,
    acc,
    initial=None,
    raw=False,
):
    rows = columns.shape[1]
    kv_local = columns.shape[0] // HD

    def visit(keys, values, seen):
        size = keys[0].shape[0]

        def score(kv):
            turned[kv, :HD, :size] = values[kv].T
            block = lax.dot_general(
                keys[kv],
                columns[kv * HD : (kv + 1) * HD, :],
                (((1,), (0,)), ((), ())),
                preferred_element_type=jnp.float32,
            )
            if seen is not None:
                block = jnp.where(seen, block, EMPTY)
            scores[kv, :size, :] = block

        def weigh(kv):
            for i in range(0, rows, TILE):
                part = slice(i, i + TILE)
                before = peaks[kv, :, part]
                block = scores[kv, :size, part]
                peak = jnp.maximum(before, jnp.max(block, axis=0, keepdims=True))
                factors[kv, :, part] = jnp.exp2((before - peak) * EXP2_SCALE)
                peaks[kv, :, part] = peak
                weight = jnp.exp2(block * EXP2_SCALE - peak[0:1] * EXP2_SCALE)
                weights[kv, :size, part] = weight.astype(jnp.bfloat16)

        def mix(kv):
            added = lax.dot_general(
                turned[kv, :, :size],
                weights[kv, :size, :],
                (((1,), (0,)), ((), ())),
                preferred_element_type=jnp.float32,
            )
            acc[kv] = acc[kv] * factors[kv, 0:1, :] + added

        for step in range(kv_local + 2):
            for offset, stage in ((0, score), (2, mix), (1, weigh)):
                if 0 <= step - offset < kv_local:
                    stage(step - offset)

    def lanes_of(array):
        return [array[:, kv * HD : (kv + 1) * HD] for kv in range(kv_local)]

    def blocks_of(ref, first, number):
        return lanes_of(ref[pl.ds(first, number)].reshape(number * ref.shape[1], ref.shape[2]))

    if initial is None:
        peaks[...] = jnp.full(peaks.shape, EMPTY, jnp.float32)
        acc[...] = jnp.zeros(acc.shape, jnp.float32)
    else:
        for copy in initial(acc, peaks):
            copy.wait()
    turned[:, HD:, :] = jnp.ones((kv_local, ONES, turned.shape[2]), jnp.bfloat16)
    if fresh is not None:
        new_key_ref, new_value_ref = fresh
        row = lax.rem(lax.broadcasted_iota(jnp.int32, (1, rows), 1), new_rows)
        seen = lax.broadcasted_iota(jnp.int32, (new_key_ref.shape[0], rows), 0) <= row
        visit(lanes_of(new_key_ref), lanes_of(new_value_ref), seen)

    def visit_blocks(number):
        def body(index, carry):
            for i in range(number):
                ready(index * number + i)
            visit(
                blocks_of(key_ref, index * number, number),
                blocks_of(value_ref, index * number, number),
                None,
            )
            return carry

        return body

    pairs = count // 2 if key_ref.shape[0] > 1 else 0
    if key_ref.shape[0] > 1:
        lax.fori_loop(0, pairs, visit_blocks(2), 0)
    lax.fori_loop(2 * pairs, count, visit_blocks(1), 0)
    if raw:
        return acc, peaks
    outs = []
    logs = []
    for kv in range(kv_local):
        total = acc[kv, HD : HD + 1, :]
        safe = jnp.where(total > 0, total, 1.0)
        logs.append(jnp.where(total > 0, peaks[kv, 0:1] * SCALE + jnp.log(safe), EMPTY))
        outs.append(acc[kv, :HD, :] * (1.0 / safe))
    return outs, logs


def prepare_kernel(query_ref, new_key_ref, new_value_ref, payload_ref, query_rows):
    new_rows = query_ref.shape[0]
    kv_width = new_key_ref.shape[1]
    for kv in range(kv_width // HD):
        for g in range(GROUP):
            head = kv * GROUP + g
            query_rows[g * new_rows : (g + 1) * new_rows, :] = query_ref[
                :, head * HD : (head + 1) * HD
            ]
        payload_ref[kv * HD : (kv + 1) * HD, :] = query_rows[...].T
    for i, new_ref in enumerate((new_key_ref, new_value_ref)):
        for piece in range(new_rows // PIECE):
            row, lane = piece_place(i, piece, new_rows, kv_width)
            payload_ref[row : row + PIECE, lane : lane + kv_width] = new_ref[
                piece * PIECE : (piece + 1) * PIECE, :
            ]


def piece_place(i, piece, new_rows, kv_width):
    index = i * (new_rows // PIECE) + piece
    beside = GROUP * new_rows // kv_width
    return kv_width + index // beside * PIECE, index % beside * kv_width


def payload_rows(new_rows, kv_width):
    return piece_place(1, new_rows // PIECE - 1, new_rows, kv_width)[0] + PIECE


def own_kernel(
    pool_size,
    prefix_ref,
    store_ref,
    slot_ref,
    payload_ref,
    new_key_ref,
    new_value_ref,
    store_keys,
    store_values,
    out_ref,
    log_ref,
    key_buf,
    value_buf,
    new_key_buf,
    new_value_buf,
    *state,
):
    *work, sems = state
    count, ready = fetch(
        pool_size,
        (prefix_ref, store_ref, slot_ref),
        lax.axis_index("pool"),
        (store_keys, store_values),
        (key_buf, value_buf),
        sems,
    )
    new_rows, kv_width = new_key_ref.shape
    for buffer, source in ((new_key_buf, new_key_ref), (new_value_buf, new_value_ref)):
        buffer[:new_rows, :] = source[...]
        buffer[new_rows:, :] = jnp.zeros((buffer.shape[0] - new_rows, kv_width), jnp.bfloat16)
    fresh = (new_key_buf, new_value_buf)
    outs, logs = attend(
        key_buf, value_buf, count, ready, fresh, new_rows, payload_ref.at[:kv_width], *work
    )
    log_ref[...] = jnp.zeros(log_ref.shape, jnp.float32)
    for kv, (out, log) in enumerate(zip(outs, logs)):
        out_ref[kv * HD : (kv + 1) * HD, :] = out
        log_ref[kv : kv + 1, :] = log


def other_kernel(pool_size, new_rows, partners, with_moved, raw, *refs):
    if partners is None:
        request = refs[0][0]
        choice = [None]
        refs = refs[1:]
    else:
        inner = is_inner(lax.axis_index("pool"))
        _, request = source_of(lax.axis_index("pool"), partners)
        choice = [
            hit for hit, mask in zip((inner, jnp.logical_not(inner)), partners) if mask is not None
        ]
    tables, refs = refs[:3], refs[3:]
    payload_refs, refs = refs[: len(choice)], refs[len(choice) :]
    moved = initial = None
    if with_moved:
        moved, *initial = refs[:3]
        refs = refs[3:]
    store_keys, store_values, *refs = refs
    results_ref, (key_buf, value_buf, *state) = refs[: 1 + raw], refs[1 + raw :]
    *work, columns, query_sem, out_buf, out_sem, sems = state
    kv_width = columns.shape[0]

    def query_copy(payload_ref):
        return pltpu.make_async_copy(payload_ref.at[:kv_width], columns, query_sem)

    def run():
        for payload_ref, hit in zip(payload_refs, choice):
            if len(choice) == 1:
                query_copy(payload_ref).start()
            else:
                pl.when(hit)(query_copy(payload_ref).start)
        count, ready = fetch(
            pool_size,
            tables,
            request,
            (store_keys, store_values),
            (key_buf, value_buf),
            sems,
            moved,
        )
        restore = None
        if initial is not None:

            def restore(*targets):
                return [
                    pltpu.make_async_copy(source, target, out_sem.at[i])
                    for i, (source, target) in enumerate(zip(initial, targets))
                ]

            for copy in restore(work[-1], work[2]):
                copy.start()
        query_copy(payload_refs[0]).wait()
        results = attend(
            key_buf, value_buf, count, ready, None, new_rows, columns, *work, restore, raw
        )
        if raw:
            copies = [
                pltpu.make_async_copy(result, out_ref, out_sem.at[i])
                for i, (out_ref, result) in enumerate(zip(results_ref, results))
            ]
            for copy in copies:
                copy.start()
            for copy in copies:
                copy.wait()
            return
        outs, logs = results
        tail = []
        copies = []

        def send_rows(start, size):
            copies.append(
                pltpu.make_async_copy(
                    out_buf.at[start : start + size],
                    results_ref[0].at[start : start + size],
                    out_sem.at[len(copies)],
                )
            )
            copies[-1].start()

        for kv, (out, log) in enumerate(zip(outs, logs)):
            out_buf[kv * HD : (kv + 1) * HD, :] = out.astype(jnp.bfloat16)
            send_rows(kv * HD, HD)
            high = log.astype(jnp.bfloat16).astype(jnp.float32)
            middle = (log - high).astype(jnp.bfloat16).astype(jnp.float32)
            tail += [high, middle, log - high - middle]
        tail.append(jnp.zeros((ONES - len(tail), columns.shape[1]), jnp.float32))
        out_buf[kv_width:, :] = jnp.concatenate(tail, axis=0).astype(jnp.bfloat16)
        send_rows(kv_width, ONES)
        for copy in copies:
            copy.wait()

    if len(choice) == 1 and choice[0] is not None:
        pl.when(choice[0])(run)
    else:
        run()


def is_inner(place):
    return (place == 1) | (place == 2)


def source_of(me, entry):
    if isinstance(entry, int):
        return jnp.bool_(True), jnp.int32(entry)
    inner = is_inner(me)
    masks = [0 if mask is None else mask for mask in entry]
    there = jnp.where(inner, entry[0] is not None, entry[1] is not None)
    return there, me ^ jnp.where(inner, masks[0], masks[1])


def push_kernel(pool_size, entries, owner_ref, *refs):
    payload_refs = refs[: len(entries)]
    key_out, value_out, sems = refs[len(entries) :]
    outs = (key_out, value_out)
    kv_width = key_out.shape[2]
    me = lax.axis_index("pool")
    total = jnp.int32(0)
    for other in range(pool_size):
        total += (owner_ref[other] == me).astype(jnp.int32)

    new_rows = key_out.shape[1]

    def copies(payload_ref, place):
        for i in range(2):
            for piece in range(new_rows // PIECE):
                row, lane = piece_place(i, piece, new_rows, kv_width)
                row += payload_ref.shape[0] - payload_rows(new_rows, kv_width)
                yield pltpu.make_async_copy(
                    payload_ref.at[row : row + PIECE, lane : lane + kv_width],
                    outs[i].at[place, piece * PIECE : (piece + 1) * PIECE],
                    sems.at[i, place, piece],
                )

    for entry, payload_ref in zip(entries, payload_refs):
        there, source = source_of(me, entry)
        rank = jnp.int32(0)
        for other in range(pool_size):
            rank += ((owner_ref[other] == me) & (other < source)).astype(jnp.int32)
        hit = there & (owner_ref[source] == me)
        for place in range(CAPP):

            @pl.when(hit & (rank == place))
            def _():
                for copy in copies(payload_ref, place):
                    copy.start()

    for place in range(CAPP):

        @pl.when(total <= place)
        def _():
            for out in outs:
                out[place] = jnp.zeros(out.shape[1:], jnp.bfloat16)

        @pl.when(total > place)
        def _():
            for copy in copies(payload_refs[0], place):
                copy.wait()


def combine_kernel(sources, last, own_ref, log_ref, *refs):
    parts = refs[: len(sources)]
    out_ref = refs[len(sources)]
    kv_width, rows = own_ref.shape
    me = lax.axis_index("pool")
    arrived = []
    tails = []
    for source, part in zip(sources, parts):
        there, request = source_of(me, source)
        arrived.append(there & (request != me))
        tails.append(part[kv_width:, :].astype(jnp.float32))
    if not last:
        refs[len(sources) + 1][...] = log_ref[...]
    for kv in range(kv_width // HD):
        logs = [log_ref[kv : kv + 1, :]]
        for there, tail in zip(arrived, tails):
            log = sum(tail[3 * kv + i : 3 * kv + i + 1] for i in range(3))
            logs.append(jnp.where(there, log, EMPTY))
        peak = functools.reduce(jnp.maximum, logs)
        shares = [jnp.exp(x - peak) for x in logs]
        total = functools.reduce(jnp.add, shares)
        shares = [x * (1.0 / total) for x in shares]
        band = slice(kv * HD, (kv + 1) * HD)
        for i in range(0, rows, TILE):
            part = slice(i, i + TILE)
            mixed = own_ref[band, part] * shares[0][:, part]
            for share, ref in zip(shares[1:], parts):
                mixed = mixed + ref[band, part].astype(jnp.float32) * share[:, part]
            if last:
                refs[len(sources) + 1][part, :] = mixed.astype(jnp.bfloat16).T
            else:
                out_ref[band, part] = mixed
        if last:
            turned = refs[len(sources) + 1]
            new_rows = out_ref.shape[0]
            for g in range(GROUP):
                head = kv * GROUP + g
                out_ref[:, head * HD : (head + 1) * HD] = turned[g * new_rows : (g + 1) * new_rows, :]
        else:
            refs[len(sources) + 1][kv : kv + 1, :] = peak + jnp.log(total)


def final_kernel(own_ref, log_ref, *refs):
    part_refs, (out_ref, buffer, turned, sems) = refs[:4], refs[4:]
    inner = is_inner(lax.axis_index("pool"))

    def copies(first):
        return [
            pltpu.make_async_copy(part_refs[first + i], buffer.at[i], sems.at[i]) for i in range(2)
        ]

    for hit, first in ((inner, 2), (jnp.logical_not(inner), 0)):

        @pl.when(hit)
        def _():
            for copy in copies(first):
                copy.start()

    for copy in copies(0):
        copy.wait()
    combine_kernel(
        [(1, 1), (2, 2)], True, own_ref, log_ref, buffer.at[0], buffer.at[1], out_ref, turned
    )


def shards(
    queries,
    new_keys,
    new_values,
    store_keys,
    store_values,
    prefix_blocks,
    hit_store,
    hit_slot,
    decode_owner,
):
    pool_size = lax.axis_size("pool")
    capacity = (MAXBLK + pool_size - 1) // pool_size
    new_rows = queries.shape[1]
    width = queries.shape[2]
    kv_width = new_keys.shape[2]
    block_len = store_keys.shape[1]
    rows = GROUP * new_rows
    tables = (prefix_blocks, hit_store, hit_slot)
    smem_spec = pl.BlockSpec(memory_space=pltpu.SMEM)
    hbm_spec = pl.BlockSpec(memory_space=pltpu.HBM)
    vmem_spec = pl.BlockSpec(memory_space=pltpu.VMEM)
    params = pltpu.CompilerParams(vmem_limit_bytes=VMEM_LIMIT)

    def cost(share):
        return pl.CostEstimate(
            flops=share * rows * block_len * kv_width * capacity,
            bytes_accessed=rows,
            transcendentals=0,
        )

    buffers = [pltpu.VMEM((capacity, block_len, kv_width), jnp.bfloat16)] * 2
    kv_local = kv_width // HD
    widest = block_len * min(2, capacity)
    work = [
        pltpu.VMEM((kv_local, widest, rows), jnp.float32),
        pltpu.VMEM((kv_local, widest, rows), jnp.bfloat16),
        pltpu.VMEM((kv_local, 8, rows), jnp.float32),
        pltpu.VMEM((kv_local, 8, rows), jnp.float32),
        pltpu.VMEM((kv_local, HD + ONES, widest), jnp.bfloat16),
        pltpu.VMEM((kv_local, HD + ONES, rows), jnp.float32),
    ]
    sems = pltpu.SemaphoreType.DMA((2, capacity))

    def own_part(payload):
        return pl.pallas_call(
            functools.partial(own_kernel, pool_size),
            in_specs=[smem_spec] * 3 + [vmem_spec] * 3 + [hbm_spec] * 2,
            out_specs=[vmem_spec] * 2,
            scratch_shapes=[
                *buffers,
                *[pltpu.VMEM((block_len, kv_width), jnp.bfloat16)] * 2,
                *work,
                sems,
            ],
            out_shape=[
                jax.ShapeDtypeStruct((kv_width, rows), jnp.float32),
                jax.ShapeDtypeStruct((8, rows), jnp.float32),
            ],
            compiler_params=params,
            cost_estimate=cost(8),
            name="own_part",
        )(*tables, payload, new_keys[0], new_values[0], store_keys, store_values)

    def other_part(partners, held, *request, share=8, moved=(), raw=False):
        if raw:
            out_shape = [
                jax.ShapeDtypeStruct((kv_local, HD + ONES, rows), jnp.float32),
                jax.ShapeDtypeStruct((kv_local, 8, rows), jnp.float32),
            ]
        else:
            out_shape = jax.ShapeDtypeStruct((kv_width + ONES, rows), jnp.bfloat16)
        more_specs = [hbm_spec] * 3 if moved else []
        return pl.pallas_call(
            functools.partial(other_kernel, pool_size, new_rows, partners, bool(moved), raw),
            in_specs=[smem_spec] * (3 + len(request))
            + [hbm_spec] * len(held)
            + more_specs
            + [hbm_spec] * 2,
            out_specs=[hbm_spec] * 2 if raw else hbm_spec,
            scratch_shapes=[
                *buffers,
                *work,
                pltpu.VMEM((kv_width, rows), jnp.bfloat16),
                pltpu.SemaphoreType.DMA,
                pltpu.VMEM((kv_width + ONES, rows), jnp.bfloat16),
                pltpu.SemaphoreType.DMA((max(2, kv_local + 1),)),
                sems,
            ],
            out_shape=out_shape,
            compiler_params=params,
            cost_estimate=cost(share),
            name="other_part",
        )(*request, *tables, *held, *moved, store_keys, store_values)

    def combine(own, log, sources, parts, last=True):
        if last:
            out_shape = jax.ShapeDtypeStruct((new_rows, width), jnp.bfloat16)
        else:
            out_shape = [
                jax.ShapeDtypeStruct((kv_width, rows), jnp.float32),
                jax.ShapeDtypeStruct((8, rows), jnp.float32),
            ]
        return pl.pallas_call(
            functools.partial(combine_kernel, tuple(sources), last),
            in_specs=[vmem_spec] * (2 + len(parts)),
            out_specs=vmem_spec if last else [vmem_spec] * 2,
            scratch_shapes=[pltpu.VMEM((rows, HD), jnp.bfloat16)] if last else [],
            out_shape=out_shape,
            compiler_params=params,
            cost_estimate=cost(0),
            name="combine",
        )(own, log, *parts)

    def final(own, log, parts):
        return pl.pallas_call(
            final_kernel,
            in_specs=[vmem_spec] * 2 + [hbm_spec] * 4,
            out_specs=vmem_spec,
            scratch_shapes=[
                pltpu.VMEM((2, kv_width + ONES, rows), jnp.bfloat16),
                pltpu.VMEM((rows, HD), jnp.bfloat16),
                pltpu.SemaphoreType.DMA((2,)),
            ],
            out_shape=jax.ShapeDtypeStruct((new_rows, width), jnp.bfloat16),
            compiler_params=params,
            name="final",
        )(own, log, *parts)

    payload = pl.pallas_call(
        prepare_kernel,
        in_specs=[vmem_spec] * 3,
        out_specs=vmem_spec,
        scratch_shapes=[pltpu.VMEM((rows, HD), jnp.bfloat16)],
        out_shape=jax.ShapeDtypeStruct((payload_rows(new_rows, kv_width), rows), jnp.bfloat16),
        compiler_params=params,
        name="prepare",
    )(queries[0], new_keys[0], new_values[0])
    own_out, own_log = own_part(payload)
    if pool_size == 4:
        def send(array, *pairs):
            return lax.ppermute(array, "pool", pairs)

        near = send(payload, (0, 1), (1, 0), (2, 3), (3, 2))
        middle = send(payload, (1, 2), (2, 1))
        blocks = pl.pallas_call(
            functools.partial(gather_kernel, pool_size),
            in_specs=[smem_spec] * 3 + [hbm_spec] * 2,
            out_specs=vmem_spec,
            scratch_shapes=[sems],
            out_shape=jax.ShapeDtypeStruct((2 * capacity, block_len, kv_width), jnp.bfloat16),
            compiler_params=params,
            name="gather_blocks",
        )(*tables, store_keys, store_values)
        blocks = send(blocks, (0, 1), (3, 2))
        near, middle, own_out, own_log = lax.optimization_barrier((near, middle, own_out, own_log))
        crossed = send(near, (1, 2), (2, 1))
        outward = send(middle, (1, 0), (2, 3))
        first = other_part((3, 1), (middle, near))
        across = send(first, (1, 2), (2, 1))
        near, first = lax.optimization_barrier((near, first))
        second = other_part((1, None), (near,))
        back = send(second, (1, 0), (2, 3))
        outward, second = lax.optimization_barrier((outward, second))
        outer_second = other_part((None, 2), (outward,))
        apart = send(outer_second, (0, 2), (3, 1))
        crossed, first, outer_second = lax.optimization_barrier((crossed, first, outer_second))
        inward = send(first, (0, 1), (3, 2))
        state = other_part((2, None), (crossed,), raw=True)
        crossed, state = lax.optimization_barrier((crossed, state))
        far = send(crossed[kv_width:], (1, 0), (2, 3))
        third = other_part((2, None), (crossed,), moved=(blocks, *state))
        ends = send(third, (1, 3), (2, 0))
        own_out, own_log, third = lax.optimization_barrier((own_out, own_log, third))
        own_out, own_log = combine(own_out, own_log, [(3, None)], [across], last=False)
        attended = final(own_out, own_log, (back, ends, apart, inward))
        moved = [
            ((0, 0), payload),
            ((1, 1), near),
            ((3, None), middle),
            ((2, None), crossed),
            ((None, 2), outward),
            ((None, 3), far),
        ]
    else:
        gathered = lax.all_gather(payload, "pool", axis=0, tiled=False)
        packed = lax.map(
            lambda pair: other_part(None, (pair[0],), pair[1].reshape(1)),
            (gathered, jnp.arange(pool_size, dtype=jnp.int32)),
        )
        parts = lax.all_to_all(packed, "pool", split_axis=0, concat_axis=0, tiled=True)
        attended = combine(own_out, own_log, list(range(pool_size)), parts)
        moved = [(source, gathered[source]) for source in range(pool_size)]

    pushed_keys, pushed_values = pl.pallas_call(
        functools.partial(push_kernel, pool_size, tuple(entry for entry, _ in moved)),
        in_specs=[smem_spec] + [hbm_spec] * len(moved),
        out_specs=[vmem_spec] * 2,
        scratch_shapes=[pltpu.SemaphoreType.DMA((2, CAPP, new_rows // PIECE))],
        out_shape=[jax.ShapeDtypeStruct((CAPP, new_rows, kv_width), jnp.bfloat16)] * 2,
        compiler_params=params,
        name="push",
    )(decode_owner, *[array for _, array in moved])
    return (attended[None], pushed_keys, pushed_values)


def solution(mesh):
    in_specs = (
        P(("groups", "pool"), None, ("tensor", "sub")),
        P(("groups", "pool"), None, ("tensor", "sub")),
        P(("groups", "pool"), None, ("tensor", "sub")),
        P(("groups", "pool"), None, ("tensor", "sub")),
        P(("groups", "pool"), None, ("tensor", "sub")),
        P("groups"),
        P("groups", None),
        P("groups", None),
        P("groups"),
    )
    out_specs = (
        P(("groups", "pool"), None, ("tensor", "sub")),
        P(("groups", "pool"), None, ("tensor", "sub")),
        P(("groups", "pool"), None, ("tensor", "sub")),
    )
    return jax.shard_map(shards, mesh=mesh, in_specs=in_specs, out_specs=out_specs, check_vma=False)
```

```python
import functools
import math

import jax
import jax.numpy as jnp
from jax import lax
from jax.experimental import pallas as pl
from jax.experimental.pallas import tpu as pltpu
from jax.sharding import PartitionSpec as P

HEADS = 64
KVH = 8
HD = 128
MAXBLK = 32
CAPP = 2
GROUP = HEADS // KVH
EMPTY = -1e30
TILE = 256
ONES = 16
PIECE = 32
EXP2_SCALE = math.log2(math.e) / math.sqrt(HD)
VMEM_LIMIT = 63 * 1024 * 1024 + 512 * 1024


def blocks_at(tables, request, place, pool_size):
    prefix_ref, store_ref, slot_ref = tables
    first = lax.rem(place - store_ref[request, 0] + pool_size, pool_size)
    count = lax.max(lax.div(prefix_ref[request] - first + pool_size - 1, pool_size), 0)
    return count, lambda entry: slot_ref[request, first + entry * pool_size]


def fetch(pool_size, tables, request, stores, buffers, sems, moved=None):
    me = lax.axis_index("pool")
    count, slot_of = blocks_at(tables, request, me if moved is None else me ^ 1, pool_size)

    def copies(entry):
        for i in range(2):
            if moved is None:
                source = stores[i].at[slot_of(entry)]
            else:
                source = moved.at[i * (moved.shape[0] // 2) + entry]
            yield pltpu.make_async_copy(source, buffers[i].at[entry], sems.at[i, entry])

    def start(entry, carry):
        for copy in copies(entry):
            copy.start()
        return carry

    lax.fori_loop(0, count, start, 0)

    def ready(entry):
        for copy in copies(entry):
            copy.wait()

    return count, ready


def gather_kernel(pool_size, prefix_ref, store_ref, slot_ref, store_keys, store_values, out_ref, sems):
    me = lax.axis_index("pool")
    capacity = out_ref.shape[0] // 2

    @pl.when(jnp.logical_not(is_inner(me)))
    def _():
        tables = (prefix_ref, store_ref, slot_ref)
        count, slot_of = blocks_at(tables, me ^ 3, me, pool_size)

        def copies(entry):
            return [
                pltpu.make_async_copy(
                    store.at[slot_of(entry)], out_ref.at[i * capacity + entry], sems.at[i, entry]
                )
                for i, store in enumerate((store_keys, store_values))
            ]

        def start(entry, carry):
            for copy in copies(entry):
                copy.start()
            return carry

        def wait(entry, carry):
            for copy in copies(entry):
                copy.wait()
            return carry

        lax.fori_loop(0, count, start, 0)
        lax.fori_loop(0, count, wait, 0)


def attend(
    key_ref,
    value_ref,
    count,
    ready,
    fresh,
    new_rows,
    columns,
    scores,
    weights,
    peaks,
    factors,
    tops,
    turned,
    acc,
    initial=None,
    raw=False,
):
    rows = columns.shape[1]
    kv_local = columns.shape[0] // HD

    def visit(keys, values, seen):
        size = keys[0].shape[0]

        def score(kv):
            turned[kv, :HD, :size] = values[kv].T
            block = lax.dot_general(
                keys[kv],
                columns[kv * HD : (kv + 1) * HD, :],
                (((1,), (0,)), ((), ())),
                preferred_element_type=jnp.float32,
            )
            block = block * EXP2_SCALE
            if seen is not None:
                block = jnp.where(seen, block, EMPTY)
            scores[kv, :size, :] = block
            tops[kv] = jnp.max(block.reshape(size // 8, 8, rows), axis=0)

        def weigh(kv):
            for i in range(0, rows, TILE):
                part = slice(i, i + TILE)
                before = peaks[kv, :, part]
                top = jnp.max(tops[kv, :, part], axis=0, keepdims=True)
                peak = jnp.maximum(before, top)
                factors[kv, :, part] = jnp.exp2(before - peak)
                peaks[kv, :, part] = peak
                weight = jnp.exp2(scores[kv, :size, part] - peak[0:1])
                weights[kv, :size, part] = weight.astype(jnp.bfloat16)

        def mix(kv):
            added = lax.dot_general(
                turned[kv, :, :size],
                weights[kv, :size, :],
                (((1,), (0,)), ((), ())),
                preferred_element_type=jnp.float32,
            )
            acc[kv] = acc[kv] * factors[kv, 0:1, :] + added

        for step in range(kv_local + 2):
            for offset, stage in ((0, score), (2, mix), (1, weigh)):
                if 0 <= step - offset < kv_local:
                    stage(step - offset)

    def lanes_of(array):
        return [array[:, kv * HD : (kv + 1) * HD] for kv in range(kv_local)]

    def blocks_of(ref, first, number):
        return lanes_of(ref[pl.ds(first, number)].reshape(number * ref.shape[1], ref.shape[2]))

    if initial is None:
        peaks[...] = jnp.full(peaks.shape, EMPTY, jnp.float32)
        acc[...] = jnp.zeros(acc.shape, jnp.float32)
    else:
        for copy in initial(acc, peaks):
            copy.wait()
    turned[:, HD:, :] = jnp.ones((kv_local, ONES, turned.shape[2]), jnp.bfloat16)
    if fresh is not None:
        new_key_ref, new_value_ref = fresh
        row = lax.rem(lax.broadcasted_iota(jnp.int32, (1, rows), 1), new_rows)
        seen = lax.broadcasted_iota(jnp.int32, (new_key_ref.shape[0], rows), 0) <= row
        visit(lanes_of(new_key_ref), lanes_of(new_value_ref), seen)

    def visit_blocks(number):
        def body(index, carry):
            for i in range(number):
                ready(index * number + i)
            visit(
                blocks_of(key_ref, index * number, number),
                blocks_of(value_ref, index * number, number),
                None,
            )
            return carry

        return body

    pairs = count // 2 if key_ref.shape[0] > 1 else 0
    if key_ref.shape[0] > 1:
        lax.fori_loop(0, pairs, visit_blocks(2), 0)
    lax.fori_loop(2 * pairs, count, visit_blocks(1), 0)
    if raw:
        return acc, peaks
    outs = []
    logs = []
    for kv in range(kv_local):
        total = acc[kv, HD : HD + 1, :]
        safe = jnp.where(total > 0, total, 1.0)
        logs.append(jnp.where(total > 0, peaks[kv, 0:1] * math.log(2.0) + jnp.log(safe), EMPTY))
        outs.append(acc[kv, :HD, :] * (1.0 / safe))
    return outs, logs


def prepare_kernel(query_ref, new_key_ref, new_value_ref, payload_ref, query_rows):
    new_rows = query_ref.shape[0]
    kv_width = new_key_ref.shape[1]
    for kv in range(kv_width // HD):
        for g in range(GROUP):
            head = kv * GROUP + g
            query_rows[g * new_rows : (g + 1) * new_rows, :] = query_ref[
                :, head * HD : (head + 1) * HD
            ]
        payload_ref[kv * HD : (kv + 1) * HD, :] = query_rows[...].T
    for i, new_ref in enumerate((new_key_ref, new_value_ref)):
        for piece in range(new_rows // PIECE):
            row, lane = piece_place(i, piece, new_rows, kv_width)
            payload_ref[row : row + PIECE, lane : lane + kv_width] = new_ref[
                piece * PIECE : (piece + 1) * PIECE, :
            ]


def piece_place(i, piece, new_rows, kv_width):
    index = i * (new_rows // PIECE) + piece
    beside = GROUP * new_rows // kv_width
    return kv_width + index // beside * PIECE, index % beside * kv_width


def payload_rows(new_rows, kv_width):
    return piece_place(1, new_rows // PIECE - 1, new_rows, kv_width)[0] + PIECE


def own_kernel(
    pool_size,
    prefix_ref,
    store_ref,
    slot_ref,
    payload_ref,
    new_key_ref,
    new_value_ref,
    store_keys,
    store_values,
    out_ref,
    log_ref,
    key_buf,
    value_buf,
    new_key_buf,
    new_value_buf,
    *state,
):
    *work, sems = state
    count, ready = fetch(
        pool_size,
        (prefix_ref, store_ref, slot_ref),
        lax.axis_index("pool"),
        (store_keys, store_values),
        (key_buf, value_buf),
        sems,
    )
    new_rows, kv_width = new_key_ref.shape
    for buffer, source in ((new_key_buf, new_key_ref), (new_value_buf, new_value_ref)):
        buffer[:new_rows, :] = source[...]
        buffer[new_rows:, :] = jnp.zeros((buffer.shape[0] - new_rows, kv_width), jnp.bfloat16)
    fresh = (new_key_buf, new_value_buf)
    outs, logs = attend(
        key_buf, value_buf, count, ready, fresh, new_rows, payload_ref.at[:kv_width], *work
    )
    log_ref[...] = jnp.zeros(log_ref.shape, jnp.float32)
    for kv, (out, log) in enumerate(zip(outs, logs)):
        out_ref[kv * HD : (kv + 1) * HD, :] = out
        log_ref[kv : kv + 1, :] = log


def other_kernel(pool_size, new_rows, partners, with_moved, raw, *refs):
    if partners is None:
        request = refs[0][0]
        choice = [None]
        refs = refs[1:]
    else:
        inner = is_inner(lax.axis_index("pool"))
        _, request = source_of(lax.axis_index("pool"), partners)
        choice = [
            hit for hit, mask in zip((inner, jnp.logical_not(inner)), partners) if mask is not None
        ]
    tables, refs = refs[:3], refs[3:]
    payload_refs, refs = refs[: len(choice)], refs[len(choice) :]
    moved = initial = None
    if with_moved:
        moved, *initial = refs[:3]
        refs = refs[3:]
    store_keys, store_values, *refs = refs
    results_ref, (key_buf, value_buf, *state) = refs[: 1 + raw], refs[1 + raw :]
    *work, columns, query_sem, out_buf, out_sem, sems = state
    kv_width = columns.shape[0]

    def query_copy(payload_ref):
        return pltpu.make_async_copy(payload_ref.at[:kv_width], columns, query_sem)

    def run():
        for payload_ref, hit in zip(payload_refs, choice):
            if len(choice) == 1:
                query_copy(payload_ref).start()
            else:
                pl.when(hit)(query_copy(payload_ref).start)
        count, ready = fetch(
            pool_size,
            tables,
            request,
            (store_keys, store_values),
            (key_buf, value_buf),
            sems,
            moved,
        )
        restore = None
        if initial is not None:

            def restore(*targets):
                return [
                    pltpu.make_async_copy(source, target, out_sem.at[i])
                    for i, (source, target) in enumerate(zip(initial, targets))
                ]

            for copy in restore(work[-1], work[2]):
                copy.start()
        query_copy(payload_refs[0]).wait()
        results = attend(
            key_buf, value_buf, count, ready, None, new_rows, columns, *work, restore, raw
        )
        if raw:
            copies = [
                pltpu.make_async_copy(result, out_ref, out_sem.at[i])
                for i, (out_ref, result) in enumerate(zip(results_ref, results))
            ]
            for copy in copies:
                copy.start()
            for copy in copies:
                copy.wait()
            return
        outs, logs = results
        tail = []
        copies = []

        def send_rows(start, size):
            copies.append(
                pltpu.make_async_copy(
                    out_buf.at[start : start + size],
                    results_ref[0].at[start : start + size],
                    out_sem.at[len(copies)],
                )
            )
            copies[-1].start()

        for kv, (out, log) in enumerate(zip(outs, logs)):
            out_buf[kv * HD : (kv + 1) * HD, :] = out.astype(jnp.bfloat16)
            send_rows(kv * HD, HD)
            high = log.astype(jnp.bfloat16).astype(jnp.float32)
            middle = (log - high).astype(jnp.bfloat16).astype(jnp.float32)
            tail += [high, middle, log - high - middle]
        tail.append(jnp.zeros((ONES - len(tail), columns.shape[1]), jnp.float32))
        out_buf[kv_width:, :] = jnp.concatenate(tail, axis=0).astype(jnp.bfloat16)
        send_rows(kv_width, ONES)
        for copy in copies:
            copy.wait()

    if len(choice) == 1 and choice[0] is not None:
        pl.when(choice[0])(run)
    else:
        run()


def is_inner(place):
    return (place == 1) | (place == 2)


def source_of(me, entry):
    if isinstance(entry, int):
        return jnp.bool_(True), jnp.int32(entry)
    inner = is_inner(me)
    masks = [0 if mask is None else mask for mask in entry]
    there = jnp.where(inner, entry[0] is not None, entry[1] is not None)
    return there, me ^ jnp.where(inner, masks[0], masks[1])


def push_kernel(pool_size, entries, owner_ref, *refs):
    payload_refs = refs[: len(entries)]
    key_out, value_out, sems = refs[len(entries) :]
    outs = (key_out, value_out)
    kv_width = key_out.shape[2]
    me = lax.axis_index("pool")
    total = jnp.int32(0)
    for other in range(pool_size):
        total += (owner_ref[other] == me).astype(jnp.int32)

    new_rows = key_out.shape[1]

    def copies(payload_ref, place):
        for i in range(2):
            for piece in range(new_rows // PIECE):
                row, lane = piece_place(i, piece, new_rows, kv_width)
                row += payload_ref.shape[0] - payload_rows(new_rows, kv_width)
                yield pltpu.make_async_copy(
                    payload_ref.at[row : row + PIECE, lane : lane + kv_width],
                    outs[i].at[place, piece * PIECE : (piece + 1) * PIECE],
                    sems.at[i, place, piece],
                )

    for entry, payload_ref in zip(entries, payload_refs):
        there, source = source_of(me, entry)
        rank = jnp.int32(0)
        for other in range(pool_size):
            rank += ((owner_ref[other] == me) & (other < source)).astype(jnp.int32)
        hit = there & (owner_ref[source] == me)
        for place in range(CAPP):

            @pl.when(hit & (rank == place))
            def _():
                for copy in copies(payload_ref, place):
                    copy.start()

    for place in range(CAPP):

        @pl.when(total <= place)
        def _():
            for out in outs:
                out[place] = jnp.zeros(out.shape[1:], jnp.bfloat16)

        @pl.when(total > place)
        def _():
            for copy in copies(payload_refs[0], place):
                copy.wait()


def combine_kernel(sources, last, own_ref, log_ref, *refs):
    parts = refs[: len(sources)]
    out_ref = refs[len(sources)]
    kv_width, rows = own_ref.shape
    me = lax.axis_index("pool")
    arrived = []
    tails = []
    for source, part in zip(sources, parts):
        there, request = source_of(me, source)
        arrived.append(there & (request != me))
        tails.append(part[kv_width:, :].astype(jnp.float32))
    if not last:
        refs[len(sources) + 1][...] = log_ref[...]
    for kv in range(kv_width // HD):
        logs = [log_ref[kv : kv + 1, :]]
        for there, tail in zip(arrived, tails):
            log = sum(tail[3 * kv + i : 3 * kv + i + 1] for i in range(3))
            logs.append(jnp.where(there, log, EMPTY))
        peak = functools.reduce(jnp.maximum, logs)
        shares = [jnp.exp(x - peak) for x in logs]
        total = functools.reduce(jnp.add, shares)
        shares = [x * (1.0 / total) for x in shares]
        band = slice(kv * HD, (kv + 1) * HD)
        for i in range(0, rows, TILE):
            part = slice(i, i + TILE)
            mixed = own_ref[band, part] * shares[0][:, part]
            for share, ref in zip(shares[1:], parts):
                mixed = mixed + ref[band, part].astype(jnp.float32) * share[:, part]
            if last:
                refs[len(sources) + 1][part, :] = mixed.astype(jnp.bfloat16).T
            else:
                out_ref[band, part] = mixed
        if last:
            turned = refs[len(sources) + 1]
            new_rows = out_ref.shape[0]
            for g in range(GROUP):
                head = kv * GROUP + g
                out_ref[:, head * HD : (head + 1) * HD] = turned[g * new_rows : (g + 1) * new_rows, :]
        else:
            refs[len(sources) + 1][kv : kv + 1, :] = peak + jnp.log(total)


def final_kernel(own_ref, log_ref, *refs):
    part_refs, (out_ref, buffer, turned, sems) = refs[:4], refs[4:]
    inner = is_inner(lax.axis_index("pool"))

    def copies(first):
        return [
            pltpu.make_async_copy(part_refs[first + i], buffer.at[i], sems.at[i]) for i in range(2)
        ]

    for hit, first in ((inner, 2), (jnp.logical_not(inner), 0)):

        @pl.when(hit)
        def _():
            for copy in copies(first):
                copy.start()

    for copy in copies(0):
        copy.wait()
    combine_kernel(
        [(1, 1), (2, 2)], True, own_ref, log_ref, buffer.at[0], buffer.at[1], out_ref, turned
    )


def shards(
    queries,
    new_keys,
    new_values,
    store_keys,
    store_values,
    prefix_blocks,
    hit_store,
    hit_slot,
    decode_owner,
):
    pool_size = lax.axis_size("pool")
    capacity = (MAXBLK + pool_size - 1) // pool_size
    new_rows = queries.shape[1]
    width = queries.shape[2]
    kv_width = new_keys.shape[2]
    block_len = store_keys.shape[1]
    rows = GROUP * new_rows
    tables = (prefix_blocks, hit_store, hit_slot)
    smem_spec = pl.BlockSpec(memory_space=pltpu.SMEM)
    hbm_spec = pl.BlockSpec(memory_space=pltpu.HBM)
    vmem_spec = pl.BlockSpec(memory_space=pltpu.VMEM)
    params = pltpu.CompilerParams(vmem_limit_bytes=VMEM_LIMIT)

    def cost(share):
        return pl.CostEstimate(
            flops=share * rows * block_len * kv_width * capacity,
            bytes_accessed=rows,
            transcendentals=0,
        )

    buffers = [pltpu.VMEM((capacity, block_len, kv_width), jnp.bfloat16)] * 2
    kv_local = kv_width // HD
    widest = block_len * min(2, capacity)
    work = [
        pltpu.VMEM((kv_local, widest, rows), jnp.float32),
        pltpu.VMEM((kv_local, widest, rows), jnp.bfloat16),
        pltpu.VMEM((kv_local, 8, rows), jnp.float32),
        pltpu.VMEM((kv_local, 8, rows), jnp.float32),
        pltpu.VMEM((kv_local, 8, rows), jnp.float32),
        pltpu.VMEM((kv_local, HD + ONES, widest), jnp.bfloat16),
        pltpu.VMEM((kv_local, HD + ONES, rows), jnp.float32),
    ]
    sems = pltpu.SemaphoreType.DMA((2, capacity))

    def own_part(payload):
        return pl.pallas_call(
            functools.partial(own_kernel, pool_size),
            in_specs=[smem_spec] * 3 + [vmem_spec] * 3 + [hbm_spec] * 2,
            out_specs=[vmem_spec] * 2,
            scratch_shapes=[
                *buffers,
                *[pltpu.VMEM((block_len, kv_width), jnp.bfloat16)] * 2,
                *work,
                sems,
            ],
            out_shape=[
                jax.ShapeDtypeStruct((kv_width, rows), jnp.float32),
                jax.ShapeDtypeStruct((8, rows), jnp.float32),
            ],
            compiler_params=params,
            cost_estimate=cost(8),
            name="own_part",
        )(*tables, payload, new_keys[0], new_values[0], store_keys, store_values)

    def other_part(partners, held, *request, share=8, moved=(), raw=False):
        if raw:
            out_shape = [
                jax.ShapeDtypeStruct((kv_local, HD + ONES, rows), jnp.float32),
                jax.ShapeDtypeStruct((kv_local, 8, rows), jnp.float32),
            ]
        else:
            out_shape = jax.ShapeDtypeStruct((kv_width + ONES, rows), jnp.bfloat16)
        more_specs = [hbm_spec] * 3 if moved else []
        return pl.pallas_call(
            functools.partial(other_kernel, pool_size, new_rows, partners, bool(moved), raw),
            in_specs=[smem_spec] * (3 + len(request))
            + [hbm_spec] * len(held)
            + more_specs
            + [hbm_spec] * 2,
            out_specs=[hbm_spec] * 2 if raw else hbm_spec,
            scratch_shapes=[
                *buffers,
                *work,
                pltpu.VMEM((kv_width, rows), jnp.bfloat16),
                pltpu.SemaphoreType.DMA,
                pltpu.VMEM((kv_width + ONES, rows), jnp.bfloat16),
                pltpu.SemaphoreType.DMA((max(2, kv_local + 1),)),
                sems,
            ],
            out_shape=out_shape,
            compiler_params=params,
            cost_estimate=cost(share),
            name="other_part",
        )(*request, *tables, *held, *moved, store_keys, store_values)

    def combine(own, log, sources, parts, last=True):
        if last:
            out_shape = jax.ShapeDtypeStruct((new_rows, width), jnp.bfloat16)
        else:
            out_shape = [
                jax.ShapeDtypeStruct((kv_width, rows), jnp.float32),
                jax.ShapeDtypeStruct((8, rows), jnp.float32),
            ]
        return pl.pallas_call(
            functools.partial(combine_kernel, tuple(sources), last),
            in_specs=[vmem_spec] * (2 + len(parts)),
            out_specs=vmem_spec if last else [vmem_spec] * 2,
            scratch_shapes=[pltpu.VMEM((rows, HD), jnp.bfloat16)] if last else [],
            out_shape=out_shape,
            compiler_params=params,
            cost_estimate=cost(0),
            name="combine",
        )(own, log, *parts)

    def final(own, log, parts):
        return pl.pallas_call(
            final_kernel,
            in_specs=[vmem_spec] * 2 + [hbm_spec] * 4,
            out_specs=vmem_spec,
            scratch_shapes=[
                pltpu.VMEM((2, kv_width + ONES, rows), jnp.bfloat16),
                pltpu.VMEM((rows, HD), jnp.bfloat16),
                pltpu.SemaphoreType.DMA((2,)),
            ],
            out_shape=jax.ShapeDtypeStruct((new_rows, width), jnp.bfloat16),
            compiler_params=params,
            name="final",
        )(own, log, *parts)

    payload = pl.pallas_call(
        prepare_kernel,
        in_specs=[vmem_spec] * 3,
        out_specs=vmem_spec,
        scratch_shapes=[pltpu.VMEM((rows, HD), jnp.bfloat16)],
        out_shape=jax.ShapeDtypeStruct((payload_rows(new_rows, kv_width), rows), jnp.bfloat16),
        compiler_params=params,
        name="prepare",
    )(queries[0], new_keys[0], new_values[0])
    own_out, own_log = own_part(payload)
    if pool_size == 4:
        def send(array, *pairs):
            return lax.ppermute(array, "pool", pairs)

        near = send(payload, (0, 1), (1, 0), (2, 3), (3, 2))
        middle = send(payload, (1, 2), (2, 1))
        blocks = pl.pallas_call(
            functools.partial(gather_kernel, pool_size),
            in_specs=[smem_spec] * 3 + [hbm_spec] * 2,
            out_specs=vmem_spec,
            scratch_shapes=[sems],
            out_shape=jax.ShapeDtypeStruct((2 * capacity, block_len, kv_width), jnp.bfloat16),
            compiler_params=params,
            name="gather_blocks",
        )(*tables, store_keys, store_values)
        blocks = send(blocks, (0, 1), (3, 2))
        near, middle, own_out, own_log = lax.optimization_barrier((near, middle, own_out, own_log))
        crossed = send(near, (1, 2), (2, 1))
        outward = send(middle, (1, 0), (2, 3))
        first = other_part((3, 1), (middle, near))
        across = send(first, (1, 2), (2, 1))
        near, first = lax.optimization_barrier((near, first))
        second = other_part((1, None), (near,))
        back = send(second, (1, 0), (2, 3))
        outward, second = lax.optimization_barrier((outward, second))
        outer_second = other_part((None, 2), (outward,))
        apart = send(outer_second, (0, 2), (3, 1))
        crossed, first, outer_second = lax.optimization_barrier((crossed, first, outer_second))
        inward = send(first, (0, 1), (3, 2))
        state = other_part((2, None), (crossed,), raw=True)
        crossed, state = lax.optimization_barrier((crossed, state))
        far = send(crossed[kv_width:], (1, 0), (2, 3))
        third = other_part((2, None), (crossed,), moved=(blocks, *state))
        ends = send(third, (1, 3), (2, 0))
        own_out, own_log, third = lax.optimization_barrier((own_out, own_log, third))
        own_out, own_log = combine(own_out, own_log, [(3, None)], [across], last=False)
        attended = final(own_out, own_log, (back, ends, apart, inward))
        moved = [
            ((0, 0), payload),
            ((1, 1), near),
            ((3, None), middle),
            ((2, None), crossed),
            ((None, 2), outward),
            ((None, 3), far),
        ]
    else:
        gathered = lax.all_gather(payload, "pool", axis=0, tiled=False)
        packed = lax.map(
            lambda pair: other_part(None, (pair[0],), pair[1].reshape(1)),
            (gathered, jnp.arange(pool_size, dtype=jnp.int32)),
        )
        parts = lax.all_to_all(packed, "pool", split_axis=0, concat_axis=0, tiled=True)
        attended = combine(own_out, own_log, list(range(pool_size)), parts)
        moved = [(source, gathered[source]) for source in range(pool_size)]

    pushed_keys, pushed_values = pl.pallas_call(
        functools.partial(push_kernel, pool_size, tuple(entry for entry, _ in moved)),
        in_specs=[smem_spec] + [hbm_spec] * len(moved),
        out_specs=[vmem_spec] * 2,
        scratch_shapes=[pltpu.SemaphoreType.DMA((2, CAPP, new_rows // PIECE))],
        out_shape=[jax.ShapeDtypeStruct((CAPP, new_rows, kv_width), jnp.bfloat16)] * 2,
        compiler_params=params,
        name="push",
    )(decode_owner, *[array for _, array in moved])
    return (attended[None], pushed_keys, pushed_values)


def solution(mesh):
    in_specs = (
        P(("groups", "pool"), None, ("tensor", "sub")),
        P(("groups", "pool"), None, ("tensor", "sub")),
        P(("groups", "pool"), None, ("tensor", "sub")),
        P(("groups", "pool"), None, ("tensor", "sub")),
        P(("groups", "pool"), None, ("tensor", "sub")),
        P("groups"),
        P("groups", None),
        P("groups", None),
        P("groups"),
    )
    out_specs = (
        P(("groups", "pool"), None, ("tensor", "sub")),
        P(("groups", "pool"), None, ("tensor", "sub")),
        P(("groups", "pool"), None, ("tensor", "sub")),
    )
    return jax.shard_map(shards, mesh=mesh, in_specs=in_specs, out_specs=out_specs, check_vma=False)
```

```python
import functools
import math

import jax
import jax.numpy as jnp
from jax import lax
from jax.experimental import pallas as pl
from jax.experimental.pallas import tpu as pltpu
from jax.sharding import PartitionSpec as P

HEADS = 64
KVH = 8
HD = 128
MAXBLK = 32
CAPP = 2
GROUP = HEADS // KVH
EMPTY = -1e30
TILE = 256
ONES = 16
PIECE = 32
EXP2_SCALE = math.log2(math.e) / math.sqrt(HD)
VMEM_LIMIT = 63 * 1024 * 1024 + 512 * 1024


def blocks_at(tables, request, place, pool_size):
    prefix_ref, store_ref, slot_ref = tables
    first = lax.rem(place - store_ref[request, 0] + pool_size, pool_size)
    count = lax.max(lax.div(prefix_ref[request] - first + pool_size - 1, pool_size), 0)
    return count, lambda entry: slot_ref[request, first + entry * pool_size]


def fetch(pool_size, tables, request, stores, buffers, sems, moved=None):
    me = lax.axis_index("pool")
    count, slot_of = blocks_at(tables, request, me if moved is None else me ^ 1, pool_size)

    def copies(entry):
        for i in range(2):
            if moved is None:
                source = stores[i].at[slot_of(entry)]
            else:
                source = moved.at[i * (moved.shape[0] // 2) + entry]
            yield pltpu.make_async_copy(source, buffers[i].at[entry], sems.at[i, entry])

    def start(entry, carry):
        for copy in copies(entry):
            copy.start()
        return carry

    lax.fori_loop(0, count, start, 0)

    def ready(entry):
        for copy in copies(entry):
            copy.wait()

    return count, ready


def gather_kernel(pool_size, prefix_ref, store_ref, slot_ref, store_keys, store_values, out_ref, sems):
    me = lax.axis_index("pool")
    capacity = out_ref.shape[0] // 2

    @pl.when(jnp.logical_not(is_inner(me)))
    def _():
        tables = (prefix_ref, store_ref, slot_ref)
        count, slot_of = blocks_at(tables, me ^ 3, me, pool_size)

        def copies(entry):
            return [
                pltpu.make_async_copy(
                    store.at[slot_of(entry)], out_ref.at[i * capacity + entry], sems.at[i, entry]
                )
                for i, store in enumerate((store_keys, store_values))
            ]

        def start(entry, carry):
            for copy in copies(entry):
                copy.start()
            return carry

        def wait(entry, carry):
            for copy in copies(entry):
                copy.wait()
            return carry

        lax.fori_loop(0, count, start, 0)
        lax.fori_loop(0, count, wait, 0)


def attend(
    key_ref,
    value_ref,
    count,
    ready,
    fresh,
    new_rows,
    columns,
    scores,
    weights,
    peaks,
    factors,
    tops,
    turned,
    acc,
    initial=None,
    raw=False,
):
    rows = columns.shape[1]
    kv_local = columns.shape[0] // HD

    def visit(keys, values, seen):
        size = keys[0].shape[0]

        def score(kv):
            turned[kv, :HD, :size] = values[kv].T
            block = lax.dot_general(
                keys[kv],
                columns[kv * HD : (kv + 1) * HD, :],
                (((1,), (0,)), ((), ())),
                preferred_element_type=jnp.float32,
            )
            block = block * EXP2_SCALE
            if seen is not None:
                block = jnp.where(seen, block, EMPTY)
            scores[kv, :size, :] = block
            tops[kv] = jnp.max(block.reshape(size // 8, 8, rows), axis=0)

        def weigh(kv):
            for i in range(0, rows, TILE):
                part = slice(i, i + TILE)
                before = peaks[kv, :, part]
                top = jnp.max(tops[kv, :, part], axis=0, keepdims=True)
                peak = jnp.maximum(before, top)
                factors[kv, :, part] = jnp.exp2(before - peak)
                peaks[kv, :, part] = peak
                weight = jnp.exp2(scores[kv, :size, part] - peak[0:1])
                weights[kv, :size, part] = weight.astype(jnp.bfloat16)

        def mix(kv):
            added = lax.dot_general(
                turned[kv, :, :size],
                weights[kv, :size, :],
                (((1,), (0,)), ((), ())),
                preferred_element_type=jnp.float32,
            )
            acc[kv] = acc[kv] * factors[kv, 0:1, :] + added

        for step in range(kv_local + 2):
            for offset, stage in ((0, score), (2, mix), (1, weigh)):
                if 0 <= step - offset < kv_local:
                    stage(step - offset)

    def lanes_of(array):
        return [array[:, kv * HD : (kv + 1) * HD] for kv in range(kv_local)]

    def blocks_of(ref, first, number):
        return lanes_of(ref[pl.ds(first, number)].reshape(number * ref.shape[1], ref.shape[2]))

    if initial is None:
        peaks[...] = jnp.full(peaks.shape, EMPTY, jnp.float32)
        acc[...] = jnp.zeros(acc.shape, jnp.float32)
    else:
        for copy in initial(acc, peaks):
            copy.wait()
    turned[:, HD:, :] = jnp.ones((kv_local, ONES, turned.shape[2]), jnp.bfloat16)
    if fresh is not None:
        new_key_ref, new_value_ref = fresh
        row = lax.rem(lax.broadcasted_iota(jnp.int32, (1, rows), 1), new_rows)
        seen = lax.broadcasted_iota(jnp.int32, (new_key_ref.shape[0], rows), 0) <= row
        visit(lanes_of(new_key_ref), lanes_of(new_value_ref), seen)

    def visit_blocks(number):
        def body(index, carry):
            for i in range(number):
                ready(index * number + i)
            visit(
                blocks_of(key_ref, index * number, number),
                blocks_of(value_ref, index * number, number),
                None,
            )
            return carry

        return body

    pairs = count // 2 if key_ref.shape[0] > 1 else 0
    if key_ref.shape[0] > 1:
        lax.fori_loop(0, pairs, visit_blocks(2), 0)
    lax.fori_loop(2 * pairs, count, visit_blocks(1), 0)
    if raw:
        return acc, peaks
    outs = []
    logs = []
    for kv in range(kv_local):
        total = acc[kv, HD : HD + 1, :]
        safe = jnp.where(total > 0, total, 1.0)
        logs.append(jnp.where(total > 0, peaks[kv, 0:1] * math.log(2.0) + jnp.log(safe), EMPTY))
        outs.append(acc[kv, :HD, :] * (1.0 / safe))
    return outs, logs


def prepare_kernel(query_ref, new_key_ref, new_value_ref, payload_ref, query_rows):
    new_rows = query_ref.shape[0]
    kv_width = new_key_ref.shape[1]
    for kv in range(kv_width // HD):
        for g in range(GROUP):
            head = kv * GROUP + g
            query_rows[g * new_rows : (g + 1) * new_rows, :] = query_ref[
                :, head * HD : (head + 1) * HD
            ]
        payload_ref[kv * HD : (kv + 1) * HD, :] = query_rows[...].T
    for i, new_ref in enumerate((new_key_ref, new_value_ref)):
        for piece in range(new_rows // PIECE):
            row, lane = piece_place(i, piece, new_rows, kv_width)
            payload_ref[row : row + PIECE, lane : lane + kv_width] = new_ref[
                piece * PIECE : (piece + 1) * PIECE, :
            ]


def piece_place(i, piece, new_rows, kv_width):
    index = i * (new_rows // PIECE) + piece
    beside = GROUP * new_rows // kv_width
    return kv_width + index // beside * PIECE, index % beside * kv_width


def payload_rows(new_rows, kv_width):
    return piece_place(1, new_rows // PIECE - 1, new_rows, kv_width)[0] + PIECE


def own_kernel(
    pool_size,
    prefix_ref,
    store_ref,
    slot_ref,
    payload_ref,
    new_key_ref,
    new_value_ref,
    store_keys,
    store_values,
    out_ref,
    log_ref,
    key_buf,
    value_buf,
    new_key_buf,
    new_value_buf,
    *state,
):
    *work, sems = state
    count, ready = fetch(
        pool_size,
        (prefix_ref, store_ref, slot_ref),
        lax.axis_index("pool"),
        (store_keys, store_values),
        (key_buf, value_buf),
        sems,
    )
    new_rows, kv_width = new_key_ref.shape
    for buffer, source in ((new_key_buf, new_key_ref), (new_value_buf, new_value_ref)):
        buffer[:new_rows, :] = source[...]
        buffer[new_rows:, :] = jnp.zeros((buffer.shape[0] - new_rows, kv_width), jnp.bfloat16)
    fresh = (new_key_buf, new_value_buf)
    outs, logs = attend(
        key_buf, value_buf, count, ready, fresh, new_rows, payload_ref.at[:kv_width], *work
    )
    log_ref[...] = jnp.zeros(log_ref.shape, jnp.float32)
    for kv, (out, log) in enumerate(zip(outs, logs)):
        out_ref[kv * HD : (kv + 1) * HD, :] = out
        log_ref[kv : kv + 1, :] = log


def other_kernel(pool_size, new_rows, partners, with_moved, raw, *refs):
    if partners is None:
        request = refs[0][0]
        choice = [None]
        refs = refs[1:]
    else:
        inner = is_inner(lax.axis_index("pool"))
        _, request = source_of(lax.axis_index("pool"), partners)
        choice = [
            hit for hit, mask in zip((inner, jnp.logical_not(inner)), partners) if mask is not None
        ]
    tables, refs = refs[:3], refs[3:]
    payload_refs, refs = refs[: len(choice)], refs[len(choice) :]
    moved = initial = None
    if with_moved:
        moved, *initial = refs[:3]
        refs = refs[3:]
    store_keys, store_values, *refs = refs
    results_ref, (key_buf, value_buf, *state) = refs[: 1 + 2 * raw], refs[1 + 2 * raw :]
    *work, columns, query_sem, out_buf, out_sem, sems = state
    kv_width = columns.shape[0]

    def query_copy(payload_ref):
        return pltpu.make_async_copy(payload_ref.at[:kv_width], columns, query_sem)

    def run():
        for payload_ref, hit in zip(payload_refs, choice):
            if len(choice) == 1:
                query_copy(payload_ref).start()
            else:
                pl.when(hit)(query_copy(payload_ref).start)
        count, ready = fetch(
            pool_size,
            tables,
            request,
            (store_keys, store_values),
            (key_buf, value_buf),
            sems,
            moved,
        )
        if raw:
            passed = pltpu.make_async_copy(
                payload_refs[0].at[kv_width:], results_ref[2], out_sem.at[2]
            )
            passed.start()
        restore = None
        if initial is not None:

            def restore(*targets):
                return [
                    pltpu.make_async_copy(source, target, out_sem.at[i])
                    for i, (source, target) in enumerate(zip(initial, targets))
                ]

            for copy in restore(work[-1], work[2]):
                copy.start()
        query_copy(payload_refs[0]).wait()
        results = attend(
            key_buf, value_buf, count, ready, None, new_rows, columns, *work, restore, raw
        )
        if raw:
            copies = [
                pltpu.make_async_copy(result, out_ref, out_sem.at[i])
                for i, (out_ref, result) in enumerate(zip(results_ref, results))
            ]
            for copy in copies:
                copy.start()
            for copy in (*copies, passed):
                copy.wait()
            return
        outs, logs = results
        tail = []
        copies = []

        def send_rows(start, size):
            copies.append(
                pltpu.make_async_copy(
                    out_buf.at[start : start + size],
                    results_ref[0].at[start : start + size],
                    out_sem.at[len(copies)],
                )
            )
            copies[-1].start()

        for kv, (out, log) in enumerate(zip(outs, logs)):
            out_buf[kv * HD : (kv + 1) * HD, :] = out.astype(jnp.bfloat16)
            send_rows(kv * HD, HD)
            high = log.astype(jnp.bfloat16).astype(jnp.float32)
            middle = (log - high).astype(jnp.bfloat16).astype(jnp.float32)
            tail += [high, middle, log - high - middle]
        tail.append(jnp.zeros((ONES - len(tail), columns.shape[1]), jnp.float32))
        out_buf[kv_width:, :] = jnp.concatenate(tail, axis=0).astype(jnp.bfloat16)
        send_rows(kv_width, ONES)
        for copy in copies:
            copy.wait()

    if len(choice) == 1 and choice[0] is not None:
        pl.when(choice[0])(run)
    else:
        run()


def is_inner(place):
    return (place == 1) | (place == 2)


def source_of(me, entry):
    if isinstance(entry, int):
        return jnp.bool_(True), jnp.int32(entry)
    inner = is_inner(me)
    masks = [0 if mask is None else mask for mask in entry]
    there = jnp.where(inner, entry[0] is not None, entry[1] is not None)
    return there, me ^ jnp.where(inner, masks[0], masks[1])


def push_kernel(pool_size, entries, owner_ref, *refs):
    payload_refs = refs[: len(entries)]
    key_out, value_out, sems = refs[len(entries) :]
    outs = (key_out, value_out)
    kv_width = key_out.shape[2]
    me = lax.axis_index("pool")
    total = jnp.int32(0)
    for other in range(pool_size):
        total += (owner_ref[other] == me).astype(jnp.int32)

    new_rows = key_out.shape[1]

    def copies(payload_ref, place):
        for i in range(2):
            for piece in range(new_rows // PIECE):
                row, lane = piece_place(i, piece, new_rows, kv_width)
                row += payload_ref.shape[0] - payload_rows(new_rows, kv_width)
                yield pltpu.make_async_copy(
                    payload_ref.at[row : row + PIECE, lane : lane + kv_width],
                    outs[i].at[place, piece * PIECE : (piece + 1) * PIECE],
                    sems.at[i, place, piece],
                )

    for entry, payload_ref in zip(entries, payload_refs):
        there, source = source_of(me, entry)
        rank = jnp.int32(0)
        for other in range(pool_size):
            rank += ((owner_ref[other] == me) & (other < source)).astype(jnp.int32)
        hit = there & (owner_ref[source] == me)
        for place in range(CAPP):

            @pl.when(hit & (rank == place))
            def _():
                for copy in copies(payload_ref, place):
                    copy.start()

    for place in range(CAPP):

        @pl.when(total <= place)
        def _():
            for out in outs:
                out[place] = jnp.zeros(out.shape[1:], jnp.bfloat16)

        @pl.when(total > place)
        def _():
            for copy in copies(payload_refs[0], place):
                copy.wait()


def combine_kernel(sources, last, own_ref, log_ref, *refs):
    parts = refs[: len(sources)]
    out_ref = refs[len(sources)]
    kv_width, rows = own_ref.shape
    me = lax.axis_index("pool")
    arrived = []
    tails = []
    for source, part in zip(sources, parts):
        there, request = source_of(me, source)
        arrived.append(there & (request != me))
        tails.append(part[kv_width:, :].astype(jnp.float32))
    if not last:
        refs[len(sources) + 1][...] = log_ref[...]
    for kv in range(kv_width // HD):
        logs = [log_ref[kv : kv + 1, :]]
        for there, tail in zip(arrived, tails):
            log = sum(tail[3 * kv + i : 3 * kv + i + 1] for i in range(3))
            logs.append(jnp.where(there, log, EMPTY))
        peak = functools.reduce(jnp.maximum, logs)
        shares = [jnp.exp(x - peak) for x in logs]
        total = functools.reduce(jnp.add, shares)
        shares = [x * (1.0 / total) for x in shares]
        band = slice(kv * HD, (kv + 1) * HD)
        for i in range(0, rows, TILE):
            part = slice(i, i + TILE)
            mixed = own_ref[band, part] * shares[0][:, part]
            for share, ref in zip(shares[1:], parts):
                mixed = mixed + ref[band, part].astype(jnp.float32) * share[:, part]
            if last:
                refs[len(sources) + 1][part, :] = mixed.astype(jnp.bfloat16).T
            else:
                out_ref[band, part] = mixed
        if last:
            turned = refs[len(sources) + 1]
            new_rows = out_ref.shape[0]
            for g in range(GROUP):
                head = kv * GROUP + g
                out_ref[:, head * HD : (head + 1) * HD] = turned[g * new_rows : (g + 1) * new_rows, :]
        else:
            refs[len(sources) + 1][kv : kv + 1, :] = peak + jnp.log(total)


def final_kernel(own_ref, log_ref, outer_ref, inner_ref, out_ref, own_buf, part_buf, out_buf, turned, sems):
    kv_width, rows = own_buf.shape
    new_rows = out_buf.shape[0]
    kv_local = kv_width // HD
    lanes = GROUP * HD
    inner = is_inner(lax.axis_index("pool"))
    bands = [slice(kv * HD, (kv + 1) * HD) for kv in range(kv_local)] + [slice(kv_width, kv_width + ONES)]

    def part_copies(ref):
        return [
            pltpu.make_async_copy(ref.at[band], part_buf.at[band], sems.at[0, i])
            for i, band in enumerate(bands)
        ]

    def start_part(ref):
        for copy in reversed(part_copies(ref)):
            copy.start()

    own_copies = [
        pltpu.make_async_copy(own_ref.at[band], own_buf.at[band], sems.at[1, i])
        for i, band in enumerate(bands[:-1])
    ]
    pl.when(inner)(functools.partial(start_part, inner_ref))
    pl.when(jnp.logical_not(inner))(functools.partial(start_part, outer_ref))
    for copy in own_copies:
        copy.start()
    arriving = part_copies(outer_ref)
    arriving[-1].wait()
    tail = part_buf[kv_width:, :].astype(jnp.float32)
    leaving = []
    for kv in range(kv_local):
        log = log_ref[kv : kv + 1, :]
        other = sum(tail[3 * kv + i : 3 * kv + i + 1] for i in range(3))
        peak = jnp.maximum(log, other)
        shares = [jnp.exp(log - peak), jnp.exp(other - peak)]
        scale = 1.0 / (shares[0] + shares[1])
        shares = [share * scale for share in shares]
        arriving[kv].wait()
        own_copies[kv].wait()
        for i in range(0, rows, TILE):
            part = slice(i, i + TILE)
            mixed = own_buf[bands[kv], part] * shares[0][:, part]
            mixed = mixed + part_buf[bands[kv], part].astype(jnp.float32) * shares[1][:, part]
            turned[part, :] = mixed.astype(jnp.bfloat16).T
        for g in range(GROUP):
            head = kv * GROUP + g
            out_buf[:, head * HD : (head + 1) * HD] = turned[g * new_rows : (g + 1) * new_rows, :]
        band = slice(kv * lanes, (kv + 1) * lanes)
        leaving.append(
            pltpu.make_async_copy(out_buf.at[:, band], out_ref.at[:, band], sems.at[2, kv])
        )
        leaving[-1].start()
    for copy in leaving:
        copy.wait()


def shards(
    queries,
    new_keys,
    new_values,
    store_keys,
    store_values,
    prefix_blocks,
    hit_store,
    hit_slot,
    decode_owner,
):
    pool_size = lax.axis_size("pool")
    capacity = (MAXBLK + pool_size - 1) // pool_size
    new_rows = queries.shape[1]
    width = queries.shape[2]
    kv_width = new_keys.shape[2]
    block_len = store_keys.shape[1]
    rows = GROUP * new_rows
    tables = (prefix_blocks, hit_store, hit_slot)
    smem_spec = pl.BlockSpec(memory_space=pltpu.SMEM)
    hbm_spec = pl.BlockSpec(memory_space=pltpu.HBM)
    vmem_spec = pl.BlockSpec(memory_space=pltpu.VMEM)
    params = pltpu.CompilerParams(vmem_limit_bytes=VMEM_LIMIT)

    def cost(share):
        return pl.CostEstimate(
            flops=share * rows * block_len * kv_width * capacity,
            bytes_accessed=rows,
            transcendentals=0,
        )

    buffers = [pltpu.VMEM((capacity, block_len, kv_width), jnp.bfloat16)] * 2
    kv_local = kv_width // HD
    widest = block_len * min(2, capacity)
    work = [
        pltpu.VMEM((kv_local, widest, rows), jnp.float32),
        pltpu.VMEM((kv_local, widest, rows), jnp.bfloat16),
        pltpu.VMEM((kv_local, 8, rows), jnp.float32),
        pltpu.VMEM((kv_local, 8, rows), jnp.float32),
        pltpu.VMEM((kv_local, 8, rows), jnp.float32),
        pltpu.VMEM((kv_local, HD + ONES, widest), jnp.bfloat16),
        pltpu.VMEM((kv_local, HD + ONES, rows), jnp.float32),
    ]
    sems = pltpu.SemaphoreType.DMA((2, capacity))

    def own_part(payload):
        return pl.pallas_call(
            functools.partial(own_kernel, pool_size),
            in_specs=[smem_spec] * 3 + [vmem_spec] * 3 + [hbm_spec] * 2,
            out_specs=[vmem_spec] * 2,
            scratch_shapes=[
                *buffers,
                *[pltpu.VMEM((block_len, kv_width), jnp.bfloat16)] * 2,
                *work,
                sems,
            ],
            out_shape=[
                jax.ShapeDtypeStruct((kv_width, rows), jnp.float32),
                jax.ShapeDtypeStruct((8, rows), jnp.float32),
            ],
            compiler_params=params,
            cost_estimate=cost(8),
            name="own_part",
        )(*tables, payload, new_keys[0], new_values[0], store_keys, store_values)

    def other_part(partners, held, *request, share=8, moved=(), raw=False):
        if raw:
            out_shape = [
                jax.ShapeDtypeStruct((kv_local, HD + ONES, rows), jnp.float32),
                jax.ShapeDtypeStruct((kv_local, 8, rows), jnp.float32),
                jax.ShapeDtypeStruct((held[0].shape[0] - kv_width, rows), jnp.bfloat16),
            ]
        else:
            out_shape = jax.ShapeDtypeStruct((kv_width + ONES, rows), jnp.bfloat16)
        more_specs = [hbm_spec] * 3 if moved else []
        return pl.pallas_call(
            functools.partial(other_kernel, pool_size, new_rows, partners, bool(moved), raw),
            in_specs=[smem_spec] * (3 + len(request))
            + [hbm_spec] * len(held)
            + more_specs
            + [hbm_spec] * 2,
            out_specs=[hbm_spec] * 3 if raw else hbm_spec,
            scratch_shapes=[
                *buffers,
                *work,
                pltpu.VMEM((kv_width, rows), jnp.bfloat16),
                pltpu.SemaphoreType.DMA,
                pltpu.VMEM((kv_width + ONES, rows), jnp.bfloat16),
                pltpu.SemaphoreType.DMA((max(3, kv_local + 1),)),
                sems,
            ],
            out_shape=out_shape,
            compiler_params=params,
            cost_estimate=cost(share),
            name="other_part",
        )(*request, *tables, *held, *moved, store_keys, store_values)

    def combine(own, log, sources, parts, last=True):
        if last:
            out_shape = jax.ShapeDtypeStruct((new_rows, width), jnp.bfloat16)
        else:
            out_shape = [
                jax.ShapeDtypeStruct((kv_width, rows), jnp.float32),
                jax.ShapeDtypeStruct((8, rows), jnp.float32),
            ]
        return pl.pallas_call(
            functools.partial(combine_kernel, tuple(sources), last),
            in_specs=[vmem_spec] * (2 + len(parts)),
            out_specs=vmem_spec if last else [vmem_spec] * 2,
            scratch_shapes=[pltpu.VMEM((rows, HD), jnp.bfloat16)] if last else [],
            out_shape=out_shape,
            compiler_params=params,
            cost_estimate=cost(0),
            name="combine",
        )(own, log, *parts)

    def final(own, log, parts):
        return pl.pallas_call(
            final_kernel,
            in_specs=[hbm_spec, vmem_spec, hbm_spec, hbm_spec],
            out_specs=hbm_spec,
            scratch_shapes=[
                pltpu.VMEM((kv_width, rows), jnp.float32),
                pltpu.VMEM((kv_width + ONES, rows), jnp.bfloat16),
                pltpu.VMEM((new_rows, width), jnp.bfloat16),
                pltpu.VMEM((rows, HD), jnp.bfloat16),
                pltpu.SemaphoreType.DMA((3, kv_local + 1)),
            ],
            out_shape=jax.ShapeDtypeStruct((new_rows, width), jnp.bfloat16),
            compiler_params=params,
            name="final",
        )(own, log, *parts)

    payload = pl.pallas_call(
        prepare_kernel,
        in_specs=[vmem_spec] * 3,
        out_specs=vmem_spec,
        scratch_shapes=[pltpu.VMEM((rows, HD), jnp.bfloat16)],
        out_shape=jax.ShapeDtypeStruct((payload_rows(new_rows, kv_width), rows), jnp.bfloat16),
        compiler_params=params,
        name="prepare",
    )(queries[0], new_keys[0], new_values[0])
    own_out, own_log = own_part(payload)
    if pool_size == 4:
        def send(array, *pairs):
            return lax.ppermute(array, "pool", pairs)

        near = send(payload, (0, 1), (1, 0), (2, 3), (3, 2))
        middle = send(payload, (1, 2), (2, 1))
        blocks = pl.pallas_call(
            functools.partial(gather_kernel, pool_size),
            in_specs=[smem_spec] * 3 + [hbm_spec] * 2,
            out_specs=vmem_spec,
            scratch_shapes=[sems],
            out_shape=jax.ShapeDtypeStruct((2 * capacity, block_len, kv_width), jnp.bfloat16),
            compiler_params=params,
            name="gather_blocks",
        )(*tables, store_keys, store_values)
        blocks = send(blocks, (0, 1), (3, 2))
        near, middle, own_out, own_log = lax.optimization_barrier((near, middle, own_out, own_log))
        crossed = send(near, (1, 2), (2, 1))
        outward = send(middle, (1, 0), (2, 3))
        first = other_part((3, 1), (middle, near))
        near, first = lax.optimization_barrier((near, first))
        second = other_part((1, None), (near,))
        first, second = lax.optimization_barrier((first, second))
        across = send(first, (1, 2), (2, 1))
        back = send(second, (1, 0), (2, 3))
        outward, second = lax.optimization_barrier((outward, second))
        outer_second = other_part((None, 2), (outward,))
        apart = send(outer_second, (0, 2), (3, 1))
        crossed, first, outer_second = lax.optimization_barrier((crossed, first, outer_second))
        inward = send(first, (0, 1), (3, 2))
        *state, fresh = other_part((2, None), (crossed,), raw=True)
        crossed, state = lax.optimization_barrier((crossed, state))
        far = send(fresh, (1, 0), (2, 3))
        third = other_part((2, None), (crossed,), moved=(blocks, *state))
        ends = send(third, (1, 3), (2, 0))
        own_out, own_log, third = lax.optimization_barrier((own_out, own_log, third))
        own_out, own_log = combine(
            own_out, own_log, [(3, None), (2, None), (None, 1)], [across, apart, back], last=False
        )
        attended = final(own_out, own_log, (ends, inward))
        moved = [
            ((0, 0), payload),
            ((1, 1), near),
            ((3, None), middle),
            ((2, None), crossed),
            ((None, 2), outward),
            ((None, 3), far),
        ]
    else:
        gathered = lax.all_gather(payload, "pool", axis=0, tiled=False)
        packed = lax.map(
            lambda pair: other_part(None, (pair[0],), pair[1].reshape(1)),
            (gathered, jnp.arange(pool_size, dtype=jnp.int32)),
        )
        parts = lax.all_to_all(packed, "pool", split_axis=0, concat_axis=0, tiled=True)
        attended = combine(own_out, own_log, list(range(pool_size)), parts)
        moved = [(source, gathered[source]) for source in range(pool_size)]

    pushed_keys, pushed_values = pl.pallas_call(
        functools.partial(push_kernel, pool_size, tuple(entry for entry, _ in moved)),
        in_specs=[smem_spec] + [hbm_spec] * len(moved),
        out_specs=[vmem_spec] * 2,
        scratch_shapes=[pltpu.SemaphoreType.DMA((2, CAPP, new_rows // PIECE))],
        out_shape=[jax.ShapeDtypeStruct((CAPP, new_rows, kv_width), jnp.bfloat16)] * 2,
        compiler_params=params,
        name="push",
    )(decode_owner, *[array for _, array in moved])
    return (attended[None], pushed_keys, pushed_values)


def solution(mesh):
    in_specs = (
        P(("groups", "pool"), None, ("tensor", "sub")),
        P(("groups", "pool"), None, ("tensor", "sub")),
        P(("groups", "pool"), None, ("tensor", "sub")),
        P(("groups", "pool"), None, ("tensor", "sub")),
        P(("groups", "pool"), None, ("tensor", "sub")),
        P("groups"),
        P("groups", None),
        P("groups", None),
        P("groups"),
    )
    out_specs = (
        P(("groups", "pool"), None, ("tensor", "sub")),
        P(("groups", "pool"), None, ("tensor", "sub")),
        P(("groups", "pool"), None, ("tensor", "sub")),
    )
    return jax.shard_map(shards, mesh=mesh, in_specs=in_specs, out_specs=out_specs, check_vma=False)
```

```python
import functools
import math

import jax
import jax.numpy as jnp
from jax import lax
from jax.experimental import pallas as pl
from jax.experimental.pallas import tpu as pltpu
from jax.sharding import PartitionSpec as P

HEADS = 64
KVH = 8
HD = 128
MAXBLK = 32
CAPP = 2
GROUP = HEADS // KVH
EMPTY = -1e30
TILE = 256
ONES = 16
PIECE = 32
EXP2_SCALE = math.log2(math.e) / math.sqrt(HD)
VMEM_LIMIT = 63 * 1024 * 1024 + 512 * 1024


def blocks_at(tables, request, place, pool_size):
    prefix_ref, store_ref, slot_ref = tables
    first = lax.rem(place - store_ref[request, 0] + pool_size, pool_size)
    count = lax.max(lax.div(prefix_ref[request] - first + pool_size - 1, pool_size), 0)
    return count, lambda entry: slot_ref[request, first + entry * pool_size]


def fetch(pool_size, tables, request, stores, buffers, sems, moved=None):
    me = lax.axis_index("pool")
    count, slot_of = blocks_at(tables, request, me if moved is None else me ^ 1, pool_size)

    def copies(entry):
        for i in range(2):
            if moved is None:
                source = stores[i].at[slot_of(entry)]
            else:
                source = moved.at[i * (moved.shape[0] // 2) + entry]
            yield pltpu.make_async_copy(source, buffers[i].at[entry], sems.at[i, entry])

    def start(entry, carry):
        for copy in copies(entry):
            copy.start()
        return carry

    lax.fori_loop(0, count, start, 0)

    def ready(entry):
        for copy in copies(entry):
            copy.wait()

    return count, ready


def gather_kernel(pool_size, prefix_ref, store_ref, slot_ref, store_keys, store_values, out_ref, sems):
    me = lax.axis_index("pool")
    capacity = out_ref.shape[0] // 2

    @pl.when(jnp.logical_not(is_inner(me)))
    def _():
        tables = (prefix_ref, store_ref, slot_ref)
        count, slot_of = blocks_at(tables, me ^ 3, me, pool_size)

        def copies(entry):
            return [
                pltpu.make_async_copy(
                    store.at[slot_of(entry)], out_ref.at[i * capacity + entry], sems.at[i, entry]
                )
                for i, store in enumerate((store_keys, store_values))
            ]

        def start(entry, carry):
            for copy in copies(entry):
                copy.start()
            return carry

        def wait(entry, carry):
            for copy in copies(entry):
                copy.wait()
            return carry

        lax.fori_loop(0, count, start, 0)
        lax.fori_loop(0, count, wait, 0)


def attend(
    key_ref,
    value_ref,
    count,
    ready,
    fresh,
    new_rows,
    columns,
    scores,
    weights,
    peaks,
    factors,
    tops,
    turned,
    acc,
    initial=None,
    raw=False,
):
    rows = columns.shape[1]
    kv_local = columns.shape[0] // HD

    def visit(keys, values, seen):
        size = keys[0].shape[0]

        def score(kv):
            turned[kv, :HD, :size] = values[kv].T
            block = lax.dot_general(
                keys[kv],
                columns[kv * HD : (kv + 1) * HD, :],
                (((1,), (0,)), ((), ())),
                preferred_element_type=jnp.float32,
            )
            block = block * EXP2_SCALE
            if seen is not None:
                block = jnp.where(seen, block, EMPTY)
            scores[kv, :size, :] = block
            tops[kv] = jnp.max(block.reshape(size // 8, 8, rows), axis=0)

        def weigh(kv):
            for i in range(0, rows, TILE):
                part = slice(i, i + TILE)
                before = peaks[kv, :, part]
                top = jnp.max(tops[kv, :, part], axis=0, keepdims=True)
                peak = jnp.maximum(before, top)
                factors[kv, :, part] = jnp.exp2(before - peak)
                peaks[kv, :, part] = peak
                weight = jnp.exp2(scores[kv, :size, part] - peak[0:1])
                weights[kv, :size, part] = weight.astype(jnp.bfloat16)

        def mix(kv):
            added = lax.dot_general(
                turned[kv, :, :size],
                weights[kv, :size, :],
                (((1,), (0,)), ((), ())),
                preferred_element_type=jnp.float32,
            )
            acc[kv] = acc[kv] * factors[kv, 0:1, :] + added

        for step in range(kv_local + 2):
            for offset, stage in ((0, score), (2, mix), (1, weigh)):
                if 0 <= step - offset < kv_local:
                    stage(step - offset)

    def lanes_of(array):
        return [array[:, kv * HD : (kv + 1) * HD] for kv in range(kv_local)]

    def blocks_of(ref, first, number):
        return lanes_of(ref[pl.ds(first, number)].reshape(number * ref.shape[1], ref.shape[2]))

    if initial is None:
        peaks[...] = jnp.full(peaks.shape, EMPTY, jnp.float32)
        acc[...] = jnp.zeros(acc.shape, jnp.float32)
    else:
        for copy in initial(acc, peaks):
            copy.wait()
    turned[:, HD:, :] = jnp.ones((kv_local, ONES, turned.shape[2]), jnp.bfloat16)
    if fresh is not None:
        new_key_ref, new_value_ref = fresh
        row = lax.rem(lax.broadcasted_iota(jnp.int32, (1, rows), 1), new_rows)
        seen = lax.broadcasted_iota(jnp.int32, (new_key_ref.shape[0], rows), 0) <= row
        visit(lanes_of(new_key_ref), lanes_of(new_value_ref), seen)

    def visit_blocks(number):
        def body(index, carry):
            for i in range(number):
                ready(index * number + i)
            visit(
                blocks_of(key_ref, index * number, number),
                blocks_of(value_ref, index * number, number),
                None,
            )
            return carry

        return body

    pairs = count // 2 if key_ref.shape[0] > 1 else 0
    if key_ref.shape[0] > 1:
        lax.fori_loop(0, pairs, visit_blocks(2), 0)
    lax.fori_loop(2 * pairs, count, visit_blocks(1), 0)
    if raw:
        return acc, peaks
    outs = []
    logs = []
    for kv in range(kv_local):
        total = acc[kv, HD : HD + 1, :]
        safe = jnp.where(total > 0, total, 1.0)
        logs.append(jnp.where(total > 0, peaks[kv, 0:1] * math.log(2.0) + jnp.log(safe), EMPTY))
        outs.append(acc[kv, :HD, :] * (1.0 / safe))
    return outs, logs


def prepare_kernel(
    query_ref, new_key_ref, new_value_ref, payload_ref, query_buf, query_rows, payload_buf, sems
):
    new_rows = query_ref.shape[0]
    kv_width = new_key_ref.shape[1]
    kv_local = kv_width // HD
    lanes = GROUP * HD
    pieces = new_rows // PIECE
    coming = [
        pltpu.make_async_copy(
            query_ref.at[:, kv * lanes : (kv + 1) * lanes],
            query_buf.at[:, kv * lanes : (kv + 1) * lanes],
            sems.at[0, kv],
        )
        for kv in range(kv_local)
    ]
    for i, new_ref in enumerate((new_key_ref, new_value_ref)):
        for piece in range(pieces):
            row, lane = piece_place(i, piece, new_rows, kv_width)
            coming.append(
                pltpu.make_async_copy(
                    new_ref.at[piece * PIECE : (piece + 1) * PIECE],
                    payload_buf.at[row : row + PIECE, lane : lane + kv_width],
                    sems.at[0, kv_local + i * pieces + piece],
                )
            )
    for copy in coming:
        copy.start()
    leaving = []

    def leave(start, stop):
        leaving.append(
            pltpu.make_async_copy(
                payload_buf.at[start:stop], payload_ref.at[start:stop], sems.at[1, len(leaving)]
            )
        )
        leaving[-1].start()

    for kv in range(kv_local):
        coming[kv].wait()
        for g in range(GROUP):
            head = kv * GROUP + g
            query_rows[kv, g * new_rows : (g + 1) * new_rows, :] = query_buf[
                :, head * HD : (head + 1) * HD
            ]
        payload_buf[kv * HD : (kv + 1) * HD, :] = query_rows[kv].T
        leave(kv * HD, (kv + 1) * HD)
    for copy in coming[kv_local:]:
        copy.wait()
    leave(kv_width, payload_buf.shape[0])
    for copy in leaving:
        copy.wait()


def piece_place(i, piece, new_rows, kv_width):
    index = i * (new_rows // PIECE) + piece
    beside = GROUP * new_rows // kv_width
    return kv_width + index // beside * PIECE, index % beside * kv_width


def payload_rows(new_rows, kv_width):
    return piece_place(1, new_rows // PIECE - 1, new_rows, kv_width)[0] + PIECE


def own_kernel(
    pool_size,
    prefix_ref,
    store_ref,
    slot_ref,
    payload_ref,
    new_key_ref,
    new_value_ref,
    store_keys,
    store_values,
    out_ref,
    log_ref,
    key_buf,
    value_buf,
    new_key_buf,
    new_value_buf,
    *state,
):
    *work, sems = state
    count, ready = fetch(
        pool_size,
        (prefix_ref, store_ref, slot_ref),
        lax.axis_index("pool"),
        (store_keys, store_values),
        (key_buf, value_buf),
        sems,
    )
    new_rows, kv_width = new_key_ref.shape
    for buffer, source in ((new_key_buf, new_key_ref), (new_value_buf, new_value_ref)):
        buffer[:new_rows, :] = source[...]
        buffer[new_rows:, :] = jnp.zeros((buffer.shape[0] - new_rows, kv_width), jnp.bfloat16)
    fresh = (new_key_buf, new_value_buf)
    outs, logs = attend(
        key_buf, value_buf, count, ready, fresh, new_rows, payload_ref.at[:kv_width], *work
    )
    log_ref[...] = jnp.zeros(log_ref.shape, jnp.float32)
    for kv, (out, log) in enumerate(zip(outs, logs)):
        out_ref[kv * HD : (kv + 1) * HD, :] = out
        log_ref[kv : kv + 1, :] = log


def other_kernel(pool_size, new_rows, partners, with_moved, raw, *refs):
    if partners is None:
        request = refs[0][0]
        choice = [None]
        refs = refs[1:]
    else:
        inner = is_inner(lax.axis_index("pool"))
        _, request = source_of(lax.axis_index("pool"), partners)
        choice = [
            hit for hit, mask in zip((inner, jnp.logical_not(inner)), partners) if mask is not None
        ]
    tables, refs = refs[:3], refs[3:]
    payload_refs, refs = refs[: len(choice)], refs[len(choice) :]
    moved = initial = None
    if with_moved:
        moved, *initial = refs[:3]
        refs = refs[3:]
    store_keys, store_values, *refs = refs
    results_ref, (key_buf, value_buf, *state) = refs[: 1 + 2 * raw], refs[1 + 2 * raw :]
    *work, columns, query_sem, out_buf, out_sem, sems = state
    kv_width = columns.shape[0]

    def query_copy(payload_ref):
        return pltpu.make_async_copy(payload_ref.at[:kv_width], columns, query_sem)

    def run():
        for payload_ref, hit in zip(payload_refs, choice):
            if len(choice) == 1:
                query_copy(payload_ref).start()
            else:
                pl.when(hit)(query_copy(payload_ref).start)
        count, ready = fetch(
            pool_size,
            tables,
            request,
            (store_keys, store_values),
            (key_buf, value_buf),
            sems,
            moved,
        )
        if raw:
            passed = pltpu.make_async_copy(
                payload_refs[0].at[kv_width:], results_ref[2], out_sem.at[2]
            )
            passed.start()
        restore = None
        if initial is not None:

            def restore(*targets):
                return [
                    pltpu.make_async_copy(source, target, out_sem.at[i])
                    for i, (source, target) in enumerate(zip(initial, targets))
                ]

            for copy in restore(work[-1], work[2]):
                copy.start()
        query_copy(payload_refs[0]).wait()
        results = attend(
            key_buf, value_buf, count, ready, None, new_rows, columns, *work, restore, raw
        )
        if raw:
            copies = [
                pltpu.make_async_copy(result, out_ref, out_sem.at[i])
                for i, (out_ref, result) in enumerate(zip(results_ref, results))
            ]
            for copy in copies:
                copy.start()
            for copy in (*copies, passed):
                copy.wait()
            return
        outs, logs = results
        tail = []
        copies = []

        def send_rows(start, size):
            copies.append(
                pltpu.make_async_copy(
                    out_buf.at[start : start + size],
                    results_ref[0].at[start : start + size],
                    out_sem.at[len(copies)],
                )
            )
            copies[-1].start()

        for kv, (out, log) in enumerate(zip(outs, logs)):
            out_buf[kv * HD : (kv + 1) * HD, :] = out.astype(jnp.bfloat16)
            send_rows(kv * HD, HD)
            high = log.astype(jnp.bfloat16).astype(jnp.float32)
            middle = (log - high).astype(jnp.bfloat16).astype(jnp.float32)
            tail += [high, middle, log - high - middle]
        tail.append(jnp.zeros((ONES - len(tail), columns.shape[1]), jnp.float32))
        out_buf[kv_width:, :] = jnp.concatenate(tail, axis=0).astype(jnp.bfloat16)
        send_rows(kv_width, ONES)
        for copy in copies:
            copy.wait()

    if len(choice) == 1 and choice[0] is not None:
        pl.when(choice[0])(run)
    else:
        run()


def is_inner(place):
    return (place == 1) | (place == 2)


def source_of(me, entry):
    if isinstance(entry, int):
        return jnp.bool_(True), jnp.int32(entry)
    inner = is_inner(me)
    masks = [0 if mask is None else mask for mask in entry]
    there = jnp.where(inner, entry[0] is not None, entry[1] is not None)
    return there, me ^ jnp.where(inner, masks[0], masks[1])


def push_kernel(pool_size, entries, owner_ref, *refs):
    payload_refs = refs[: len(entries)]
    key_out, value_out, sems = refs[len(entries) :]
    outs = (key_out, value_out)
    kv_width = key_out.shape[2]
    me = lax.axis_index("pool")
    total = jnp.int32(0)
    for other in range(pool_size):
        total += (owner_ref[other] == me).astype(jnp.int32)

    new_rows = key_out.shape[1]

    def copies(payload_ref, place):
        for i in range(2):
            for piece in range(new_rows // PIECE):
                row, lane = piece_place(i, piece, new_rows, kv_width)
                row += payload_ref.shape[0] - payload_rows(new_rows, kv_width)
                yield pltpu.make_async_copy(
                    payload_ref.at[row : row + PIECE, lane : lane + kv_width],
                    outs[i].at[place, piece * PIECE : (piece + 1) * PIECE],
                    sems.at[i, place, piece],
                )

    for entry, payload_ref in zip(entries, payload_refs):
        there, source = source_of(me, entry)
        rank = jnp.int32(0)
        for other in range(pool_size):
            rank += ((owner_ref[other] == me) & (other < source)).astype(jnp.int32)
        hit = there & (owner_ref[source] == me)
        for place in range(CAPP):

            @pl.when(hit & (rank == place))
            def _():
                for copy in copies(payload_ref, place):
                    copy.start()

    for place in range(CAPP):

        @pl.when(total <= place)
        def _():
            for out in outs:
                out[place] = jnp.zeros(out.shape[1:], jnp.bfloat16)

        @pl.when(total > place)
        def _():
            for copy in copies(payload_refs[0], place):
                copy.wait()


def combine_kernel(sources, last, own_ref, log_ref, *refs):
    parts = refs[: len(sources)]
    out_ref = refs[len(sources)]
    kv_width, rows = own_ref.shape
    me = lax.axis_index("pool")
    arrived = []
    tails = []
    for source, part in zip(sources, parts):
        there, request = source_of(me, source)
        arrived.append(there & (request != me))
        tails.append(part[kv_width:, :].astype(jnp.float32))
    if not last:
        refs[len(sources) + 1][...] = log_ref[...]
    for kv in range(kv_width // HD):
        logs = [log_ref[kv : kv + 1, :]]
        for there, tail in zip(arrived, tails):
            log = sum(tail[3 * kv + i : 3 * kv + i + 1] for i in range(3))
            logs.append(jnp.where(there, log, EMPTY))
        peak = functools.reduce(jnp.maximum, logs)
        shares = [jnp.exp(x - peak) for x in logs]
        total = functools.reduce(jnp.add, shares)
        shares = [x * (1.0 / total) for x in shares]
        band = slice(kv * HD, (kv + 1) * HD)
        for i in range(0, rows, TILE):
            part = slice(i, i + TILE)
            mixed = own_ref[band, part] * shares[0][:, part]
            for share, ref in zip(shares[1:], parts):
                mixed = mixed + ref[band, part].astype(jnp.float32) * share[:, part]
            if last:
                refs[len(sources) + 1][part, :] = mixed.astype(jnp.bfloat16).T
            else:
                out_ref[band, part] = mixed
        if last:
            turned = refs[len(sources) + 1]
            new_rows = out_ref.shape[0]
            for g in range(GROUP):
                head = kv * GROUP + g
                out_ref[:, head * HD : (head + 1) * HD] = turned[g * new_rows : (g + 1) * new_rows, :]
        else:
            refs[len(sources) + 1][kv : kv + 1, :] = peak + jnp.log(total)


def final_kernel(own_ref, log_ref, outer_ref, inner_ref, out_ref, own_buf, part_buf, out_buf, turned, sems):
    kv_width, rows = own_buf.shape
    new_rows = out_buf.shape[0]
    kv_local = kv_width // HD
    lanes = GROUP * HD
    inner = is_inner(lax.axis_index("pool"))
    bands = [slice(kv * HD, (kv + 1) * HD) for kv in range(kv_local)] + [slice(kv_width, kv_width + ONES)]

    def part_copies(ref):
        return [
            pltpu.make_async_copy(ref.at[band], part_buf.at[band], sems.at[0, i])
            for i, band in enumerate(bands)
        ]

    def start_part(ref):
        for copy in reversed(part_copies(ref)):
            copy.start()

    own_copies = [
        pltpu.make_async_copy(own_ref.at[band], own_buf.at[band], sems.at[1, i])
        for i, band in enumerate(bands[:-1])
    ]
    pl.when(inner)(functools.partial(start_part, inner_ref))
    pl.when(jnp.logical_not(inner))(functools.partial(start_part, outer_ref))
    for copy in own_copies:
        copy.start()
    arriving = part_copies(outer_ref)
    arriving[-1].wait()
    tail = part_buf[kv_width:, :].astype(jnp.float32)
    leaving = []
    for kv in range(kv_local):
        log = log_ref[kv : kv + 1, :]
        other = sum(tail[3 * kv + i : 3 * kv + i + 1] for i in range(3))
        peak = jnp.maximum(log, other)
        shares = [jnp.exp(log - peak), jnp.exp(other - peak)]
        scale = 1.0 / (shares[0] + shares[1])
        shares = [share * scale for share in shares]
        arriving[kv].wait()
        own_copies[kv].wait()
        for i in range(0, rows, TILE):
            part = slice(i, i + TILE)
            mixed = own_buf[bands[kv], part] * shares[0][:, part]
            mixed = mixed + part_buf[bands[kv], part].astype(jnp.float32) * shares[1][:, part]
            turned[part, :] = mixed.astype(jnp.bfloat16).T
        for g in range(GROUP):
            head = kv * GROUP + g
            out_buf[:, head * HD : (head + 1) * HD] = turned[g * new_rows : (g + 1) * new_rows, :]
        band = slice(kv * lanes, (kv + 1) * lanes)
        leaving.append(
            pltpu.make_async_copy(out_buf.at[:, band], out_ref.at[:, band], sems.at[2, kv])
        )
        leaving[-1].start()
    for copy in leaving:
        copy.wait()


def shards(
    queries,
    new_keys,
    new_values,
    store_keys,
    store_values,
    prefix_blocks,
    hit_store,
    hit_slot,
    decode_owner,
):
    pool_size = lax.axis_size("pool")
    capacity = (MAXBLK + pool_size - 1) // pool_size
    new_rows = queries.shape[1]
    width = queries.shape[2]
    kv_width = new_keys.shape[2]
    block_len = store_keys.shape[1]
    rows = GROUP * new_rows
    tables = (prefix_blocks, hit_store, hit_slot)
    smem_spec = pl.BlockSpec(memory_space=pltpu.SMEM)
    hbm_spec = pl.BlockSpec(memory_space=pltpu.HBM)
    vmem_spec = pl.BlockSpec(memory_space=pltpu.VMEM)
    params = pltpu.CompilerParams(vmem_limit_bytes=VMEM_LIMIT)

    def cost(share):
        return pl.CostEstimate(
            flops=share * rows * block_len * kv_width * capacity,
            bytes_accessed=rows,
            transcendentals=0,
        )

    buffers = [pltpu.VMEM((capacity, block_len, kv_width), jnp.bfloat16)] * 2
    kv_local = kv_width // HD
    widest = block_len * min(2, capacity)
    work = [
        pltpu.VMEM((kv_local, widest, rows), jnp.float32),
        pltpu.VMEM((kv_local, widest, rows), jnp.bfloat16),
        pltpu.VMEM((kv_local, 8, rows), jnp.float32),
        pltpu.VMEM((kv_local, 8, rows), jnp.float32),
        pltpu.VMEM((kv_local, 8, rows), jnp.float32),
        pltpu.VMEM((kv_local, HD + ONES, widest), jnp.bfloat16),
        pltpu.VMEM((kv_local, HD + ONES, rows), jnp.float32),
    ]
    sems = pltpu.SemaphoreType.DMA((2, capacity))

    def own_part(payload):
        return pl.pallas_call(
            functools.partial(own_kernel, pool_size),
            in_specs=[smem_spec] * 3 + [vmem_spec] * 3 + [hbm_spec] * 2,
            out_specs=[vmem_spec] * 2,
            scratch_shapes=[
                *buffers,
                *[pltpu.VMEM((block_len, kv_width), jnp.bfloat16)] * 2,
                *work,
                sems,
            ],
            out_shape=[
                jax.ShapeDtypeStruct((kv_width, rows), jnp.float32),
                jax.ShapeDtypeStruct((8, rows), jnp.float32),
            ],
            compiler_params=params,
            cost_estimate=cost(8),
            name="own_part",
        )(*tables, payload, new_keys[0], new_values[0], store_keys, store_values)

    def other_part(partners, held, *request, share=8, moved=(), raw=False):
        if raw:
            out_shape = [
                jax.ShapeDtypeStruct((kv_local, HD + ONES, rows), jnp.float32),
                jax.ShapeDtypeStruct((kv_local, 8, rows), jnp.float32),
                jax.ShapeDtypeStruct((held[0].shape[0] - kv_width, rows), jnp.bfloat16),
            ]
        else:
            out_shape = jax.ShapeDtypeStruct((kv_width + ONES, rows), jnp.bfloat16)
        more_specs = [hbm_spec] * 3 if moved else []
        return pl.pallas_call(
            functools.partial(other_kernel, pool_size, new_rows, partners, bool(moved), raw),
            in_specs=[smem_spec] * (3 + len(request))
            + [hbm_spec] * len(held)
            + more_specs
            + [hbm_spec] * 2,
            out_specs=[hbm_spec] * 3 if raw else hbm_spec,
            scratch_shapes=[
                *buffers,
                *work,
                pltpu.VMEM((kv_width, rows), jnp.bfloat16),
                pltpu.SemaphoreType.DMA,
                pltpu.VMEM((kv_width + ONES, rows), jnp.bfloat16),
                pltpu.SemaphoreType.DMA((max(3, kv_local + 1),)),
                sems,
            ],
            out_shape=out_shape,
            compiler_params=params,
            cost_estimate=cost(share),
            name="other_part",
        )(*request, *tables, *held, *moved, store_keys, store_values)

    def combine(own, log, sources, parts, last=True):
        if last:
            out_shape = jax.ShapeDtypeStruct((new_rows, width), jnp.bfloat16)
        else:
            out_shape = [
                jax.ShapeDtypeStruct((kv_width, rows), jnp.float32),
                jax.ShapeDtypeStruct((8, rows), jnp.float32),
            ]
        return pl.pallas_call(
            functools.partial(combine_kernel, tuple(sources), last),
            in_specs=[vmem_spec] * (2 + len(parts)),
            out_specs=vmem_spec if last else [vmem_spec] * 2,
            scratch_shapes=[pltpu.VMEM((rows, HD), jnp.bfloat16)] if last else [],
            out_shape=out_shape,
            compiler_params=params,
            cost_estimate=cost(0),
            name="combine",
        )(own, log, *parts)

    def final(own, log, parts):
        return pl.pallas_call(
            final_kernel,
            in_specs=[hbm_spec, vmem_spec, hbm_spec, hbm_spec],
            out_specs=hbm_spec,
            scratch_shapes=[
                pltpu.VMEM((kv_width, rows), jnp.float32),
                pltpu.VMEM((kv_width + ONES, rows), jnp.bfloat16),
                pltpu.VMEM((new_rows, width), jnp.bfloat16),
                pltpu.VMEM((rows, HD), jnp.bfloat16),
                pltpu.SemaphoreType.DMA((3, kv_local + 1)),
            ],
            out_shape=jax.ShapeDtypeStruct((new_rows, width), jnp.bfloat16),
            compiler_params=params,
            name="final",
        )(own, log, *parts)

    payload = pl.pallas_call(
        prepare_kernel,
        in_specs=[hbm_spec] * 3,
        out_specs=hbm_spec,
        scratch_shapes=[
            pltpu.VMEM((new_rows, width), jnp.bfloat16),
            pltpu.VMEM((kv_local, rows, HD), jnp.bfloat16),
            pltpu.VMEM((payload_rows(new_rows, kv_width), rows), jnp.bfloat16),
            pltpu.SemaphoreType.DMA((2, kv_local + 2 * (new_rows // PIECE))),
        ],
        out_shape=jax.ShapeDtypeStruct((payload_rows(new_rows, kv_width), rows), jnp.bfloat16),
        compiler_params=params,
        name="prepare",
    )(queries[0], new_keys[0], new_values[0])
    own_out, own_log = own_part(payload)
    if pool_size == 4:
        def send(array, *pairs):
            return lax.ppermute(array, "pool", pairs)

        near = send(payload, (0, 1), (1, 0), (2, 3), (3, 2))
        middle = send(payload, (1, 2), (2, 1))
        blocks = pl.pallas_call(
            functools.partial(gather_kernel, pool_size),
            in_specs=[smem_spec] * 3 + [hbm_spec] * 2,
            out_specs=vmem_spec,
            scratch_shapes=[sems],
            out_shape=jax.ShapeDtypeStruct((2 * capacity, block_len, kv_width), jnp.bfloat16),
            compiler_params=params,
            name="gather_blocks",
        )(*tables, store_keys, store_values)
        blocks = send(blocks, (0, 1), (3, 2))
        near, middle, own_out, own_log = lax.optimization_barrier((near, middle, own_out, own_log))
        crossed = send(near, (1, 2), (2, 1))
        outward = send(middle, (1, 0), (2, 3))
        first = other_part((3, 1), (middle, near))
        near, first = lax.optimization_barrier((near, first))
        second = other_part((1, None), (near,))
        first, second = lax.optimization_barrier((first, second))
        across = send(first, (1, 2), (2, 1))
        back = send(second, (1, 0), (2, 3))
        outward, second = lax.optimization_barrier((outward, second))
        outer_second = other_part((None, 2), (outward,))
        apart = send(outer_second, (0, 2), (3, 1))
        crossed, first, outer_second = lax.optimization_barrier((crossed, first, outer_second))
        inward = send(first, (0, 1), (3, 2))
        *state, fresh = other_part((2, None), (crossed,), raw=True)
        crossed, state = lax.optimization_barrier((crossed, state))
        far = send(fresh, (1, 0), (2, 3))
        third = other_part((2, None), (crossed,), moved=(blocks, *state))
        ends = send(third, (1, 3), (2, 0))
        own_out, own_log, third = lax.optimization_barrier((own_out, own_log, third))
        own_out, own_log = combine(
            own_out, own_log, [(3, None), (2, None), (None, 1)], [across, apart, back], last=False
        )
        attended = final(own_out, own_log, (ends, inward))
        moved = [
            ((0, 0), payload),
            ((1, 1), near),
            ((3, None), middle),
            ((2, None), crossed),
            ((None, 2), outward),
            ((None, 3), far),
        ]
    else:
        gathered = lax.all_gather(payload, "pool", axis=0, tiled=False)
        packed = lax.map(
            lambda pair: other_part(None, (pair[0],), pair[1].reshape(1)),
            (gathered, jnp.arange(pool_size, dtype=jnp.int32)),
        )
        parts = lax.all_to_all(packed, "pool", split_axis=0, concat_axis=0, tiled=True)
        attended = combine(own_out, own_log, list(range(pool_size)), parts)
        moved = [(source, gathered[source]) for source in range(pool_size)]

    pushed_keys, pushed_values = pl.pallas_call(
        functools.partial(push_kernel, pool_size, tuple(entry for entry, _ in moved)),
        in_specs=[smem_spec] + [hbm_spec] * len(moved),
        out_specs=[vmem_spec] * 2,
        scratch_shapes=[pltpu.SemaphoreType.DMA((2, CAPP, new_rows // PIECE))],
        out_shape=[jax.ShapeDtypeStruct((CAPP, new_rows, kv_width), jnp.bfloat16)] * 2,
        compiler_params=params,
        name="push",
    )(decode_owner, *[array for _, array in moved])
    return (attended[None], pushed_keys, pushed_values)


def solution(mesh):
    in_specs = (
        P(("groups", "pool"), None, ("tensor", "sub")),
        P(("groups", "pool"), None, ("tensor", "sub")),
        P(("groups", "pool"), None, ("tensor", "sub")),
        P(("groups", "pool"), None, ("tensor", "sub")),
        P(("groups", "pool"), None, ("tensor", "sub")),
        P("groups"),
        P("groups", None),
        P("groups", None),
        P("groups"),
    )
    out_specs = (
        P(("groups", "pool"), None, ("tensor", "sub")),
        P(("groups", "pool"), None, ("tensor", "sub")),
        P(("groups", "pool"), None, ("tensor", "sub")),
    )
    return jax.shard_map(shards, mesh=mesh, in_specs=in_specs, out_specs=out_specs, check_vma=False)
```

```python
import functools
import math

import jax
import jax.numpy as jnp
from jax import lax
from jax.experimental import pallas as pl
from jax.experimental.pallas import tpu as pltpu
from jax.sharding import PartitionSpec as P

HEADS = 64
KVH = 8
HD = 128
MAXBLK = 32
CAPP = 2
GROUP = HEADS // KVH
EMPTY = -1e30
TILE = 256
ONES = 16
PIECE = 32
EXP2_SCALE = math.log2(math.e) / math.sqrt(HD)
VMEM_LIMIT = 63 * 1024 * 1024 + 512 * 1024


def blocks_at(tables, request, place, pool_size):
    prefix_ref, store_ref, slot_ref = tables
    first = lax.rem(place - store_ref[request, 0] + pool_size, pool_size)
    count = lax.max(lax.div(prefix_ref[request] - first + pool_size - 1, pool_size), 0)
    return count, lambda entry: slot_ref[request, first + entry * pool_size]


def fetch(pool_size, tables, request, stores, buffers, sems, moved=None):
    me = lax.axis_index("pool")
    count, slot_of = blocks_at(tables, request, me if moved is None else me ^ 1, pool_size)

    def copies(entry):
        for i in range(2):
            if moved is None:
                source = stores[i].at[slot_of(entry)]
            else:
                source = moved.at[i * (moved.shape[0] // 2) + entry]
            yield pltpu.make_async_copy(source, buffers[i].at[entry], sems.at[i, entry])

    def start(entry, carry):
        for copy in copies(entry):
            copy.start()
        return carry

    lax.fori_loop(0, count, start, 0)

    def ready(entry):
        for copy in copies(entry):
            copy.wait()

    return count, ready


def gather_kernel(pool_size, prefix_ref, store_ref, slot_ref, store_keys, store_values, out_ref, sems):
    me = lax.axis_index("pool")
    capacity = out_ref.shape[0] // 2

    @pl.when(jnp.logical_not(is_inner(me)))
    def _():
        tables = (prefix_ref, store_ref, slot_ref)
        count, slot_of = blocks_at(tables, me ^ 3, me, pool_size)

        def copies(entry):
            return [
                pltpu.make_async_copy(
                    store.at[slot_of(entry)], out_ref.at[i * capacity + entry], sems.at[i, entry]
                )
                for i, store in enumerate((store_keys, store_values))
            ]

        def start(entry, carry):
            for copy in copies(entry):
                copy.start()
            return carry

        def wait(entry, carry):
            for copy in copies(entry):
                copy.wait()
            return carry

        lax.fori_loop(0, count, start, 0)
        lax.fori_loop(0, count, wait, 0)


def attend(
    key_ref,
    value_ref,
    count,
    ready,
    fresh,
    new_rows,
    columns,
    scores,
    weights,
    peaks,
    factors,
    tops,
    turned,
    acc,
    initial=None,
    raw=False,
):
    rows = columns.shape[1]
    kv_local = columns.shape[0] // HD

    def visit(keys, values, seen):
        size = keys[0].shape[0]

        def score(kv):
            turned[kv, :HD, :size] = values[kv].T
            block = lax.dot_general(
                keys[kv],
                columns[kv * HD : (kv + 1) * HD, :],
                (((1,), (0,)), ((), ())),
                preferred_element_type=jnp.float32,
            )
            block = block * EXP2_SCALE
            if seen is not None:
                block = jnp.where(seen, block, EMPTY)
            scores[kv, :size, :] = block
            tops[kv] = jnp.max(block.reshape(size // 8, 8, rows), axis=0)

        def weigh(kv):
            for i in range(0, rows, TILE):
                part = slice(i, i + TILE)
                before = peaks[kv, :, part]
                top = jnp.max(tops[kv, :, part], axis=0, keepdims=True)
                peak = jnp.maximum(before, top)
                factors[kv, :, part] = jnp.exp2(before - peak)
                peaks[kv, :, part] = peak
                weight = jnp.exp2(scores[kv, :size, part] - peak[0:1])
                weights[kv, :size, part] = weight.astype(jnp.bfloat16)

        def mix(kv):
            added = lax.dot_general(
                turned[kv, :, :size],
                weights[kv, :size, :],
                (((1,), (0,)), ((), ())),
                preferred_element_type=jnp.float32,
            )
            acc[kv] = acc[kv] * factors[kv, 0:1, :] + added

        for step in range(kv_local + 2):
            for offset, stage in ((0, score), (2, mix), (1, weigh)):
                if 0 <= step - offset < kv_local:
                    stage(step - offset)

    def lanes_of(array):
        return [array[:, kv * HD : (kv + 1) * HD] for kv in range(kv_local)]

    def blocks_of(ref, first, number):
        return lanes_of(ref[pl.ds(first, number)].reshape(number * ref.shape[1], ref.shape[2]))

    if initial is None:
        peaks[...] = jnp.full(peaks.shape, EMPTY, jnp.float32)
        acc[...] = jnp.zeros(acc.shape, jnp.float32)
    else:
        for copy in initial(acc, peaks):
            copy.wait()
    turned[:, HD:, :] = jnp.ones((kv_local, ONES, turned.shape[2]), jnp.bfloat16)
    if fresh is not None:
        new_key_ref, new_value_ref = fresh
        row = lax.rem(lax.broadcasted_iota(jnp.int32, (1, rows), 1), new_rows)
        seen = lax.broadcasted_iota(jnp.int32, (new_key_ref.shape[0], rows), 0) <= row
        visit(lanes_of(new_key_ref), lanes_of(new_value_ref), seen)

    def visit_blocks(number, first):
        def body(index, carry):
            entry = first + index * number
            for i in range(number):
                ready(entry + i)
            visit(
                blocks_of(key_ref, entry, number),
                blocks_of(value_ref, entry, number),
                None,
            )
            return carry

        return body

    done = 0
    for number in (4, 2, 1):
        if number <= key_ref.shape[0]:
            steps = (count - done) // number
            lax.fori_loop(0, steps, visit_blocks(number, done), 0)
            done = done + steps * number
    if raw:
        return acc, peaks
    outs = []
    logs = []
    for kv in range(kv_local):
        total = acc[kv, HD : HD + 1, :]
        safe = jnp.where(total > 0, total, 1.0)
        logs.append(jnp.where(total > 0, peaks[kv, 0:1] * math.log(2.0) + jnp.log(safe), EMPTY))
        outs.append(acc[kv, :HD, :] * (1.0 / safe))
    return outs, logs


def prepare_kernel(query_ref, new_key_ref, new_value_ref, payload_ref, query_rows):
    new_rows = query_ref.shape[0]
    kv_width = new_key_ref.shape[1]
    for kv in range(kv_width // HD):
        for g in range(GROUP):
            head = kv * GROUP + g
            query_rows[g * new_rows : (g + 1) * new_rows, :] = query_ref[
                :, head * HD : (head + 1) * HD
            ]
        payload_ref[kv * HD : (kv + 1) * HD, :] = query_rows[...].T
    for i, new_ref in enumerate((new_key_ref, new_value_ref)):
        for piece in range(new_rows // PIECE):
            row, lane = piece_place(i, piece, new_rows, kv_width)
            payload_ref[row : row + PIECE, lane : lane + kv_width] = new_ref[
                piece * PIECE : (piece + 1) * PIECE, :
            ]


def piece_place(i, piece, new_rows, kv_width):
    index = i * (new_rows // PIECE) + piece
    beside = GROUP * new_rows // kv_width
    return kv_width + index // beside * PIECE, index % beside * kv_width


def payload_rows(new_rows, kv_width):
    return piece_place(1, new_rows // PIECE - 1, new_rows, kv_width)[0] + PIECE


def own_kernel(
    pool_size,
    prefix_ref,
    store_ref,
    slot_ref,
    payload_ref,
    new_key_ref,
    new_value_ref,
    store_keys,
    store_values,
    out_ref,
    log_ref,
    key_buf,
    value_buf,
    new_key_buf,
    new_value_buf,
    *state,
):
    *work, sems = state
    count, ready = fetch(
        pool_size,
        (prefix_ref, store_ref, slot_ref),
        lax.axis_index("pool"),
        (store_keys, store_values),
        (key_buf, value_buf),
        sems,
    )
    new_rows, kv_width = new_key_ref.shape
    for buffer, source in ((new_key_buf, new_key_ref), (new_value_buf, new_value_ref)):
        buffer[:new_rows, :] = source[...]
        buffer[new_rows:, :] = jnp.zeros((buffer.shape[0] - new_rows, kv_width), jnp.bfloat16)
    fresh = (new_key_buf, new_value_buf)
    outs, logs = attend(
        key_buf, value_buf, count, ready, fresh, new_rows, payload_ref.at[:kv_width], *work
    )
    log_ref[...] = jnp.zeros(log_ref.shape, jnp.float32)
    for kv, (out, log) in enumerate(zip(outs, logs)):
        out_ref[kv * HD : (kv + 1) * HD, :] = out
        log_ref[kv : kv + 1, :] = log


def other_kernel(pool_size, new_rows, partners, with_moved, raw, *refs):
    if partners is None:
        request = refs[0][0]
        choice = [None]
        refs = refs[1:]
    else:
        inner = is_inner(lax.axis_index("pool"))
        _, request = source_of(lax.axis_index("pool"), partners)
        choice = [
            hit for hit, mask in zip((inner, jnp.logical_not(inner)), partners) if mask is not None
        ]
    tables, refs = refs[:3], refs[3:]
    payload_refs, refs = refs[: len(choice)], refs[len(choice) :]
    moved = initial = None
    if with_moved:
        moved, *initial = refs[:3]
        refs = refs[3:]
    store_keys, store_values, *refs = refs
    results_ref, (key_buf, value_buf, *state) = refs[: 1 + 2 * raw], refs[1 + 2 * raw :]
    *work, columns, query_sem, out_buf, out_sem, sems = state
    kv_width = columns.shape[0]

    def query_copy(payload_ref):
        return pltpu.make_async_copy(payload_ref.at[:kv_width], columns, query_sem)

    def run():
        for payload_ref, hit in zip(payload_refs, choice):
            if len(choice) == 1:
                query_copy(payload_ref).start()
            else:
                pl.when(hit)(query_copy(payload_ref).start)
        if raw:
            passed = pltpu.make_async_copy(
                payload_refs[0].at[kv_width:], results_ref[2], out_sem.at[2]
            )
            passed.start()
        restore = None
        if initial is not None:

            def restore(*targets):
                return [
                    pltpu.make_async_copy(source, target, out_sem.at[i])
                    for i, (source, target) in enumerate(zip(initial, targets))
                ]

            for copy in restore(work[-1], work[2]):
                copy.start()
        count, ready = fetch(
            pool_size,
            tables,
            request,
            (store_keys, store_values),
            (key_buf, value_buf),
            sems,
            moved,
        )
        query_copy(payload_refs[0]).wait()
        results = attend(
            key_buf, value_buf, count, ready, None, new_rows, columns, *work, restore, raw
        )
        if raw:
            copies = [
                pltpu.make_async_copy(result, out_ref, out_sem.at[i])
                for i, (out_ref, result) in enumerate(zip(results_ref, results))
            ]
            for copy in copies:
                copy.start()
            for copy in (*copies, passed):
                copy.wait()
            return
        outs, logs = results
        tail = []
        copies = []

        def send_rows(start, size):
            copies.append(
                pltpu.make_async_copy(
                    out_buf.at[start : start + size],
                    results_ref[0].at[start : start + size],
                    out_sem.at[len(copies)],
                )
            )
            copies[-1].start()

        for kv, (out, log) in enumerate(zip(outs, logs)):
            out_buf[kv * HD : (kv + 1) * HD, :] = out.astype(jnp.bfloat16)
            send_rows(kv * HD, HD)
            high = log.astype(jnp.bfloat16).astype(jnp.float32)
            middle = (log - high).astype(jnp.bfloat16).astype(jnp.float32)
            tail += [high, middle, log - high - middle]
        tail.append(jnp.zeros((ONES - len(tail), columns.shape[1]), jnp.float32))
        out_buf[kv_width:, :] = jnp.concatenate(tail, axis=0).astype(jnp.bfloat16)
        send_rows(kv_width, ONES)
        for copy in copies:
            copy.wait()

    if len(choice) == 1 and choice[0] is not None:
        pl.when(choice[0])(run)
    else:
        run()


def is_inner(place):
    return (place == 1) | (place == 2)


def source_of(me, entry):
    if isinstance(entry, int):
        return jnp.bool_(True), jnp.int32(entry)
    inner = is_inner(me)
    masks = [0 if mask is None else mask for mask in entry]
    there = jnp.where(inner, entry[0] is not None, entry[1] is not None)
    return there, me ^ jnp.where(inner, masks[0], masks[1])


def push_kernel(pool_size, entries, owner_ref, *refs):
    payload_refs = refs[: len(entries)]
    key_out, value_out, sems = refs[len(entries) :]
    outs = (key_out, value_out)
    kv_width = key_out.shape[2]
    me = lax.axis_index("pool")
    total = jnp.int32(0)
    for other in range(pool_size):
        total += (owner_ref[other] == me).astype(jnp.int32)

    new_rows = key_out.shape[1]

    def copies(payload_ref, place):
        for i in range(2):
            for piece in range(new_rows // PIECE):
                row, lane = piece_place(i, piece, new_rows, kv_width)
                row += payload_ref.shape[0] - payload_rows(new_rows, kv_width)
                yield pltpu.make_async_copy(
                    payload_ref.at[row : row + PIECE, lane : lane + kv_width],
                    outs[i].at[place, piece * PIECE : (piece + 1) * PIECE],
                    sems.at[i, place, piece],
                )

    for entry, payload_ref in zip(entries, payload_refs):
        there, source = source_of(me, entry)
        rank = jnp.int32(0)
        for other in range(pool_size):
            rank += ((owner_ref[other] == me) & (other < source)).astype(jnp.int32)
        hit = there & (owner_ref[source] == me)
        for place in range(CAPP):

            @pl.when(hit & (rank == place))
            def _():
                for copy in copies(payload_ref, place):
                    copy.start()

    for place in range(CAPP):

        @pl.when(total <= place)
        def _():
            for out in outs:
                out[place] = jnp.zeros(out.shape[1:], jnp.bfloat16)

        @pl.when(total > place)
        def _():
            for copy in copies(payload_refs[0], place):
                copy.wait()


def combine_kernel(sources, last, own_ref, log_ref, *refs):
    parts = refs[: len(sources)]
    out_ref = refs[len(sources)]
    kv_width, rows = own_ref.shape
    me = lax.axis_index("pool")
    arrived = []
    tails = []
    for source, part in zip(sources, parts):
        there, request = source_of(me, source)
        arrived.append(there & (request != me))
        tails.append(part[kv_width:, :].astype(jnp.float32))
    if not last:
        refs[len(sources) + 1][...] = log_ref[...]
    for kv in range(kv_width // HD):
        logs = [log_ref[kv : kv + 1, :]]
        for there, tail in zip(arrived, tails):
            log = sum(tail[3 * kv + i : 3 * kv + i + 1] for i in range(3))
            logs.append(jnp.where(there, log, EMPTY))
        peak = functools.reduce(jnp.maximum, logs)
        shares = [jnp.exp(x - peak) for x in logs]
        total = functools.reduce(jnp.add, shares)
        shares = [x * (1.0 / total) for x in shares]
        band = slice(kv * HD, (kv + 1) * HD)
        for i in range(0, rows, TILE):
            part = slice(i, i + TILE)
            mixed = own_ref[band, part] * shares[0][:, part]
            for share, ref in zip(shares[1:], parts):
                mixed = mixed + ref[band, part].astype(jnp.float32) * share[:, part]
            if last:
                refs[len(sources) + 1][part, :] = mixed.astype(jnp.bfloat16).T
            else:
                out_ref[band, part] = mixed
        if last:
            turned = refs[len(sources) + 1]
            new_rows = out_ref.shape[0]
            for g in range(GROUP):
                head = kv * GROUP + g
                out_ref[:, head * HD : (head + 1) * HD] = turned[g * new_rows : (g + 1) * new_rows, :]
        else:
            refs[len(sources) + 1][kv : kv + 1, :] = peak + jnp.log(total)


def final_kernel(own_ref, log_ref, outer_ref, inner_ref, out_ref, own_buf, part_buf, out_buf, turned, sems):
    kv_width, rows = own_buf.shape
    new_rows = out_buf.shape[0]
    kv_local = kv_width // HD
    lanes = GROUP * HD
    inner = is_inner(lax.axis_index("pool"))
    bands = [slice(kv * HD, (kv + 1) * HD) for kv in range(kv_local)] + [slice(kv_width, kv_width + ONES)]

    def part_copies(ref):
        return [
            pltpu.make_async_copy(ref.at[band], part_buf.at[band], sems.at[0, i])
            for i, band in enumerate(bands)
        ]

    def start_part(ref):
        for copy in reversed(part_copies(ref)):
            copy.start()

    own_copies = [
        pltpu.make_async_copy(own_ref.at[band], own_buf.at[band], sems.at[1, i])
        for i, band in enumerate(bands[:-1])
    ]
    pl.when(inner)(functools.partial(start_part, inner_ref))
    pl.when(jnp.logical_not(inner))(functools.partial(start_part, outer_ref))
    for copy in own_copies:
        copy.start()
    arriving = part_copies(outer_ref)
    arriving[-1].wait()
    tail = part_buf[kv_width:, :].astype(jnp.float32)
    leaving = []
    for kv in range(kv_local):
        log = log_ref[kv : kv + 1, :]
        other = sum(tail[3 * kv + i : 3 * kv + i + 1] for i in range(3))
        peak = jnp.maximum(log, other)
        shares = [jnp.exp(log - peak), jnp.exp(other - peak)]
        scale = 1.0 / (shares[0] + shares[1])
        shares = [share * scale for share in shares]
        arriving[kv].wait()
        own_copies[kv].wait()
        for i in range(0, rows, TILE):
            part = slice(i, i + TILE)
            mixed = own_buf[bands[kv], part] * shares[0][:, part]
            mixed = mixed + part_buf[bands[kv], part].astype(jnp.float32) * shares[1][:, part]
            turned[part, :] = mixed.astype(jnp.bfloat16).T
        for g in range(GROUP):
            head = kv * GROUP + g
            out_buf[:, head * HD : (head + 1) * HD] = turned[g * new_rows : (g + 1) * new_rows, :]
        band = slice(kv * lanes, (kv + 1) * lanes)
        leaving.append(
            pltpu.make_async_copy(out_buf.at[:, band], out_ref.at[:, band], sems.at[2, kv])
        )
        leaving[-1].start()
    for copy in leaving:
        copy.wait()


def shards(
    queries,
    new_keys,
    new_values,
    store_keys,
    store_values,
    prefix_blocks,
    hit_store,
    hit_slot,
    decode_owner,
):
    pool_size = lax.axis_size("pool")
    capacity = (MAXBLK + pool_size - 1) // pool_size
    new_rows = queries.shape[1]
    width = queries.shape[2]
    kv_width = new_keys.shape[2]
    block_len = store_keys.shape[1]
    rows = GROUP * new_rows
    tables = (prefix_blocks, hit_store, hit_slot)
    smem_spec = pl.BlockSpec(memory_space=pltpu.SMEM)
    hbm_spec = pl.BlockSpec(memory_space=pltpu.HBM)
    vmem_spec = pl.BlockSpec(memory_space=pltpu.VMEM)
    params = pltpu.CompilerParams(vmem_limit_bytes=VMEM_LIMIT)

    def cost(share):
        return pl.CostEstimate(
            flops=share * rows * block_len * kv_width * capacity,
            bytes_accessed=rows,
            transcendentals=0,
        )

    buffers = [pltpu.VMEM((capacity, block_len, kv_width), jnp.bfloat16)] * 2
    kv_local = kv_width // HD
    widest = block_len * min(4, capacity)
    work = [
        pltpu.VMEM((kv_local, widest, rows), jnp.float32),
        pltpu.VMEM((kv_local, widest, rows), jnp.bfloat16),
        pltpu.VMEM((kv_local, 8, rows), jnp.float32),
        pltpu.VMEM((kv_local, 8, rows), jnp.float32),
        pltpu.VMEM((kv_local, 8, rows), jnp.float32),
        pltpu.VMEM((kv_local, HD + ONES, widest), jnp.bfloat16),
        pltpu.VMEM((kv_local, HD + ONES, rows), jnp.float32),
    ]
    sems = pltpu.SemaphoreType.DMA((2, capacity))

    def own_part(payload):
        return pl.pallas_call(
            functools.partial(own_kernel, pool_size),
            in_specs=[smem_spec] * 3 + [vmem_spec] * 3 + [hbm_spec] * 2,
            out_specs=[vmem_spec] * 2,
            scratch_shapes=[
                *buffers,
                *[pltpu.VMEM((block_len, kv_width), jnp.bfloat16)] * 2,
                *work,
                sems,
            ],
            out_shape=[
                jax.ShapeDtypeStruct((kv_width, rows), jnp.float32),
                jax.ShapeDtypeStruct((8, rows), jnp.float32),
            ],
            compiler_params=params,
            cost_estimate=cost(8),
            name="own_part",
        )(*tables, payload, new_keys[0], new_values[0], store_keys, store_values)

    def other_part(partners, held, *request, share=8, moved=(), raw=False):
        if raw:
            out_shape = [
                jax.ShapeDtypeStruct((kv_local, HD + ONES, rows), jnp.float32),
                jax.ShapeDtypeStruct((kv_local, 8, rows), jnp.float32),
                jax.ShapeDtypeStruct((held[0].shape[0] - kv_width, rows), jnp.bfloat16),
            ]
        else:
            out_shape = jax.ShapeDtypeStruct((kv_width + ONES, rows), jnp.bfloat16)
        more_specs = [hbm_spec] * 3 if moved else []
        return pl.pallas_call(
            functools.partial(other_kernel, pool_size, new_rows, partners, bool(moved), raw),
            in_specs=[smem_spec] * (3 + len(request))
            + [hbm_spec] * len(held)
            + more_specs
            + [hbm_spec] * 2,
            out_specs=[hbm_spec] * 3 if raw else hbm_spec,
            scratch_shapes=[
                *buffers,
                *work,
                pltpu.VMEM((kv_width, rows), jnp.bfloat16),
                pltpu.SemaphoreType.DMA,
                pltpu.VMEM((kv_width + ONES, rows), jnp.bfloat16),
                pltpu.SemaphoreType.DMA((max(3, kv_local + 1),)),
                sems,
            ],
            out_shape=out_shape,
            compiler_params=params,
            cost_estimate=cost(share),
            name="other_part",
        )(*request, *tables, *held, *moved, store_keys, store_values)

    def combine(own, log, sources, parts, last=True):
        if last:
            out_shape = jax.ShapeDtypeStruct((new_rows, width), jnp.bfloat16)
        else:
            out_shape = [
                jax.ShapeDtypeStruct((kv_width, rows), jnp.float32),
                jax.ShapeDtypeStruct((8, rows), jnp.float32),
            ]
        return pl.pallas_call(
            functools.partial(combine_kernel, tuple(sources), last),
            in_specs=[vmem_spec] * (2 + len(parts)),
            out_specs=vmem_spec if last else [vmem_spec] * 2,
            scratch_shapes=[pltpu.VMEM((rows, HD), jnp.bfloat16)] if last else [],
            out_shape=out_shape,
            compiler_params=params,
            cost_estimate=cost(0),
            name="combine",
        )(own, log, *parts)

    def final(own, log, parts):
        return pl.pallas_call(
            final_kernel,
            in_specs=[hbm_spec, vmem_spec, hbm_spec, hbm_spec],
            out_specs=hbm_spec,
            scratch_shapes=[
                pltpu.VMEM((kv_width, rows), jnp.float32),
                pltpu.VMEM((kv_width + ONES, rows), jnp.bfloat16),
                pltpu.VMEM((new_rows, width), jnp.bfloat16),
                pltpu.VMEM((rows, HD), jnp.bfloat16),
                pltpu.SemaphoreType.DMA((3, kv_local + 1)),
            ],
            out_shape=jax.ShapeDtypeStruct((new_rows, width), jnp.bfloat16),
            compiler_params=params,
            name="final",
        )(own, log, *parts)

    payload = pl.pallas_call(
        prepare_kernel,
        in_specs=[vmem_spec] * 3,
        out_specs=vmem_spec,
        scratch_shapes=[pltpu.VMEM((rows, HD), jnp.bfloat16)],
        out_shape=jax.ShapeDtypeStruct((payload_rows(new_rows, kv_width), rows), jnp.bfloat16),
        compiler_params=params,
        name="prepare",
    )(queries[0], new_keys[0], new_values[0])
    own_out, own_log = own_part(payload)
    if pool_size == 4:
        def send(array, *pairs):
            return lax.ppermute(array, "pool", pairs)

        near = send(payload, (0, 1), (1, 0), (2, 3), (3, 2))
        middle = send(payload, (1, 2), (2, 1))
        blocks = pl.pallas_call(
            functools.partial(gather_kernel, pool_size),
            in_specs=[smem_spec] * 3 + [hbm_spec] * 2,
            out_specs=vmem_spec,
            scratch_shapes=[sems],
            out_shape=jax.ShapeDtypeStruct((2 * capacity, block_len, kv_width), jnp.bfloat16),
            compiler_params=params,
            name="gather_blocks",
        )(*tables, store_keys, store_values)
        blocks = send(blocks, (0, 1), (3, 2))
        near, middle, own_out, own_log = lax.optimization_barrier((near, middle, own_out, own_log))
        crossed = send(near, (1, 2), (2, 1))
        outward = send(middle, (1, 0), (2, 3))
        first = other_part((3, 1), (middle, near))
        near, first = lax.optimization_barrier((near, first))
        second = other_part((1, None), (near,))
        first, second = lax.optimization_barrier((first, second))
        across = send(first, (1, 2), (2, 1))
        back = send(second, (1, 0), (2, 3))
        outward, second = lax.optimization_barrier((outward, second))
        outer_second = other_part((None, 2), (outward,))
        apart = send(outer_second, (0, 2), (3, 1))
        crossed, first, outer_second = lax.optimization_barrier((crossed, first, outer_second))
        inward = send(first, (0, 1), (3, 2))
        *state, fresh = other_part((2, None), (crossed,), raw=True)
        crossed, state = lax.optimization_barrier((crossed, state))
        far = send(fresh, (1, 0), (2, 3))
        third = other_part((2, None), (crossed,), moved=(blocks, *state))
        ends = send(third, (1, 3), (2, 0))
        own_out, own_log, third = lax.optimization_barrier((own_out, own_log, third))
        own_out, own_log = combine(
            own_out, own_log, [(3, None), (2, None), (None, 1)], [across, apart, back], last=False
        )
        attended = final(own_out, own_log, (ends, inward))
        moved = [
            ((0, 0), payload),
            ((1, 1), near),
            ((3, None), middle),
            ((2, None), crossed),
            ((None, 2), outward),
            ((None, 3), far),
        ]
    else:
        gathered = lax.all_gather(payload, "pool", axis=0, tiled=False)
        packed = lax.map(
            lambda pair: other_part(None, (pair[0],), pair[1].reshape(1)),
            (gathered, jnp.arange(pool_size, dtype=jnp.int32)),
        )
        parts = lax.all_to_all(packed, "pool", split_axis=0, concat_axis=0, tiled=True)
        attended = combine(own_out, own_log, list(range(pool_size)), parts)
        moved = [(source, gathered[source]) for source in range(pool_size)]

    pushed_keys, pushed_values = pl.pallas_call(
        functools.partial(push_kernel, pool_size, tuple(entry for entry, _ in moved)),
        in_specs=[smem_spec] + [hbm_spec] * len(moved),
        out_specs=[vmem_spec] * 2,
        scratch_shapes=[pltpu.SemaphoreType.DMA((2, CAPP, new_rows // PIECE))],
        out_shape=[jax.ShapeDtypeStruct((CAPP, new_rows, kv_width), jnp.bfloat16)] * 2,
        compiler_params=params,
        name="push",
    )(decode_owner, *[array for _, array in moved])
    return (attended[None], pushed_keys, pushed_values)


def solution(mesh):
    in_specs = (
        P(("groups", "pool"), None, ("tensor", "sub")),
        P(("groups", "pool"), None, ("tensor", "sub")),
        P(("groups", "pool"), None, ("tensor", "sub")),
        P(("groups", "pool"), None, ("tensor", "sub")),
        P(("groups", "pool"), None, ("tensor", "sub")),
        P("groups"),
        P("groups", None),
        P("groups", None),
        P("groups"),
    )
    out_specs = (
        P(("groups", "pool"), None, ("tensor", "sub")),
        P(("groups", "pool"), None, ("tensor", "sub")),
        P(("groups", "pool"), None, ("tensor", "sub")),
    )
    return jax.shard_map(shards, mesh=mesh, in_specs=in_specs, out_specs=out_specs, check_vma=False)
```

```python
import functools
import math

import jax
import jax.numpy as jnp
from jax import lax
from jax.experimental import pallas as pl
from jax.experimental.pallas import tpu as pltpu
from jax.sharding import PartitionSpec as P

HEADS = 64
KVH = 8
HD = 128
MAXBLK = 32
CAPP = 2
GROUP = HEADS // KVH
EMPTY = -1e30
TILE = 256
ONES = 16
PIECE = 32
EXP2_SCALE = math.log2(math.e) / math.sqrt(HD)
VMEM_LIMIT = 63 * 1024 * 1024 + 512 * 1024


def blocks_at(tables, request, place, pool_size):
    prefix_ref, store_ref, slot_ref = tables
    first = lax.rem(place - store_ref[request, 0] + pool_size, pool_size)
    count = lax.max(lax.div(prefix_ref[request] - first + pool_size - 1, pool_size), 0)
    return count, lambda entry: slot_ref[request, first + entry * pool_size]


def fetch(pool_size, tables, request, stores, buffers, sems, moved=None):
    me = lax.axis_index("pool")
    count, slot_of = blocks_at(tables, request, me if moved is None else me ^ 1, pool_size)

    def copies(entry):
        for i in range(2):
            if moved is None:
                source = stores[i].at[slot_of(entry)]
            else:
                source = moved.at[i * (moved.shape[0] // 2) + entry]
            yield pltpu.make_async_copy(source, buffers[i].at[entry], sems.at[i, entry])

    def start(entry, carry):
        for copy in copies(entry):
            copy.start()
        return carry

    lax.fori_loop(0, count, start, 0)

    def ready(entry):
        for copy in copies(entry):
            copy.wait()

    return count, ready


def gather_kernel(pool_size, prefix_ref, store_ref, slot_ref, store_keys, store_values, out_ref, sems):
    me = lax.axis_index("pool")
    capacity = out_ref.shape[0] // 2

    @pl.when(jnp.logical_not(is_inner(me)))
    def _():
        tables = (prefix_ref, store_ref, slot_ref)
        count, slot_of = blocks_at(tables, me ^ 3, me, pool_size)

        def copies(entry):
            return [
                pltpu.make_async_copy(
                    store.at[slot_of(entry)], out_ref.at[i * capacity + entry], sems.at[i, entry]
                )
                for i, store in enumerate((store_keys, store_values))
            ]

        def start(entry, carry):
            for copy in copies(entry):
                copy.start()
            return carry

        def wait(entry, carry):
            for copy in copies(entry):
                copy.wait()
            return carry

        lax.fori_loop(0, count, start, 0)
        lax.fori_loop(0, count, wait, 0)


def attend(
    key_ref,
    value_ref,
    count,
    ready,
    fresh,
    new_rows,
    columns,
    scores,
    weights,
    peaks,
    factors,
    tops,
    turned,
    acc,
    initial=None,
    raw=False,
):
    rows = columns.shape[1]
    kv_local = columns.shape[0] // HD

    def visit(keys, values, seen):
        size = keys[0].shape[0]

        def score(kv):
            turned[kv, :HD, :size] = values[kv].T
            block = lax.dot_general(
                keys[kv],
                columns[kv * HD : (kv + 1) * HD, :],
                (((1,), (0,)), ((), ())),
                preferred_element_type=jnp.float32,
            )
            block = block * EXP2_SCALE
            if seen is not None:
                block = jnp.where(seen, block, EMPTY)
            scores[kv, :size, :] = block
            tops[kv] = jnp.max(block.reshape(size // 8, 8, rows), axis=0)

        def weigh(kv):
            for i in range(0, rows, TILE):
                part = slice(i, i + TILE)
                before = peaks[kv, :, part]
                top = jnp.max(tops[kv, :, part], axis=0, keepdims=True)
                peak = jnp.maximum(before, top)
                factors[kv, :, part] = jnp.exp2(before - peak)
                peaks[kv, :, part] = peak
                weight = jnp.exp2(scores[kv, :size, part] - peak[0:1])
                weights[kv, :size, part] = weight.astype(jnp.bfloat16)

        def mix(kv):
            added = lax.dot_general(
                turned[kv, :, :size],
                weights[kv, :size, :],
                (((1,), (0,)), ((), ())),
                preferred_element_type=jnp.float32,
            )
            acc[kv] = acc[kv] * factors[kv, 0:1, :] + added

        for step in range(kv_local + 2):
            for offset, stage in ((0, score), (2, mix), (1, weigh)):
                if 0 <= step - offset < kv_local:
                    stage(step - offset)

    def lanes_of(array):
        return [array[:, kv * HD : (kv + 1) * HD] for kv in range(kv_local)]

    def blocks_of(ref, first, number):
        return lanes_of(ref[pl.ds(first, number)].reshape(number * ref.shape[1], ref.shape[2]))

    if initial is None:
        peaks[...] = jnp.full(peaks.shape, EMPTY, jnp.float32)
        acc[...] = jnp.zeros(acc.shape, jnp.float32)
    else:
        for copy in initial(acc, peaks):
            copy.wait()
    turned[:, HD:, :] = jnp.ones((kv_local, ONES, turned.shape[2]), jnp.bfloat16)
    if fresh is not None:
        new_key_ref, new_value_ref = fresh
        row = lax.rem(lax.broadcasted_iota(jnp.int32, (1, rows), 1), new_rows)
        seen = lax.broadcasted_iota(jnp.int32, (new_key_ref.shape[0], rows), 0) <= row
        visit(lanes_of(new_key_ref), lanes_of(new_value_ref), seen)

    def visit_blocks(number):
        def body(index, carry):
            for i in range(number):
                ready(index * number + i)
            visit(
                blocks_of(key_ref, index * number, number),
                blocks_of(value_ref, index * number, number),
                None,
            )
            return carry

        return body

    pairs = count // 2 if key_ref.shape[0] > 1 else 0
    if key_ref.shape[0] > 1:
        lax.fori_loop(0, pairs, visit_blocks(2), 0)
    lax.fori_loop(2 * pairs, count, visit_blocks(1), 0)
    if raw:
        return acc, peaks
    outs = []
    logs = []
    for kv in range(kv_local):
        total = acc[kv, HD : HD + 1, :]
        safe = jnp.where(total > 0, total, 1.0)
        logs.append(jnp.where(total > 0, peaks[kv, 0:1] * math.log(2.0) + jnp.log(safe), EMPTY))
        outs.append(acc[kv, :HD, :] * (1.0 / safe))
    return outs, logs


def prepare_kernel(query_ref, new_key_ref, new_value_ref, payload_ref, query_rows):
    new_rows = query_ref.shape[0]
    kv_width = new_key_ref.shape[1]
    for kv in range(kv_width // HD):
        for g in range(GROUP):
            head = kv * GROUP + g
            query_rows[g * new_rows : (g + 1) * new_rows, :] = query_ref[
                :, head * HD : (head + 1) * HD
            ]
        payload_ref[kv * HD : (kv + 1) * HD, :] = query_rows[...].T
    for i, new_ref in enumerate((new_key_ref, new_value_ref)):
        for piece in range(new_rows // PIECE):
            row, lane = piece_place(i, piece, new_rows, kv_width)
            payload_ref[row : row + PIECE, lane : lane + kv_width] = new_ref[
                piece * PIECE : (piece + 1) * PIECE, :
            ]


def piece_place(i, piece, new_rows, kv_width):
    index = i * (new_rows // PIECE) + piece
    beside = GROUP * new_rows // kv_width
    return kv_width + index // beside * PIECE, index % beside * kv_width


def payload_rows(new_rows, kv_width):
    return piece_place(1, new_rows // PIECE - 1, new_rows, kv_width)[0] + PIECE


def own_kernel(
    pool_size,
    prefix_ref,
    store_ref,
    slot_ref,
    payload_ref,
    new_key_ref,
    new_value_ref,
    store_keys,
    store_values,
    out_ref,
    log_ref,
    key_buf,
    value_buf,
    new_key_buf,
    new_value_buf,
    *state,
):
    *work, sems = state
    count, ready = fetch(
        pool_size,
        (prefix_ref, store_ref, slot_ref),
        lax.axis_index("pool"),
        (store_keys, store_values),
        (key_buf, value_buf),
        sems,
    )
    new_rows, kv_width = new_key_ref.shape
    for buffer, source in ((new_key_buf, new_key_ref), (new_value_buf, new_value_ref)):
        buffer[:new_rows, :] = source[...]
        buffer[new_rows:, :] = jnp.zeros((buffer.shape[0] - new_rows, kv_width), jnp.bfloat16)
    fresh = (new_key_buf, new_value_buf)
    outs, logs = attend(
        key_buf, value_buf, count, ready, fresh, new_rows, payload_ref.at[:kv_width], *work
    )
    log_ref[...] = jnp.zeros(log_ref.shape, jnp.float32)
    for kv, (out, log) in enumerate(zip(outs, logs)):
        out_ref[kv * HD : (kv + 1) * HD, :] = out
        log_ref[kv : kv + 1, :] = log


def other_kernel(pool_size, new_rows, partners, with_moved, raw, *refs):
    if partners is None:
        request = refs[0][0]
        choice = [None]
        refs = refs[1:]
    else:
        inner = is_inner(lax.axis_index("pool"))
        _, request = source_of(lax.axis_index("pool"), partners)
        choice = [
            hit for hit, mask in zip((inner, jnp.logical_not(inner)), partners) if mask is not None
        ]
    tables, refs = refs[:3], refs[3:]
    payload_refs, refs = refs[: len(choice)], refs[len(choice) :]
    moved = initial = None
    if with_moved:
        moved, *initial = refs[:3]
        refs = refs[3:]
    store_keys, store_values, *refs = refs
    results_ref, (key_buf, value_buf, *state) = refs[: 1 + 2 * raw], refs[1 + 2 * raw :]
    *work, columns, query_sem, out_buf, out_sem, sems = state
    kv_width = columns.shape[0]

    def query_copy(payload_ref):
        return pltpu.make_async_copy(payload_ref.at[:kv_width], columns, query_sem)

    def run():
        for payload_ref, hit in zip(payload_refs, choice):
            if len(choice) == 1:
                query_copy(payload_ref).start()
            else:
                pl.when(hit)(query_copy(payload_ref).start)
        if raw:
            passed = pltpu.make_async_copy(
                payload_refs[0].at[kv_width:], results_ref[2], out_sem.at[2]
            )
            passed.start()
        restore = None
        if initial is not None:

            def restore(*targets):
                return [
                    pltpu.make_async_copy(source, target, out_sem.at[i])
                    for i, (source, target) in enumerate(zip(initial, targets))
                ]

            for copy in restore(work[-1], work[2]):
                copy.start()
        count, ready = fetch(
            pool_size,
            tables,
            request,
            (store_keys, store_values),
            (key_buf, value_buf),
            sems,
            moved,
        )
        query_copy(payload_refs[0]).wait()
        results = attend(
            key_buf, value_buf, count, ready, None, new_rows, columns, *work, restore, raw
        )
        if raw:
            copies = [
                pltpu.make_async_copy(result, out_ref, out_sem.at[i])
                for i, (out_ref, result) in enumerate(zip(results_ref, results))
            ]
            for copy in copies:
                copy.start()
            for copy in (*copies, passed):
                copy.wait()
            return
        outs, logs = results
        tail = []
        copies = []

        def send_rows(start, size):
            copies.append(
                pltpu.make_async_copy(
                    out_buf.at[start : start + size],
                    results_ref[0].at[start : start + size],
                    out_sem.at[len(copies)],
                )
            )
            copies[-1].start()

        for kv, (out, log) in enumerate(zip(outs, logs)):
            out_buf[kv * HD : (kv + 1) * HD, :] = out.astype(jnp.bfloat16)
            send_rows(kv * HD, HD)
            high = log.astype(jnp.bfloat16).astype(jnp.float32)
            middle = (log - high).astype(jnp.bfloat16).astype(jnp.float32)
            tail += [high, middle, log - high - middle]
        tail.append(jnp.zeros((ONES - len(tail), columns.shape[1]), jnp.float32))
        out_buf[kv_width:, :] = jnp.concatenate(tail, axis=0).astype(jnp.bfloat16)
        send_rows(kv_width, ONES)
        for copy in copies:
            copy.wait()

    if len(choice) == 1 and choice[0] is not None:
        pl.when(choice[0])(run)
    else:
        run()


def is_inner(place):
    return (place == 1) | (place == 2)


def source_of(me, entry):
    if isinstance(entry, int):
        return jnp.bool_(True), jnp.int32(entry)
    inner = is_inner(me)
    masks = [0 if mask is None else mask for mask in entry]
    there = jnp.where(inner, entry[0] is not None, entry[1] is not None)
    return there, me ^ jnp.where(inner, masks[0], masks[1])


def push_kernel(pool_size, entries, owner_ref, *refs):
    payload_refs = refs[: len(entries)]
    key_out, value_out, sems = refs[len(entries) :]
    outs = (key_out, value_out)
    kv_width = key_out.shape[2]
    me = lax.axis_index("pool")
    total = jnp.int32(0)
    for other in range(pool_size):
        total += (owner_ref[other] == me).astype(jnp.int32)

    new_rows = key_out.shape[1]

    def copies(payload_ref, place):
        for i in range(2):
            for piece in range(new_rows // PIECE):
                row, lane = piece_place(i, piece, new_rows, kv_width)
                row += payload_ref.shape[0] - payload_rows(new_rows, kv_width)
                yield pltpu.make_async_copy(
                    payload_ref.at[row : row + PIECE, lane : lane + kv_width],
                    outs[i].at[place, piece * PIECE : (piece + 1) * PIECE],
                    sems.at[i, place, piece],
                )

    for entry, payload_ref in zip(entries, payload_refs):
        there, source = source_of(me, entry)
        rank = jnp.int32(0)
        for other in range(pool_size):
            rank += ((owner_ref[other] == me) & (other < source)).astype(jnp.int32)
        hit = there & (owner_ref[source] == me)
        for place in range(CAPP):

            @pl.when(hit & (rank == place))
            def _():
                for copy in copies(payload_ref, place):
                    copy.start()

    for place in range(CAPP):

        @pl.when(total <= place)
        def _():
            for out in outs:
                out[place] = jnp.zeros(out.shape[1:], jnp.bfloat16)

        @pl.when(total > place)
        def _():
            for copy in copies(payload_refs[0], place):
                copy.wait()


def combine_kernel(sources, last, own_ref, log_ref, *refs):
    parts = refs[: len(sources)]
    out_ref = refs[len(sources)]
    kv_width, rows = own_ref.shape
    me = lax.axis_index("pool")
    arrived = []
    tails = []
    for source, part in zip(sources, parts):
        there, request = source_of(me, source)
        arrived.append(there & (request != me))
        tails.append(part[kv_width:, :].astype(jnp.float32))
    if not last:
        refs[len(sources) + 1][...] = log_ref[...]
    for kv in range(kv_width // HD):
        logs = [log_ref[kv : kv + 1, :]]
        for there, tail in zip(arrived, tails):
            log = sum(tail[3 * kv + i : 3 * kv + i + 1] for i in range(3))
            logs.append(jnp.where(there, log, EMPTY))
        peak = functools.reduce(jnp.maximum, logs)
        shares = [jnp.exp(x - peak) for x in logs]
        total = functools.reduce(jnp.add, shares)
        shares = [x * (1.0 / total) for x in shares]
        band = slice(kv * HD, (kv + 1) * HD)
        for i in range(0, rows, TILE):
            part = slice(i, i + TILE)
            mixed = own_ref[band, part] * shares[0][:, part]
            for share, ref in zip(shares[1:], parts):
                mixed = mixed + ref[band, part].astype(jnp.float32) * share[:, part]
            if last:
                refs[len(sources) + 1][part, :] = mixed.astype(jnp.bfloat16).T
            else:
                out_ref[band, part] = mixed
        if last:
            turned = refs[len(sources) + 1]
            new_rows = out_ref.shape[0]
            for g in range(GROUP):
                head = kv * GROUP + g
                out_ref[:, head * HD : (head + 1) * HD] = turned[g * new_rows : (g + 1) * new_rows, :]
        else:
            refs[len(sources) + 1][kv : kv + 1, :] = peak + jnp.log(total)


def final_kernel(own_ref, log_ref, outer_ref, inner_ref, out_ref, own_buf, part_buf, out_buf, turned, sems):
    kv_width, rows = own_buf.shape
    new_rows = out_buf.shape[0]
    kv_local = kv_width // HD
    lanes = GROUP * HD
    inner = is_inner(lax.axis_index("pool"))
    bands = [slice(kv * HD, (kv + 1) * HD) for kv in range(kv_local)] + [slice(kv_width, kv_width + ONES)]

    def part_copies(ref):
        return [
            pltpu.make_async_copy(ref.at[band], part_buf.at[band], sems.at[0, i])
            for i, band in enumerate(bands)
        ]

    def start_part(ref):
        for copy in reversed(part_copies(ref)):
            copy.start()

    own_copies = [
        pltpu.make_async_copy(own_ref.at[band], own_buf.at[band], sems.at[1, i])
        for i, band in enumerate(bands[:-1])
    ]
    pl.when(inner)(functools.partial(start_part, inner_ref))
    pl.when(jnp.logical_not(inner))(functools.partial(start_part, outer_ref))
    for copy in own_copies:
        copy.start()
    arriving = part_copies(outer_ref)
    arriving[-1].wait()
    tail = part_buf[kv_width:, :].astype(jnp.float32)
    leaving = []
    for kv in range(kv_local):
        log = log_ref[kv : kv + 1, :]
        other = sum(tail[3 * kv + i : 3 * kv + i + 1] for i in range(3))
        peak = jnp.maximum(log, other)
        shares = [jnp.exp(log - peak), jnp.exp(other - peak)]
        scale = 1.0 / (shares[0] + shares[1])
        shares = [share * scale for share in shares]
        arriving[kv].wait()
        own_copies[kv].wait()
        for i in range(0, rows, TILE):
            part = slice(i, i + TILE)
            mixed = own_buf[bands[kv], part] * shares[0][:, part]
            mixed = mixed + part_buf[bands[kv], part].astype(jnp.float32) * shares[1][:, part]
            turned[part, :] = mixed.astype(jnp.bfloat16).T
        for g in range(GROUP):
            head = kv * GROUP + g
            out_buf[:, head * HD : (head + 1) * HD] = turned[g * new_rows : (g + 1) * new_rows, :]
        band = slice(kv * lanes, (kv + 1) * lanes)
        leaving.append(
            pltpu.make_async_copy(out_buf.at[:, band], out_ref.at[:, band], sems.at[2, kv])
        )
        leaving[-1].start()
    for copy in leaving:
        copy.wait()


def shards(
    queries,
    new_keys,
    new_values,
    store_keys,
    store_values,
    prefix_blocks,
    hit_store,
    hit_slot,
    decode_owner,
):
    pool_size = lax.axis_size("pool")
    capacity = (MAXBLK + pool_size - 1) // pool_size
    new_rows = queries.shape[1]
    width = queries.shape[2]
    kv_width = new_keys.shape[2]
    block_len = store_keys.shape[1]
    rows = GROUP * new_rows
    tables = (prefix_blocks, hit_store, hit_slot)
    smem_spec = pl.BlockSpec(memory_space=pltpu.SMEM)
    hbm_spec = pl.BlockSpec(memory_space=pltpu.HBM)
    vmem_spec = pl.BlockSpec(memory_space=pltpu.VMEM)
    params = pltpu.CompilerParams(vmem_limit_bytes=VMEM_LIMIT)

    def cost(share):
        return pl.CostEstimate(
            flops=share * rows * block_len * kv_width * capacity,
            bytes_accessed=rows,
            transcendentals=0,
        )

    buffers = [pltpu.VMEM((capacity, block_len, kv_width), jnp.bfloat16)] * 2
    kv_local = kv_width // HD
    widest = block_len * min(2, capacity)
    work = [
        pltpu.VMEM((kv_local, widest, rows), jnp.float32),
        pltpu.VMEM((kv_local, widest, rows), jnp.bfloat16),
        pltpu.VMEM((kv_local, 8, rows), jnp.float32),
        pltpu.VMEM((kv_local, 8, rows), jnp.float32),
        pltpu.VMEM((kv_local, 8, rows), jnp.float32),
        pltpu.VMEM((kv_local, HD + ONES, widest), jnp.bfloat16),
        pltpu.VMEM((kv_local, HD + ONES, rows), jnp.float32),
    ]
    sems = pltpu.SemaphoreType.DMA((2, capacity))

    def own_part(payload):
        return pl.pallas_call(
            functools.partial(own_kernel, pool_size),
            in_specs=[smem_spec] * 3 + [vmem_spec] * 3 + [hbm_spec] * 2,
            out_specs=[vmem_spec] * 2,
            scratch_shapes=[
                *buffers,
                *[pltpu.VMEM((block_len, kv_width), jnp.bfloat16)] * 2,
                *work,
                sems,
            ],
            out_shape=[
                jax.ShapeDtypeStruct((kv_width, rows), jnp.float32),
                jax.ShapeDtypeStruct((8, rows), jnp.float32),
            ],
            compiler_params=params,
            cost_estimate=cost(8),
            name="own_part",
        )(*tables, payload, new_keys[0], new_values[0], store_keys, store_values)

    def other_part(partners, held, *request, share=8, moved=(), raw=False):
        if raw:
            out_shape = [
                jax.ShapeDtypeStruct((kv_local, HD + ONES, rows), jnp.float32),
                jax.ShapeDtypeStruct((kv_local, 8, rows), jnp.float32),
                jax.ShapeDtypeStruct((held[0].shape[0] - kv_width, rows), jnp.bfloat16),
            ]
        else:
            out_shape = jax.ShapeDtypeStruct((kv_width + ONES, rows), jnp.bfloat16)
        more_specs = [hbm_spec] * 3 if moved else []
        return pl.pallas_call(
            functools.partial(other_kernel, pool_size, new_rows, partners, bool(moved), raw),
            in_specs=[smem_spec] * (3 + len(request))
            + [hbm_spec] * len(held)
            + more_specs
            + [hbm_spec] * 2,
            out_specs=[hbm_spec] * 3 if raw else hbm_spec,
            scratch_shapes=[
                *buffers,
                *work,
                pltpu.VMEM((kv_width, rows), jnp.bfloat16),
                pltpu.SemaphoreType.DMA,
                pltpu.VMEM((kv_width + ONES, rows), jnp.bfloat16),
                pltpu.SemaphoreType.DMA((max(3, kv_local + 1),)),
                sems,
            ],
            out_shape=out_shape,
            compiler_params=params,
            cost_estimate=cost(share),
            name="other_part",
        )(*request, *tables, *held, *moved, store_keys, store_values)

    def combine(own, log, sources, parts, last=True):
        if last:
            out_shape = jax.ShapeDtypeStruct((new_rows, width), jnp.bfloat16)
        else:
            out_shape = [
                jax.ShapeDtypeStruct((kv_width, rows), jnp.float32),
                jax.ShapeDtypeStruct((8, rows), jnp.float32),
            ]
        return pl.pallas_call(
            functools.partial(combine_kernel, tuple(sources), last),
            in_specs=[vmem_spec] * (2 + len(parts)),
            out_specs=vmem_spec if last else [vmem_spec] * 2,
            scratch_shapes=[pltpu.VMEM((rows, HD), jnp.bfloat16)] if last else [],
            out_shape=out_shape,
            compiler_params=params,
            cost_estimate=cost(0),
            name="combine",
        )(own, log, *parts)

    def final(own, log, parts):
        return pl.pallas_call(
            final_kernel,
            in_specs=[hbm_spec, vmem_spec, hbm_spec, hbm_spec],
            out_specs=hbm_spec,
            scratch_shapes=[
                pltpu.VMEM((kv_width, rows), jnp.float32),
                pltpu.VMEM((kv_width + ONES, rows), jnp.bfloat16),
                pltpu.VMEM((new_rows, width), jnp.bfloat16),
                pltpu.VMEM((rows, HD), jnp.bfloat16),
                pltpu.SemaphoreType.DMA((3, kv_local + 1)),
            ],
            out_shape=jax.ShapeDtypeStruct((new_rows, width), jnp.bfloat16),
            compiler_params=params,
            name="final",
        )(own, log, *parts)

    payload = pl.pallas_call(
        prepare_kernel,
        in_specs=[vmem_spec] * 3,
        out_specs=vmem_spec,
        scratch_shapes=[pltpu.VMEM((rows, HD), jnp.bfloat16)],
        out_shape=jax.ShapeDtypeStruct((payload_rows(new_rows, kv_width), rows), jnp.bfloat16),
        compiler_params=params,
        name="prepare",
    )(queries[0], new_keys[0], new_values[0])
    own_out, own_log = own_part(payload)
    if pool_size == 4:
        def send(array, *pairs):
            return lax.ppermute(array, "pool", pairs)

        near = send(payload, (0, 1), (1, 0), (2, 3), (3, 2))
        middle = send(payload, (1, 2), (2, 1))
        blocks = pl.pallas_call(
            functools.partial(gather_kernel, pool_size),
            in_specs=[smem_spec] * 3 + [hbm_spec] * 2,
            out_specs=vmem_spec,
            scratch_shapes=[sems],
            out_shape=jax.ShapeDtypeStruct((2 * capacity, block_len, kv_width), jnp.bfloat16),
            compiler_params=params,
            name="gather_blocks",
        )(*tables, store_keys, store_values)
        blocks = send(blocks, (0, 1), (3, 2))
        near, middle, own_out, own_log = lax.optimization_barrier((near, middle, own_out, own_log))
        crossed = send(near, (1, 2), (2, 1))
        outward = send(middle, (1, 0), (2, 3))
        first = other_part((3, 1), (middle, near))
        near, first = lax.optimization_barrier((near, first))
        second = other_part((1, None), (near,))
        first, second = lax.optimization_barrier((first, second))
        across = send(first, (1, 2), (2, 1))
        back = send(second, (1, 0), (2, 3))
        outward, second = lax.optimization_barrier((outward, second))
        outer_second = other_part((None, 2), (outward,))
        apart = send(outer_second, (0, 2), (3, 1))
        crossed, first, outer_second = lax.optimization_barrier((crossed, first, outer_second))
        inward = send(first, (0, 1), (3, 2))
        *state, fresh = other_part((2, None), (crossed,), raw=True)
        crossed, state = lax.optimization_barrier((crossed, state))
        far = send(fresh, (1, 0), (2, 3))
        third = other_part((2, None), (crossed,), moved=(blocks, *state))
        ends = send(third, (1, 3), (2, 0))
        own_out, own_log, third = lax.optimization_barrier((own_out, own_log, third))
        own_out, own_log = combine(
            own_out, own_log, [(3, None), (2, None), (None, 1)], [across, apart, back], last=False
        )
        attended = final(own_out, own_log, (ends, inward))
        moved = [
            ((0, 0), payload),
            ((1, 1), near),
            ((3, None), middle),
            ((2, None), crossed),
            ((None, 2), outward),
            ((None, 3), far),
        ]
    else:
        gathered = lax.all_gather(payload, "pool", axis=0, tiled=False)
        packed = lax.map(
            lambda pair: other_part(None, (pair[0],), pair[1].reshape(1)),
            (gathered, jnp.arange(pool_size, dtype=jnp.int32)),
        )
        parts = lax.all_to_all(packed, "pool", split_axis=0, concat_axis=0, tiled=True)
        attended = combine(own_out, own_log, list(range(pool_size)), parts)
        moved = [(source, gathered[source]) for source in range(pool_size)]

    pushed_keys, pushed_values = pl.pallas_call(
        functools.partial(push_kernel, pool_size, tuple(entry for entry, _ in moved)),
        in_specs=[smem_spec] + [hbm_spec] * len(moved),
        out_specs=[vmem_spec] * 2,
        scratch_shapes=[pltpu.SemaphoreType.DMA((2, CAPP, new_rows // PIECE))],
        out_shape=[jax.ShapeDtypeStruct((CAPP, new_rows, kv_width), jnp.bfloat16)] * 2,
        compiler_params=params,
        name="push",
    )(decode_owner, *[array for _, array in moved])
    return (attended[None], pushed_keys, pushed_values)


def solution(mesh):
    in_specs = (
        P(("groups", "pool"), None, ("tensor", "sub")),
        P(("groups", "pool"), None, ("tensor", "sub")),
        P(("groups", "pool"), None, ("tensor", "sub")),
        P(("groups", "pool"), None, ("tensor", "sub")),
        P(("groups", "pool"), None, ("tensor", "sub")),
        P("groups"),
        P("groups", None),
        P("groups", None),
        P("groups"),
    )
    out_specs = (
        P(("groups", "pool"), None, ("tensor", "sub")),
        P(("groups", "pool"), None, ("tensor", "sub")),
        P(("groups", "pool"), None, ("tensor", "sub")),
    )
    return jax.shard_map(shards, mesh=mesh, in_specs=in_specs, out_specs=out_specs, check_vma=False)
```
